32 devices in a mesh: shard: 16 (over z, x, core), rep: 2 (over y).
Axes of the slice: x: 2, y: 2, z: 4, core: 2. Of those that a mesh axis runs over, the one named last changes fastest.
Arguments:
- tokens: bfloat16 [64, 320, 1024], P(('shard', 'rep')), may hold values from -6 to 6
- kept: int32 [64], P(('shard', 'rep')), may hold values from 1 to 256, as said below
- attn_gain: bfloat16 [2, 1024], P(None, 'shard'), may hold values from 0.25 to 1.75
- attn_shift: bfloat16 [2, 1024], P(None, 'shard'), may hold values from -1.75 to 1.75
- qkv_weight: bfloat16 [2, 1024, 3072], P(None, 'shard'), may hold values from -0.1875 to 0.1875
- qv_bias: bfloat16 [2, 2048], P(None, 'shard'), may hold values from -1.75 to 1.75
- proj_weight: bfloat16 [2, 1024, 1024], P(None, 'shard'), may hold values from -1.5 to 1.5
- proj_bias: bfloat16 [2, 1024], P(None, 'shard'), may hold values from -1.75 to 1.75
- mlp_gain: bfloat16 [2, 1024], P(None, 'shard'), may hold values from 0.25 to 1.75
- mlp_shift: bfloat16 [2, 1024], P(None, 'shard'), may hold values from -1.75 to 1.75
- fc1_weight: bfloat16 [2, 1024, 4096], P(None, 'shard'), may hold values from -0.1875 to 0.1875
- fc1_bias: bfloat16 [2, 4096], P(None, 'shard'), may hold values from -1.75 to 1.75
- fc2_weight: bfloat16 [2, 4096, 1024], P(None, 'shard'), may hold values from -0.125 to 0.125
- fc2_bias: bfloat16 [2, 1024], P(None, 'shard'), may hold values from -1.75 to 1.75
- cotangent: bfloat16 [64, 320, 1024], P(('shard', 'rep')), may hold values from -6 to 6
Outputs:
- mixed: bfloat16 [64, 320, 1024], P(('shard', 'rep'))
- tokens_grad: float32 [64, 320, 1024], P(('shard', 'rep'))
- attn_gain_grad: float32 [2, 1024], P(None, 'shard')
- attn_shift_grad: float32 [2, 1024], P(None, 'shard')
- qkv_weight_grad: float32 [2, 1024, 3072], P(None, 'shard')
- qv_bias_grad: float32 [2, 2048], P(None, 'shard')
- proj_weight_grad: float32 [2, 1024, 1024], P(None, 'shard')
- proj_bias_grad: float32 [2, 1024], P(None, 'shard')
- mlp_gain_grad: float32 [2, 1024], P(None, 'shard')
- mlp_shift_grad: float32 [2, 1024], P(None, 'shard')
- fc1_weight_grad: float32 [2, 1024, 4096], P(None, 'shard')
- fc1_bias_grad: float32 [2, 4096], P(None, 'shard')
- fc2_weight_grad: float32 [2, 4096, 1024], P(None, 'shard')
- fc2_bias_grad: float32 [2, 1024], P(None, 'shard')
The draws below stay inside these ranges and needn't reach their ends.
Inputs may be any that keep to these rules, and one draw needn't show every extreme that they name: kept[i] image slots of image i are live after its 64 buffer slots; some image keeps all 256.
All inputs are finite; a program needn't handle non-finite values.
Results may differ from the reference program's by a relative error of at most 0.018.
Values may be sent and summed in bfloat16 or wider, within the bound.
No kernel may reach another device: no remote copies, remote signals or barrier semaphores. Data moves between devices by JAX's collectives and lax.ppermute only.
A program may use at most 320 MiB of HBM per device.

```python
import math
from functools import partial
import jax
import jax.numpy as jnp
from jax import lax

D = 1024
HEADS = 16
HEAD_DIM = 64
FF = 4096
BUFFER = 64
PATCHES = 256
LAYERS = 2
SLOTS = 320
IMAGES = 64


def draw_kept(key, part):
    key = jax.random.fold_in(key, 5)
    count_key, full_key = jax.random.split(key)
    counts = jax.random.randint(count_key, (IMAGES,), 1, PATCHES + 1)
    chosen = jax.random.randint(full_key, (), 0, IMAGES)
    return jnp.where(jnp.arange(IMAGES) == chosen, PATCHES, counts).astype(jnp.int32)


def shard_levels(rng, extent, cuts, least, high):
    level = 1.0
    for axis_at, parts in cuts:
        heights = jax.random.uniform(jax.random.fold_in(jax.random.fold_in(rng, 6), axis_at), (parts,), jnp.float32, least / len(cuts), high / len(cuts))
        level = level * jnp.repeat(jnp.exp(heights), extent[axis_at] // parts).reshape((-1,) + (1,) * (len(extent) - 1 - axis_at))
    return level


def normal_values(stream_key, shape, deviation, bound, cuts=(), dtype=jnp.bfloat16):
    values = deviation * jax.random.normal(stream_key, shape, jnp.float32)
    if cuts:
        values = values * shard_levels(stream_key, shape, cuts, -0.22, 0.18)
    return jnp.clip(values, -bound, bound).astype(dtype)


def setup_inputs(seed: int = 0) -> dict:
    keys = jax.random.split(jax.random.key(seed), 16)
    return {
        "tokens": normal_values(keys[0], (IMAGES, SLOTS, D), 1.0, 6.0, ((0, 32),)),
        "kept": draw_kept(jax.random.fold_in(keys[15], 71), 0),
        "attn_gain": jnp.clip(1.0 + 0.15 * jax.random.normal(keys[2], (LAYERS, D), jnp.float32), 0.25, 1.75).astype(jnp.bfloat16),
        "attn_shift": normal_values(keys[3], (LAYERS, D), 0.3, 1.75, ((1, 16),)),
        "qkv_weight": normal_values(keys[4], (LAYERS, D, 3 * D), D ** -0.5, 0.1875, ((1, 16),)),
        "qv_bias": normal_values(keys[5], (LAYERS, 2 * D), 0.3, 1.75, ((1, 16),)),
        "proj_weight": normal_values(keys[6], (LAYERS, D, D), (D // 64) ** -0.5, 1.5, ((1, 16),)),
        "proj_bias": normal_values(keys[7], (LAYERS, D), 0.3, 1.75, ((1, 16),)),
        "mlp_gain": jnp.clip(1.0 + 0.15 * jax.random.normal(keys[8], (LAYERS, D), jnp.float32), 0.25, 1.75).astype(jnp.bfloat16),
        "mlp_shift": normal_values(keys[9], (LAYERS, D), 0.3, 1.75, ((1, 16),)),
        "fc1_weight": normal_values(keys[10], (LAYERS, D, FF), D ** -0.5, 0.1875, ((1, 16),)),
        "fc1_bias": normal_values(keys[11], (LAYERS, FF), 0.3, 1.75, ((1, 16),)),
        "fc2_weight": normal_values(keys[12], (LAYERS, FF, D), (FF // 2) ** -0.5, 0.125, ((1, 16),)),
        "fc2_bias": normal_values(keys[13], (LAYERS, D), 0.3, 1.75, ((1, 16),)),
        "cotangent": normal_values(keys[14], (IMAGES, SLOTS, D), 1.0, 6.0, ((0, 32),)),
    }


EPS = 1e-06
HIGH = lax.Precision.HIGHEST

@jax.custom_vjp
def low(v):
    return lax.optimization_barrier(v.astype(jnp.bfloat16)).astype(jnp.float32)

@jax.custom_vjp
def low_back(v):
    return v

def low_keep(v):
    return (low(v), None)

def low_pass(kept, grad):
    return (grad,)

def back_keep(v):
    return (v, None)

def back_low(kept, grad):
    return (low(grad),)
low.defvjp(low_keep, low_pass)
low_back.defvjp(back_keep, back_low)

def both_ways(value):
    return low_back(low(value))

def layer_norm(rows, gain, shift):
    mean = lax.optimization_barrier(jnp.mean(rows, axis=-1, keepdims=True))
    centered = rows - mean
    spread = lax.optimization_barrier(jnp.mean(centered * centered, axis=-1, keepdims=True))
    return centered * lax.rsqrt(spread + EPS) * gain + shift

def encoder_layer(state, live, weights):
    attn_gain, attn_shift, qkv_weight, qv_bias, proj_weight, proj_bias, mlp_gain, mlp_shift, fc1_weight, fc1_bias, fc2_weight, fc2_bias = weights
    images, slots, width = state.shape
    rows = state.reshape(images * slots, width)
    first = low(layer_norm(rows, attn_gain, attn_shift))
    full_bias = jnp.concatenate([qv_bias[:width], jnp.zeros((width,), jnp.float32), qv_bias[width:]])
    projected = both_ways(jnp.dot(first, qkv_weight, precision=HIGH) + full_bias)
    split_view = projected.reshape(images, slots, 3, HEADS, HEAD_DIM)
    queries = split_view[:, :, 0]
    keys_part = split_view[:, :, 1]
    values = split_view[:, :, 2]
    scale = HEAD_DIM ** (-0.5)
    scores = low_back(jnp.einsum('bqhe,bkhe->bhqk', queries, keys_part, precision=HIGH) * scale)
    scores = jnp.where(live[:, None, None, :], scores, -1e+30)
    peak = lax.optimization_barrier(jnp.max(scores, axis=-1, keepdims=True))
    expo = jnp.exp(scores - peak)
    probs = low(expo / lax.optimization_barrier(jnp.sum(expo, axis=-1, keepdims=True)))
    attended = jnp.einsum('bhqk,bkhe->bqhe', probs, values, precision=HIGH)
    attended = both_ways(attended.reshape(images * slots, width))
    middle = rows + low_back(jnp.dot(attended, proj_weight, precision=HIGH) + proj_bias)
    second = low(layer_norm(middle, mlp_gain, mlp_shift))
    pre = low_back(jnp.dot(second, fc1_weight, precision=HIGH) + fc1_bias)
    hidden = low(jax.nn.gelu(pre, approximate=False))
    output = middle + low_back(jnp.dot(hidden, fc2_weight, precision=HIGH) + fc2_bias)
    return output.reshape(images, slots, width)

def run_blocks(weights, tokens, live):
    state = tokens
    for layer in range(LAYERS):
        state = encoder_layer(state, live, tuple((w[layer] for w in weights)))
    return jnp.where(live[:, :, None], state, 0.0)

def reference(tokens, kept, attn_gain, attn_shift, qkv_weight, qv_bias, proj_weight, proj_bias, mlp_gain, mlp_shift, fc1_weight, fc1_bias, fc2_weight, fc2_bias, cotangent):
    weights = tuple((w.astype(jnp.float32) for w in (attn_gain, attn_shift, qkv_weight, qv_bias, proj_weight, proj_bias, mlp_gain, mlp_shift, fc1_weight, fc1_bias, fc2_weight, fc2_bias)))
    group = math.gcd(IMAGES, 8)
    count = IMAGES // group
    token_groups = tokens.astype(jnp.float32).reshape(count, group, SLOTS, D)
    kept_groups = kept.reshape(count, group)
    cot_groups = cotangent.astype(jnp.float32).reshape(count, group, SLOTS, D)

    def step(totals, item):
        token_part, kept_part, cot_part = item
        slot_index = lax.broadcasted_iota(jnp.int32, (group, SLOTS), 1)
        live = slot_index < BUFFER + kept_part[:, None].astype(jnp.int32)
        result, pullback = jax.vjp(partial(run_blocks, live=live), weights, token_part)
        weight_grads, token_grads = pullback(cot_part)
        totals = jax.tree.map(jnp.add, totals, weight_grads)
        return (totals, (result.astype(jnp.bfloat16), token_grads))
    zeros = tuple((jnp.zeros_like(w) for w in weights))
    totals, (mixed, token_grads) = lax.scan(step, zeros, (token_groups, kept_groups, cot_groups))
    mixed = mixed.reshape(IMAGES, SLOTS, D)
    token_grads = token_grads.reshape(IMAGES, SLOTS, D)
    return (mixed, token_grads, totals[0], totals[1], totals[2], totals[3], totals[4], totals[5], totals[6], totals[7], totals[8], totals[9], totals[10], totals[11])
```

```python
from functools import partial

import jax
import jax.numpy as jnp
from jax import lax
from jax.experimental import pallas as pl
from jax.experimental.pallas import tpu as pltpu
from jax.sharding import PartitionSpec as P

HEADS = 16
HEAD_DIM = 64
BUFFER = 64
EPS = 1e-06
SCALE = HEAD_DIM ** (-0.5)
AX = ("shard", "rep")
BF = jnp.bfloat16
F32 = jnp.float32
LIMIT = 56 * 2**20
SMALL = ("ag", "as", "qvb", "pb", "mg", "ms", "f1b", "f2b")


class Plan:
    def __init__(self, mesh):
        self.shards = mesh.shape["shard"]
        self.rep = mesh.shape["rep"]
        self.chips = self.shards // 2
        self.ny = 2 if self.rep == 2 else 1
        self.bits = self.chips.bit_length() - 1

    def swap(self, v, flip_shard, flip_rep=0):
        pairs = []
        for s in range(self.shards):
            for y in range(self.rep):
                pairs.append((s * self.rep + y, (s ^ flip_shard) * self.rep + (y ^ flip_rep)))
        return lax.ppermute(v, AX, pairs)

    def core(self, v):
        return self.swap(v, 1)

    def flip(self, v, axis):
        if axis == 0:
            return self.swap(v, 0, 1)
        return self.swap(v, 2 << (self.bits - axis))


def dot(x, w):
    return lax.dot_general(x, w, (((1,), (0,)), ((), ())), preferred_element_type=F32)


def dot_t(x, w):
    return lax.dot_general(x, w, (((1,), (1,)), ((), ())), preferred_element_type=F32)


def t_dot(x, w):
    return lax.dot_general(x, w, (((0,), (0,)), ((), ())), preferred_element_type=F32)


def columns(width, first):
    return ("columns", width, first)


def row_call(body, where, kept, gathered, picks, blocked, whole, outs, images, slots, flops=0):
    in_specs, args = [], []
    for kind, width, first in picks:
        if kind == "columns":
            depth = gathered.shape[0]
            in_specs.append(pl.BlockSpec((depth, width), lambda i, w, k, f=first: (0, f + w[0])))
            args.append(gathered)
        else:
            view = gathered.reshape(HEADS // 2, 2, HEAD_DIM, gathered.shape[1])
            in_specs.append(pl.BlockSpec((HEADS // 2, None, HEAD_DIM, width), lambda i, w, k, f=first: (0, w[0], 0, f)))
            args.append(view)
    for v in blocked:
        if v.ndim == 2:
            in_specs.append(pl.BlockSpec((slots, v.shape[1]), lambda i, *_: (i, 0)))
        else:
            in_specs.append(pl.BlockSpec((1,) + v.shape[1:], lambda i, *_, n=v.ndim: (i,) + (0,) * (n - 1)))
        args.append(v)
    for v in whole:
        in_specs.append(pl.BlockSpec(v.shape, lambda i, *_, n=v.ndim: (0,) * n))
        args.append(v)
    out_specs, out_shape = [], []
    for kind, shape, dtype in outs:
        out_shape.append(jax.ShapeDtypeStruct(shape, dtype))
        if kind == "rows":
            out_specs.append(pl.BlockSpec((slots, shape[1]), lambda i, *_: (i, 0)))
        elif kind == "image":
            out_specs.append(pl.BlockSpec((1,) + shape[1:], lambda i, *_, n=len(shape): (i,) + (0,) * (n - 1)))
        else:
            out_specs.append(pl.BlockSpec(shape, lambda i, *_, n=len(shape): (0,) * n))
    n_p, n_b, n_in = len(picks), len(blocked), len(args)

    def kernel(where_ref, kept_ref, *refs):
        ins, res = refs[:n_in], refs[n_in:]
        body(kept_ref, ins[:n_p], ins[n_p : n_p + n_b], ins[n_p + n_b :], res)

    return pl.pallas_call(
        kernel,
        grid_spec=pltpu.PrefetchScalarGridSpec(
            num_scalar_prefetch=2, grid=(images,), in_specs=in_specs, out_specs=out_specs
        ),
        out_shape=out_shape,
        compiler_params=pltpu.CompilerParams(vmem_limit_bytes=LIMIT),
        cost_estimate=pl.CostEstimate(
            flops=flops, bytes_accessed=sum(v.size * v.dtype.itemsize for v in args[n_p:]), transcendentals=0
        ),
    )(where, kept, *args)


def normed_of(rows):
    width = rows.shape[-1]
    mean = jnp.sum(rows, axis=-1, keepdims=True) * (1.0 / width)
    centered = rows - mean
    spread = jnp.sum(centered * centered, axis=-1, keepdims=True) * (1.0 / width)
    factor = lax.rsqrt(spread + EPS)
    return centered * factor, factor


def norm_rows(rows, gain, shift):
    return normed_of(rows)[0] * gain + shift


def norm_back(dz, rows, gain):
    normed, factor = normed_of(rows)
    width = rows.shape[-1]
    prod = dz * normed
    dn = dz * gain
    m1 = jnp.sum(dn, axis=-1, keepdims=True) * (1.0 / width)
    m2 = jnp.sum(dn * normed, axis=-1, keepdims=True) * (1.0 / width)
    back = factor * (dn - m1 - normed * m2)
    return back, jnp.sum(prod, axis=0, keepdims=True), jnp.sum(dz, axis=0, keepdims=True)


def chunks(total, size):
    size = min(size, total)
    return [(k, size) for k in range(0, total, size)]


def qkv_body(kept, w, blocked, whole, outs):
    x = blocked[0][...]
    for k, n in chunks(outs[0].shape[1], 512):
        cols = pl.ds(k, n)
        outs[0][:, cols] = (dot(x, w[0][:, cols]) + whole[0][:, cols]).astype(BF)


def heads_of(ref):
    return ref[...].reshape(-1, ref.shape[-1])


def pairs_dot(x_ref, w_ref):
    depth = w_ref.shape[0]
    total = None
    for k in range(0, w_ref.shape[1], depth):
        term = dot(x_ref[:, k : k + depth], w_ref[:, k : k + depth])
        total = term if total is None else total + term
    return total


def attend(kept, proj_ref, probs_ref, att_ref):
    slots, third = proj_ref.shape[0], proj_ref.shape[1] // 3
    bound = BUFFER + kept[pl.program_id(0)]
    alive = lax.broadcasted_iota(jnp.int32, (slots, slots), 1) < bound
    outs = []
    for h in range(third // HEAD_DIM):
        lo = h * HEAD_DIM
        q = proj_ref[:, lo : lo + HEAD_DIM]
        k = proj_ref[:, third + lo : third + lo + HEAD_DIM]
        v = proj_ref[:, 2 * third + lo : 2 * third + lo + HEAD_DIM]
        s = jnp.where(alive, dot_t(q, k) * SCALE, -1e30)
        e = jnp.exp(s - jnp.max(s, axis=-1, keepdims=True))
        p = (e * (1.0 / jnp.sum(e, axis=-1, keepdims=True))).astype(BF)
        probs_ref[0, h] = p
        outs.append(dot(p, v).astype(BF))
        if h % 2:
            att_ref[:, lo - HEAD_DIM : lo + HEAD_DIM] = jnp.concatenate(outs, axis=1)
            outs = []


def attend_other(kept, w, blocked, whole, outs):
    attend(kept, blocked[0], outs[0], outs[1])
    outs[2][...] = dot(outs[1][...], heads_of(w[0]))


def attend_own(kept, w, blocked, whole, outs):
    attend(kept, blocked[0], outs[0], outs[1])
    middle = blocked[2][...] + (dot(outs[1][...], heads_of(w[0])) + blocked[1][...]) + whole[0][...]
    outs[2][...] = middle
    outs[3][...] = norm_rows(middle, whole[1][...], whole[2][...]).astype(BF)


def up_body(kept, w, blocked, whole, outs):
    x = blocked[0][...]
    for k, n in chunks(outs[0].shape[1], 256):
        cols = pl.ds(k, n)
        pre = dot(x, w[0][:, cols]) + whole[0][:, cols]
        phi = 0.5 + 0.5 * lax.erf(pre * (2.0**-0.5))
        dens = jnp.exp(-0.5 * (pre * pre)) * 0.3989422804014327
        outs[0][:, cols] = (pre * phi).astype(BF)
        outs[1][:, cols] = (phi + pre * dens).astype(BF)


def down_other(kept, w, blocked, whole, outs):
    outs[0][...] = pairs_dot(blocked[0], w[0])


def down_own(kept, w, blocked, whole, outs):
    state = blocked[2][...] + (pairs_dot(blocked[0], w[0]) + blocked[1][...]) + whole[0][...]
    outs[0][...] = state
    outs[1][...] = norm_rows(state, whole[1][...], whole[2][...]).astype(BF)


def down_last(kept, w, blocked, whole, outs):
    state = blocked[2][...] + (pairs_dot(blocked[0], w[0]) + blocked[1][...]) + whole[0][...]
    alive = lax.broadcasted_iota(jnp.int32, state.shape, 0) < BUFFER + kept[pl.program_id(0)]
    outs[0][...] = jnp.where(alive, state, 0.0).astype(BF)


def mlp_back(w, blocked, outs):
    low = blocked[0][...]
    depth = w[0].shape[0]
    for k, n in chunks(outs[0].shape[1], 512):
        cols = pl.ds(k, n)
        block = k // depth * depth
        t = dot_t(low, w[0][pl.ds(k - block, n), block : block + depth])
        outs[0][:, cols] = (t * blocked[1][:, cols].astype(F32)).astype(BF)
    return dot_t(outs[0][...], w[1][...])


def mlp_back_other(kept, w, blocked, whole, outs):
    outs[1][...] = mlp_back(w, blocked, outs)


def add_sums(ref, rows):
    sums = jnp.concatenate(rows + [jnp.zeros((8 - len(rows), rows[0].shape[1]), F32)], axis=0)

    @pl.when(pl.program_id(0) == 0)
    def _():
        ref[...] = sums

    @pl.when(pl.program_id(0) != 0)
    def _():
        ref[...] += sums


def mlp_back_own(kept, w, blocked, whole, outs):
    dz = mlp_back(w, blocked, outs) + blocked[2][...]
    back, gain, shift = norm_back(dz, blocked[3][...], whole[0][...])
    grad = blocked[4][...] + back
    low = grad.astype(BF)
    outs[1][...] = grad
    outs[2][...] = low
    add_sums(outs[3], [gain, shift, jnp.sum(low.astype(F32), axis=0, keepdims=True)])


def attend_back(w, blocked, outs):
    branch, proj_ref, probs_ref = blocked[0], blocked[1], blocked[2]
    third = proj_ref.shape[1] // 3
    datt = dot_t(branch[...], heads_of(w[0])).astype(BF)
    pairs = [[], [], []]
    for h in range(third // HEAD_DIM):
        lo = h * HEAD_DIM
        q = proj_ref[:, lo : lo + HEAD_DIM]
        k = proj_ref[:, third + lo : third + lo + HEAD_DIM]
        v = proj_ref[:, 2 * third + lo : 2 * third + lo + HEAD_DIM]
        da = datt[:, lo : lo + HEAD_DIM]
        p = probs_ref[0, h]
        dp = dot_t(da, v)
        pf = p.astype(F32)
        ds = (pf * (dp - jnp.sum(pf * dp, axis=-1, keepdims=True))).astype(BF)
        pairs[0].append((dot(ds, k) * SCALE).astype(BF))
        pairs[1].append((t_dot(ds, q) * SCALE).astype(BF))
        pairs[2].append(t_dot(p, da).astype(BF))
        if h % 2:
            for j in range(3):
                at = j * third + lo - HEAD_DIM
                outs[0][:, at : at + 2 * HEAD_DIM] = jnp.concatenate(pairs[j], axis=1)
            pairs = [[], [], []]
    return dot_t(outs[0][...], w[1][...])


def attend_back_other(kept, w, blocked, whole, outs):
    outs[1][...] = attend_back(w, blocked, outs)


def attend_back_own(kept, w, blocked, whole, outs):
    dz = attend_back(w, blocked, outs) + blocked[3][...]
    back, gain, shift = norm_back(dz, blocked[4][...], whole[0][...])
    grad = blocked[5][...] + back
    outs[1][...] = grad
    low = grad.astype(BF)
    outs[2][...] = low
    add_sums(outs[3], [gain, shift, jnp.sum(low.astype(F32), axis=0, keepdims=True)])


def weight_grad(plan, where, xs, ys, groups, first, sums):
    depth, n_x = xs[0].shape
    cols = ys[0].shape[1]
    ny, chips, bits = plan.ny, plan.chips, plan.bits
    half = cols // ny
    chunk = half if half <= 768 else 512
    steps = half // chunk
    rows = n_x // chips
    part = rows // groups
    dims = [ny] + [2] * bits
    dims[first] = 1
    block = [1] + dims[1:] + [rows, chunk]
    shape = dims + [rows, half]

    def kernel(where_ref, xo, xt, yo, yt, *rest):
        keep, send = rest[0], rest[1]
        flip, acc = rest[-2], rest[-1]
        step = pl.program_id(0)

        @pl.when(step == 0)
        def _():
            flip[:, :depth] = xo[...].T
            flip[:, depth:] = xt[...].T

        acc[...] = dot(flip[:, :depth], yo[...]) + dot(flip[:, depth:], yt[...])
        if sums:
            rest[2][...] = jnp.sum(yo[...].astype(F32), axis=0, keepdims=True) + jnp.sum(
                yt[...].astype(F32), axis=0, keepdims=True
            )

        def put(ref, r):
            at = [0]
            for k in range(1, bits + 1):
                at.append((r >> (bits - k)) & 1 if k != first else 0)
            chip = jnp.bitwise_xor(where_ref[1], r)
            for g in range(groups):
                start = pl.multiple_of(g * part * chips + chip * part, 16)
                ref[tuple(at) + (pl.ds(g * part, part),)] = acc[pl.ds(start, part)].astype(BF)

        if first:
            for r in range(chips):
                put(send if (r >> (bits - first)) & 1 else keep, r)
        else:

            @pl.when(step < steps)
            def _():
                for r in range(chips):
                    put(keep, r)

            @pl.when(step >= steps)
            def _():
                for r in range(chips):
                    put(send, r)

    def column(i, w):
        if ny == 1:
            return i
        return jnp.bitwise_xor(i // steps, w[2]) * steps + i % steps

    zeros = (0,) * (bits + 1)
    x_spec = pl.BlockSpec((depth, n_x), lambda i, w: (0, 0))
    y_spec = pl.BlockSpec((depth, chunk), lambda i, w: (0, column(i, w)))
    if first:
        specs = [pl.BlockSpec(block, lambda i, w: (i // steps,) + zeros + (i % steps,))] * 2
    else:
        specs = [
            pl.BlockSpec(block, lambda i, w: (0,) + zeros + (jnp.minimum(i, steps - 1),)),
            pl.BlockSpec(block, lambda i, w: (0,) + zeros + (jnp.maximum(i - steps, 0),)),
        ]
    out_shape = [jax.ShapeDtypeStruct(shape, BF)] * 2
    if sums:
        specs = specs + [pl.BlockSpec((1, chunk), lambda i, w: (0, column(i, w)))]
        out_shape = out_shape + [jax.ShapeDtypeStruct((1, cols), F32)]
    return pl.pallas_call(
        kernel,
        grid_spec=pltpu.PrefetchScalarGridSpec(
            num_scalar_prefetch=1,
            grid=(ny * steps,),
            in_specs=[x_spec, x_spec, y_spec, y_spec],
            out_specs=specs,
            scratch_shapes=[pltpu.VMEM((n_x, 2 * depth), BF), pltpu.VMEM((n_x, chunk), F32)],
        ),
        out_shape=out_shape,
        compiler_params=pltpu.CompilerParams(vmem_limit_bytes=LIMIT),
        cost_estimate=pl.CostEstimate(
            flops=4 * depth * n_x * cols, bytes_accessed=2 * (2 * depth * (n_x + cols) + n_x * cols), transcendentals=0
        ),
    )(where, *xs, *ys)


def sum_over(plan, keep, send, axes):
    for at, axis in enumerate(axes):
        got = plan.flip(send, axis)
        total = keep.astype(F32) + got.astype(F32)
        if at + 1 == len(axes):
            return total.reshape(total.shape[-2:])
        after = axes[at + 1]
        send = lax.slice_in_dim(total, 1, 2, axis=after).astype(BF)
        keep = lax.slice_in_dim(total, 0, 1, axis=after).astype(BF)


def pick(flag, a, b):
    return jnp.where(flag == 0, a, b)


def join_core(plan, v, c, groups):
    rows, cols = v.shape
    v = v.reshape(groups, 2, rows // groups // 2, cols)
    mine = pick(c, v[:, 0], v[:, 1]).astype(BF)
    got = plan.core(pick(c, v[:, 1], v[:, 0]).astype(BF))
    return jnp.stack([pick(c, mine, got), pick(c, got, mine)])


def join_rep(plan, v, y):
    if plan.ny == 1:
        return lax.psum(v, "rep").astype(F32)[..., None, :]
    got = plan.flip(v, 0)
    return jnp.stack([pick(y, v, got), pick(y, got, v)], axis=-2).astype(F32)


def per_device(
    plan,
    tokens,
    kept,
    attn_gain,
    attn_shift,
    qkv_weight,
    qv_bias,
    proj_weight,
    proj_bias,
    mlp_gain,
    mlp_shift,
    fc1_weight,
    fc1_bias,
    fc2_weight,
    fc2_bias,
    cotangent,
):
    images, slots, width = tokens.shape
    layers = attn_gain.shape[0]
    rows = images * slots
    n = plan.shards
    deep = qkv_weight.shape[1]
    shard = lax.axis_index("shard")
    c, chip, y = lax.rem(shard, 2), shard // 2, lax.axis_index("rep")
    where = jnp.stack([c, chip, y]).astype(jnp.int32)
    ff = fc2_weight.shape[1] * n
    quarters = fc2_weight.shape[1] // deep
    wide, half_width, half_ff = 3 * width // 2, width // 2, ff // 2
    half_heads = HEADS // 2

    small = jnp.concatenate(
        [attn_gain, attn_shift, qv_bias, proj_bias, mlp_gain, mlp_shift, fc1_bias, fc2_bias], axis=1
    )
    sizes = [v.shape[1] for v in (attn_gain, attn_shift, qv_bias, proj_bias, mlp_gain, mlp_shift, fc1_bias, fc2_bias)]
    lines = small.size // 128
    extra = jnp.pad(small.reshape(lines, 128), ((0, deep - lines), (0, 0)))

    def merged(layer):
        qkv = qkv_weight[layer].reshape(deep, 3 * half_heads, 2, HEAD_DIM).swapaxes(1, 2).reshape(deep, 3 * width)
        fc1 = fc1_weight[layer].reshape(deep, n, quarters, deep).swapaxes(1, 2).reshape(deep, ff)
        fc2 = [fc2_weight[layer, k * deep : (k + 1) * deep] for k in range(quarters)]
        return [qkv, proj_weight[layer], fc1] + fc2 + ([] if layer else [extra])

    gathered = [
        lax.all_gather(jnp.concatenate(merged(layer), axis=1), "shard", axis=0, tiled=True) for layer in range(layers)
    ]
    picks = {
        "qkv": columns(wide, 0),
        "proj": ("heads", width, 3),
        "fc1": columns(half_ff, 4 * width // half_ff),
        "fc2": columns(half_ff, (4 * width + ff) // half_ff),
    }

    every = gathered[0].reshape(n, deep, -1)[:, :lines, 4 * width + 2 * ff :]
    every = every.reshape(n, layers, small.shape[1]).astype(F32)
    vecs = []
    for layer in range(layers):
        at, d = 0, {}
        for name, size in zip(SMALL, sizes):
            d[name] = every[:, layer, at : at + size].reshape(1, n * size)
            at += size
        q = d["qvb"].reshape(2 * half_heads, 2, HEAD_DIM)
        q = pick(c, q[:, 0], q[:, 1]).reshape(2, half_width)
        d["qvb_c"] = jnp.stack([q[0], jnp.zeros_like(q[0]), q[1]]).reshape(1, wide)
        f = d["f1b"].reshape(n, quarters, deep).swapaxes(0, 1).reshape(2, half_ff)
        d["f1b_c"] = pick(c, f[0:1], f[1:2])
        vecs.append(d)

    kept_oth = plan.core(kept)
    state = tokens.astype(F32).reshape(rows, width)
    live = lax.broadcasted_iota(jnp.int32, (images, slots), 1) < BUFFER + kept[:, None]
    grad = jnp.where(live[:, :, None], cotangent.astype(F32), 0.0).reshape(rows, width)
    low_own = grad.astype(BF)
    low_oth = plan.core(low_own)
    first_own = norm_rows(state, vecs[0]["ag"], vecs[0]["as"]).astype(BF)

    qkv_flops = 2 * rows * width * wide
    att_flops = 4 * rows * slots * half_width + 2 * rows * half_width * width
    ff_flops = 2 * rows * width * half_ff
    f32_rows, low_rows = ("rows", (rows, width), F32), ("rows", (rows, width), BF)
    wide_rows, ff_rows = ("rows", (rows, wide), BF), ("rows", (rows, half_ff), BF)
    att_outs = [("image", (images, half_heads, slots, slots), BF), ("rows", (rows, half_width), BF)]
    full_sums = ("full", (8, width), F32)

    def call(body, layer, own, names, blocked, whole, outs, flops):
        chosen = [picks[name] for name in names]
        k = kept if own else kept_oth
        return row_call(body, where, k, gathered[layer], chosen, blocked, whole, outs, images, slots, flops)

    saved = []
    mixed = None
    for layer in range(layers):
        v = vecs[layer]
        first_oth = plan.core(first_own)
        proj_oth = call(qkv_body, layer, 0, ["qkv"], [first_oth], [v["qvb_c"]], [wide_rows], qkv_flops)[0]
        probs_oth, att_oth, part = call(attend_other, layer, 0, ["proj"], [proj_oth], [], att_outs + [f32_rows], att_flops)
        part = plan.core(part)
        proj_own = call(qkv_body, layer, 1, ["qkv"], [first_own], [v["qvb_c"]], [wide_rows], qkv_flops)[0]
        probs_own, att_own, middle, second_own = call(
            attend_own, layer, 1, ["proj"], [proj_own, part, state], [v["pb"], v["mg"], v["ms"]], att_outs + [f32_rows, low_rows], att_flops
        )
        second_oth = plan.core(second_own)
        hid_oth, slope_oth = call(up_body, layer, 0, ["fc1"], [second_oth], [v["f1b_c"]], [ff_rows] * 2, ff_flops)
        part = call(down_other, layer, 0, ["fc2"], [hid_oth], [], [f32_rows], ff_flops)[0]
        part = plan.core(part)
        hid_own, slope_own = call(up_body, layer, 1, ["fc1"], [second_own], [v["f1b_c"]], [ff_rows] * 2, ff_flops)
        saved.append(
            dict(
                state=state,
                first=(first_own, first_oth),
                proj=(proj_own, proj_oth),
                probs=(probs_own, probs_oth),
                att=(att_own, att_oth),
                middle=middle,
                second=(second_own, second_oth),
                hid=(hid_own, hid_oth),
                slope=(slope_own, slope_oth),
            )
        )
        if layer + 1 < layers:
            w = vecs[layer + 1]
            state, first_own = call(
                down_own, layer, 1, ["fc2"], [hid_own, part, middle], [v["f2b"], w["ag"], w["as"]], [f32_rows, low_rows], ff_flops
            )
        else:
            mixed = call(down_last, layer, 1, ["fc2"], [hid_own, part, middle], [v["f2b"]], [low_rows], ff_flops)[0]

    axes = list(range(plan.bits + 1)) if plan.ny == 2 else list(range(1, plan.bits + 1))
    x_axis = plan.bits
    z_axes = list(range(plan.bits - 1, 0, -1))
    y_axes = [0] if plan.ny == 2 else []
    order_y = y_axes + [x_axis] + z_axes
    order_x = [x_axis] + z_axes + y_axes
    order_z = z_axes[:1] + y_axes + [x_axis] + z_axes[1:]
    big = [None] * layers
    sums = [None] * layers
    f2b_sum = jnp.sum(low_own.astype(F32), axis=0, keepdims=True)
    mlp_flops = 4 * rows * width * half_ff
    back_flops = 12 * rows * slots * half_width + 2 * rows * width * (wide + half_width)
    for layer in reversed(range(layers)):
        v, s = vecs[layer], saved[layer]
        res2 = weight_grad(plan, where, s["hid"], (low_own, low_oth), 2, order_y[0], False)
        pre_oth, part = call(
            mlp_back_other, layer, 0, ["fc2", "fc1"], [low_oth, s["slope"][1]], [], [ff_rows, f32_rows], mlp_flops
        )
        part = plan.core(part)
        pre_own, mid_grad, branch_own, sum1 = call(
            mlp_back_own,
            layer,
            1,
            ["fc2", "fc1"],
            [low_own, s["slope"][0], part, s["middle"], grad],
            [v["mg"]],
            [ff_rows, f32_rows, low_rows, full_sums],
            mlp_flops,
        )
        branch_oth = plan.core(branch_own)
        res1 = weight_grad(plan, where, s["second"], (pre_own, pre_oth), 1, order_x[0], True)
        dproj_oth, part = call(
            attend_back_other,
            layer,
            0,
            ["proj", "qkv"],
            [branch_oth, s["proj"][1], s["probs"][1]],
            [],
            [wide_rows, f32_rows],
            back_flops,
        )
        part = plan.core(part)
        if n == HEADS:
            resp = weight_grad(plan, where, s["att"], (branch_own, branch_oth), 1, order_y[0], False)
            proj_part = sum_over(plan, *resp, order_y).astype(BF)
            proj_grad = join_rep(plan, proj_part, y).reshape(deep, width)
        else:
            term = t_dot(s["att"][0], branch_own) + t_dot(s["att"][1], branch_oth)
            term = term.astype(BF).reshape(half_heads, HEAD_DIM, width)
            none = jnp.zeros_like(term)
            term = jnp.stack([pick(c, term, none), pick(c, none, term)], axis=1).reshape(width, width)
            term = lax.psum_scatter(term, "shard", scatter_dimension=0, tiled=True)
            proj_grad = lax.psum(term, "rep").astype(F32)
        dproj_own, grad, low_own, sum2 = call(
            attend_back_own,
            layer,
            1,
            ["proj", "qkv"],
            [branch_own, s["proj"][0], s["probs"][0], part, s["state"], mid_grad],
            [v["ag"]],
            [wide_rows, f32_rows, low_rows, full_sums],
            back_flops,
        )
        if layer:
            low_oth = plan.core(low_own)
        resq = weight_grad(plan, where, s["first"], (dproj_own, dproj_oth), 1, order_z[0], True)

        fc2_part = join_rep(plan, join_core(plan, sum_over(plan, *res2, order_y), c, 2), y)
        fc2_grad = fc2_part.reshape(quarters * deep, width)
        fc1_part = join_rep(plan, join_core(plan, sum_over(plan, *res1[:2], order_x), c, 1), y)
        fc1_grad = fc1_part.reshape(2, deep, half_ff).swapaxes(0, 1)
        fc1_grad = fc1_grad.reshape(deep, quarters, n, deep).swapaxes(1, 2).reshape(deep, ff)
        qkv_part = join_rep(plan, join_core(plan, sum_over(plan, *resq[:2], order_z), c, 1), y)
        qkv_grad = qkv_part.reshape(2, deep, 3 * half_heads, HEAD_DIM).transpose(1, 2, 0, 3).reshape(deep, 3 * width)
        big[layer] = (qkv_grad, proj_grad, fc1_grad, fc2_grad)

        q = resq[2].reshape(3, half_heads, 1, HEAD_DIM)
        q = jnp.concatenate([q[:1], q[2:]])
        none = jnp.zeros_like(q)
        q = jnp.concatenate([pick(c, q, none), pick(c, none, q)], axis=2)
        f = res1[2]
        none = jnp.zeros_like(f)
        f = jnp.concatenate([pick(c, f, none), pick(c, none, f)], axis=0)
        f = f.reshape(quarters, n, deep).swapaxes(0, 1)
        full = {"ag": sum2[0], "as": sum2[1], "qvb": q, "pb": sum1[2], "mg": sum1[0], "ms": sum1[1], "f1b": f, "f2b": f2b_sum}
        f2b_sum = sum2[2]
        vec = jnp.concatenate([full[name].reshape(n, -1) for name in SMALL], axis=1)
        vec = vec + plan.core(vec)
        for axis in axes:
            vec = vec + plan.flip(vec, axis)
        if plan.ny == 1:
            vec = lax.psum(vec, "rep")
        sums[layer] = lax.dynamic_slice_in_dim(vec, shard, 1, axis=0)

    vec = jnp.concatenate(sums, axis=0)
    out, at = {}, 0
    for name, size in zip(SMALL, sizes):
        out[name] = vec[:, at : at + size]
        at += size
    qkv_g, proj_g, fc1_g, fc2_g = (jnp.stack([big[layer][k] for layer in range(layers)]) for k in range(4))
    return (
        mixed.reshape(images, slots, width),
        grad.reshape(images, slots, width),
        out["ag"],
        out["as"],
        qkv_g,
        out["qvb"],
        proj_g,
        out["pb"],
        out["mg"],
        out["ms"],
        fc1_g,
        out["f1b"],
        fc2_g,
        out["f2b"],
    )


def solution(mesh):
    rows = P(("shard", "rep"), None, None)
    vec = P(None, "shard")
    mat = P(None, "shard", None)
    return jax.shard_map(
        partial(per_device, Plan(mesh)),
        mesh=mesh,
        in_specs=(rows, P(("shard", "rep")), vec, vec, mat, vec, mat, vec, vec, vec, mat, vec, mat, vec, rows),
        out_specs=(rows, rows, vec, vec, mat, vec, mat, vec, vec, vec, mat, vec, mat, vec),
        check_vma=False,
    )
```

```python
from functools import partial

import jax
import jax.numpy as jnp
from jax import lax
from jax.experimental import pallas as pl
from jax.experimental.pallas import tpu as pltpu
from jax.sharding import PartitionSpec as P

HEADS = 16
HEAD_DIM = 64
BUFFER = 64
EPS = 1e-06
SCALE = HEAD_DIM ** (-0.5)
AX = ("shard", "rep")
BF = jnp.bfloat16
F32 = jnp.float32
LIMIT = 32 * 2**20
ONCE = pl.Buffered(1)
ANY = pl.BlockSpec(memory_space=pl.ANY)
FORWARD = pl.CostEstimate(flops=10**9 * 3, bytes_accessed=0, transcendentals=0)
BACKWARD = pl.CostEstimate(flops=10**9 * 100, bytes_accessed=0, transcendentals=0)
SMALL = ("ag", "as", "qvb", "pb", "mg", "ms", "f1b", "f2b")


class Plan:
    def __init__(self, mesh):
        self.shards = mesh.shape["shard"]
        self.rep = mesh.shape["rep"]
        self.chips = self.shards // 2
        self.ny = 2 if self.rep == 2 else 1
        self.bits = self.chips.bit_length() - 1

    def swap(self, v, flip_shard, flip_rep=0):
        pairs = []
        for s in range(self.shards):
            for y in range(self.rep):
                pairs.append((s * self.rep + y, (s ^ flip_shard) * self.rep + (y ^ flip_rep)))
        return lax.ppermute(v, AX, pairs)

    def core(self, v):
        return self.swap(v, 1)

    def flip(self, v, axis):
        if axis == 0:
            return self.swap(v, 0, 1)
        return self.swap(v, 2 << (self.bits - axis))


def dot(x, w):
    return lax.dot_general(x, w, (((1,), (0,)), ((), ())), preferred_element_type=F32)


def dot_t(x, w):
    return lax.dot_general(x, w, (((1,), (1,)), ((), ())), preferred_element_type=F32)


def t_dot(x, w):
    return lax.dot_general(x, w, (((0,), (0,)), ((), ())), preferred_element_type=F32)


def columns(width, first, stride):
    return ("columns", width, (first, stride))


def row_call(body, where, kept, weights, blocked, whole, outs, images, slots, after=(), cost=FORWARD):
    in_specs, args = [], []
    for v, pick_of in (part for w in weights for part in w):
        if pick_of is None:
            in_specs.append(pl.BlockSpec(v.shape, lambda i, w, k: (0, 0), pipeline_mode=ONCE))
            args.append(v)
            continue
        kind, width, first = pick_of
        if kind == "columns":
            spec = pl.BlockSpec((v.shape[0], width), lambda i, w, k, f=first: (0, f[0] + f[1] * w[0]), pipeline_mode=ONCE)
            in_specs.append(spec)
            args.append(v)
        elif kind == "quarter":
            at, stride, part = first
            spec = pl.BlockSpec(
                (v.shape[0], width),
                lambda i, w, k, f=(at, stride, part): (0, f[0] + f[1] * w[0] + jnp.bitwise_xor(f[2], w[3])),
                pipeline_mode=ONCE,
            )
            in_specs.append(spec)
            args.append(v)
        else:
            view = v.reshape(HEADS // 2, 2, HEAD_DIM, v.shape[1])
            spec = pl.BlockSpec((HEADS // 2, None, HEAD_DIM, width), lambda i, w, k, f=first: (0, w[0], 0, f), pipeline_mode=ONCE)
            in_specs.append(spec)
            args.append(view)
    for v in blocked:
        if v.ndim == 2:
            in_specs.append(pl.BlockSpec((slots, v.shape[1]), lambda i, *_: (i, 0)))
        else:
            in_specs.append(pl.BlockSpec((1,) + v.shape[1:], lambda i, *_, n=v.ndim: (i,) + (0,) * (n - 1)))
        args.append(v)
    for v in whole:
        in_specs.append(pl.BlockSpec(v.shape, lambda i, *_, n=v.ndim: (0,) * n))
        args.append(v)
    out_specs, out_shape = [], []
    for kind, shape, dtype in outs:
        out_shape.append(jax.ShapeDtypeStruct(shape, dtype))
        if kind == "rows":
            out_specs.append(pl.BlockSpec((slots, shape[1]), lambda i, *_: (i, 0)))
        elif kind == "image":
            out_specs.append(pl.BlockSpec((1,) + shape[1:], lambda i, *_, n=len(shape): (i,) + (0,) * (n - 1)))
        else:
            out_specs.append(pl.BlockSpec(shape, lambda i, *_, n=len(shape): (0,) * n))
    n_p, n_b, n_in = sum(len(w) for w in weights), len(blocked), len(args)
    in_specs += [ANY] * len(after)
    args += list(after)

    def kernel(where_ref, kept_ref, *refs):
        ins, res = refs[:n_in], refs[n_in + len(after) :]
        held, at = [], 0
        for w in weights:
            held.append(ins[at : at + len(w)])
            at += len(w)
        body(kept_ref, held, ins[n_p : n_p + n_b], ins[n_p + n_b : n_in], res)

    return pl.pallas_call(
        kernel,
        grid_spec=pltpu.PrefetchScalarGridSpec(
            num_scalar_prefetch=2, grid=(images,), in_specs=in_specs, out_specs=out_specs
        ),
        out_shape=out_shape,
        compiler_params=pltpu.CompilerParams(vmem_limit_bytes=LIMIT),
        cost_estimate=cost,
    )(where, kept, *args)


def normed_of(rows):
    width = rows.shape[-1]
    mean = jnp.sum(rows, axis=-1, keepdims=True) * (1.0 / width)
    centered = rows - mean
    spread = jnp.sum(centered * centered, axis=-1, keepdims=True) * (1.0 / width)
    factor = lax.rsqrt(spread + EPS)
    return centered * factor, factor


def norm_rows(rows, gain, shift):
    return normed_of(rows)[0] * gain + shift


def norm_back(dz, rows, gain):
    normed, factor = normed_of(rows)
    width = rows.shape[-1]
    prod = dz * normed
    dn = dz * gain
    m1 = jnp.sum(dn, axis=-1, keepdims=True) * (1.0 / width)
    m2 = jnp.sum(dn * normed, axis=-1, keepdims=True) * (1.0 / width)
    back = factor * (dn - m1 - normed * m2)
    return back, jnp.sum(prod, axis=0, keepdims=True), jnp.sum(dz, axis=0, keepdims=True)


def chunks(total, size):
    size = min(size, total)
    return [(k, size) for k in range(0, total, size)]


def qkv_body(kept, w, blocked, whole, outs):
    x = blocked[0][...]
    for k, n in chunks(outs[0].shape[1], 512):
        cols = pl.ds(k, n)
        outs[0][:, cols] = (dot(x, w[0][0][:, cols]) + whole[0][:, cols]).astype(BF)


def heads_of(ref):
    return ref[...].reshape(-1, ref.shape[-1])


def pairs_dot(x_ref, parts):
    total, at = None, 0
    for w_ref in parts:
        term = dot(x_ref[:, at : at + w_ref.shape[0]], w_ref[...])
        total = term if total is None else total + term
        at += w_ref.shape[0]
    return total


def attend(kept, proj_ref, probs_ref, att_ref):
    slots, third = proj_ref.shape[0], proj_ref.shape[1] // 3
    bound = BUFFER + kept[pl.program_id(0)]
    alive = lax.broadcasted_iota(jnp.int32, (slots, slots), 1) < bound
    outs = []
    for h in range(third // HEAD_DIM):
        lo = h * HEAD_DIM
        q = proj_ref[:, lo : lo + HEAD_DIM]
        k = proj_ref[:, third + lo : third + lo + HEAD_DIM]
        v = proj_ref[:, 2 * third + lo : 2 * third + lo + HEAD_DIM]
        s = jnp.where(alive, dot_t(q, k) * SCALE, -1e30)
        e = jnp.exp(s - jnp.max(s, axis=-1, keepdims=True))
        p = (e * (1.0 / jnp.sum(e, axis=-1, keepdims=True))).astype(BF)
        probs_ref[0, h] = p
        outs.append(dot(p, v).astype(BF))
        if h % 2:
            att_ref[:, lo - HEAD_DIM : lo + HEAD_DIM] = jnp.concatenate(outs, axis=1)
            outs = []


def attend_other(kept, w, blocked, whole, outs):
    attend(kept, blocked[0], outs[0], outs[1])
    outs[2][...] = dot(outs[1][...], heads_of(w[0][0]))


def attend_own(kept, w, blocked, whole, outs):
    attend(kept, blocked[0], outs[0], outs[1])
    middle = blocked[2][...] + (dot(outs[1][...], heads_of(w[0][0])) + blocked[1][...]) + whole[0][...]
    outs[2][...] = middle
    outs[3][...] = norm_rows(middle, whole[1][...], whole[2][...]).astype(BF)


def up_body(kept, w, blocked, whole, outs):
    x = blocked[0][...]
    for k, n in chunks(outs[0].shape[1], 256):
        cols = pl.ds(k, n)
        held = w[0][k // w[0][0].shape[1]]
        pre = dot(x, held[:, pl.ds(k % held.shape[1], n)]) + whole[0][:, cols]
        phi = 0.5 + 0.5 * lax.erf(pre * (2.0**-0.5))
        dens = jnp.exp(-0.5 * (pre * pre)) * 0.3989422804014327
        outs[0][:, cols] = (pre * phi).astype(BF)
        outs[1][:, cols] = (phi + pre * dens).astype(BF)


def down_other(kept, w, blocked, whole, outs):
    outs[0][...] = pairs_dot(blocked[0], w[0])


def down_own(kept, w, blocked, whole, outs):
    state = blocked[2][...] + (pairs_dot(blocked[0], w[0]) + blocked[1][...]) + whole[0][...]
    outs[0][...] = state
    outs[1][...] = norm_rows(state, whole[1][...], whole[2][...]).astype(BF)


def down_last(kept, w, blocked, whole, outs):
    state = blocked[2][...] + (pairs_dot(blocked[0], w[0]) + blocked[1][...]) + whole[0][...]
    alive = lax.broadcasted_iota(jnp.int32, state.shape, 0) < BUFFER + kept[pl.program_id(0)]
    outs[0][...] = jnp.where(alive, state, 0.0).astype(BF)


def mlp_back(w, blocked, outs):
    low = blocked[0][...]
    for k, n in chunks(outs[0].shape[1], 512):
        cols = pl.ds(k, n)
        held = w[0][k // w[0][0].shape[0]]
        t = dot_t(low, held[pl.ds(k % held.shape[0], n), :])
        outs[0][:, cols] = (t * blocked[1][:, cols].astype(F32)).astype(BF)
    total, at = None, 0
    for held in w[1]:
        term = dot_t(outs[0][:, at : at + held.shape[1]], held[...])
        total = term if total is None else total + term
        at += held.shape[1]
    return total


def mlp_back_other(kept, w, blocked, whole, outs):
    outs[1][...] = mlp_back(w, blocked, outs)


def add_sums(ref, rows):
    sums = jnp.concatenate(rows + [jnp.zeros((8 - len(rows), rows[0].shape[1]), F32)], axis=0)

    @pl.when(pl.program_id(0) == 0)
    def _():
        ref[...] = sums

    @pl.when(pl.program_id(0) != 0)
    def _():
        ref[...] += sums


def mlp_back_own(kept, w, blocked, whole, outs):
    dz = mlp_back(w, blocked, outs) + blocked[2][...]
    back, gain, shift = norm_back(dz, blocked[3][...], whole[0][...])
    grad = blocked[4][...] + back
    low = grad.astype(BF)
    outs[1][...] = grad
    outs[2][...] = low
    add_sums(outs[3], [gain, shift, jnp.sum(low.astype(F32), axis=0, keepdims=True)])


def attend_back(w, blocked, outs):
    branch, proj_ref, probs_ref = blocked[0], blocked[1], blocked[2]
    third = proj_ref.shape[1] // 3
    datt = dot_t(branch[...], heads_of(w[0][0])).astype(BF)
    pairs = [[], [], []]
    for h in range(third // HEAD_DIM):
        lo = h * HEAD_DIM
        q = proj_ref[:, lo : lo + HEAD_DIM]
        k = proj_ref[:, third + lo : third + lo + HEAD_DIM]
        v = proj_ref[:, 2 * third + lo : 2 * third + lo + HEAD_DIM]
        da = datt[:, lo : lo + HEAD_DIM]
        p = probs_ref[0, h]
        dp = dot_t(da, v)
        pf = p.astype(F32)
        ds = (pf * (dp - jnp.sum(pf * dp, axis=-1, keepdims=True))).astype(BF)
        pairs[0].append((dot(ds, k) * SCALE).astype(BF))
        pairs[1].append((t_dot(ds, q) * SCALE).astype(BF))
        pairs[2].append(t_dot(p, da).astype(BF))
        if h % 2:
            for j in range(3):
                at = j * third + lo - HEAD_DIM
                outs[0][:, at : at + 2 * HEAD_DIM] = jnp.concatenate(pairs[j], axis=1)
            pairs = [[], [], []]
    return dot_t(outs[0][...], w[1][0][...])


def attend_back_other(kept, w, blocked, whole, outs):
    outs[1][...] = attend_back(w, blocked, outs)


def attend_back_own(kept, w, blocked, whole, outs):
    dz = attend_back(w, blocked, outs) + blocked[3][...]
    back, gain, shift = norm_back(dz, blocked[4][...], whole[0][...])
    grad = blocked[5][...] + back
    outs[1][...] = grad
    low = grad.astype(BF)
    outs[2][...] = low
    add_sums(outs[3], [gain, shift, jnp.sum(low.astype(F32), axis=0, keepdims=True)])


def weight_grad(plan, where, xs, ys, groups, first, sums=False, extra=0, relative=False, after=()):
    depth, n_x = xs[0].shape
    cols = ys[0].shape[1]
    ny, chips, bits = plan.ny, plan.chips, plan.bits
    half = cols // ny
    size = half
    chunk = size if size <= 768 else 512
    steps = size // chunk
    rows = n_x // chips
    part = rows // groups
    dims = [ny] + [2] * bits
    dims[first] = 1
    block = [1] + dims[1:] + [rows, chunk]
    shape = dims + [rows, size + extra]
    n_after = len(after)

    def kernel(where_ref, xo, xt, yo, yt, *rest):
        rest = rest[n_after:]
        keep, send = rest[0], rest[1]
        flip, acc = rest[-2], rest[-1]
        step = pl.program_id(0)

        @pl.when(step == 0)
        def _():
            flip[:, :depth] = xo[...].T
            flip[:, depth:] = xt[...].T

        acc[...] = dot(flip[:, :depth], yo[...]) + dot(flip[:, depth:], yt[...])
        if sums:
            rest[2][...] = jnp.sum(yo[...].astype(F32), axis=0, keepdims=True) + jnp.sum(
                yt[...].astype(F32), axis=0, keepdims=True
            )

        def put(ref, r):
            at = [0]
            for k in range(1, bits + 1):
                at.append((r >> (bits - k)) & 1 if k != first else 0)
            chip = jnp.bitwise_xor(where_ref[1], r)
            for g in range(groups):
                start = pl.multiple_of(g * part * chips + chip * part, 16)
                place = g
                if groups == 2 and ny == 2:
                    place = jnp.bitwise_xor(g, where_ref[2])
                place = pl.multiple_of(place * part, 16)
                ref[tuple(at) + (pl.ds(place, part),)] = acc[pl.ds(start, part)].astype(BF)

        if first:
            for r in range(chips):
                put(send if (r >> (bits - first)) & 1 else keep, r)
        else:

            @pl.when(step < steps)
            def _():
                for r in range(chips):
                    put(keep, r)

            @pl.when(step >= steps)
            def _():
                for r in range(chips):
                    put(send, r)

    per_rep = half // chunk

    def column(i, w):
        own = w[2] if ny == 2 and not relative else 0
        return jnp.bitwise_xor(i // steps, own) * per_rep + i % steps

    zeros = (0,) * (bits + 1)
    x_spec = pl.BlockSpec((depth, n_x), lambda i, w: (0, 0), pipeline_mode=ONCE)
    y_spec = pl.BlockSpec((depth, chunk), lambda i, w: (0, column(i, w)))
    if first:
        specs = [pl.BlockSpec(block, lambda i, w: (i // steps,) + zeros + (i % steps,))] * 2
    else:
        specs = [
            pl.BlockSpec(block, lambda i, w: (0,) + zeros + (jnp.minimum(i, steps - 1),)),
            pl.BlockSpec(block, lambda i, w: (0,) + zeros + (jnp.maximum(i - steps, 0),)),
        ]
    out_shape = [jax.ShapeDtypeStruct(shape, BF)] * 2
    if sums:
        specs = specs + [pl.BlockSpec((1, chunk), lambda i, w: (0, column(i, w)))]
        out_shape = out_shape + [jax.ShapeDtypeStruct((1, cols), F32)]
    return pl.pallas_call(
        kernel,
        grid_spec=pltpu.PrefetchScalarGridSpec(
            num_scalar_prefetch=1,
            grid=(ny * steps,),
            in_specs=[x_spec, x_spec, y_spec, y_spec] + [ANY] * n_after,
            out_specs=specs,
            scratch_shapes=[pltpu.VMEM((n_x, 2 * depth), BF), pltpu.VMEM((n_x, chunk), F32)],
        ),
        out_shape=out_shape,
        compiler_params=pltpu.CompilerParams(vmem_limit_bytes=LIMIT),
        cost_estimate=BACKWARD,
    )(where, *xs, *ys, *after)


def proj_grad_into(plan, where, xs, ys, first, keep, send):
    depth, n_x = xs[0].shape
    cols = ys[0].shape[1]
    ny, chips, bits = plan.ny, plan.chips, plan.bits
    half = cols // ny
    part = n_x // chips
    width = half * part // keep.shape[-2]
    stacked = half // width
    at_col = keep.shape[-1] // width - 1
    block = [1] + list(keep.shape[1:-1]) + [width]

    def kernel(where_ref, xo, xt, yo, yt, k_in, s_in, keep_ref, send_ref, acc):
        acc[...] = t_dot(xo[...], yo[...]) + t_dot(xt[...], yt[...])
        for r in range(chips):
            at = [0]
            for k in range(1, bits + 1):
                at.append((r >> (bits - k)) & 1 if k != first else 0)
            ref = send_ref if (r >> (bits - first)) & 1 else keep_ref
            start = pl.multiple_of(jnp.bitwise_xor(where_ref[1], r) * part, 16)
            for g in range(stacked):
                piece = acc[pl.ds(start, part), g * width : (g + 1) * width]
                ref[tuple(at) + (pl.ds(g * part, part),)] = piece.astype(BF)

    zeros = (0,) * (bits + 1)
    own = (lambda w: w[2]) if ny == 2 else (lambda w: 0)
    x_spec = pl.BlockSpec((depth, n_x), lambda i, w: (0, 0), pipeline_mode=ONCE)
    y_spec = pl.BlockSpec((depth, half), lambda i, w: (0, jnp.bitwise_xor(i, own(w))))
    spec = pl.BlockSpec(block, lambda i, w: (i,) + zeros + (at_col,))
    return pl.pallas_call(
        kernel,
        grid_spec=pltpu.PrefetchScalarGridSpec(
            num_scalar_prefetch=1,
            grid=(ny,),
            in_specs=[x_spec, x_spec, y_spec, y_spec, ANY, ANY],
            out_specs=[spec, spec],
            scratch_shapes=[pltpu.VMEM((n_x, half), F32)],
        ),
        out_shape=[jax.ShapeDtypeStruct(keep.shape, BF)] * 2,
        input_output_aliases={5: 0, 6: 1},
        compiler_params=pltpu.CompilerParams(vmem_limit_bytes=LIMIT),
        cost_estimate=BACKWARD,
    )(where, *xs, *ys, keep, send)


class Term:
    def __init__(self, plan, keep, send, order):
        self.plan, self.keep, self.order = plan, keep, list(order)
        self.got = plan.flip(send, self.order.pop(0))

    def step(self, after):
        axis = self.order.pop(0)
        self.keep, send = combine(self.keep, self.got, axis, after)
        self.got = self.plan.flip(send, axis)
        return send


def combine(keep, got, axis, after):
    shape = keep.shape
    rows, cols = shape[-2:]
    cuts = 2
    block = shape[:-2] + (rows // cuts, cols)
    out = shape[:axis] + (1,) + shape[axis + 1 :]
    out_block = out[:-2] + (rows // cuts, cols)
    lead = len(shape) - 2

    def kernel(k, g, *rest):
        stay, go = rest[-2:]
        for side, ref in ((0, stay), (1, go)):
            at = tuple(pl.ds(side, 1) if d == axis else slice(None) for d in range(lead))
            ref[...] = (k[at].astype(F32) + g[at].astype(F32)).astype(BF)

    index = lambda i: (0,) * lead + (i, 0)
    return pl.pallas_call(
        kernel,
        grid=(cuts,),
        in_specs=[pl.BlockSpec(block, index)] * 2 + [ANY] * len(after),
        out_specs=[pl.BlockSpec(out_block, index)] * 2,
        out_shape=[jax.ShapeDtypeStruct(out, BF)] * 2,
        compiler_params=pltpu.CompilerParams(vmem_limit_bytes=LIMIT),
        cost_estimate=BACKWARD,
    )(keep, got, *after)


def last_combine(terms, axis, rows, after):
    ins, specs, widths = [], [], []
    for t in terms:
        ins += [t.keep, t.got]
        widths.append(t.keep.shape[-1] * (t.keep.shape[-2] // rows))
    total = sum(widths)
    n_in = len(ins)

    def kernel(*refs):
        stay, go = refs[-2:]
        at = 0
        for j, t in enumerate(terms):
            k, g = refs[2 * j], refs[2 * j + 1]
            lead = k.ndim - 2
            cols = k.shape[-1]
            for block in range(k.shape[-2] // rows):
                for side, ref in ((0, stay), (1, go)):
                    idx = tuple(side if d == axis else 0 for d in range(lead)) + (pl.ds(block * rows, rows),)
                    ref[:, at : at + cols] = (k[idx].astype(F32) + g[idx].astype(F32)).astype(BF)
                at += cols

    whole = [pl.BlockSpec(v.shape, lambda n=v.ndim: (0,) * n) for v in ins]
    return pl.pallas_call(
        kernel,
        in_specs=whole + [ANY] * len(after),
        out_specs=[pl.BlockSpec((rows, total), lambda: (0, 0))] * 2,
        out_shape=[jax.ShapeDtypeStruct((rows, total), BF)] * 2,
        compiler_params=pltpu.CompilerParams(vmem_limit_bytes=LIMIT),
        cost_estimate=BACKWARD,
    )(*ins, *after)


def pick(flag, a, b):
    return jnp.where(flag == 0, a, b)


def small_call(kernel, where, ins, shapes, after, grid=None):
    n = len(ins)

    def body(where_ref, *refs):
        kernel(where_ref, refs[:n], refs[n + len(after) :])

    return pl.pallas_call(
        body,
        grid_spec=pltpu.PrefetchScalarGridSpec(
            num_scalar_prefetch=1,
            grid=(1,),
            in_specs=[pl.BlockSpec(v.shape, lambda i, w, n=v.ndim: (0,) * n) for v in ins] + [ANY] * len(after),
            out_specs=[pl.BlockSpec(s, lambda i, w, n=len(s): (0,) * n) for s, _ in shapes],
        ),
        out_shape=[jax.ShapeDtypeStruct(s, t) for s, t in shapes],
        compiler_params=pltpu.CompilerParams(vmem_limit_bytes=LIMIT),
        cost_estimate=BACKWARD,
    )(where, *ins, *after)


class Ending:
    def __init__(self, plan, where, terms, axis, rows, tail, after):
        self.plan, self.where, self.rows, self.tail = plan, where, rows, tail
        self.keep, self.sent = last_combine(terms, axis, rows, after)
        self.got = plan.flip(self.sent, axis)

    def core(self, after):
        rows, tail = self.rows // 2, self.tail
        cols = self.cols = self.keep.shape[1] - tail

        def kernel(where, ins, outs):
            c = where[0]
            for ref, row in ((outs[0], c), (outs[1], 1 - c)):
                at = pl.ds(pl.multiple_of(row * rows, 16), rows)
                ref[:, :cols] = (ins[0][at, :cols].astype(F32) + ins[1][at, :cols].astype(F32)).astype(BF)
            if tail:
                for g in range(2):
                    at = pl.ds(g * rows, rows)
                    piece = ins[0][at, cols:].astype(F32) + ins[1][at, cols:].astype(F32)
                    outs[0][:, cols + g * tail : cols + (g + 1) * tail] = piece.astype(BF)

        shapes = [((rows, cols + 2 * tail), BF), ((rows, cols), BF)]
        self.mine, sent = small_call(kernel, self.where, [self.keep, self.got], shapes, after)
        self.came = self.plan.core(sent)
        return sent

    def rep(self, after):
        rows, cols, tail = self.rows // 2, self.cols, self.tail

        def kernel(where, ins, outs):
            outs[0][:, :cols] = ins[0][:, :cols]
            outs[0][:, cols : 2 * cols] = ins[1][...]
            if tail:
                outs[0][:, 2 * cols :] = ins[0][:, cols:]

        shapes = [((rows, 2 * cols + 2 * tail), BF)]
        v = small_call(kernel, self.where, [self.mine, self.came], shapes, after)[0]
        self.pair = [v, self.plan.flip(v, 0)] if self.plan.ny == 2 else [lax.psum(v, "rep")]
        return v


def place_grads(plan, where, layer, layers, end2, rest, sizes, before, after):
    deep, width, ff, quarters = sizes
    n, ny, halves = plan.shards, plan.ny, quarters // 2
    wide, half_ff = 3 * width // 2, ff // 2
    cols2, cols = end2.cols, rest.cols
    fused = bool(rest.tail)
    ins = end2.pair + rest.pair

    def kernel(where_ref, *refs):
        refs_in = refs[: 2 * ny]
        outs = refs[-(4 if fused else 3) :]
        c, y = where_ref[0], where_ref[2]

        def source(group, p, q, at, size):
            total = (cols2, cols)[group]
            step = (at // 128) * 128
            span = (at + size - step + 127) // 128 * 128
            first = pl.multiple_of(jnp.where(p == c, 0, total) + step, 128)
            v = refs_in[group * ny][:, pl.ds(first, span)]
            if ny == 2:
                v = jnp.where(y == q, v, refs_in[group * ny + 1][:, pl.ds(first, span)])
            return v[:, at - step : at - step + size].astype(F32)

        def core_columns(p, at, size, total, first):
            part = total // ny
            return source(1, p, at // part, first + at % part, size)

        for k in range(3 * HEADS // 2):
            pieces = [core_columns(p, k * HEAD_DIM, HEAD_DIM, wide, 0) for p in range(2)]
            outs[0][0, :, k * 2 * HEAD_DIM : (k + 1) * 2 * HEAD_DIM] = jnp.concatenate(pieces, axis=1)
        for k in range(n):
            pieces = []
            for p in range(2):
                for h in range(halves):
                    pieces.append(core_columns(p, (h * n + k) * deep, deep, half_ff, wide // ny))
            outs[1][0, :, k * quarters * deep : (k + 1) * quarters * deep] = jnp.concatenate(pieces, axis=1)
        part = width // ny
        for p in range(2):
            for h in range(halves):
                for q in range(ny):
                    at = pl.ds((p * halves + h) * deep, deep)
                    outs[2][0, at, q * part : (q + 1) * part] = source(0, p, q, h * part, part)
        if fused:
            for q in range(ny):
                v = refs_in[ny][:, 2 * cols :]
                if ny == 2:
                    v = jnp.where(y == q, v, refs_in[ny + 1][:, 2 * cols :])
                outs[3][0, :, q * part : (q + 1) * part] = v.astype(F32)

    shapes = [(deep, 3 * width), (deep, ff), (quarters * deep, width)] + ([(deep, width)] if fused else [])
    in_specs = [pl.BlockSpec(v.shape, lambda i, w: (0, 0)) for v in ins]
    args = list(ins) + list(before or []) + list(after)
    n_before = len(before or [])
    return pl.pallas_call(
        kernel,
        grid_spec=pltpu.PrefetchScalarGridSpec(
            num_scalar_prefetch=1,
            grid=(1,),
            in_specs=in_specs + [ANY] * (n_before + len(after)),
            out_specs=[pl.BlockSpec((1,) + s, lambda i, w: (layer, 0, 0)) for s in shapes],
        ),
        out_shape=[jax.ShapeDtypeStruct((layers,) + s, F32) for s in shapes],
        input_output_aliases={1 + len(ins) + k: k for k in range(n_before)},
        compiler_params=pltpu.CompilerParams(vmem_limit_bytes=LIMIT),
        cost_estimate=BACKWARD,
    )(where, *args)


def per_device(
    plan,
    tokens,
    kept,
    attn_gain,
    attn_shift,
    qkv_weight,
    qv_bias,
    proj_weight,
    proj_bias,
    mlp_gain,
    mlp_shift,
    fc1_weight,
    fc1_bias,
    fc2_weight,
    fc2_bias,
    cotangent,
):
    images, slots, width = tokens.shape
    layers = attn_gain.shape[0]
    rows = images * slots
    n = plan.shards
    deep = qkv_weight.shape[1]
    shard = lax.axis_index("shard")
    c, chip, y = lax.rem(shard, 2), shard // 2, lax.axis_index("rep")
    where = jnp.stack([c, chip, y, y if plan.ny == 2 else 0 * y]).astype(jnp.int32)
    ff = fc2_weight.shape[1] * n
    quarters = fc2_weight.shape[1] // deep
    wide, half_width, half_ff = 3 * width // 2, width // 2, ff // 2
    half_heads = HEADS // 2

    small = jnp.concatenate(
        [attn_gain, attn_shift, qv_bias, proj_bias, mlp_gain, mlp_shift, fc1_bias, fc2_bias], axis=1
    )
    sizes = [v.shape[1] for v in (attn_gain, attn_shift, qv_bias, proj_bias, mlp_gain, mlp_shift, fc1_bias, fc2_bias)]
    lines = small.size // 128
    extra = jnp.pad(small.reshape(lines, 128), ((0, deep - lines), (0, 0)))

    halves = quarters // 2
    lead = 4 * width
    block = n * deep
    each = halves // plan.ny

    def merged(layer):
        qkv = qkv_weight[layer].reshape(deep, 3 * half_heads, 2, HEAD_DIM).swapaxes(1, 2).reshape(deep, 3 * width)
        fc1 = fc1_weight[layer].reshape(deep, n, quarters, deep).swapaxes(1, 2).reshape(deep, ff)
        fc2 = fc2_weight[layer].reshape(2, halves, deep, width)
        if plan.ny == 2:
            fc2 = pick(y, fc2[:, :1], fc2[:, 1:])
        fc2 = [fc2[p, k] for p in range(2) for k in range(each)]
        return [qkv, proj_weight[layer], fc1] + fc2 + ([] if layer else [extra])

    operands = lax.optimization_barrier([jnp.concatenate(merged(layer), axis=1) for layer in range(layers)])
    gathered = [lax.all_gather(v, "shard", axis=0, tiled=True) for v in operands]
    at_fc1, at_fc2 = lead // block, (lead + ff) // block
    mlp_parts = []
    for layer in range(layers):
        found = {"fc1": [(gathered[layer], ("quarter", block, (at_fc1, halves, k))) for k in range(halves)]}
        found["fc2"] = [(gathered[layer], columns(block, at_fc2 + k, each)) for k in range(each)]
        if plan.ny == 2:
            mine = lax.dynamic_slice_in_dim(gathered[layer], (at_fc2 + c) * block, block, axis=1)
            found["fc2"].append((plan.flip(mine, 0), None))
            found["sent"] = (mine,)
        mlp_parts.append(found)

    def weight_of(layer, name):
        if name == "qkv":
            return [(gathered[layer], columns(wide, 0, 1))]
        if name == "proj":
            return [(gathered[layer], ("heads", width, 3))]
        return mlp_parts[layer][name]

    every = gathered[0].reshape(n, deep, -1)[:, :lines, lead + ff + 2 * each * block :]
    every = every.reshape(n, layers, small.shape[1]).astype(F32)
    vecs = []
    for layer in range(layers):
        at, d = 0, {}
        for name, size in zip(SMALL, sizes):
            d[name] = every[:, layer, at : at + size].reshape(1, n * size)
            at += size
        q = d["qvb"].reshape(2 * half_heads, 2, HEAD_DIM)
        q = pick(c, q[:, 0], q[:, 1]).reshape(2, half_width)
        d["qvb_c"] = jnp.stack([q[0], jnp.zeros_like(q[0]), q[1]]).reshape(1, wide)
        f = d["f1b"].reshape(n, 2, halves, deep).transpose(1, 2, 0, 3).reshape(2, halves, block)
        f = pick(c, f[0], f[1])
        if plan.ny == 2:
            f = pick(y, f, f[::-1])
        d["f1b_c"] = f.reshape(1, half_ff)
        vecs.append(d)

    kept_oth = plan.core(kept)
    state = tokens.astype(F32).reshape(rows, width)
    live = lax.broadcasted_iota(jnp.int32, (images, slots), 1) < BUFFER + kept[:, None]
    grad = jnp.where(live[:, :, None], cotangent.astype(F32), 0.0).reshape(rows, width)
    low_own = grad.astype(BF)
    low_oth = plan.core(low_own)
    first_own = norm_rows(state, vecs[0]["ag"], vecs[0]["as"]).astype(BF)

    f32_rows, low_rows = ("rows", (rows, width), F32), ("rows", (rows, width), BF)
    wide_rows, ff_rows = ("rows", (rows, wide), BF), ("rows", (rows, half_ff), BF)
    att_outs = [("image", (images, half_heads, slots, slots), BF), ("rows", (rows, half_width), BF)]
    full_sums = ("full", (8, width), F32)

    def call(body, layer, own, names, blocked, whole, outs, after=(), cost=None):
        chosen = [weight_of(layer, name) for name in names]
        k = kept if own else kept_oth
        return row_call(body, where, k, chosen, blocked, whole, outs, images, slots, after, cost or (BACKWARD if after else FORWARD))

    saved = []
    for layer in range(layers):
        v = vecs[layer]
        first_oth = plan.core(first_own)
        sent = mlp_parts[layer].get("sent", ())
        proj_oth = call(qkv_body, layer, 0, ["qkv"], [first_oth], [v["qvb_c"]], [wide_rows], sent, FORWARD)[0]
        probs_oth, att_oth, part = call(attend_other, layer, 0, ["proj"], [proj_oth], [], att_outs + [f32_rows])
        part = plan.core(part)
        proj_own = call(qkv_body, layer, 1, ["qkv"], [first_own], [v["qvb_c"]], [wide_rows])[0]
        probs_own, att_own, middle, second_own = call(
            attend_own, layer, 1, ["proj"], [proj_own, part, state], [v["pb"], v["mg"], v["ms"]], att_outs + [f32_rows, low_rows])
        second_oth = plan.core(second_own)
        hid_oth, slope_oth = call(up_body, layer, 0, ["fc1"], [second_oth], [v["f1b_c"]], [ff_rows] * 2)
        if layer + 1 < layers:
            part = call(down_other, layer, 0, ["fc2"], [hid_oth], [], [f32_rows])[0]
            part = plan.core(part)
        hid_own, slope_own = call(up_body, layer, 1, ["fc1"], [second_own], [v["f1b_c"]], [ff_rows] * 2)
        saved.append(
            dict(
                state=state,
                first=(first_own, first_oth),
                proj=(proj_own, proj_oth),
                probs=(probs_own, probs_oth),
                att=(att_own, att_oth),
                middle=middle,
                second=(second_own, second_oth),
                hid=(hid_own, hid_oth),
                slope=(slope_own, slope_oth),
            )
        )
        if layer + 1 < layers:
            w = vecs[layer + 1]
            state, first_own = call(
                down_own, layer, 1, ["fc2"], [hid_own, part, middle], [v["f2b"], w["ag"], w["as"]], [f32_rows, low_rows])

    axes = list(range(1 if plan.ny == 1 else 0, plan.bits + 1))
    last_axis, z_axis, x_axis = 1, plan.bits - 1, plan.bits
    y_axis = 0 if plan.ny == 2 else 2
    order_f2 = [y_axis, x_axis, z_axis]
    orders_f1 = [[x_axis, y_axis, z_axis]] + [[z_axis, x_axis, y_axis]] * (layers - 1)
    orders_q = [[z_axis, x_axis, y_axis]] + [[x_axis, z_axis, y_axis]] * (layers - 1)
    own_rows = 2 * deep
    tail = width // plan.ny * HEAD_DIM // own_rows
    fused = n == HEADS
    tail = tail if fused else 0
    big = [[None] * 4 for _ in range(layers)]
    sums = [None] * layers
    f2b_sum = jnp.sum(low_own.astype(F32), axis=0, keepdims=True)

    def end_fc2(layer, prev):
        ends["f2", layer] = Ending(plan, where, [terms["f2", layer]], last_axis, own_rows, 0, prev)
        return (ends["f2", layer].sent,)

    def end_rest(layer, prev):
        group = [terms["q", layer], terms["f1", layer]]
        ends["rest", layer] = Ending(plan, where, group, last_axis, own_rows, tail, prev)
        return (ends["rest", layer].sent,)

    def place(layer, before, prev):
        return place_grads(
            plan, where, layer, layers, ends["f2", layer], ends["rest", layer], (deep, width, ff, quarters), before, prev
        )

    ends = {}
    prev = (hid_own,)
    terms = {}
    for layer in reversed(range(layers)):
        v, s = vecs[layer], saved[layer]
        top = layer == layers - 1

        def grad_fc2(prev):
            r = weight_grad(plan, where, s["hid"], (low_own, low_oth), 2, order_f2[0], after=prev)
            terms["f2", layer] = Term(plan, *r, order_f2)
            return (r[1],)

        if top:
            prev = grad_fc2(prev)
        pre_oth, part = call(
            mlp_back_other, layer, 0, ["fc2", "fc1"], [low_oth, s["slope"][1]], [], [ff_rows, f32_rows], prev
        )
        part = plan.core(part)
        prev = (pre_oth,)
        if top:
            last_part = call(down_other, layer, 0, ["fc2"], [s["hid"][1]], [], [f32_rows], prev)[0]
            prev = (last_part,)
            last_part = plan.core(last_part)
        else:
            prev = grad_fc2(prev)
            prev += (terms["f1", layer + 1].step(prev[:1]),)
            prev += end_fc2(layer + 1, prev[:1])
        pre_own, mid_grad, branch_own, sum1 = call(
            mlp_back_own,
            layer,
            1,
            ["fc2", "fc1"],
            [low_own, s["slope"][0], part, s["middle"], grad],
            [v["mg"]],
            [ff_rows, f32_rows, low_rows, full_sums],
            prev,
        )
        branch_oth = plan.core(branch_own)
        prev = (branch_own,)
        if not top:
            prev += (terms["q", layer + 1].step(prev),)
        res1 = weight_grad(
            plan, where, s["second"], (pre_own, pre_oth), 1, orders_f1[layer][0], sums=True, extra=tail, relative=True, after=prev
        )
        keep, send = res1[:2]
        if fused:
            keep, send = proj_grad_into(plan, where, s["att"], (branch_own, branch_oth), orders_f1[layer][0], keep, send)
        else:
            term = t_dot(s["att"][0], branch_own) + t_dot(s["att"][1], branch_oth)
            term = term.astype(BF).reshape(half_heads, HEAD_DIM, width)
            none = jnp.zeros_like(term)
            term = jnp.stack([pick(c, term, none), pick(c, none, term)], axis=1).reshape(width, width)
            term = lax.psum_scatter(term, "shard", scatter_dimension=0, tiled=True)
            big[layer][1] = lax.psum(term, "rep").astype(F32)
        terms["f1", layer] = Term(plan, keep, send, orders_f1[layer])
        prev = (send,)
        if top:
            prev += (terms["f2", layer].step(prev),)
        else:
            prev += (terms["q", layer + 1].step(prev[:1]),)
            prev += (ends["f2", layer + 1].core(prev[:1]),)
        dproj_oth, part = call(
            attend_back_other,
            layer,
            0,
            ["proj", "qkv"],
            [branch_oth, s["proj"][1], s["probs"][1]],
            [],
            [wide_rows, f32_rows],
            prev,
        )
        part = plan.core(part)
        prev = (dproj_oth,)
        if not top:
            prev += (terms["f2", layer].step(prev[:1]),)
            prev += (terms["f1", layer + 1].step(prev[:1]),)
            prev += (ends["f2", layer + 1].rep(prev[:1]),)
        dproj_own, grad, low_own, sum2 = call(
            attend_back_own,
            layer,
            1,
            ["proj", "qkv"],
            [branch_own, s["proj"][0], s["probs"][0], part, s["state"], mid_grad],
            [v["ag"]],
            [wide_rows, f32_rows, low_rows, full_sums],
            prev,
        )
        prev = (dproj_own,)
        if layer:
            low_oth = plan.core(low_own)
        if top:
            prev += (terms["f2", layer].step(prev),)
        resq = weight_grad(plan, where, s["first"], (dproj_own, dproj_oth), 1, orders_q[layer][0], sums=True, after=prev)
        terms["q", layer] = Term(plan, *resq[:2], orders_q[layer])
        prev = (resq[1],)
        q = resq[2].reshape(3, half_heads, 1, HEAD_DIM)
        q = jnp.concatenate([q[:1], q[2:]])
        none = jnp.zeros_like(q)
        q = jnp.concatenate([pick(c, q, none), pick(c, none, q)], axis=2)
        f = res1[2].reshape(halves, block)
        if plan.ny == 2:
            f = pick(y, f, f[::-1])
        none = jnp.zeros_like(f)
        f = jnp.concatenate([pick(c, f, none), pick(c, none, f)], axis=0)
        f = f.reshape(quarters, n, deep).swapaxes(0, 1)
        full = {"ag": sum2[0], "as": sum2[1], "qvb": q, "pb": sum1[2], "mg": sum1[0], "ms": sum1[1], "f1b": f, "f2b": f2b_sum}
        f2b_sum = sum2[2]
        vec = jnp.concatenate([full[name].reshape(n, -1) for name in SMALL], axis=1)
        sums[layer] = vec

    vec = jnp.concatenate(sums, axis=0).reshape(layers, n, -1)
    got_vec = plan.core(vec)
    vec_axes = list(axes)

    def step_vec():
        nonlocal vec, got_vec
        vec = vec + got_vec
        sent = vec
        got_vec = plan.flip(vec, vec_axes.pop(0)) if vec_axes else None
        return (sent,)

    prev += (terms["f1", 0].step(prev[:1]),)
    prev += end_rest(1, prev[:1])
    w = layers - 1
    mixed = call(
        down_last, w, 1, ["fc2"], [saved[w]["hid"][0], last_part, saved[w]["middle"]], [vecs[w]["f2b"]], [low_rows], prev
    )[0]
    prev = (terms["f2", 0].step((mixed,)),) + step_vec()
    prev = (ends["rest", 1].core(prev),) + step_vec()
    prev = (terms["q", 0].step(prev),)
    prev = (terms["f1", 0].step(prev),) + step_vec()
    prev = (ends["rest", 1].rep(prev),)
    prev = end_fc2(0, prev)
    prev = (terms["q", 0].step(prev),) + step_vec()
    prev = (ends["f2", 0].core(prev),)
    while got_vec is not None:
        prev += step_vec()
    prev = end_rest(0, prev)
    prev = (ends["f2", 0].rep(prev),)
    placed = place(1, None, prev)
    prev = (ends["rest", 0].core((placed[0],)),)
    prev = (ends["rest", 0].rep(prev),)
    placed = place(0, placed, prev)
    if plan.ny == 1:
        vec = lax.psum(vec, "rep")
    vec = lax.dynamic_slice_in_dim(vec, shard, 1, axis=1)[:, 0]
    out, at = {}, 0
    for name, size in zip(SMALL, sizes):
        out[name] = vec[:, at : at + size]
        at += size
    qkv_g, fc1_g, fc2_g = placed[:3]
    proj_g = placed[3] if fused else jnp.stack([big[layer][1] for layer in range(layers)])
    return (
        mixed.reshape(images, slots, width),
        grad.reshape(images, slots, width),
        out["ag"],
        out["as"],
        qkv_g,
        out["qvb"],
        proj_g,
        out["pb"],
        out["mg"],
        out["ms"],
        fc1_g,
        out["f1b"],
        fc2_g,
        out["f2b"],
    )


def solution(mesh):
    rows = P(("shard", "rep"), None, None)
    vec = P(None, "shard")
    mat = P(None, "shard", None)
    return jax.shard_map(
        partial(per_device, Plan(mesh)),
        mesh=mesh,
        in_specs=(rows, P(("shard", "rep")), vec, vec, mat, vec, mat, vec, vec, vec, mat, vec, mat, vec, rows),
        out_specs=(rows, rows, vec, vec, mat, vec, mat, vec, vec, vec, mat, vec, mat, vec),
        check_vma=False,
    )
```

```python
from functools import partial

import jax
import jax.numpy as jnp
from jax import lax
from jax.experimental import pallas as pl
from jax.experimental.pallas import tpu as pltpu
from jax.sharding import PartitionSpec as P

HEADS = 16
HEAD_DIM = 64
BUFFER = 64
EPS = 1e-06
SCALE = HEAD_DIM ** (-0.5)
AX = ("shard", "rep")
BF = jnp.bfloat16
F32 = jnp.float32
LIMIT = 32 * 2**20
ONCE = pl.Buffered(1)
ANY = pl.BlockSpec(memory_space=pl.ANY)
FORWARD = pl.CostEstimate(flops=10**9, bytes_accessed=0, transcendentals=0)
BACKWARD = pl.CostEstimate(flops=10**9 * 30, bytes_accessed=0, transcendentals=0)
SMALL = ("ag", "as", "qvb", "pb", "mg", "ms", "f1b", "f2b")


class Plan:
    def __init__(self, mesh):
        self.shards = mesh.shape["shard"]
        self.rep = mesh.shape["rep"]
        self.chips = self.shards // 2
        self.ny = 2 if self.rep == 2 else 1
        self.bits = self.chips.bit_length() - 1

    def swap(self, v, flip_shard, flip_rep=0):
        pairs = []
        for s in range(self.shards):
            for y in range(self.rep):
                pairs.append((s * self.rep + y, (s ^ flip_shard) * self.rep + (y ^ flip_rep)))
        return lax.ppermute(v, AX, pairs)

    def core(self, v):
        return self.swap(v, 1)

    def flip(self, v, axis):
        if axis == 0:
            return self.swap(v, 0, 1)
        return self.swap(v, 2 << (self.bits - axis))


def dot(x, w):
    return lax.dot_general(x, w, (((1,), (0,)), ((), ())), preferred_element_type=F32)


def dot_t(x, w):
    return lax.dot_general(x, w, (((1,), (1,)), ((), ())), preferred_element_type=F32)


def t_dot(x, w):
    return lax.dot_general(x, w, (((0,), (0,)), ((), ())), preferred_element_type=F32)


def columns(width, first, stride):
    return ("columns", width, (first, stride))


def row_call(body, where, kept, weights, blocked, whole, outs, images, slots, after=(), cost=FORWARD):
    in_specs, args = [], []
    for v, pick_of in (part for w in weights for part in w):
        if pick_of is None:
            in_specs.append(pl.BlockSpec(v.shape, lambda i, w, k: (0, 0), pipeline_mode=ONCE))
            args.append(v)
            continue
        kind, width, first = pick_of
        if kind == "columns":
            spec = pl.BlockSpec((v.shape[0], width), lambda i, w, k, f=first: (0, f[0] + f[1] * w[0]), pipeline_mode=ONCE)
            in_specs.append(spec)
            args.append(v)
        elif kind == "quarter":
            at, stride, part = first
            spec = pl.BlockSpec(
                (v.shape[0], width),
                lambda i, w, k, f=(at, stride, part): (0, f[0] + f[1] * w[0] + jnp.bitwise_xor(f[2], w[3])),
                pipeline_mode=ONCE,
            )
            in_specs.append(spec)
            args.append(v)
        else:
            view = v.reshape(HEADS // 2, 2, HEAD_DIM, v.shape[1])
            spec = pl.BlockSpec((HEADS // 2, None, HEAD_DIM, width), lambda i, w, k, f=first: (0, w[0], 0, f), pipeline_mode=ONCE)
            in_specs.append(spec)
            args.append(view)
    for v in blocked:
        if v.ndim == 2:
            in_specs.append(pl.BlockSpec((slots, v.shape[1]), lambda i, *_: (i, 0)))
        else:
            in_specs.append(pl.BlockSpec((1,) + v.shape[1:], lambda i, *_, n=v.ndim: (i,) + (0,) * (n - 1)))
        args.append(v)
    for v in whole:
        in_specs.append(pl.BlockSpec(v.shape, lambda i, *_, n=v.ndim: (0,) * n))
        args.append(v)
    out_specs, out_shape = [], []
    for kind, shape, dtype in outs:
        out_shape.append(jax.ShapeDtypeStruct(shape, dtype))
        if kind == "rows":
            out_specs.append(pl.BlockSpec((slots, shape[1]), lambda i, *_: (i, 0)))
        elif kind == "image":
            out_specs.append(pl.BlockSpec((1,) + shape[1:], lambda i, *_, n=len(shape): (i,) + (0,) * (n - 1)))
        else:
            out_specs.append(pl.BlockSpec(shape, lambda i, *_, n=len(shape): (0,) * n))
    n_p, n_b, n_in = sum(len(w) for w in weights), len(blocked), len(args)
    in_specs += [ANY] * len(after)
    args += list(after)

    def kernel(where_ref, kept_ref, *refs):
        ins, res = refs[:n_in], refs[n_in + len(after) :]
        held, at = [], 0
        for w in weights:
            held.append(ins[at : at + len(w)])
            at += len(w)
        body(kept_ref, held, ins[n_p : n_p + n_b], ins[n_p + n_b : n_in], res)

    return pl.pallas_call(
        kernel,
        grid_spec=pltpu.PrefetchScalarGridSpec(
            num_scalar_prefetch=2, grid=(images,), in_specs=in_specs, out_specs=out_specs
        ),
        out_shape=out_shape,
        compiler_params=pltpu.CompilerParams(vmem_limit_bytes=LIMIT),
        cost_estimate=cost,
    )(where, kept, *args)


def normed_of(rows):
    width = rows.shape[-1]
    mean = jnp.sum(rows, axis=-1, keepdims=True) * (1.0 / width)
    centered = rows - mean
    spread = jnp.sum(centered * centered, axis=-1, keepdims=True) * (1.0 / width)
    factor = lax.rsqrt(spread + EPS)
    return centered * factor, factor


def norm_rows(rows, gain, shift):
    return normed_of(rows)[0] * gain + shift


def norm_back(dz, rows, gain):
    normed, factor = normed_of(rows)
    width = rows.shape[-1]
    prod = dz * normed
    dn = dz * gain
    m1 = jnp.sum(dn, axis=-1, keepdims=True) * (1.0 / width)
    m2 = jnp.sum(dn * normed, axis=-1, keepdims=True) * (1.0 / width)
    back = factor * (dn - m1 - normed * m2)
    return back, jnp.sum(prod, axis=0, keepdims=True), jnp.sum(dz, axis=0, keepdims=True)


def chunks(total, size):
    size = min(size, total)
    return [(k, size) for k in range(0, total, size)]


def qkv_body(kept, w, blocked, whole, outs):
    x = blocked[0][...]
    for k, n in chunks(outs[0].shape[1], 512):
        cols = pl.ds(k, n)
        outs[0][:, cols] = (dot(x, w[0][0][:, cols]) + whole[0][:, cols]).astype(BF)


def heads_of(ref):
    return ref[...].reshape(-1, ref.shape[-1])


def pairs_dot(x_ref, parts):
    total, at = None, 0
    for w_ref in parts:
        term = dot(x_ref[:, at : at + w_ref.shape[0]], w_ref[...])
        total = term if total is None else total + term
        at += w_ref.shape[0]
    return total


def attend(kept, proj_ref, probs_ref, att_ref):
    slots, third = proj_ref.shape[0], proj_ref.shape[1] // 3
    bound = BUFFER + kept[pl.program_id(0)]
    alive = lax.broadcasted_iota(jnp.int32, (slots, slots), 1) < bound
    outs = []
    for h in range(third // HEAD_DIM):
        lo = h * HEAD_DIM
        q = proj_ref[:, lo : lo + HEAD_DIM]
        k = proj_ref[:, third + lo : third + lo + HEAD_DIM]
        v = proj_ref[:, 2 * third + lo : 2 * third + lo + HEAD_DIM]
        s = jnp.where(alive, dot_t(q, k) * SCALE, -1e30)
        e = jnp.exp(s - jnp.max(s, axis=-1, keepdims=True))
        p = (e * (1.0 / jnp.sum(e, axis=-1, keepdims=True))).astype(BF)
        probs_ref[0, h] = p
        outs.append(dot(p, v).astype(BF))
        if h % 2:
            att_ref[:, lo - HEAD_DIM : lo + HEAD_DIM] = jnp.concatenate(outs, axis=1)
            outs = []


def attend_other(kept, w, blocked, whole, outs):
    attend(kept, blocked[0], outs[0], outs[1])
    outs[2][...] = dot(outs[1][...], heads_of(w[0][0]))


def attend_own(kept, w, blocked, whole, outs):
    attend(kept, blocked[0], outs[0], outs[1])
    middle = blocked[2][...] + (dot(outs[1][...], heads_of(w[0][0])) + blocked[1][...]) + whole[0][...]
    outs[2][...] = middle
    outs[3][...] = norm_rows(middle, whole[1][...], whole[2][...]).astype(BF)


def up_body(kept, w, blocked, whole, outs):
    x = blocked[0][...]
    for k, n in chunks(outs[0].shape[1], 256):
        cols = pl.ds(k, n)
        held = w[0][k // w[0][0].shape[1]]
        pre = dot(x, held[:, pl.ds(k % held.shape[1], n)]) + whole[0][:, cols]
        phi = 0.5 + 0.5 * lax.erf(pre * (2.0**-0.5))
        dens = jnp.exp(-0.5 * (pre * pre)) * 0.3989422804014327
        outs[0][:, cols] = (pre * phi).astype(BF)
        outs[1][:, cols] = (phi + pre * dens).astype(BF)


def down_other(kept, w, blocked, whole, outs):
    outs[0][...] = pairs_dot(blocked[0], w[0])


def down_own(kept, w, blocked, whole, outs):
    state = blocked[2][...] + (pairs_dot(blocked[0], w[0]) + blocked[1][...]) + whole[0][...]
    outs[0][...] = state
    outs[1][...] = norm_rows(state, whole[1][...], whole[2][...]).astype(BF)


def down_last(kept, w, blocked, whole, outs):
    state = blocked[2][...] + (pairs_dot(blocked[0], w[0]) + blocked[1][...]) + whole[0][...]
    alive = lax.broadcasted_iota(jnp.int32, state.shape, 0) < BUFFER + kept[pl.program_id(0)]
    outs[0][...] = jnp.where(alive, state, 0.0).astype(BF)


def mlp_back(w, blocked, outs):
    low = blocked[0][...]
    for k, n in chunks(outs[0].shape[1], 512):
        cols = pl.ds(k, n)
        held = w[0][k // w[0][0].shape[0]]
        t = dot_t(low, held[pl.ds(k % held.shape[0], n), :])
        outs[0][:, cols] = (t * blocked[1][:, cols].astype(F32)).astype(BF)
    total, at = None, 0
    for held in w[1]:
        term = dot_t(outs[0][:, at : at + held.shape[1]], held[...])
        total = term if total is None else total + term
        at += held.shape[1]
    return total


def mlp_back_other(kept, w, blocked, whole, outs):
    outs[1][...] = mlp_back(w, blocked, outs)


def add_sums(ref, rows):
    sums = jnp.concatenate(rows + [jnp.zeros((8 - len(rows), rows[0].shape[1]), F32)], axis=0)

    @pl.when(pl.program_id(0) == 0)
    def _():
        ref[...] = sums

    @pl.when(pl.program_id(0) != 0)
    def _():
        ref[...] += sums


def mlp_back_own(kept, w, blocked, whole, outs):
    dz = mlp_back(w, blocked, outs) + blocked[2][...]
    back, gain, shift = norm_back(dz, blocked[3][...], whole[0][...])
    grad = blocked[4][...] + back
    low = grad.astype(BF)
    outs[1][...] = grad
    outs[2][...] = low
    add_sums(outs[3], [gain, shift, jnp.sum(low.astype(F32), axis=0, keepdims=True)])


def attend_back(w, blocked, outs):
    branch, proj_ref, probs_ref = blocked[0], blocked[1], blocked[2]
    third = proj_ref.shape[1] // 3
    datt = dot_t(branch[...], heads_of(w[0][0])).astype(BF)
    pairs = [[], [], []]
    for h in range(third // HEAD_DIM):
        lo = h * HEAD_DIM
        q = proj_ref[:, lo : lo + HEAD_DIM]
        k = proj_ref[:, third + lo : third + lo + HEAD_DIM]
        v = proj_ref[:, 2 * third + lo : 2 * third + lo + HEAD_DIM]
        da = datt[:, lo : lo + HEAD_DIM]
        p = probs_ref[0, h]
        dp = dot_t(da, v)
        pf = p.astype(F32)
        ds = (pf * (dp - jnp.sum(pf * dp, axis=-1, keepdims=True))).astype(BF)
        pairs[0].append((dot(ds, k) * SCALE).astype(BF))
        pairs[1].append((t_dot(ds, q) * SCALE).astype(BF))
        pairs[2].append(t_dot(p, da).astype(BF))
        if h % 2:
            for j in range(3):
                at = j * third + lo - HEAD_DIM
                outs[0][:, at : at + 2 * HEAD_DIM] = jnp.concatenate(pairs[j], axis=1)
            pairs = [[], [], []]
    return dot_t(outs[0][...], w[1][0][...])


def attend_back_other(kept, w, blocked, whole, outs):
    outs[1][...] = attend_back(w, blocked, outs)


def attend_back_own(kept, w, blocked, whole, outs):
    dz = attend_back(w, blocked, outs) + blocked[3][...]
    back, gain, shift = norm_back(dz, blocked[4][...], whole[0][...])
    grad = blocked[5][...] + back
    outs[1][...] = grad
    low = grad.astype(BF)
    outs[2][...] = low
    add_sums(outs[3], [gain, shift, jnp.sum(low.astype(F32), axis=0, keepdims=True)])


def weight_grad(plan, where, xs, ys, groups, first, sums=False, extra=0, relative=False, window=(0, 1), after=()):
    depth, n_x = xs[0].shape
    cols = ys[0].shape[1]
    ny, chips, bits = plan.ny, plan.chips, plan.bits
    half = cols // ny
    size = half // window[1]
    chunk = size if size <= 768 else 512
    steps = size // chunk
    rows = n_x // chips
    part = rows // groups
    dims = [ny] + [2] * bits
    dims[first] = 1
    block = [1] + dims[1:] + [rows, chunk]
    shape = dims + [rows, size + extra]
    n_after = len(after)

    def kernel(where_ref, xo, xt, yo, yt, *rest):
        rest = rest[n_after:]
        keep, send = rest[0], rest[1]
        flip, acc = rest[-2], rest[-1]
        step = pl.program_id(0)

        @pl.when(step == 0)
        def _():
            flip[:, :depth] = xo[...].T
            flip[:, depth:] = xt[...].T

        acc[...] = dot(flip[:, :depth], yo[...]) + dot(flip[:, depth:], yt[...])
        if sums:
            rest[2][...] = jnp.sum(yo[...].astype(F32), axis=0, keepdims=True) + jnp.sum(
                yt[...].astype(F32), axis=0, keepdims=True
            )

        def put(ref, r):
            at = [0]
            for k in range(1, bits + 1):
                at.append((r >> (bits - k)) & 1 if k != first else 0)
            chip = jnp.bitwise_xor(where_ref[1], r)
            for g in range(groups):
                start = pl.multiple_of(g * part * chips + chip * part, 16)
                place = g
                if groups == 2 and ny == 2:
                    place = jnp.bitwise_xor(g, where_ref[2])
                place = pl.multiple_of(place * part, 16)
                ref[tuple(at) + (pl.ds(place, part),)] = acc[pl.ds(start, part)].astype(BF)

        if first:
            for r in range(chips):
                put(send if (r >> (bits - first)) & 1 else keep, r)
        else:

            @pl.when(step < steps)
            def _():
                for r in range(chips):
                    put(keep, r)

            @pl.when(step >= steps)
            def _():
                for r in range(chips):
                    put(send, r)

    per_rep = half // chunk

    def column(i, w):
        own = w[2] if ny == 2 and not relative else 0
        return jnp.bitwise_xor(i // steps, own) * per_rep + window[0] * steps + i % steps

    zeros = (0,) * (bits + 1)
    x_spec = pl.BlockSpec((depth, n_x), lambda i, w: (0, 0), pipeline_mode=ONCE)
    y_spec = pl.BlockSpec((depth, chunk), lambda i, w: (0, column(i, w)))
    if first:
        specs = [pl.BlockSpec(block, lambda i, w: (i // steps,) + zeros + (i % steps,))] * 2
    else:
        specs = [
            pl.BlockSpec(block, lambda i, w: (0,) + zeros + (jnp.minimum(i, steps - 1),)),
            pl.BlockSpec(block, lambda i, w: (0,) + zeros + (jnp.maximum(i - steps, 0),)),
        ]
    out_shape = [jax.ShapeDtypeStruct(shape, BF)] * 2
    if sums:
        own = (lambda w: w[2]) if ny == 2 and not relative else (lambda w: 0)
        specs = specs + [
            pl.BlockSpec((1, chunk), lambda i, w: (0, jnp.bitwise_xor(i // steps, own(w)) * steps + i % steps))
        ]
        out_shape = out_shape + [jax.ShapeDtypeStruct((1, size * ny), F32)]
    return pl.pallas_call(
        kernel,
        grid_spec=pltpu.PrefetchScalarGridSpec(
            num_scalar_prefetch=1,
            grid=(ny * steps,),
            in_specs=[x_spec, x_spec, y_spec, y_spec] + [ANY] * n_after,
            out_specs=specs,
            scratch_shapes=[pltpu.VMEM((n_x, 2 * depth), BF), pltpu.VMEM((n_x, chunk), F32)],
        ),
        out_shape=out_shape,
        compiler_params=pltpu.CompilerParams(vmem_limit_bytes=LIMIT),
        cost_estimate=BACKWARD,
    )(where, *xs, *ys, *after)


def chip_grad(plan, where, xs, ys, groups, after=()):
    depth, n_x = xs[0].shape
    cols = ys[0].shape[1]
    chips = plan.chips
    chunk = min(cols, 512)
    rows = n_x // chips
    part = rows // groups
    n_after = len(after)

    def kernel(where_ref, xo, xt, yo, yt, *rest):
        out, flip, acc = rest[n_after:]

        @pl.when(pl.program_id(0) == 0)
        def _():
            flip[:, :depth] = xo[...].T
            flip[:, depth:] = xt[...].T

        acc[...] = dot(flip[:, :depth], yo[...]) + dot(flip[:, depth:], yt[...])
        for g in range(groups):
            place = jnp.bitwise_xor(g, where_ref[3]) * part
            for chip in range(chips):
                at = pl.ds(pl.multiple_of(place + chip * rows, 16), part)
                first = (g * chips + chip) * part
                out[at, :] = acc[first : first + part].astype(BF)

    x_spec = pl.BlockSpec((depth, n_x), lambda i, w: (0, 0), pipeline_mode=ONCE)
    y_spec = pl.BlockSpec((depth, chunk), lambda i, w: (0, i))
    return pl.pallas_call(
        kernel,
        grid_spec=pltpu.PrefetchScalarGridSpec(
            num_scalar_prefetch=1,
            grid=(cols // chunk,),
            in_specs=[x_spec, x_spec, y_spec, y_spec] + [ANY] * n_after,
            out_specs=pl.BlockSpec((n_x, chunk), lambda i, w: (0, i)),
            scratch_shapes=[pltpu.VMEM((n_x, 2 * depth), BF), pltpu.VMEM((n_x, chunk), F32)],
        ),
        out_shape=jax.ShapeDtypeStruct((n_x, cols), BF),
        compiler_params=pltpu.CompilerParams(vmem_limit_bytes=LIMIT),
        cost_estimate=BACKWARD,
    )(where, *xs, *ys, *after)


def proj_grad_into(plan, where, xs, ys, first, keep, send, after=()):
    depth, n_x = xs[0].shape
    cols = ys[0].shape[1]
    ny, chips, bits = plan.ny, plan.chips, plan.bits
    half = cols // ny
    part = n_x // chips
    width = half * part // keep.shape[-2]
    stacked = half // width
    at_col = keep.shape[-1] // width - 1
    block = [1] + list(keep.shape[1:-1]) + [width]

    n_after = len(after)

    def kernel(where_ref, xo, xt, yo, yt, k_in, s_in, *rest):
        keep_ref, send_ref, acc = rest[n_after:]
        acc[...] = t_dot(xo[...], yo[...]) + t_dot(xt[...], yt[...])

        def put(ref, r):
            at = [0]
            for k in range(1, bits + 1):
                at.append((r >> (bits - k)) & 1 if k != first else 0)
            start = pl.multiple_of(jnp.bitwise_xor(where_ref[1], r) * part, 16)
            for g in range(stacked):
                piece = acc[pl.ds(start, part), g * width : (g + 1) * width]
                ref[tuple(at) + (pl.ds(g * part, part),)] = piece.astype(BF)

        if first:
            for r in range(chips):
                put(send_ref if (r >> (bits - first)) & 1 else keep_ref, r)
        else:

            @pl.when(pl.program_id(0) == 0)
            def _():
                for r in range(chips):
                    put(keep_ref, r)

            @pl.when(pl.program_id(0) != 0)
            def _():
                for r in range(chips):
                    put(send_ref, r)

    zeros = (0,) * (bits + 1)
    own = (lambda w: w[2]) if ny == 2 else (lambda w: 0)
    x_spec = pl.BlockSpec((depth, n_x), lambda i, w: (0, 0), pipeline_mode=ONCE)
    y_spec = pl.BlockSpec((depth, half), lambda i, w: (0, jnp.bitwise_xor(i, own(w))))
    spec = pl.BlockSpec(block, lambda i, w: (i if first else 0,) + zeros + (at_col,))
    return pl.pallas_call(
        kernel,
        grid_spec=pltpu.PrefetchScalarGridSpec(
            num_scalar_prefetch=1,
            grid=(ny,),
            in_specs=[x_spec, x_spec, y_spec, y_spec, ANY, ANY] + [ANY] * n_after,
            out_specs=[spec, spec],
            scratch_shapes=[pltpu.VMEM((n_x, half), F32)],
        ),
        out_shape=[jax.ShapeDtypeStruct(keep.shape, BF)] * 2,
        input_output_aliases={5: 0, 6: 1},
        compiler_params=pltpu.CompilerParams(vmem_limit_bytes=LIMIT),
        cost_estimate=BACKWARD,
    )(where, *xs, *ys, keep, send, *after)


class Term:
    def __init__(self, plan, keep, send, order):
        self.plan, self.keep, self.order = plan, keep, list(order)
        self.got = plan.flip(send, self.order.pop(0))

    def step(self, after):
        axis = self.order.pop(0)
        self.keep, send = combine(self.keep, self.got, axis, after)
        self.got = self.plan.flip(send, axis)
        return send


def combine(keep, got, axis, after):
    shape = keep.shape
    rows, cols = shape[-2:]
    cuts = 2
    block = shape[:-2] + (rows // cuts, cols)
    out = shape[:axis] + (1,) + shape[axis + 1 :]
    out_block = out[:-2] + (rows // cuts, cols)
    lead = len(shape) - 2

    def kernel(k, g, *rest):
        stay, go = rest[-2:]
        for side, ref in ((0, stay), (1, go)):
            at = tuple(pl.ds(side, 1) if d == axis else slice(None) for d in range(lead))
            ref[...] = (k[at].astype(F32) + g[at].astype(F32)).astype(BF)

    index = lambda i: (0,) * lead + (i, 0)
    return pl.pallas_call(
        kernel,
        grid=(cuts,),
        in_specs=[pl.BlockSpec(block, index)] * 2 + [ANY] * len(after),
        out_specs=[pl.BlockSpec(out_block, index)] * 2,
        out_shape=[jax.ShapeDtypeStruct(out, BF)] * 2,
        compiler_params=pltpu.CompilerParams(vmem_limit_bytes=LIMIT),
        cost_estimate=BACKWARD,
    )(keep, got, *after)


def last_combine(terms, axis, rows, after):
    ins, specs, widths = [], [], []
    for t in terms:
        ins += [t.keep, t.got]
        widths.append(t.keep.shape[-1] * (t.keep.shape[-2] // rows))
    total = sum(widths)
    n_in = len(ins)

    def kernel(*refs):
        stay, go = refs[-2:]
        at = 0
        for j, t in enumerate(terms):
            k, g = refs[2 * j], refs[2 * j + 1]
            lead = k.ndim - 2
            cols = k.shape[-1]
            for block in range(k.shape[-2] // rows):
                for side, ref in ((0, stay), (1, go)):
                    idx = tuple(side if d == axis else 0 for d in range(lead)) + (pl.ds(block * rows, rows),)
                    ref[:, at : at + cols] = (k[idx].astype(F32) + g[idx].astype(F32)).astype(BF)
                at += cols

    whole = [pl.BlockSpec(v.shape, lambda n=v.ndim: (0,) * n) for v in ins]
    return pl.pallas_call(
        kernel,
        in_specs=whole + [ANY] * len(after),
        out_specs=[pl.BlockSpec((rows, total), lambda: (0, 0))] * 2,
        out_shape=[jax.ShapeDtypeStruct((rows, total), BF)] * 2,
        compiler_params=pltpu.CompilerParams(vmem_limit_bytes=LIMIT),
        cost_estimate=BACKWARD,
    )(*ins, *after)


def pick(flag, a, b):
    return jnp.where(flag == 0, a, b)


def small_call(kernel, where, ins, shapes, after, grid=None):
    n = len(ins)

    def body(where_ref, *refs):
        kernel(where_ref, refs[:n], refs[n + len(after) :])

    return pl.pallas_call(
        body,
        grid_spec=pltpu.PrefetchScalarGridSpec(
            num_scalar_prefetch=1,
            grid=(1,),
            in_specs=[pl.BlockSpec(v.shape, lambda i, w, n=v.ndim: (0,) * n) for v in ins] + [ANY] * len(after),
            out_specs=[pl.BlockSpec(s, lambda i, w, n=len(s): (0,) * n) for s, _ in shapes],
        ),
        out_shape=[jax.ShapeDtypeStruct(s, t) for s, t in shapes],
        compiler_params=pltpu.CompilerParams(vmem_limit_bytes=LIMIT),
        cost_estimate=BACKWARD,
    )(where, *ins, *after)


class Ending:
    def __init__(self, plan, where, terms, axis, rows, tail, after):
        self.plan, self.where, self.rows, self.tail = plan, where, rows, tail
        self.keep, self.sent = last_combine(terms, axis, rows, after)
        self.got = plan.flip(self.sent, axis)

    def core(self, after):
        rows, tail = self.rows // 2, self.tail
        cols = self.cols = self.keep.shape[1] - tail

        def kernel(where, ins, outs):
            c = where[0]
            for ref, row in ((outs[0], c), (outs[1], 1 - c)):
                at = pl.ds(pl.multiple_of(row * rows, 16), rows)
                ref[:, :cols] = (ins[0][at, :cols].astype(F32) + ins[1][at, :cols].astype(F32)).astype(BF)
            if tail:
                for g in range(2):
                    at = pl.ds(g * rows, rows)
                    piece = ins[0][at, cols:].astype(F32) + ins[1][at, cols:].astype(F32)
                    outs[0][:, cols + g * tail : cols + (g + 1) * tail] = piece.astype(BF)

        shapes = [((rows, cols + 2 * tail), BF), ((rows, cols), BF)]
        self.mine, sent = small_call(kernel, self.where, [self.keep, self.got], shapes, after)
        self.came = self.plan.core(sent)
        return sent

    def rep(self, after):
        rows, cols, tail = self.rows // 2, self.cols, self.tail

        def kernel(where, ins, outs):
            outs[0][:, :cols] = ins[0][:, :cols]
            outs[0][:, cols : 2 * cols] = ins[1][...]
            if tail:
                outs[0][:, 2 * cols :] = ins[0][:, cols:]

        shapes = [((rows, 2 * cols + 2 * tail), BF)]
        v = small_call(kernel, self.where, [self.mine, self.came], shapes, after)[0]
        self.pair = [v, self.plan.flip(v, 0)] if self.plan.ny == 2 else [lax.psum(v, "rep")]
        return v


class ChipEnding:
    def __init__(self, plan, where, term):
        self.plan, self.where = plan, where
        groups = [[2 * chip + c for chip in range(plan.chips)] for c in range(2)]
        self.term = lax.psum_scatter(term, "shard", scatter_dimension=0, axis_index_groups=groups, tiled=True)

    def core(self, after):
        rows, cols = self.term.shape
        part = rows // 4

        def kernel(where, ins, outs):
            c = where[0]
            for ref, row in ((outs[0], c), (outs[1], 1 - c)):
                for k in range(2):
                    at = pl.ds(pl.multiple_of((2 * k + row) * part, 16), part)
                    ref[k * part : (k + 1) * part] = ins[0][at]

        shapes = [((rows // 2, cols), BF)] * 2
        self.mine, sent = small_call(kernel, self.where, [self.term], shapes, after)
        self.came = self.plan.core(sent)
        return sent

    def rep(self, after):
        rows, cols = self.mine.shape

        def kernel(where, ins, outs):
            outs[0][:rows] = ins[0][...]
            outs[0][rows:] = ins[1][...]

        v = small_call(kernel, self.where, [self.mine, self.came], [((2 * rows, cols), BF)], after)[0]
        self.pair = [v, self.plan.flip(v, 0)] if self.plan.ny == 2 else [lax.psum(v, "rep")]
        return v


def place_grads(plan, where, layer, layers, end2, rest, sizes, before, after):
    deep, width, ff, quarters = sizes
    n, ny, halves = plan.shards, plan.ny, quarters // 2
    wide, half_ff = 3 * width // 2, ff // 2
    cols = rest.cols
    fused = bool(rest.tail)
    ins = end2.pair + rest.pair

    def kernel(where_ref, *refs):
        refs_in = refs[: 2 * ny]
        outs = refs[-(4 if fused else 3) :]
        c, y = where_ref[0], where_ref[2]

        def source(p, q, at, size):
            step = (at // 128) * 128
            span = (at + size - step + 127) // 128 * 128
            first = pl.multiple_of(jnp.where(p == c, 0, cols) + step, 128)
            v = refs_in[ny][:, pl.ds(first, span)]
            if ny == 2:
                v = jnp.where(y == q, v, refs_in[ny + 1][:, pl.ds(first, span)])
            return v[:, at - step : at - step + size].astype(F32)

        def core_columns(p, at, size, total, first):
            part = total // ny
            return source(p, at // part, first + at % part, size)

        for k in range(3 * HEADS // 2):
            pieces = [core_columns(p, k * HEAD_DIM, HEAD_DIM, wide, 0) for p in range(2)]
            outs[0][0, :, k * 2 * HEAD_DIM : (k + 1) * 2 * HEAD_DIM] = jnp.concatenate(pieces, axis=1)
        for k in range(n):
            pieces = []
            for p in range(2):
                for h in range(halves):
                    pieces.append(core_columns(p, (h * n + k) * deep, deep, half_ff, wide // ny))
            outs[1][0, :, k * quarters * deep : (k + 1) * quarters * deep] = jnp.concatenate(pieces, axis=1)
        part = width // ny
        for p in range(2):
            at = pl.ds(pl.multiple_of(jnp.where(p == c, 0, halves * deep), 16), halves * deep)
            v = refs_in[0][at].astype(F32)
            if ny == 2:
                v = v + refs_in[1][at].astype(F32)
            outs[2][0, p * halves * deep : (p + 1) * halves * deep] = v
        if fused:
            for q in range(ny):
                v = refs_in[ny][:, 2 * cols :]
                if ny == 2:
                    v = jnp.where(y == q, v, refs_in[ny + 1][:, 2 * cols :])
                outs[3][0, :, q * part : (q + 1) * part] = v.astype(F32)

    shapes = [(deep, 3 * width), (deep, ff), (quarters * deep, width)] + ([(deep, width)] if fused else [])
    in_specs = [pl.BlockSpec(v.shape, lambda i, w: (0, 0)) for v in ins]
    args = list(ins) + list(before or []) + list(after)
    n_before = len(before or [])
    return pl.pallas_call(
        kernel,
        grid_spec=pltpu.PrefetchScalarGridSpec(
            num_scalar_prefetch=1,
            grid=(1,),
            in_specs=in_specs + [ANY] * (n_before + len(after)),
            out_specs=[pl.BlockSpec((1,) + s, lambda i, w: (layer, 0, 0)) for s in shapes],
        ),
        out_shape=[jax.ShapeDtypeStruct((layers,) + s, F32) for s in shapes],
        input_output_aliases={1 + len(ins) + k: k for k in range(n_before)},
        compiler_params=pltpu.CompilerParams(vmem_limit_bytes=LIMIT),
        cost_estimate=BACKWARD,
    )(where, *args)


def per_device(
    plan,
    tokens,
    kept,
    attn_gain,
    attn_shift,
    qkv_weight,
    qv_bias,
    proj_weight,
    proj_bias,
    mlp_gain,
    mlp_shift,
    fc1_weight,
    fc1_bias,
    fc2_weight,
    fc2_bias,
    cotangent,
):
    images, slots, width = tokens.shape
    layers = attn_gain.shape[0]
    rows = images * slots
    n = plan.shards
    deep = qkv_weight.shape[1]
    shard = lax.axis_index("shard")
    c, chip, y = lax.rem(shard, 2), shard // 2, lax.axis_index("rep")
    where = jnp.stack([c, chip, y, y if plan.ny == 2 else 0 * y]).astype(jnp.int32)
    ff = fc2_weight.shape[1] * n
    quarters = fc2_weight.shape[1] // deep
    wide, half_width, half_ff = 3 * width // 2, width // 2, ff // 2
    half_heads = HEADS // 2

    small = jnp.concatenate(
        [attn_gain, attn_shift, qv_bias, proj_bias, mlp_gain, mlp_shift, fc1_bias, fc2_bias], axis=1
    )
    sizes = [v.shape[1] for v in (attn_gain, attn_shift, qv_bias, proj_bias, mlp_gain, mlp_shift, fc1_bias, fc2_bias)]
    lines = small.size // 128
    extra = jnp.pad(small.reshape(lines, 128), ((0, deep - lines), (0, 0)))

    halves = quarters // 2
    lead = 4 * width
    block = n * deep
    each = halves // plan.ny

    def merged(layer):
        qkv = qkv_weight[layer].reshape(deep, 3 * half_heads, 2, HEAD_DIM).swapaxes(1, 2).reshape(deep, 3 * width)
        fc1 = fc1_weight[layer].reshape(deep, n, quarters, deep).swapaxes(1, 2).reshape(deep, ff)
        fc2 = fc2_weight[layer].reshape(2, halves, deep, width)
        if plan.ny == 2:
            fc2 = pick(y, fc2[:, :1], fc2[:, 1:])
        fc2 = [fc2[p, k] for p in range(2) for k in range(each)]
        return [qkv, proj_weight[layer], fc1] + fc2 + ([] if layer else [extra])

    operands = [jnp.concatenate(merged(layer), axis=1) for layer in range(layers)]
    gathered = [lax.all_gather(v, "shard", axis=0, tiled=True) for v in operands]
    at_fc1, at_fc2 = lead // block, (lead + ff) // block
    mlp_parts = []
    for layer in range(layers):
        found = {"fc1": [(gathered[layer], ("quarter", block, (at_fc1, halves, k))) for k in range(halves)]}
        found["fc2"] = [(gathered[layer], columns(block, at_fc2 + k, each)) for k in range(each)]
        if plan.ny == 2:
            mine = lax.dynamic_slice_in_dim(gathered[layer], (at_fc2 + c) * block, block, axis=1)
            found["fc2"].append((plan.flip(mine, 0), None))
            found["sent"], found["came"] = (mine,), (found["fc2"][-1][0],)
        mlp_parts.append(found)

    def weight_of(layer, name):
        if name == "qkv":
            return [(gathered[layer], columns(wide, 0, 1))]
        if name == "proj":
            return [(gathered[layer], ("heads", width, 3))]
        return mlp_parts[layer][name]

    every = gathered[0].reshape(n, deep, -1)[:, :lines, lead + ff + 2 * each * block :]
    every = every.reshape(n, layers, small.shape[1]).astype(F32)
    vecs = []
    for layer in range(layers):
        at, d = 0, {}
        for name, size in zip(SMALL, sizes):
            d[name] = every[:, layer, at : at + size].reshape(1, n * size)
            at += size
        q = d["qvb"].reshape(2 * half_heads, 2, HEAD_DIM)
        q = pick(c, q[:, 0], q[:, 1]).reshape(2, half_width)
        d["qvb_c"] = jnp.stack([q[0], jnp.zeros_like(q[0]), q[1]]).reshape(1, wide)
        f = d["f1b"].reshape(n, 2, halves, deep).transpose(1, 2, 0, 3).reshape(2, halves, block)
        f = pick(c, f[0], f[1])
        if plan.ny == 2:
            f = pick(y, f, f[::-1])
        d["f1b_c"] = f.reshape(1, half_ff)
        vecs.append(d)

    kept_oth = plan.core(kept)
    state = tokens.astype(F32).reshape(rows, width)
    live = lax.broadcasted_iota(jnp.int32, (images, slots), 1) < BUFFER + kept[:, None]
    grad = jnp.where(live[:, :, None], cotangent.astype(F32), 0.0).reshape(rows, width)
    low_own = grad.astype(BF)
    low_oth = plan.core(low_own)
    first_own = norm_rows(state, vecs[0]["ag"], vecs[0]["as"]).astype(BF)

    f32_rows, low_rows = ("rows", (rows, width), F32), ("rows", (rows, width), BF)
    wide_rows, ff_rows = ("rows", (rows, wide), BF), ("rows", (rows, half_ff), BF)
    att_outs = [("image", (images, half_heads, slots, slots), BF), ("rows", (rows, half_width), BF)]
    full_sums = ("full", (8, width), F32)

    def call(body, layer, own, names, blocked, whole, outs, after=(), cost=None):
        chosen = [weight_of(layer, name) for name in names]
        k = kept if own else kept_oth
        return row_call(body, where, k, chosen, blocked, whole, outs, images, slots, after, cost or (BACKWARD if after else FORWARD))

    saved = []
    for layer in range(layers):
        v = vecs[layer]
        first_oth = plan.core(first_own)
        sent = mlp_parts[layer].get("sent", ())
        proj_oth = call(qkv_body, layer, 0, ["qkv"], [first_oth], [v["qvb_c"]], [wide_rows], sent, FORWARD)[0]
        probs_oth, att_oth, part = call(attend_other, layer, 0, ["proj"], [proj_oth], [], att_outs + [f32_rows])
        part = plan.core(part)
        proj_own = call(qkv_body, layer, 1, ["qkv"], [first_own], [v["qvb_c"]], [wide_rows])[0]
        probs_own, att_own, middle, second_own = call(
            attend_own, layer, 1, ["proj"], [proj_own, part, state], [v["pb"], v["mg"], v["ms"]], att_outs + [f32_rows, low_rows])
        second_oth = plan.core(second_own)
        came = mlp_parts[layer].get("came", ())
        hid_oth, slope_oth = call(up_body, layer, 0, ["fc1"], [second_oth], [v["f1b_c"]], [ff_rows] * 2, came, FORWARD)
        if layer + 1 < layers:
            part = call(down_other, layer, 0, ["fc2"], [hid_oth], [], [f32_rows])[0]
            part = plan.core(part)
        hid_own, slope_own = call(up_body, layer, 1, ["fc1"], [second_own], [v["f1b_c"]], [ff_rows] * 2)
        saved.append(
            dict(
                state=state,
                first=(first_own, first_oth),
                proj=(proj_own, proj_oth),
                probs=(probs_own, probs_oth),
                att=(att_own, att_oth),
                middle=middle,
                second=(second_own, second_oth),
                hid=(hid_own, hid_oth),
                slope=(slope_own, slope_oth),
            )
        )
        if layer + 1 < layers:
            w = vecs[layer + 1]
            state, first_own = call(
                down_own, layer, 1, ["fc2"], [hid_own, part, middle], [v["f2b"], w["ag"], w["as"]], [f32_rows, low_rows])

    axes = list(range(1 if plan.ny == 1 else 0, plan.bits + 1))
    last_axis, z_axis, x_axis = 1, plan.bits - 1, plan.bits
    y_axis = 0 if plan.ny == 2 else 2
    orders_f1 = [[y_axis, x_axis, z_axis]] * layers
    orders_q = [[[z_axis, x_axis, y_axis], [y_axis, z_axis, x_axis]]] + [[[x_axis, z_axis, y_axis]]] * (layers - 1)
    own_rows = 2 * deep
    tail = width // plan.ny * HEAD_DIM // own_rows
    fused = n == HEADS
    tail = tail if fused else 0
    big = [[None] * 4 for _ in range(layers)]
    sums = [None] * layers
    f2b_sum = jnp.sum(low_own.astype(F32), axis=0, keepdims=True)

    def end_rest(layer, prev):
        group = terms["q", layer] + [terms["f1", layer]]
        ends["rest", layer] = Ending(plan, where, group, last_axis, own_rows, tail, prev)
        return (ends["rest", layer].sent,)

    def place(layer, before, prev):
        return place_grads(
            plan, where, layer, layers, ends["f2", layer], ends["rest", layer], (deep, width, ff, quarters), before, prev
        )

    ends = {}
    prev = (hid_own,)
    terms = {}
    for layer in reversed(range(layers)):
        v, s = vecs[layer], saved[layer]
        top = layer == layers - 1

        def grad_fc2(prev):
            term = chip_grad(plan, where, s["hid"], (low_own, low_oth), 2, prev)
            ends["f2", layer] = ChipEnding(plan, where, term)
            return (term,)

        if top:
            prev = grad_fc2(prev)
        pre_oth, part = call(
            mlp_back_other, layer, 0, ["fc2", "fc1"], [low_oth, s["slope"][1]], [], [ff_rows, f32_rows], prev
        )
        part = plan.core(part)
        prev = (pre_oth,)
        if top:
            last_part = call(down_other, layer, 0, ["fc2"], [s["hid"][1]], [], [f32_rows], prev)[0]
            prev = (last_part,)
            last_part = plan.core(last_part)
        else:
            prev += (terms["f1", layer + 1].step(prev[:1]),)
            prev = grad_fc2(prev)
        pre_own, mid_grad, branch_own, sum1 = call(
            mlp_back_own,
            layer,
            1,
            ["fc2", "fc1"],
            [low_own, s["slope"][0], part, s["middle"], grad],
            [v["mg"]],
            [ff_rows, f32_rows, low_rows, full_sums],
            prev,
        )
        branch_oth = plan.core(branch_own)
        prev = (branch_own,)
        if not top:
            prev += (terms["q", layer + 1][0].step(prev),)
        res1 = weight_grad(
            plan, where, s["second"], (pre_own, pre_oth), 1, orders_f1[layer][0], sums=True, extra=tail, relative=True, after=prev
        )
        prev = tuple(res1[:1])
        if not top:
            prev += (terms["f1", layer + 1].step(prev[:1]),)
            prev += (ends["f2", layer + 1].core(prev[:1]),)
        dproj_oth, part = call(
            attend_back_other,
            layer,
            0,
            ["proj", "qkv"],
            [branch_oth, s["proj"][1], s["probs"][1]],
            [],
            [wide_rows, f32_rows],
            prev,
        )
        part = plan.core(part)
        prev = (dproj_oth,)
        keep, send = res1[:2]
        if fused:
            keep, send = proj_grad_into(
                plan, where, s["att"], (branch_own, branch_oth), orders_f1[layer][0], keep, send, prev
            )
        else:
            term = t_dot(s["att"][0], branch_own) + t_dot(s["att"][1], branch_oth)
            term = term.astype(BF).reshape(half_heads, HEAD_DIM, width)
            none = jnp.zeros_like(term)
            term = jnp.stack([pick(c, term, none), pick(c, none, term)], axis=1).reshape(width, width)
            term = lax.psum_scatter(term, "shard", scatter_dimension=0, tiled=True)
            big[layer][1] = lax.psum(term, "rep").astype(F32)
        terms["f1", layer] = Term(plan, keep, send, orders_f1[layer])
        prev = (send,)
        if not top:
            prev += (terms["q", layer + 1][0].step(prev[:1]),)
            prev += (ends["f2", layer + 1].rep(prev[:1]),)
        dproj_own, grad, low_own, sum2 = call(
            attend_back_own,
            layer,
            1,
            ["proj", "qkv"],
            [branch_own, s["proj"][0], s["probs"][0], part, s["state"], mid_grad],
            [v["ag"]],
            [wide_rows, f32_rows, low_rows, full_sums],
            prev,
        )
        prev = (dproj_own,)
        if layer:
            low_oth = plan.core(low_own)
        if not top:
            prev += end_rest(layer + 1, prev[:1])
            prev += (ends["f2", layer].core(prev[:1]),)
        terms["q", layer], q_sums = [], []
        of = len(orders_q[layer])
        for k, order in enumerate(orders_q[layer]):
            resq = weight_grad(
                plan, where, s["first"], (dproj_own, dproj_oth), 1, order[0], sums=True, window=(k, of), after=prev
            )
            terms["q", layer].append(Term(plan, *resq[:2], order))
            q_sums.append(resq[2].reshape(plan.ny, -1))
            prev = (resq[1],)
        q = jnp.concatenate(q_sums, axis=1).reshape(3, half_heads, 1, HEAD_DIM)
        q = jnp.concatenate([q[:1], q[2:]])
        none = jnp.zeros_like(q)
        q = jnp.concatenate([pick(c, q, none), pick(c, none, q)], axis=2)
        f = res1[2].reshape(halves, block)
        if plan.ny == 2:
            f = pick(y, f, f[::-1])
        none = jnp.zeros_like(f)
        f = jnp.concatenate([pick(c, f, none), pick(c, none, f)], axis=0)
        f = f.reshape(quarters, n, deep).swapaxes(0, 1)
        full = {"ag": sum2[0], "as": sum2[1], "qvb": q, "pb": sum1[2], "mg": sum1[0], "ms": sum1[1], "f1b": f, "f2b": f2b_sum}
        f2b_sum = sum2[2]
        vec = jnp.concatenate([full[name].reshape(n, -1) for name in SMALL], axis=1)
        sums[layer] = vec

    vec = jnp.concatenate(sums, axis=0).reshape(layers, n, -1)
    got_vec = plan.core(vec)
    vec_axes = list(axes)

    def step_vec():
        nonlocal vec, got_vec
        vec = vec + got_vec
        sent = vec
        got_vec = plan.flip(vec, vec_axes.pop(0)) if vec_axes else None
        return (sent,)

    prev += (terms["f1", 0].step(prev[:1]),)
    prev += (ends["rest", 1].core(prev[:1]),)
    w = layers - 1
    mixed = call(
        down_last, w, 1, ["fc2"], [saved[w]["hid"][0], last_part, saved[w]["middle"]], [vecs[w]["f2b"]], [low_rows], prev
    )[0]
    qa, qb = terms["q", 0]
    prev = (qa.step((mixed,)),) + step_vec()
    prev = (qb.step(prev),)
    prev = (ends["rest", 1].rep(prev),) + step_vec()
    prev = (qa.step(prev),)
    prev = (terms["f1", 0].step(prev),)
    prev = (qb.step(prev),) + step_vec()
    prev = end_rest(0, prev) + step_vec()
    prev = (ends["f2", 0].rep(prev),)
    placed = place(1, None, prev)
    prev = (placed[0],)
    while got_vec is not None:
        prev += step_vec()
    prev = (ends["rest", 0].core(prev),)
    prev = (ends["rest", 0].rep(prev),)
    placed = place(0, placed, prev)
    if plan.ny == 1:
        vec = lax.psum(vec, "rep")
    vec = lax.dynamic_slice_in_dim(vec, shard, 1, axis=1)[:, 0]
    out, at = {}, 0
    for name, size in zip(SMALL, sizes):
        out[name] = vec[:, at : at + size]
        at += size
    qkv_g, fc1_g, fc2_g = placed[:3]
    proj_g = placed[3] if fused else jnp.stack([big[layer][1] for layer in range(layers)])
    return (
        mixed.reshape(images, slots, width),
        grad.reshape(images, slots, width),
        out["ag"],
        out["as"],
        qkv_g,
        out["qvb"],
        proj_g,
        out["pb"],
        out["mg"],
        out["ms"],
        fc1_g,
        out["f1b"],
        fc2_g,
        out["f2b"],
    )


def solution(mesh):
    rows = P(("shard", "rep"), None, None)
    vec = P(None, "shard")
    mat = P(None, "shard", None)
    return jax.shard_map(
        partial(per_device, Plan(mesh)),
        mesh=mesh,
        in_specs=(rows, P(("shard", "rep")), vec, vec, mat, vec, mat, vec, vec, vec, mat, vec, mat, vec, rows),
        out_specs=(rows, rows, vec, vec, mat, vec, mat, vec, vec, vec, mat, vec, mat, vec),
        check_vma=False,
    )
```

```python
from functools import partial

import jax
import jax.numpy as jnp
from jax import lax
from jax.experimental import pallas as pl
from jax.experimental.pallas import tpu as pltpu
from jax.sharding import PartitionSpec as P

HEADS = 16
HEAD_DIM = 64
BUFFER = 64
EPS = 1e-06
SCALE = HEAD_DIM ** (-0.5)
AX = ("shard", "rep")
BF = jnp.bfloat16
F32 = jnp.float32
LIMIT = 60 * 2**20
SMALL_LIMIT = 16 * 2**20
ONCE = pl.Buffered(1)
ANY = pl.BlockSpec(memory_space=pl.ANY)
FORWARD = pl.CostEstimate(flops=10**7, bytes_accessed=0, transcendentals=0)
BACKWARD = pl.CostEstimate(flops=10**9 * 30, bytes_accessed=0, transcendentals=0)
SMALL = ("ag", "as", "qvb", "pb", "mg", "ms", "f1b", "f2b")


class Plan:
    def __init__(self, mesh):
        self.shards = mesh.shape["shard"]
        self.rep = mesh.shape["rep"]
        self.chips = self.shards // 2
        self.ny = 2 if self.rep == 2 else 1
        self.bits = self.chips.bit_length() - 1

    def swap(self, v, flip_shard, flip_rep=0):
        pairs = []
        for s in range(self.shards):
            for y in range(self.rep):
                pairs.append((s * self.rep + y, (s ^ flip_shard) * self.rep + (y ^ flip_rep)))
        return lax.ppermute(v, AX, pairs)

    def core(self, v):
        return self.swap(v, 1)

    def flip(self, v, axis):
        if axis == 0:
            return self.swap(v, 0, 1)
        return self.swap(v, 2 << (self.bits - axis))


def dot(x, w):
    return lax.dot_general(x, w, (((1,), (0,)), ((), ())), preferred_element_type=F32)


def dot_t(x, w):
    return lax.dot_general(x, w, (((1,), (1,)), ((), ())), preferred_element_type=F32)


def t_dot(x, w):
    return lax.dot_general(x, w, (((0,), (0,)), ((), ())), preferred_element_type=F32)


def columns(width, first, stride):
    return ("columns", width, (first, stride))


def row_call(body, where, kept, weights, blocked, whole, outs, images, slots, after=(), cost=FORWARD):
    in_specs, args = [], []
    for v, pick_of in (part for w in weights for part in w):
        if pick_of is None:
            in_specs.append(pl.BlockSpec(v.shape, lambda i, w, k: (0, 0), pipeline_mode=ONCE))
            args.append(v)
            continue
        kind, width, first = pick_of
        if kind == "columns":
            spec = pl.BlockSpec((v.shape[0], width), lambda i, w, k, f=first: (0, f[0] + f[1] * w[0]), pipeline_mode=ONCE)
            in_specs.append(spec)
            args.append(v)
        elif kind == "quarter":
            at, stride, part = first
            spec = pl.BlockSpec(
                (v.shape[0], width),
                lambda i, w, k, f=(at, stride, part): (0, f[0] + f[1] * w[0] + jnp.bitwise_xor(f[2], w[3])),
                pipeline_mode=ONCE,
            )
            in_specs.append(spec)
            args.append(v)
        else:
            view = v.reshape(HEADS // 2, 2, HEAD_DIM, v.shape[1])
            spec = pl.BlockSpec((HEADS // 2, None, HEAD_DIM, width), lambda i, w, k, f=first: (0, w[0], 0, f), pipeline_mode=ONCE)
            in_specs.append(spec)
            args.append(view)
    for v in blocked:
        if v.ndim == 2:
            in_specs.append(pl.BlockSpec((slots, v.shape[1]), lambda i, *_: (i, 0)))
        else:
            in_specs.append(pl.BlockSpec((1,) + v.shape[1:], lambda i, *_, n=v.ndim: (i,) + (0,) * (n - 1)))
        args.append(v)
    for v in whole:
        in_specs.append(pl.BlockSpec(v.shape, lambda i, *_, n=v.ndim: (0,) * n))
        args.append(v)
    out_specs, out_shape = [], []
    for kind, shape, dtype in outs:
        out_shape.append(jax.ShapeDtypeStruct(shape, dtype))
        if kind == "rows":
            out_specs.append(pl.BlockSpec((slots, shape[1]), lambda i, *_: (i, 0)))
        elif kind == "image":
            out_specs.append(pl.BlockSpec((1,) + shape[1:], lambda i, *_, n=len(shape): (i,) + (0,) * (n - 1)))
        else:
            out_specs.append(pl.BlockSpec(shape, lambda i, *_, n=len(shape): (0,) * n))
    n_p, n_b, n_in = sum(len(w) for w in weights), len(blocked), len(args)
    in_specs += [ANY] * len(after)
    args += list(after)

    def kernel(where_ref, kept_ref, *refs):
        ins, res = refs[:n_in], refs[n_in + len(after) :]
        held, at = [], 0
        for w in weights:
            held.append(ins[at : at + len(w)])
            at += len(w)
        body(kept_ref, held, ins[n_p : n_p + n_b], ins[n_p + n_b : n_in], res)

    return pl.pallas_call(
        kernel,
        grid_spec=pltpu.PrefetchScalarGridSpec(
            num_scalar_prefetch=2, grid=(images,), in_specs=in_specs, out_specs=out_specs
        ),
        out_shape=out_shape,
        compiler_params=pltpu.CompilerParams(vmem_limit_bytes=LIMIT),
        cost_estimate=cost,
    )(where, kept, *args)


def normed_of(rows):
    width = rows.shape[-1]
    mean = jnp.sum(rows, axis=-1, keepdims=True) * (1.0 / width)
    centered = rows - mean
    spread = jnp.sum(centered * centered, axis=-1, keepdims=True) * (1.0 / width)
    factor = lax.rsqrt(spread + EPS)
    return centered * factor, factor


def norm_rows(rows, gain, shift):
    return normed_of(rows)[0] * gain + shift


def norm_back(dz, rows, gain):
    normed, factor = normed_of(rows)
    width = rows.shape[-1]
    prod = dz * normed
    dn = dz * gain
    m1 = jnp.sum(dn, axis=-1, keepdims=True) * (1.0 / width)
    m2 = jnp.sum(dn * normed, axis=-1, keepdims=True) * (1.0 / width)
    back = factor * (dn - m1 - normed * m2)
    return back, jnp.sum(prod, axis=0, keepdims=True), jnp.sum(dz, axis=0, keepdims=True)


def chunks(total, size):
    size = min(size, total)
    return [(k, size) for k in range(0, total, size)]


def qkv_body(kept, w, blocked, whole, outs):
    x = blocked[0][...]
    for k, n in chunks(outs[0].shape[1], 512):
        cols = pl.ds(k, n)
        outs[0][:, cols] = (dot(x, w[0][0][:, cols]) + whole[0][:, cols]).astype(BF)


def heads_of(ref):
    return ref[...].reshape(-1, ref.shape[-1])


def pairs_dot(x_ref, parts):
    total, at = None, 0
    for w_ref in parts:
        term = dot(x_ref[:, at : at + w_ref.shape[0]], w_ref[...])
        total = term if total is None else total + term
        at += w_ref.shape[0]
    return total


def attend(kept, proj_ref, probs_ref, att_ref):
    slots, third = proj_ref.shape[0], proj_ref.shape[1] // 3
    bound = BUFFER + kept[pl.program_id(0)]
    alive = lax.broadcasted_iota(jnp.int32, (slots, slots), 1) < bound
    outs = []
    for h in range(third // HEAD_DIM):
        lo = h * HEAD_DIM
        q = proj_ref[:, lo : lo + HEAD_DIM]
        k = proj_ref[:, third + lo : third + lo + HEAD_DIM]
        v = proj_ref[:, 2 * third + lo : 2 * third + lo + HEAD_DIM]
        s = jnp.where(alive, dot_t(q, k) * SCALE, -1e30)
        e = jnp.exp(s - jnp.max(s, axis=-1, keepdims=True))
        p = (e * (1.0 / jnp.sum(e, axis=-1, keepdims=True))).astype(BF)
        probs_ref[0, h] = p
        outs.append(dot(p, v).astype(BF))
        if h % 2:
            att_ref[:, lo - HEAD_DIM : lo + HEAD_DIM] = jnp.concatenate(outs, axis=1)
            outs = []


def attend_other(kept, w, blocked, whole, outs):
    attend(kept, blocked[0], outs[0], outs[1])
    outs[2][...] = dot(outs[1][...], heads_of(w[0][0]))


def attend_own(kept, w, blocked, whole, outs):
    attend(kept, blocked[0], outs[0], outs[1])
    middle = blocked[2][...] + (dot(outs[1][...], heads_of(w[0][0])) + blocked[1][...]) + whole[0][...]
    outs[2][...] = middle
    outs[3][...] = norm_rows(middle, whole[1][...], whole[2][...]).astype(BF)


def up_body(kept, w, blocked, whole, outs):
    x = blocked[0][...]
    for k, n in chunks(outs[0].shape[1], 256):
        cols = pl.ds(k, n)
        held = w[0][k // w[0][0].shape[1]]
        pre = dot(x, held[:, pl.ds(k % held.shape[1], n)]) + whole[0][:, cols]
        phi = 0.5 + 0.5 * lax.erf(pre * (2.0**-0.5))
        dens = jnp.exp(-0.5 * (pre * pre)) * 0.3989422804014327
        outs[0][:, cols] = (pre * phi).astype(BF)
        outs[1][:, cols] = (phi + pre * dens).astype(BF)


def down_other(kept, w, blocked, whole, outs):
    outs[0][...] = pairs_dot(blocked[0], w[0])


def down_own(kept, w, blocked, whole, outs):
    state = blocked[2][...] + (pairs_dot(blocked[0], w[0]) + blocked[1][...]) + whole[0][...]
    outs[0][...] = state
    outs[1][...] = norm_rows(state, whole[1][...], whole[2][...]).astype(BF)


def down_last(kept, w, blocked, whole, outs):
    state = blocked[2][...] + (pairs_dot(blocked[0], w[0]) + blocked[1][...]) + whole[0][...]
    alive = lax.broadcasted_iota(jnp.int32, state.shape, 0) < BUFFER + kept[pl.program_id(0)]
    outs[0][...] = jnp.where(alive, state, 0.0).astype(BF)


def mlp_back(w, blocked, outs):
    low = blocked[0][...]
    for k, n in chunks(outs[0].shape[1], 512):
        cols = pl.ds(k, n)
        held, first = w[0][0], 0
        for part in w[0][1:]:
            if k >= first + held.shape[0]:
                first += held.shape[0]
                held = part
        t = dot_t(low, held[pl.ds(k - first, n), :])
        outs[0][:, cols] = (t * blocked[1][:, cols].astype(F32)).astype(BF)
    total, at = None, 0
    for held in w[1]:
        term = dot_t(outs[0][:, at : at + held.shape[1]], held[...])
        total = term if total is None else total + term
        at += held.shape[1]
    return total


def mlp_back_other(kept, w, blocked, whole, outs):
    outs[1][...] = mlp_back(w, blocked, outs)


def add_sums(ref, rows):
    sums = jnp.concatenate(rows + [jnp.zeros((8 - len(rows), rows[0].shape[1]), F32)], axis=0)

    @pl.when(pl.program_id(0) == 0)
    def _():
        ref[...] = sums

    @pl.when(pl.program_id(0) != 0)
    def _():
        ref[...] += sums


def mlp_back_own(kept, w, blocked, whole, outs):
    dz = mlp_back(w, blocked, outs) + blocked[2][...]
    back, gain, shift = norm_back(dz, blocked[3][...], whole[0][...])
    grad = blocked[4][...] + back
    low = grad.astype(BF)
    outs[1][...] = grad
    outs[2][...] = low
    add_sums(outs[3], [gain, shift, jnp.sum(low.astype(F32), axis=0, keepdims=True)])


def attend_back(w, blocked, outs):
    branch, proj_ref, probs_ref = blocked[0], blocked[1], blocked[2]
    third = proj_ref.shape[1] // 3
    datt = dot_t(branch[...], heads_of(w[0][0])).astype(BF)
    pairs = [[], [], []]
    for h in range(third // HEAD_DIM):
        lo = h * HEAD_DIM
        q = proj_ref[:, lo : lo + HEAD_DIM]
        k = proj_ref[:, third + lo : third + lo + HEAD_DIM]
        v = proj_ref[:, 2 * third + lo : 2 * third + lo + HEAD_DIM]
        da = datt[:, lo : lo + HEAD_DIM]
        p = probs_ref[0, h]
        dp = dot_t(da, v)
        pf = p.astype(F32)
        ds = (pf * (dp - jnp.sum(pf * dp, axis=-1, keepdims=True))).astype(BF)
        pairs[0].append((dot(ds, k) * SCALE).astype(BF))
        pairs[1].append((t_dot(ds, q) * SCALE).astype(BF))
        pairs[2].append(t_dot(p, da).astype(BF))
        if h % 2:
            for j in range(3):
                at = j * third + lo - HEAD_DIM
                outs[0][:, at : at + 2 * HEAD_DIM] = jnp.concatenate(pairs[j], axis=1)
            pairs = [[], [], []]
    return dot_t(outs[0][...], w[1][0][...])


def attend_back_other(kept, w, blocked, whole, outs):
    outs[1][...] = attend_back(w, blocked, outs)


def attend_back_own(kept, w, blocked, whole, outs):
    dz = attend_back(w, blocked, outs) + blocked[3][...]
    back, gain, shift = norm_back(dz, blocked[4][...], whole[0][...])
    grad = blocked[5][...] + back
    outs[1][...] = grad
    low = grad.astype(BF)
    outs[2][...] = low
    add_sums(outs[3], [gain, shift, jnp.sum(low.astype(F32), axis=0, keepdims=True)])


def weight_grad(plan, where, xs, ys, groups, first, sums=False, extra=0, relative=False, window=(0, 1), after=()):
    depth, n_x = xs[0].shape
    cols = ys[0].shape[1]
    ny, chips, bits = plan.ny, plan.chips, plan.bits
    half = cols // ny
    size = half // window[1]
    chunk = size if size <= 768 else 512
    steps = size // chunk
    rows = n_x // chips
    part = rows // groups
    dims = [ny] + [2] * bits
    dims[first] = 1
    block = [1] + dims[1:] + [rows, chunk]
    shape = dims + [rows, size + extra]
    n_after = len(after)

    def kernel(where_ref, xo, xt, yo, yt, *rest):
        rest = rest[n_after:]
        keep, send = rest[0], rest[1]
        flip, acc = rest[-2], rest[-1]
        step = pl.program_id(0)

        @pl.when(step == 0)
        def _():
            flip[:, :depth] = xo[...].T
            flip[:, depth:] = xt[...].T

        acc[...] = dot(flip[:, :depth], yo[...]) + dot(flip[:, depth:], yt[...])
        if sums:
            rest[2][...] = jnp.sum(yo[...].astype(F32), axis=0, keepdims=True) + jnp.sum(
                yt[...].astype(F32), axis=0, keepdims=True
            )

        def put(ref, r):
            at = [0]
            for k in range(1, bits + 1):
                at.append((r >> (bits - k)) & 1 if k != first else 0)
            chip = jnp.bitwise_xor(where_ref[1], r)
            for g in range(groups):
                start = pl.multiple_of(g * part * chips + chip * part, 16)
                place = g
                if groups == 2 and ny == 2:
                    place = jnp.bitwise_xor(g, where_ref[2])
                place = pl.multiple_of(place * part, 16)
                ref[tuple(at) + (pl.ds(place, part),)] = acc[pl.ds(start, part)].astype(BF)

        if first:
            for r in range(chips):
                put(send if (r >> (bits - first)) & 1 else keep, r)
        else:

            @pl.when(step < steps)
            def _():
                for r in range(chips):
                    put(keep, r)

            @pl.when(step >= steps)
            def _():
                for r in range(chips):
                    put(send, r)

    per_rep = half // chunk

    def column(i, w):
        own = w[2] if ny == 2 and not relative else 0
        return jnp.bitwise_xor(i // steps, own) * per_rep + window[0] * steps + i % steps

    zeros = (0,) * (bits + 1)
    x_spec = pl.BlockSpec((depth, n_x), lambda i, w: (0, 0), pipeline_mode=ONCE)
    y_spec = pl.BlockSpec((depth, chunk), lambda i, w: (0, column(i, w)))
    if first:
        specs = [pl.BlockSpec(block, lambda i, w: (i // steps,) + zeros + (i % steps,))] * 2
    else:
        specs = [
            pl.BlockSpec(block, lambda i, w: (0,) + zeros + (jnp.minimum(i, steps - 1),)),
            pl.BlockSpec(block, lambda i, w: (0,) + zeros + (jnp.maximum(i - steps, 0),)),
        ]
    out_shape = [jax.ShapeDtypeStruct(shape, BF)] * 2
    if sums:
        own = (lambda w: w[2]) if ny == 2 and not relative else (lambda w: 0)
        specs = specs + [
            pl.BlockSpec((1, chunk), lambda i, w: (0, jnp.bitwise_xor(i // steps, own(w)) * steps + i % steps))
        ]
        out_shape = out_shape + [jax.ShapeDtypeStruct((1, size * ny), F32)]
    return pl.pallas_call(
        kernel,
        grid_spec=pltpu.PrefetchScalarGridSpec(
            num_scalar_prefetch=1,
            grid=(ny * steps,),
            in_specs=[x_spec, x_spec, y_spec, y_spec] + [ANY] * n_after,
            out_specs=specs,
            scratch_shapes=[pltpu.VMEM((n_x, 2 * depth), BF), pltpu.VMEM((n_x, chunk), F32)],
        ),
        out_shape=out_shape,
        compiler_params=pltpu.CompilerParams(vmem_limit_bytes=LIMIT),
        cost_estimate=BACKWARD,
    )(where, *xs, *ys, *after)


def chip_grad(plan, where, xs, ys, groups, after=()):
    depth, n_x = xs[0].shape
    cols = ys[0].shape[1]
    chips = plan.chips
    chunk = min(cols, 512)
    rows = n_x // chips
    part = rows // groups
    n_after = len(after)

    def kernel(where_ref, xo, xt, yo, yt, *rest):
        out, flip, acc = rest[n_after:]

        @pl.when(pl.program_id(0) == 0)
        def _():
            flip[:, :depth] = xo[...].T
            flip[:, depth:] = xt[...].T

        acc[...] = dot(flip[:, :depth], yo[...]) + dot(flip[:, depth:], yt[...])
        for g in range(groups):
            place = jnp.bitwise_xor(g, where_ref[3]) * part
            for chip in range(chips):
                at = pl.ds(pl.multiple_of(place + chip * rows, 16), part)
                first = (g * chips + chip) * part
                out[at, :] = acc[first : first + part].astype(BF)

    x_spec = pl.BlockSpec((depth, n_x), lambda i, w: (0, 0), pipeline_mode=ONCE)
    y_spec = pl.BlockSpec((depth, chunk), lambda i, w: (0, i))
    return pl.pallas_call(
        kernel,
        grid_spec=pltpu.PrefetchScalarGridSpec(
            num_scalar_prefetch=1,
            grid=(cols // chunk,),
            in_specs=[x_spec, x_spec, y_spec, y_spec] + [ANY] * n_after,
            out_specs=pl.BlockSpec((n_x, chunk), lambda i, w: (0, i)),
            scratch_shapes=[pltpu.VMEM((n_x, 2 * depth), BF), pltpu.VMEM((n_x, chunk), F32)],
        ),
        out_shape=jax.ShapeDtypeStruct((n_x, cols), BF),
        compiler_params=pltpu.CompilerParams(vmem_limit_bytes=LIMIT),
        cost_estimate=BACKWARD,
    )(where, *xs, *ys, *after)


def proj_grad_into(plan, where, xs, ys, first, keep, send, after=()):
    depth, n_x = xs[0].shape
    cols = ys[0].shape[1]
    ny, chips, bits = plan.ny, plan.chips, plan.bits
    half = cols // ny
    part = n_x // chips
    width = half * part // keep.shape[-2]
    stacked = half // width
    at_col = keep.shape[-1] // width - 1
    block = [1] + list(keep.shape[1:-1]) + [width]

    n_after = len(after)

    def kernel(where_ref, xo, xt, yo, yt, k_in, s_in, *rest):
        keep_ref, send_ref, acc = rest[n_after:]
        acc[...] = t_dot(xo[...], yo[...]) + t_dot(xt[...], yt[...])

        def put(ref, r):
            at = [0]
            for k in range(1, bits + 1):
                at.append((r >> (bits - k)) & 1 if k != first else 0)
            start = pl.multiple_of(jnp.bitwise_xor(where_ref[1], r) * part, 16)
            for g in range(stacked):
                piece = acc[pl.ds(start, part), g * width : (g + 1) * width]
                ref[tuple(at) + (pl.ds(g * part, part),)] = piece.astype(BF)

        if first:
            for r in range(chips):
                put(send_ref if (r >> (bits - first)) & 1 else keep_ref, r)
        else:

            @pl.when(pl.program_id(0) == 0)
            def _():
                for r in range(chips):
                    put(keep_ref, r)

            @pl.when(pl.program_id(0) != 0)
            def _():
                for r in range(chips):
                    put(send_ref, r)

    zeros = (0,) * (bits + 1)
    own = (lambda w: w[2]) if ny == 2 else (lambda w: 0)
    x_spec = pl.BlockSpec((depth, n_x), lambda i, w: (0, 0), pipeline_mode=ONCE)
    y_spec = pl.BlockSpec((depth, half), lambda i, w: (0, jnp.bitwise_xor(i, own(w))))
    spec = pl.BlockSpec(block, lambda i, w: (i if first else 0,) + zeros + (at_col,))
    return pl.pallas_call(
        kernel,
        grid_spec=pltpu.PrefetchScalarGridSpec(
            num_scalar_prefetch=1,
            grid=(ny,),
            in_specs=[x_spec, x_spec, y_spec, y_spec, ANY, ANY] + [ANY] * n_after,
            out_specs=[spec, spec],
            scratch_shapes=[pltpu.VMEM((n_x, half), F32)],
        ),
        out_shape=[jax.ShapeDtypeStruct(keep.shape, BF)] * 2,
        input_output_aliases={5: 0, 6: 1},
        compiler_params=pltpu.CompilerParams(vmem_limit_bytes=LIMIT),
        cost_estimate=BACKWARD,
    )(where, *xs, *ys, keep, send, *after)


class Term:
    def __init__(self, plan, keep, send, order):
        self.plan, self.keep, self.order = plan, keep, list(order)
        self.got = plan.flip(send, self.order.pop(0))

    def step(self, after):
        axis = self.order.pop(0)
        self.keep, send = combine(self.keep, self.got, axis, after)
        self.got = self.plan.flip(send, axis)
        return send


def combine(keep, got, axis, after):
    shape = keep.shape
    rows, cols = shape[-2:]
    cuts = 2
    block = shape[:-2] + (rows // cuts, cols)
    out = shape[:axis] + (1,) + shape[axis + 1 :]
    out_block = out[:-2] + (rows // cuts, cols)
    lead = len(shape) - 2

    def kernel(k, g, *rest):
        stay, go = rest[-2:]
        for side, ref in ((0, stay), (1, go)):
            at = tuple(pl.ds(side, 1) if d == axis else slice(None) for d in range(lead))
            ref[...] = (k[at].astype(F32) + g[at].astype(F32)).astype(BF)

    index = lambda i: (0,) * lead + (i, 0)
    return pl.pallas_call(
        kernel,
        grid=(cuts,),
        in_specs=[pl.BlockSpec(block, index)] * 2 + [ANY] * len(after),
        out_specs=[pl.BlockSpec(out_block, index)] * 2,
        out_shape=[jax.ShapeDtypeStruct(out, BF)] * 2,
        compiler_params=pltpu.CompilerParams(vmem_limit_bytes=SMALL_LIMIT),
        cost_estimate=BACKWARD,
    )(keep, got, *after)


def last_combine(terms, axis, rows, after):
    ins, specs, widths = [], [], []
    for t in terms:
        ins += [t.keep, t.got]
        widths.append(t.keep.shape[-1] * (t.keep.shape[-2] // rows))
    total = sum(widths)
    n_in = len(ins)

    def kernel(*refs):
        stay, go = refs[-2:]
        at = 0
        for j, t in enumerate(terms):
            k, g = refs[2 * j], refs[2 * j + 1]
            lead = k.ndim - 2
            cols = k.shape[-1]
            for block in range(k.shape[-2] // rows):
                for side, ref in ((0, stay), (1, go)):
                    idx = tuple(side if d == axis else 0 for d in range(lead)) + (pl.ds(block * rows, rows),)
                    ref[:, at : at + cols] = (k[idx].astype(F32) + g[idx].astype(F32)).astype(BF)
                at += cols

    whole = [pl.BlockSpec(v.shape, lambda n=v.ndim: (0,) * n) for v in ins]
    return pl.pallas_call(
        kernel,
        in_specs=whole + [ANY] * len(after),
        out_specs=[pl.BlockSpec((rows, total), lambda: (0, 0))] * 2,
        out_shape=[jax.ShapeDtypeStruct((rows, total), BF)] * 2,
        compiler_params=pltpu.CompilerParams(vmem_limit_bytes=SMALL_LIMIT),
        cost_estimate=BACKWARD,
    )(*ins, *after)


def pick(flag, a, b):
    return jnp.where(flag == 0, a, b)


def small_call(kernel, where, ins, shapes, after, grid=None):
    n = len(ins)

    def body(where_ref, *refs):
        kernel(where_ref, refs[:n], refs[n + len(after) :])

    return pl.pallas_call(
        body,
        grid_spec=pltpu.PrefetchScalarGridSpec(
            num_scalar_prefetch=1,
            grid=(1,),
            in_specs=[pl.BlockSpec(v.shape, lambda i, w, n=v.ndim: (0,) * n) for v in ins] + [ANY] * len(after),
            out_specs=[pl.BlockSpec(s, lambda i, w, n=len(s): (0,) * n) for s, _ in shapes],
        ),
        out_shape=[jax.ShapeDtypeStruct(s, t) for s, t in shapes],
        compiler_params=pltpu.CompilerParams(vmem_limit_bytes=SMALL_LIMIT),
        cost_estimate=BACKWARD,
    )(where, *ins, *after)


class Ending:
    def __init__(self, plan, where, terms, axis, rows, tail, after):
        self.plan, self.where, self.rows, self.tail = plan, where, rows, tail
        self.keep, self.sent = last_combine(terms, axis, rows, after)
        self.got = plan.flip(self.sent, axis)

    def core(self, after):
        rows, tail = self.rows // 2, self.tail
        cols = self.cols = self.keep.shape[1] - tail

        def kernel(where, ins, outs):
            c = where[0]
            for ref, row in ((outs[0], c), (outs[1], 1 - c)):
                at = pl.ds(pl.multiple_of(row * rows, 16), rows)
                ref[:, :cols] = (ins[0][at, :cols].astype(F32) + ins[1][at, :cols].astype(F32)).astype(BF)
            if tail:
                for g in range(2):
                    at = pl.ds(g * rows, rows)
                    piece = ins[0][at, cols:].astype(F32) + ins[1][at, cols:].astype(F32)
                    outs[0][:, cols + g * tail : cols + (g + 1) * tail] = piece.astype(BF)

        shapes = [((rows, cols + 2 * tail), BF), ((rows, cols), BF)]
        self.mine, sent = small_call(kernel, self.where, [self.keep, self.got], shapes, after)
        self.came = self.plan.core(sent)
        return sent

    def rep(self, after):
        rows, cols, tail = self.rows // 2, self.cols, self.tail

        def kernel(where, ins, outs):
            outs[0][:, :cols] = ins[0][:, :cols]
            outs[0][:, cols : 2 * cols] = ins[1][...]
            if tail:
                outs[0][:, 2 * cols :] = ins[0][:, cols:]

        shapes = [((rows, 2 * cols + 2 * tail), BF)]
        v = small_call(kernel, self.where, [self.mine, self.came], shapes, after)[0]
        self.pair = [v, self.plan.flip(v, 0)] if self.plan.ny == 2 else [lax.psum(v, "rep")]
        return v


class ChipEnding:
    def __init__(self, plan, where, term):
        self.plan, self.where = plan, where
        groups = [[2 * chip + c for chip in range(plan.chips)] for c in range(2)]
        self.term = lax.psum_scatter(term, "shard", scatter_dimension=0, axis_index_groups=groups, tiled=True)

    def core(self, after):
        rows, cols = self.term.shape
        part = rows // 4

        def kernel(where, ins, outs):
            c = where[0]
            for ref, row in ((outs[0], c), (outs[1], 1 - c)):
                for k in range(2):
                    at = pl.ds(pl.multiple_of((2 * k + row) * part, 16), part)
                    ref[k * part : (k + 1) * part] = ins[0][at]

        shapes = [((rows // 2, cols), BF)] * 2
        self.mine, sent = small_call(kernel, self.where, [self.term], shapes, after)
        self.came = self.plan.core(sent)
        return sent

    def rep(self, after):
        rows, cols = self.mine.shape

        def kernel(where, ins, outs):
            outs[0][:rows] = ins[0][...]
            outs[0][rows:] = ins[1][...]

        v = small_call(kernel, self.where, [self.mine, self.came], [((2 * rows, cols), BF)], after)[0]
        self.pair = [v, self.plan.flip(v, 0)] if self.plan.ny == 2 else [lax.psum(v, "rep")]
        return v


def place_grads(plan, where, layer, layers, end2, rest, sizes, before, after):
    deep, width, ff, quarters = sizes
    n, ny, halves = plan.shards, plan.ny, quarters // 2
    wide, half_ff = 3 * width // 2, ff // 2
    cols = rest.cols
    fused = bool(rest.tail)
    ins = end2.pair + rest.pair

    def kernel(where_ref, *refs):
        refs_in = refs[: 2 * ny]
        outs = refs[-(4 if fused else 3) :]
        c, y = where_ref[0], where_ref[2]

        def source(p, q, at, size):
            step = (at // 128) * 128
            span = (at + size - step + 127) // 128 * 128
            first = pl.multiple_of(jnp.where(p == c, 0, cols) + step, 128)
            v = refs_in[ny][:, pl.ds(first, span)]
            if ny == 2:
                v = jnp.where(y == q, v, refs_in[ny + 1][:, pl.ds(first, span)])
            return v[:, at - step : at - step + size].astype(F32)

        def core_columns(p, at, size, total, first):
            part = total // ny
            return source(p, at // part, first + at % part, size)

        for k in range(3 * HEADS // 2):
            pieces = [core_columns(p, k * HEAD_DIM, HEAD_DIM, wide, 0) for p in range(2)]
            outs[0][0, :, k * 2 * HEAD_DIM : (k + 1) * 2 * HEAD_DIM] = jnp.concatenate(pieces, axis=1)
        for k in range(n):
            pieces = []
            for p in range(2):
                for h in range(halves):
                    pieces.append(core_columns(p, (h * n + k) * deep, deep, half_ff, wide // ny))
            outs[1][0, :, k * quarters * deep : (k + 1) * quarters * deep] = jnp.concatenate(pieces, axis=1)
        part = width // ny
        for p in range(2):
            at = pl.ds(pl.multiple_of(jnp.where(p == c, 0, halves * deep), 16), halves * deep)
            v = refs_in[0][at].astype(F32)
            if ny == 2:
                v = v + refs_in[1][at].astype(F32)
            outs[2][0, p * halves * deep : (p + 1) * halves * deep] = v
        if fused:
            for q in range(ny):
                v = refs_in[ny][:, 2 * cols :]
                if ny == 2:
                    v = jnp.where(y == q, v, refs_in[ny + 1][:, 2 * cols :])
                outs[3][0, :, q * part : (q + 1) * part] = v.astype(F32)

    shapes = [(deep, 3 * width), (deep, ff), (quarters * deep, width)] + ([(deep, width)] if fused else [])
    in_specs = [pl.BlockSpec(v.shape, lambda i, w: (0, 0)) for v in ins]
    args = list(ins) + list(before or []) + list(after)
    n_before = len(before or [])
    return pl.pallas_call(
        kernel,
        grid_spec=pltpu.PrefetchScalarGridSpec(
            num_scalar_prefetch=1,
            grid=(1,),
            in_specs=in_specs + [ANY] * (n_before + len(after)),
            out_specs=[pl.BlockSpec((1,) + s, lambda i, w: (layer, 0, 0)) for s in shapes],
        ),
        out_shape=[jax.ShapeDtypeStruct((layers,) + s, F32) for s in shapes],
        input_output_aliases={1 + len(ins) + k: k for k in range(n_before)},
        compiler_params=pltpu.CompilerParams(vmem_limit_bytes=LIMIT),
        cost_estimate=BACKWARD,
    )(where, *args)


def per_device(
    plan,
    tokens,
    kept,
    attn_gain,
    attn_shift,
    qkv_weight,
    qv_bias,
    proj_weight,
    proj_bias,
    mlp_gain,
    mlp_shift,
    fc1_weight,
    fc1_bias,
    fc2_weight,
    fc2_bias,
    cotangent,
):
    images, slots, width = tokens.shape
    layers = attn_gain.shape[0]
    rows = images * slots
    n = plan.shards
    deep = qkv_weight.shape[1]
    shard = lax.axis_index("shard")
    c, chip, y = lax.rem(shard, 2), shard // 2, lax.axis_index("rep")
    where = jnp.stack([c, chip, y, y if plan.ny == 2 else 0 * y]).astype(jnp.int32)
    ff = fc2_weight.shape[1] * n
    quarters = fc2_weight.shape[1] // deep
    wide, half_width, half_ff = 3 * width // 2, width // 2, ff // 2
    half_heads = HEADS // 2

    small = jnp.concatenate(
        [attn_gain, attn_shift, qv_bias, proj_bias, mlp_gain, mlp_shift, fc1_bias, fc2_bias], axis=1
    )
    sizes = [v.shape[1] for v in (attn_gain, attn_shift, qv_bias, proj_bias, mlp_gain, mlp_shift, fc1_bias, fc2_bias)]
    lines = small.size // 128
    extra = jnp.pad(small.reshape(lines, 128), ((0, deep - lines), (0, 0)))

    halves = quarters // 2
    lead = 4 * width
    block = n * deep
    each = halves // plan.ny

    def merged(layer):
        qkv = qkv_weight[layer].reshape(deep, 3 * half_heads, 2, HEAD_DIM).swapaxes(1, 2).reshape(deep, 3 * width)
        fc1 = fc1_weight[layer].reshape(deep, n, quarters, deep).swapaxes(1, 2).reshape(deep, ff)
        fc2 = fc2_weight[layer].reshape(2, halves, deep, width)
        if plan.ny == 2:
            fc2 = pick(y, fc2[:, :1], fc2[:, 1:])
        fc2 = [fc2[p, k] for p in range(2) for k in range(each)]
        return [qkv, proj_weight[layer], fc1] + fc2 + ([] if layer else [extra])

    operands = [jnp.concatenate(merged(layer), axis=1) for layer in range(layers)]
    gathered = [lax.all_gather(v, "shard", axis=0, tiled=True) for v in operands]
    at_fc1, at_fc2 = lead // block, (lead + ff) // block
    mlp_parts = []
    for layer in range(layers):
        found = {"fc1": [(gathered[layer], ("quarter", block, (at_fc1, halves, k))) for k in range(halves)]}
        found["fc2"] = [(gathered[layer], columns(block, at_fc2 + k, each)) for k in range(each)]
        if plan.ny == 2:
            found["sent"], found["came"] = (), ()
            for k in range(1):
                mine = lax.dynamic_slice(
                    gathered[layer], (0, (at_fc2 + c) * block), (block, block)
                )
                found["sent"] += (mine,)
                found["came"] += (plan.flip(mine, 0),)
                found["fc2"].append((found["came"][k], None))
        mlp_parts.append(found)

    def weight_of(layer, name):
        if name == "qkv":
            return [(gathered[layer], columns(wide, 0, 1))]
        if name == "proj":
            return [(gathered[layer], ("heads", width, 3))]
        return mlp_parts[layer][name]

    every = gathered[0].reshape(n, deep, -1)[:, :lines, lead + ff + 2 * each * block :]
    every = every.reshape(n, layers, small.shape[1]).astype(F32)
    vecs = []
    for layer in range(layers):
        at, d = 0, {}
        for name, size in zip(SMALL, sizes):
            d[name] = every[:, layer, at : at + size].reshape(1, n * size)
            at += size
        q = d["qvb"].reshape(2 * half_heads, 2, HEAD_DIM)
        q = pick(c, q[:, 0], q[:, 1]).reshape(2, half_width)
        d["qvb_c"] = jnp.stack([q[0], jnp.zeros_like(q[0]), q[1]]).reshape(1, wide)
        f = d["f1b"].reshape(n, 2, halves, deep).transpose(1, 2, 0, 3).reshape(2, halves, block)
        f = pick(c, f[0], f[1])
        if plan.ny == 2:
            f = pick(y, f, f[::-1])
        d["f1b_c"] = f.reshape(1, half_ff)
        vecs.append(d)

    kept_oth = plan.core(kept)
    state = tokens.astype(F32).reshape(rows, width)
    live = lax.broadcasted_iota(jnp.int32, (images, slots), 1) < BUFFER + kept[:, None]
    grad = jnp.where(live[:, :, None], cotangent.astype(F32), 0.0).reshape(rows, width)
    low_own = grad.astype(BF)
    low_oth = plan.core(low_own)
    first_own = norm_rows(state, vecs[0]["ag"], vecs[0]["as"]).astype(BF)

    f32_rows, low_rows = ("rows", (rows, width), F32), ("rows", (rows, width), BF)
    wide_rows, ff_rows = ("rows", (rows, wide), BF), ("rows", (rows, half_ff), BF)
    att_outs = [("image", (images, half_heads, slots, slots), BF), ("rows", (rows, half_width), BF)]
    full_sums = ("full", (8, width), F32)

    def call(body, layer, own, names, blocked, whole, outs, after=(), cost=None):
        chosen = [weight_of(layer, name) for name in names]
        k = kept if own else kept_oth
        return row_call(body, where, k, chosen, blocked, whole, outs, images, slots, after, cost or (BACKWARD if after else FORWARD))

    saved = []
    for layer in range(layers):
        v = vecs[layer]
        first_oth = plan.core(first_own)
        sent, came = mlp_parts[layer].get("sent", ()), mlp_parts[layer].get("came", ())
        proj_oth = call(qkv_body, layer, 0, ["qkv"], [first_oth], [v["qvb_c"]], [wide_rows], sent, FORWARD)[0]
        probs_oth, att_oth, part = call(attend_other, layer, 0, ["proj"], [proj_oth], [], att_outs + [f32_rows])
        part = plan.core(part)
        proj_own = call(qkv_body, layer, 1, ["qkv"], [first_own], [v["qvb_c"]], [wide_rows])[0]
        probs_own, att_own, middle, second_own = call(
            attend_own, layer, 1, ["proj"], [proj_own, part, state], [v["pb"], v["mg"], v["ms"]], att_outs + [f32_rows, low_rows])
        second_oth = plan.core(second_own)
        hid_oth, slope_oth = call(up_body, layer, 0, ["fc1"], [second_oth], [v["f1b_c"]], [ff_rows] * 2)
        if layer + 1 < layers:
            part = call(down_other, layer, 0, ["fc2"], [hid_oth], [], [f32_rows])[0]
            part = plan.core(part)
        hid_own, slope_own = call(up_body, layer, 1, ["fc1"], [second_own], [v["f1b_c"]], [ff_rows] * 2)
        saved.append(
            dict(
                state=state,
                first=(first_own, first_oth),
                proj=(proj_own, proj_oth),
                probs=(probs_own, probs_oth),
                att=(att_own, att_oth),
                middle=middle,
                second=(second_own, second_oth),
                hid=(hid_own, hid_oth),
                slope=(slope_own, slope_oth),
            )
        )
        if layer + 1 < layers:
            w = vecs[layer + 1]
            state, first_own = call(
                down_own, layer, 1, ["fc2"], [hid_own, part, middle], [v["f2b"], w["ag"], w["as"]], [f32_rows, low_rows])

    axes = list(range(1 if plan.ny == 1 else 0, plan.bits + 1))
    last_axis, z_axis, x_axis = 1, plan.bits - 1, plan.bits
    y_axis = 0 if plan.ny == 2 else 2
    orders_f1 = [[y_axis, x_axis, z_axis]] * layers
    orders_q = [[[z_axis, y_axis, x_axis], [y_axis, z_axis, x_axis]]] + [[[x_axis, z_axis, y_axis]]] * (layers - 1)
    own_rows = 2 * deep
    tail = width // plan.ny * HEAD_DIM // own_rows
    fused = n == HEADS
    tail = tail if fused else 0
    big = [[None] * 4 for _ in range(layers)]
    sums = [None] * layers
    f2b_sum = jnp.sum(low_own.astype(F32), axis=0, keepdims=True)

    def end_rest(layer, prev):
        group = terms["q", layer] + [terms["f1", layer]]
        ends["rest", layer] = Ending(plan, where, group, last_axis, own_rows, tail, prev)
        return (ends["rest", layer].sent,)

    def place(layer, before, prev):
        return place_grads(
            plan, where, layer, layers, ends["f2", layer], ends["rest", layer], (deep, width, ff, quarters), before, prev
        )

    ends = {}
    prev = (hid_own,) + mlp_parts[layers - 1].get("came", ())
    terms = {}
    for layer in reversed(range(layers)):
        v, s = vecs[layer], saved[layer]
        top = layer == layers - 1

        def grad_fc2(prev):
            term = chip_grad(plan, where, s["hid"], (low_own, low_oth), 2, prev)
            ends["f2", layer] = ChipEnding(plan, where, term)
            return (term,)

        if top:
            prev = grad_fc2(prev)
        pre_oth, part = call(
            mlp_back_other, layer, 0, ["fc2", "fc1"], [low_oth, s["slope"][1]], [], [ff_rows, f32_rows], prev
        )
        part = plan.core(part)
        prev = (pre_oth,)
        if top:
            last_part = call(down_other, layer, 0, ["fc2"], [s["hid"][1]], [], [f32_rows], prev)[0]
            prev = (last_part,)
            last_part = plan.core(last_part)
        else:
            prev = grad_fc2(prev)
            prev += (terms["f1", layer + 1].step(prev[:1]),)
        pre_own, mid_grad, branch_own, sum1 = call(
            mlp_back_own,
            layer,
            1,
            ["fc2", "fc1"],
            [low_own, s["slope"][0], part, s["middle"], grad],
            [v["mg"]],
            [ff_rows, f32_rows, low_rows, full_sums],
            prev,
        )
        branch_oth = plan.core(branch_own)
        prev = (branch_own,)
        if not top:
            prev += (terms["q", layer + 1][0].step(prev),)
        res1 = weight_grad(
            plan, where, s["second"], (pre_own, pre_oth), 1, orders_f1[layer][0], sums=True, extra=tail, relative=True, after=prev
        )
        prev = tuple(res1[:1])
        if not top:
            prev += (terms["q", layer + 1][0].step(prev[:1]),)
            prev += (terms["f1", layer + 1].step(prev[:1]),)
            prev += (ends["f2", layer + 1].core(prev[:1]),)
        dproj_oth, part = call(
            attend_back_other,
            layer,
            0,
            ["proj", "qkv"],
            [branch_oth, s["proj"][1], s["probs"][1]],
            [],
            [wide_rows, f32_rows],
            prev,
        )
        part = plan.core(part)
        prev = (dproj_oth,)
        keep, send = res1[:2]
        if fused:
            keep, send = proj_grad_into(
                plan, where, s["att"], (branch_own, branch_oth), orders_f1[layer][0], keep, send, prev
            )
        else:
            term = t_dot(s["att"][0], branch_own) + t_dot(s["att"][1], branch_oth)
            term = term.astype(BF).reshape(half_heads, HEAD_DIM, width)
            none = jnp.zeros_like(term)
            term = jnp.stack([pick(c, term, none), pick(c, none, term)], axis=1).reshape(width, width)
            term = lax.psum_scatter(term, "shard", scatter_dimension=0, tiled=True)
            big[layer][1] = lax.psum(term, "rep").astype(F32)
        terms["f1", layer] = Term(plan, keep, send, orders_f1[layer])
        prev = (send,)
        if not top:
            prev += (ends["f2", layer + 1].rep(prev[:1]),)
        dproj_own, grad, low_own, sum2 = call(
            attend_back_own,
            layer,
            1,
            ["proj", "qkv"],
            [branch_own, s["proj"][0], s["probs"][0], part, s["state"], mid_grad],
            [v["ag"]],
            [wide_rows, f32_rows, low_rows, full_sums],
            prev,
        )
        prev = (dproj_own,)
        if layer:
            low_oth = plan.core(low_own)
        if not top:
            prev += end_rest(layer + 1, prev[:1])
            prev += (ends["f2", layer].core(prev[:1]),)
        terms["q", layer], q_sums = [], []
        of = len(orders_q[layer])
        for k, order in enumerate(orders_q[layer]):
            resq = weight_grad(
                plan, where, s["first"], (dproj_own, dproj_oth), 1, order[0], sums=True, window=(k, of), after=prev
            )
            terms["q", layer].append(Term(plan, *resq[:2], order))
            q_sums.append(resq[2].reshape(plan.ny, -1))
            prev = (resq[1],)
        q = jnp.concatenate(q_sums, axis=1).reshape(3, half_heads, 1, HEAD_DIM)
        q = jnp.concatenate([q[:1], q[2:]])
        none = jnp.zeros_like(q)
        q = jnp.concatenate([pick(c, q, none), pick(c, none, q)], axis=2)
        f = res1[2].reshape(halves, block)
        if plan.ny == 2:
            f = pick(y, f, f[::-1])
        none = jnp.zeros_like(f)
        f = jnp.concatenate([pick(c, f, none), pick(c, none, f)], axis=0)
        f = f.reshape(quarters, n, deep).swapaxes(0, 1)
        full = {"ag": sum2[0], "as": sum2[1], "qvb": q, "pb": sum1[2], "mg": sum1[0], "ms": sum1[1], "f1b": f, "f2b": f2b_sum}
        f2b_sum = sum2[2]
        vec = jnp.concatenate([full[name].reshape(n, -1) for name in SMALL], axis=1)
        sums[layer] = vec

    vec = jnp.concatenate(sums, axis=0).reshape(layers, n, -1)
    got_vec = plan.core(vec)
    vec_axes = list(axes)

    def step_vec():
        nonlocal vec, got_vec
        vec = vec + got_vec
        sent = vec
        got_vec = plan.flip(vec, vec_axes.pop(0)) if vec_axes else None
        return (sent,)

    prev += (terms["f1", 0].step(prev[:1]),)
    prev += (ends["rest", 1].core(prev[:1]),)
    w = layers - 1
    mixed = call(
        down_last, w, 1, ["fc2"], [saved[w]["hid"][0], last_part, saved[w]["middle"]], [vecs[w]["f2b"]], [low_rows], prev
    )[0]
    qa, qb = terms["q", 0]
    prev = (qa.step((mixed,)),) + step_vec()
    prev = (qb.step(prev),)
    prev = (ends["rest", 1].rep(prev),) + step_vec()
    prev = (qa.step(prev),)
    prev = (terms["f1", 0].step(prev),)
    prev = (qb.step(prev),) + step_vec()
    prev = end_rest(0, prev) + step_vec()
    prev = (ends["f2", 0].rep(prev),)
    placed = place(1, None, prev)
    prev = (placed[0],)
    while got_vec is not None:
        prev += step_vec()
    prev = (ends["rest", 0].core(prev),)
    prev = (ends["rest", 0].rep(prev),)
    placed = place(0, placed, prev)
    if plan.ny == 1:
        vec = lax.psum(vec, "rep")
    vec = lax.dynamic_slice_in_dim(vec, shard, 1, axis=1)[:, 0]
    out, at = {}, 0
    for name, size in zip(SMALL, sizes):
        out[name] = vec[:, at : at + size]
        at += size
    qkv_g, fc1_g, fc2_g = placed[:3]
    proj_g = placed[3] if fused else jnp.stack([big[layer][1] for layer in range(layers)])
    return (
        mixed.reshape(images, slots, width),
        grad.reshape(images, slots, width),
        out["ag"],
        out["as"],
        qkv_g,
        out["qvb"],
        proj_g,
        out["pb"],
        out["mg"],
        out["ms"],
        fc1_g,
        out["f1b"],
        fc2_g,
        out["f2b"],
    )


def solution(mesh):
    rows = P(("shard", "rep"), None, None)
    vec = P(None, "shard")
    mat = P(None, "shard", None)
    return jax.shard_map(
        partial(per_device, Plan(mesh)),
        mesh=mesh,
        in_specs=(rows, P(("shard", "rep")), vec, vec, mat, vec, mat, vec, vec, vec, mat, vec, mat, vec, rows),
        out_specs=(rows, rows, vec, vec, mat, vec, mat, vec, vec, vec, mat, vec, mat, vec),
        check_vma=False,
    )
```

```python
from functools import partial

import jax
import jax.numpy as jnp
from jax import lax
from jax.experimental import pallas as pl
from jax.experimental.pallas import tpu as pltpu
from jax.sharding import PartitionSpec as P

HEADS = 16
HEAD_DIM = 64
BUFFER = 64
EPS = 1e-06
SCALE = HEAD_DIM ** (-0.5)
AX = ("shard", "rep")
BF = jnp.bfloat16
F32 = jnp.float32
LIMIT = 60 * 2**20
SMALL_LIMIT = 16 * 2**20
ONCE = pl.Buffered(1)
ANY = pl.BlockSpec(memory_space=pl.ANY)
FORWARD = pl.CostEstimate(flops=10**7, bytes_accessed=0, transcendentals=0)
BACKWARD = pl.CostEstimate(flops=10**9 * 30, bytes_accessed=0, transcendentals=0)
SMALL = ("ag", "as", "qvb", "pb", "mg", "ms", "f1b", "f2b")


class Plan:
    def __init__(self, mesh):
        self.shards = mesh.shape["shard"]
        self.rep = mesh.shape["rep"]
        self.chips = self.shards // 2
        self.ny = 2 if self.rep == 2 else 1
        self.bits = self.chips.bit_length() - 1

    def swap(self, v, flip_shard, flip_rep=0):
        pairs = []
        for s in range(self.shards):
            for y in range(self.rep):
                pairs.append((s * self.rep + y, (s ^ flip_shard) * self.rep + (y ^ flip_rep)))
        return lax.ppermute(v, AX, pairs)

    def core(self, v):
        return self.swap(v, 1)

    def flip(self, v, axis):
        if axis == 0:
            return self.swap(v, 0, 1)
        return self.swap(v, 2 << (self.bits - axis))


def dot(x, w):
    return lax.dot_general(x, w, (((1,), (0,)), ((), ())), preferred_element_type=F32)


def dot_t(x, w):
    return lax.dot_general(x, w, (((1,), (1,)), ((), ())), preferred_element_type=F32)


def t_dot(x, w):
    return lax.dot_general(x, w, (((0,), (0,)), ((), ())), preferred_element_type=F32)


def columns(width, first, stride):
    return ("columns", width, (first, stride))


def row_call(body, where, kept, weights, blocked, whole, outs, images, slots, after=(), cost=FORWARD):
    in_specs, args = [], []
    for v, pick_of in (part for w in weights for part in w):
        if pick_of is None:
            in_specs.append(pl.BlockSpec(v.shape, lambda i, w, k: (0, 0), pipeline_mode=ONCE))
            args.append(v)
            continue
        kind, width, first = pick_of
        if kind == "columns":
            spec = pl.BlockSpec((v.shape[0], width), lambda i, w, k, f=first: (0, f[0] + f[1] * w[0]), pipeline_mode=ONCE)
            in_specs.append(spec)
            args.append(v)
        elif kind == "quarter":
            at, stride, part = first
            spec = pl.BlockSpec(
                (v.shape[0], width),
                lambda i, w, k, f=(at, stride, part): (0, f[0] + f[1] * w[0] + jnp.bitwise_xor(f[2], w[3])),
                pipeline_mode=ONCE,
            )
            in_specs.append(spec)
            args.append(v)
        else:
            view = v.reshape(HEADS // 2, 2, HEAD_DIM, v.shape[1])
            spec = pl.BlockSpec((HEADS // 2, None, HEAD_DIM, width), lambda i, w, k, f=first: (0, w[0], 0, f), pipeline_mode=ONCE)
            in_specs.append(spec)
            args.append(view)
    for v in blocked:
        if v.ndim == 2:
            in_specs.append(pl.BlockSpec((slots, v.shape[1]), lambda i, *_: (i, 0)))
        else:
            in_specs.append(pl.BlockSpec((1,) + v.shape[1:], lambda i, *_, n=v.ndim: (i,) + (0,) * (n - 1)))
        args.append(v)
    for v in whole:
        in_specs.append(pl.BlockSpec(v.shape, lambda i, *_, n=v.ndim: (0,) * n))
        args.append(v)
    out_specs, out_shape = [], []
    for kind, shape, dtype in outs:
        out_shape.append(jax.ShapeDtypeStruct(shape, dtype))
        if kind == "rows":
            out_specs.append(pl.BlockSpec((slots, shape[1]), lambda i, *_: (i, 0)))
        elif kind == "image":
            out_specs.append(pl.BlockSpec((1,) + shape[1:], lambda i, *_, n=len(shape): (i,) + (0,) * (n - 1)))
        else:
            out_specs.append(pl.BlockSpec(shape, lambda i, *_, n=len(shape): (0,) * n))
    n_p, n_b, n_in = sum(len(w) for w in weights), len(blocked), len(args)
    in_specs += [ANY] * len(after)
    args += list(after)

    def kernel(where_ref, kept_ref, *refs):
        ins, res = refs[:n_in], refs[n_in + len(after) :]
        held, at = [], 0
        for w in weights:
            held.append(ins[at : at + len(w)])
            at += len(w)
        body(kept_ref, held, ins[n_p : n_p + n_b], ins[n_p + n_b : n_in], res)

    return pl.pallas_call(
        kernel,
        grid_spec=pltpu.PrefetchScalarGridSpec(
            num_scalar_prefetch=2, grid=(images,), in_specs=in_specs, out_specs=out_specs
        ),
        out_shape=out_shape,
        compiler_params=pltpu.CompilerParams(vmem_limit_bytes=LIMIT),
        cost_estimate=cost,
    )(where, kept, *args)


def normed_of(rows):
    width = rows.shape[-1]
    mean = jnp.sum(rows, axis=-1, keepdims=True) * (1.0 / width)
    centered = rows - mean
    spread = jnp.sum(centered * centered, axis=-1, keepdims=True) * (1.0 / width)
    factor = lax.rsqrt(spread + EPS)
    return centered * factor, factor


def norm_rows(rows, gain, shift):
    return normed_of(rows)[0] * gain + shift


def norm_back(dz, rows, gain):
    normed, factor = normed_of(rows)
    width = rows.shape[-1]
    prod = dz * normed
    dn = dz * gain
    m1 = jnp.sum(dn, axis=-1, keepdims=True) * (1.0 / width)
    m2 = jnp.sum(dn * normed, axis=-1, keepdims=True) * (1.0 / width)
    back = factor * (dn - m1 - normed * m2)
    return back, jnp.sum(prod, axis=0, keepdims=True), jnp.sum(dz, axis=0, keepdims=True)


def chunks(total, size):
    size = min(size, total)
    return [(k, size) for k in range(0, total, size)]


def qkv_body(kept, w, blocked, whole, outs):
    x = blocked[0][...]
    for k, n in chunks(outs[0].shape[1], 512):
        cols = pl.ds(k, n)
        outs[0][:, cols] = (dot(x, w[0][0][:, cols]) + whole[0][:, cols]).astype(BF)


def heads_of(ref):
    return ref[...].reshape(-1, ref.shape[-1])


def pairs_dot(x_ref, parts):
    total, at = None, 0
    for w_ref in parts:
        term = dot(x_ref[:, at : at + w_ref.shape[0]], w_ref[...])
        total = term if total is None else total + term
        at += w_ref.shape[0]
    return total


def attend(kept, proj_ref, probs_ref, att_ref):
    slots, third = proj_ref.shape[0], proj_ref.shape[1] // 3
    bound = BUFFER + kept[pl.program_id(0)]
    alive = lax.broadcasted_iota(jnp.int32, (slots, slots), 1) < bound
    outs = []
    for h in range(third // HEAD_DIM):
        lo = h * HEAD_DIM
        q = proj_ref[:, lo : lo + HEAD_DIM]
        k = proj_ref[:, third + lo : third + lo + HEAD_DIM]
        v = proj_ref[:, 2 * third + lo : 2 * third + lo + HEAD_DIM]
        s = jnp.where(alive, dot_t(q, k) * SCALE, -1e30)
        e = jnp.exp(s - jnp.max(s, axis=-1, keepdims=True))
        p = (e * (1.0 / jnp.sum(e, axis=-1, keepdims=True))).astype(BF)
        probs_ref[0, h] = p
        outs.append(dot(p, v).astype(BF))
        if h % 2:
            att_ref[:, lo - HEAD_DIM : lo + HEAD_DIM] = jnp.concatenate(outs, axis=1)
            outs = []


def attend_other(kept, w, blocked, whole, outs):
    attend(kept, blocked[0], outs[0], outs[1])
    outs[2][...] = dot(outs[1][...], heads_of(w[0][0]))


def attend_own(kept, w, blocked, whole, outs):
    attend(kept, blocked[0], outs[0], outs[1])
    middle = blocked[2][...] + (dot(outs[1][...], heads_of(w[0][0])) + blocked[1][...]) + whole[0][...]
    outs[2][...] = middle
    outs[3][...] = norm_rows(middle, whole[1][...], whole[2][...]).astype(BF)


def up_body(kept, w, blocked, whole, outs):
    x = blocked[0][...]
    for k, n in chunks(outs[0].shape[1], 256):
        cols = pl.ds(k, n)
        held = w[0][k // w[0][0].shape[1]]
        pre = dot(x, held[:, pl.ds(k % held.shape[1], n)]) + whole[0][:, cols]
        phi = 0.5 + 0.5 * lax.erf(pre * (2.0**-0.5))
        dens = jnp.exp(-0.5 * (pre * pre)) * 0.3989422804014327
        outs[0][:, cols] = (pre * phi).astype(BF)
        outs[1][:, cols] = (phi + pre * dens).astype(BF)


def down_other(kept, w, blocked, whole, outs):
    outs[0][...] = pairs_dot(blocked[0], w[0])


def down_own(kept, w, blocked, whole, outs):
    state = blocked[2][...] + (pairs_dot(blocked[0], w[0]) + blocked[1][...]) + whole[0][...]
    outs[0][...] = state
    outs[1][...] = norm_rows(state, whole[1][...], whole[2][...]).astype(BF)


def down_last(kept, w, blocked, whole, outs):
    state = blocked[2][...] + (pairs_dot(blocked[0], w[0]) + blocked[1][...]) + whole[0][...]
    alive = lax.broadcasted_iota(jnp.int32, state.shape, 0) < BUFFER + kept[pl.program_id(0)]
    outs[0][...] = jnp.where(alive, state, 0.0).astype(BF)


def mlp_back(w, blocked, outs):
    low = blocked[0][...]
    for k, n in chunks(outs[0].shape[1], 512):
        cols = pl.ds(k, n)
        held, first = w[0][0], 0
        for part in w[0][1:]:
            if k >= first + held.shape[0]:
                first += held.shape[0]
                held = part
        t = dot_t(low, held[pl.ds(k - first, n), :])
        outs[0][:, cols] = (t * blocked[1][:, cols].astype(F32)).astype(BF)
    total, at = None, 0
    for held in w[1]:
        term = dot_t(outs[0][:, at : at + held.shape[1]], held[...])
        total = term if total is None else total + term
        at += held.shape[1]
    return total


def mlp_back_other(kept, w, blocked, whole, outs):
    outs[1][...] = mlp_back(w, blocked, outs)


def add_sums(ref, rows):
    sums = jnp.concatenate(rows + [jnp.zeros((8 - len(rows), rows[0].shape[1]), F32)], axis=0)

    @pl.when(pl.program_id(0) == 0)
    def _():
        ref[...] = sums

    @pl.when(pl.program_id(0) != 0)
    def _():
        ref[...] += sums


def mlp_back_own(kept, w, blocked, whole, outs):
    dz = mlp_back(w, blocked, outs) + blocked[2][...]
    back, gain, shift = norm_back(dz, blocked[3][...], whole[0][...])
    grad = blocked[4][...] + back
    low = grad.astype(BF)
    outs[1][...] = grad
    outs[2][...] = low
    add_sums(outs[3], [gain, shift, jnp.sum(low.astype(F32), axis=0, keepdims=True)])


def attend_back(w, blocked, outs):
    branch, proj_ref, probs_ref = blocked[0], blocked[1], blocked[2]
    third = proj_ref.shape[1] // 3
    datt = dot_t(branch[...], heads_of(w[0][0])).astype(BF)
    pairs = [[], [], []]
    for h in range(third // HEAD_DIM):
        lo = h * HEAD_DIM
        q = proj_ref[:, lo : lo + HEAD_DIM]
        k = proj_ref[:, third + lo : third + lo + HEAD_DIM]
        v = proj_ref[:, 2 * third + lo : 2 * third + lo + HEAD_DIM]
        da = datt[:, lo : lo + HEAD_DIM]
        p = probs_ref[0, h]
        dp = dot_t(da, v)
        pf = p.astype(F32)
        ds = (pf * (dp - jnp.sum(pf * dp, axis=-1, keepdims=True))).astype(BF)
        pairs[0].append((dot(ds, k) * SCALE).astype(BF))
        pairs[1].append((t_dot(ds, q) * SCALE).astype(BF))
        pairs[2].append(t_dot(p, da).astype(BF))
        if h % 2:
            for j in range(3):
                at = j * third + lo - HEAD_DIM
                outs[0][:, at : at + 2 * HEAD_DIM] = jnp.concatenate(pairs[j], axis=1)
            pairs = [[], [], []]
    return dot_t(outs[0][...], w[1][0][...])


def attend_back_other(kept, w, blocked, whole, outs):
    outs[1][...] = attend_back(w, blocked, outs)


def attend_back_own(kept, w, blocked, whole, outs):
    dz = attend_back(w, blocked, outs) + blocked[3][...]
    back, gain, shift = norm_back(dz, blocked[4][...], whole[0][...])
    grad = blocked[5][...] + back
    outs[1][...] = grad
    low = grad.astype(BF)
    outs[2][...] = low
    add_sums(outs[3], [gain, shift, jnp.sum(low.astype(F32), axis=0, keepdims=True)])


def weight_grad(plan, where, xs, ys, groups, first, sums=False, extra=0, relative=False, window=(0, 1), after=()):
    depth, n_x = xs[0].shape
    cols = ys[0].shape[1]
    ny, chips, bits = plan.ny, plan.chips, plan.bits
    half = cols // ny
    size = half // window[1]
    chunk = size if size <= 768 else 512
    steps = size // chunk
    rows = n_x // chips
    part = rows // groups
    dims = [ny] + [2] * bits
    dims[first] = 1
    block = [1] + dims[1:] + [rows, chunk]
    shape = dims + [rows, size + extra]
    n_after = len(after)

    def kernel(where_ref, xo, xt, yo, yt, *rest):
        rest = rest[n_after:]
        keep, send = rest[0], rest[1]
        flip, acc = rest[-2], rest[-1]
        step = pl.program_id(0)

        @pl.when(step == 0)
        def _():
            flip[:, :depth] = xo[...].T
            flip[:, depth:] = xt[...].T

        acc[...] = dot(flip[:, :depth], yo[...]) + dot(flip[:, depth:], yt[...])
        if sums:
            rest[2][...] = jnp.sum(yo[...].astype(F32), axis=0, keepdims=True) + jnp.sum(
                yt[...].astype(F32), axis=0, keepdims=True
            )

        def put(ref, r):
            at = [0]
            for k in range(1, bits + 1):
                at.append((r >> (bits - k)) & 1 if k != first else 0)
            chip = jnp.bitwise_xor(where_ref[1], r)
            for g in range(groups):
                start = pl.multiple_of(g * part * chips + chip * part, 16)
                place = g
                if groups == 2 and ny == 2:
                    place = jnp.bitwise_xor(g, where_ref[2])
                place = pl.multiple_of(place * part, 16)
                ref[tuple(at) + (pl.ds(place, part),)] = acc[pl.ds(start, part)].astype(BF)

        if first:
            for r in range(chips):
                put(send if (r >> (bits - first)) & 1 else keep, r)
        else:

            @pl.when(step < steps)
            def _():
                for r in range(chips):
                    put(keep, r)

            @pl.when(step >= steps)
            def _():
                for r in range(chips):
                    put(send, r)

    per_rep = half // chunk

    def column(i, w):
        own = w[2] if ny == 2 and not relative else 0
        return jnp.bitwise_xor(i // steps, own) * per_rep + window[0] * steps + i % steps

    zeros = (0,) * (bits + 1)
    x_spec = pl.BlockSpec((depth, n_x), lambda i, w: (0, 0), pipeline_mode=ONCE)
    y_spec = pl.BlockSpec((depth, chunk), lambda i, w: (0, column(i, w)))
    if first:
        specs = [pl.BlockSpec(block, lambda i, w: (i // steps,) + zeros + (i % steps,))] * 2
    else:
        specs = [
            pl.BlockSpec(block, lambda i, w: (0,) + zeros + (jnp.minimum(i, steps - 1),)),
            pl.BlockSpec(block, lambda i, w: (0,) + zeros + (jnp.maximum(i - steps, 0),)),
        ]
    out_shape = [jax.ShapeDtypeStruct(shape, BF)] * 2
    if sums:
        own = (lambda w: w[2]) if ny == 2 and not relative else (lambda w: 0)
        specs = specs + [
            pl.BlockSpec((1, chunk), lambda i, w: (0, jnp.bitwise_xor(i // steps, own(w)) * steps + i % steps))
        ]
        out_shape = out_shape + [jax.ShapeDtypeStruct((1, size * ny), F32)]
    return pl.pallas_call(
        kernel,
        grid_spec=pltpu.PrefetchScalarGridSpec(
            num_scalar_prefetch=1,
            grid=(ny * steps,),
            in_specs=[x_spec, x_spec, y_spec, y_spec] + [ANY] * n_after,
            out_specs=specs,
            scratch_shapes=[pltpu.VMEM((n_x, 2 * depth), BF), pltpu.VMEM((n_x, chunk), F32)],
        ),
        out_shape=out_shape,
        compiler_params=pltpu.CompilerParams(vmem_limit_bytes=LIMIT),
        cost_estimate=BACKWARD,
    )(where, *xs, *ys, *after)


def chip_grad(plan, where, xs, ys, groups, after=()):
    depth, n_x = xs[0].shape
    cols = ys[0].shape[1]
    chips = plan.chips
    chunk = min(cols, 512)
    rows = n_x // chips
    part = rows // groups
    n_after = len(after)

    def kernel(where_ref, xo, xt, yo, yt, *rest):
        out, flip, acc = rest[n_after:]

        @pl.when(pl.program_id(0) == 0)
        def _():
            flip[:, :depth] = xo[...].T
            flip[:, depth:] = xt[...].T

        acc[...] = dot(flip[:, :depth], yo[...]) + dot(flip[:, depth:], yt[...])
        for g in range(groups):
            place = jnp.bitwise_xor(g, where_ref[3]) * part
            for chip in range(chips):
                at = pl.ds(pl.multiple_of(place + chip * rows, 16), part)
                first = (g * chips + chip) * part
                out[at, :] = acc[first : first + part].astype(BF)

    x_spec = pl.BlockSpec((depth, n_x), lambda i, w: (0, 0), pipeline_mode=ONCE)
    y_spec = pl.BlockSpec((depth, chunk), lambda i, w: (0, i))
    return pl.pallas_call(
        kernel,
        grid_spec=pltpu.PrefetchScalarGridSpec(
            num_scalar_prefetch=1,
            grid=(cols // chunk,),
            in_specs=[x_spec, x_spec, y_spec, y_spec] + [ANY] * n_after,
            out_specs=pl.BlockSpec((n_x, chunk), lambda i, w: (0, i)),
            scratch_shapes=[pltpu.VMEM((n_x, 2 * depth), BF), pltpu.VMEM((n_x, chunk), F32)],
        ),
        out_shape=jax.ShapeDtypeStruct((n_x, cols), BF),
        compiler_params=pltpu.CompilerParams(vmem_limit_bytes=LIMIT),
        cost_estimate=BACKWARD,
    )(where, *xs, *ys, *after)


def proj_grad_into(plan, where, xs, ys, first, keep, send, after=()):
    depth, n_x = xs[0].shape
    cols = ys[0].shape[1]
    ny, chips, bits = plan.ny, plan.chips, plan.bits
    half = cols // ny
    part = n_x // chips
    width = half * part // keep.shape[-2]
    stacked = half // width
    at_col = keep.shape[-1] // width - 1
    block = [1] + list(keep.shape[1:-1]) + [width]

    n_after = len(after)

    def kernel(where_ref, xo, xt, yo, yt, k_in, s_in, *rest):
        keep_ref, send_ref, acc = rest[n_after:]
        acc[...] = t_dot(xo[...], yo[...]) + t_dot(xt[...], yt[...])

        def put(ref, r):
            at = [0]
            for k in range(1, bits + 1):
                at.append((r >> (bits - k)) & 1 if k != first else 0)
            start = pl.multiple_of(jnp.bitwise_xor(where_ref[1], r) * part, 16)
            for g in range(stacked):
                piece = acc[pl.ds(start, part), g * width : (g + 1) * width]
                ref[tuple(at) + (pl.ds(g * part, part),)] = piece.astype(BF)

        if first:
            for r in range(chips):
                put(send_ref if (r >> (bits - first)) & 1 else keep_ref, r)
        else:

            @pl.when(pl.program_id(0) == 0)
            def _():
                for r in range(chips):
                    put(keep_ref, r)

            @pl.when(pl.program_id(0) != 0)
            def _():
                for r in range(chips):
                    put(send_ref, r)

    zeros = (0,) * (bits + 1)
    own = (lambda w: w[2]) if ny == 2 else (lambda w: 0)
    x_spec = pl.BlockSpec((depth, n_x), lambda i, w: (0, 0), pipeline_mode=ONCE)
    y_spec = pl.BlockSpec((depth, half), lambda i, w: (0, jnp.bitwise_xor(i, own(w))))
    spec = pl.BlockSpec(block, lambda i, w: (i if first else 0,) + zeros + (at_col,))
    return pl.pallas_call(
        kernel,
        grid_spec=pltpu.PrefetchScalarGridSpec(
            num_scalar_prefetch=1,
            grid=(ny,),
            in_specs=[x_spec, x_spec, y_spec, y_spec, ANY, ANY] + [ANY] * n_after,
            out_specs=[spec, spec],
            scratch_shapes=[pltpu.VMEM((n_x, half), F32)],
        ),
        out_shape=[jax.ShapeDtypeStruct(keep.shape, BF)] * 2,
        input_output_aliases={5: 0, 6: 1},
        compiler_params=pltpu.CompilerParams(vmem_limit_bytes=LIMIT),
        cost_estimate=BACKWARD,
    )(where, *xs, *ys, keep, send, *after)


class Term:
    def __init__(self, plan, keep, send, order):
        self.plan, self.keep, self.order = plan, keep, list(order)
        self.got = plan.flip(send, self.order.pop(0))

    def step(self, after):
        axis = self.order.pop(0)
        self.keep, send = combine(self.keep, self.got, axis, after)
        self.got = self.plan.flip(send, axis)
        return send


def combine(keep, got, axis, after):
    shape = keep.shape
    rows, cols = shape[-2:]
    cuts = 2
    block = shape[:-2] + (rows // cuts, cols)
    out = shape[:axis] + (1,) + shape[axis + 1 :]
    out_block = out[:-2] + (rows // cuts, cols)
    lead = len(shape) - 2

    def kernel(k, g, *rest):
        stay, go = rest[-2:]
        for side, ref in ((0, stay), (1, go)):
            at = tuple(pl.ds(side, 1) if d == axis else slice(None) for d in range(lead))
            ref[...] = (k[at].astype(F32) + g[at].astype(F32)).astype(BF)

    index = lambda i: (0,) * lead + (i, 0)
    return pl.pallas_call(
        kernel,
        grid=(cuts,),
        in_specs=[pl.BlockSpec(block, index)] * 2 + [ANY] * len(after),
        out_specs=[pl.BlockSpec(out_block, index)] * 2,
        out_shape=[jax.ShapeDtypeStruct(out, BF)] * 2,
        compiler_params=pltpu.CompilerParams(vmem_limit_bytes=SMALL_LIMIT),
        cost_estimate=BACKWARD,
    )(keep, got, *after)


def last_combine(terms, axis, rows, after):
    ins, specs, widths = [], [], []
    for t in terms:
        ins += [t.keep, t.got]
        widths.append(t.keep.shape[-1] * (t.keep.shape[-2] // rows))
    total = sum(widths)
    n_in = len(ins)

    def kernel(*refs):
        stay, go = refs[-2:]
        at = 0
        for j, t in enumerate(terms):
            k, g = refs[2 * j], refs[2 * j + 1]
            lead = k.ndim - 2
            cols = k.shape[-1]
            for block in range(k.shape[-2] // rows):
                for side, ref in ((0, stay), (1, go)):
                    idx = tuple(side if d == axis else 0 for d in range(lead)) + (pl.ds(block * rows, rows),)
                    ref[:, at : at + cols] = (k[idx].astype(F32) + g[idx].astype(F32)).astype(BF)
                at += cols

    whole = [pl.BlockSpec(v.shape, lambda n=v.ndim: (0,) * n) for v in ins]
    return pl.pallas_call(
        kernel,
        in_specs=whole + [ANY] * len(after),
        out_specs=[pl.BlockSpec((rows, total), lambda: (0, 0))] * 2,
        out_shape=[jax.ShapeDtypeStruct((rows, total), BF)] * 2,
        compiler_params=pltpu.CompilerParams(vmem_limit_bytes=SMALL_LIMIT),
        cost_estimate=BACKWARD,
    )(*ins, *after)


def pick(flag, a, b):
    return jnp.where(flag == 0, a, b)


def small_call(kernel, where, ins, shapes, after, grid=None):
    n = len(ins)

    def body(where_ref, *refs):
        kernel(where_ref, refs[:n], refs[n + len(after) :])

    return pl.pallas_call(
        body,
        grid_spec=pltpu.PrefetchScalarGridSpec(
            num_scalar_prefetch=1,
            grid=(1,),
            in_specs=[pl.BlockSpec(v.shape, lambda i, w, n=v.ndim: (0,) * n) for v in ins] + [ANY] * len(after),
            out_specs=[pl.BlockSpec(s, lambda i, w, n=len(s): (0,) * n) for s, _ in shapes],
        ),
        out_shape=[jax.ShapeDtypeStruct(s, t) for s, t in shapes],
        compiler_params=pltpu.CompilerParams(vmem_limit_bytes=SMALL_LIMIT),
        cost_estimate=BACKWARD,
    )(where, *ins, *after)


class Ending:
    def __init__(self, plan, where, terms, axis, rows, tail, after):
        self.plan, self.where, self.rows, self.tail = plan, where, rows, tail
        self.keep, self.sent = last_combine(terms, axis, rows, after)
        self.got = plan.flip(self.sent, axis)

    def core(self, after):
        rows, tail = self.rows // 2, self.tail
        cols = self.cols = self.keep.shape[1] - tail

        def kernel(where, ins, outs):
            c = where[0]
            for ref, row in ((outs[0], c), (outs[1], 1 - c)):
                at = pl.ds(pl.multiple_of(row * rows, 16), rows)
                ref[:, :cols] = (ins[0][at, :cols].astype(F32) + ins[1][at, :cols].astype(F32)).astype(BF)
            if tail:
                for g in range(2):
                    at = pl.ds(g * rows, rows)
                    piece = ins[0][at, cols:].astype(F32) + ins[1][at, cols:].astype(F32)
                    outs[0][:, cols + g * tail : cols + (g + 1) * tail] = piece.astype(BF)

        shapes = [((rows, cols + 2 * tail), BF), ((rows, cols), BF)]
        self.mine, sent = small_call(kernel, self.where, [self.keep, self.got], shapes, after)
        self.came = self.plan.core(sent)
        return sent

    def rep(self, after):
        rows, cols, tail = self.rows // 2, self.cols, self.tail

        def kernel(where, ins, outs):
            outs[0][:, :cols] = ins[0][:, :cols]
            outs[0][:, cols : 2 * cols] = ins[1][...]
            if tail:
                outs[0][:, 2 * cols :] = ins[0][:, cols:]

        shapes = [((rows, 2 * cols + 2 * tail), BF)]
        v = small_call(kernel, self.where, [self.mine, self.came], shapes, after)[0]
        self.pair = [v, self.plan.flip(v, 0)] if self.plan.ny == 2 else [lax.psum(v, "rep")]
        return v


class ChipEnding:
    def __init__(self, plan, where, term):
        self.plan, self.where = plan, where
        groups = [[2 * chip + c for chip in range(plan.chips)] for c in range(2)]
        self.term = lax.psum_scatter(term, "shard", scatter_dimension=0, axis_index_groups=groups, tiled=True)

    def core(self, after):
        rows, cols = self.term.shape
        part = rows // 4

        def kernel(where, ins, outs):
            c = where[0]
            for ref, row in ((outs[0], c), (outs[1], 1 - c)):
                for k in range(2):
                    at = pl.ds(pl.multiple_of((2 * k + row) * part, 16), part)
                    ref[k * part : (k + 1) * part] = ins[0][at]

        shapes = [((rows // 2, cols), BF)] * 2
        self.mine, sent = small_call(kernel, self.where, [self.term], shapes, after)
        self.came = self.plan.core(sent)
        return sent

    def rep(self, after):
        rows, cols = self.mine.shape

        def kernel(where, ins, outs):
            outs[0][:rows] = ins[0][...]
            outs[0][rows:] = ins[1][...]

        v = small_call(kernel, self.where, [self.mine, self.came], [((2 * rows, cols), BF)], after)[0]
        self.pair = [v, self.plan.flip(v, 0)] if self.plan.ny == 2 else [lax.psum(v, "rep")]
        return v


def place_grads(plan, where, layer, layers, end2, rest, sizes, before, after):
    deep, width, ff, quarters = sizes
    n, ny, halves = plan.shards, plan.ny, quarters // 2
    wide, half_ff = 3 * width // 2, ff // 2
    cols = rest.cols
    fused = bool(rest.tail)
    ins = end2.pair + rest.pair

    def kernel(where_ref, *refs):
        refs_in = refs[: 2 * ny]
        outs = refs[-(4 if fused else 3) :]
        c, y = where_ref[0], where_ref[2]

        def source(p, q, at, size):
            step = (at // 128) * 128
            span = (at + size - step + 127) // 128 * 128
            first = pl.multiple_of(jnp.where(p == c, 0, cols) + step, 128)
            v = refs_in[ny][:, pl.ds(first, span)]
            if ny == 2:
                v = jnp.where(y == q, v, refs_in[ny + 1][:, pl.ds(first, span)])
            return v[:, at - step : at - step + size].astype(F32)

        def core_columns(p, at, size, total, first):
            part = total // ny
            return source(p, at // part, first + at % part, size)

        for k in range(3 * HEADS // 2):
            pieces = [core_columns(p, k * HEAD_DIM, HEAD_DIM, wide, 0) for p in range(2)]
            outs[0][0, :, k * 2 * HEAD_DIM : (k + 1) * 2 * HEAD_DIM] = jnp.concatenate(pieces, axis=1)
        for k in range(n):
            pieces = []
            for p in range(2):
                for h in range(halves):
                    pieces.append(core_columns(p, (h * n + k) * deep, deep, half_ff, wide // ny))
            outs[1][0, :, k * quarters * deep : (k + 1) * quarters * deep] = jnp.concatenate(pieces, axis=1)
        part = width // ny
        for p in range(2):
            at = pl.ds(pl.multiple_of(jnp.where(p == c, 0, halves * deep), 16), halves * deep)
            v = refs_in[0][at].astype(F32)
            if ny == 2:
                v = v + refs_in[1][at].astype(F32)
            outs[2][0, p * halves * deep : (p + 1) * halves * deep] = v
        if fused:
            for q in range(ny):
                v = refs_in[ny][:, 2 * cols :]
                if ny == 2:
                    v = jnp.where(y == q, v, refs_in[ny + 1][:, 2 * cols :])
                outs[3][0, :, q * part : (q + 1) * part] = v.astype(F32)

    shapes = [(deep, 3 * width), (deep, ff), (quarters * deep, width)] + ([(deep, width)] if fused else [])
    in_specs = [pl.BlockSpec(v.shape, lambda i, w: (0, 0)) for v in ins]
    args = list(ins) + list(before or []) + list(after)
    n_before = len(before or [])
    return pl.pallas_call(
        kernel,
        grid_spec=pltpu.PrefetchScalarGridSpec(
            num_scalar_prefetch=1,
            grid=(1,),
            in_specs=in_specs + [ANY] * (n_before + len(after)),
            out_specs=[pl.BlockSpec((1,) + s, lambda i, w: (layer, 0, 0)) for s in shapes],
        ),
        out_shape=[jax.ShapeDtypeStruct((layers,) + s, F32) for s in shapes],
        input_output_aliases={1 + len(ins) + k: k for k in range(n_before)},
        compiler_params=pltpu.CompilerParams(vmem_limit_bytes=LIMIT),
        cost_estimate=BACKWARD,
    )(where, *args)


def pack(plan, where, layer, qkv, proj, fc1, fc2, extra, after):
    deep, width = proj.shape[1:]
    ff, n = fc1.shape[2], plan.shards
    quarters = fc2.shape[1] // deep
    halves = quarters // 2
    each = halves // plan.ny
    ins = [qkv, proj, fc1, fc2] + ([extra] if extra is not None else [])
    total = 4 * width + ff + 2 * each * width + (extra.shape[1] if extra is not None else 0)

    def kernel(where_ref, *refs):
        out = refs[-1]

        def lay(at, pieces):
            held, wide = [], 0
            for p in pieces:
                held.append(p)
                wide += p.shape[1]
                if wide % 128 == 0:
                    out[:, at : at + wide] = held[0] if len(held) == 1 else jnp.concatenate(held, axis=1)
                    at, held, wide = at + wide, [], 0

        for p in range(2):
            cols = [k * 2 * HEAD_DIM + p * HEAD_DIM for k in range(3 * HEADS // 2)]
            lay(p * (3 * width // 2), [refs[0][0, :, k : k + HEAD_DIM] for k in cols])
        out[:, 3 * width : 4 * width] = refs[1][0]
        cols = [s * quarters * deep + k * deep for k in range(quarters) for s in range(n)]
        lay(4 * width, [refs[2][0, :, k : k + deep] for k in cols])
        at = 4 * width + ff
        for p in range(2):
            for k in range(each):
                row = (p * halves + k) * deep + where_ref[3] * deep
                out[:, at : at + width] = refs[3][0, pl.ds(pl.multiple_of(row, 16), deep)]
                at += width
        if extra is not None:
            out[:, at:] = refs[4][...]

    specs = [pl.BlockSpec((1,) + v.shape[1:], lambda i, w: (layer, 0, 0)) for v in ins[:4]]
    specs += [pl.BlockSpec(v.shape, lambda i, w: (0, 0)) for v in ins[4:]]
    return pl.pallas_call(
        kernel,
        grid_spec=pltpu.PrefetchScalarGridSpec(
            num_scalar_prefetch=1,
            grid=(1,),
            in_specs=specs + [ANY] * len(after),
            out_specs=pl.BlockSpec((deep, total), lambda i, w: (0, 0)),
        ),
        out_shape=jax.ShapeDtypeStruct((deep, total), BF),
        compiler_params=pltpu.CompilerParams(vmem_limit_bytes=SMALL_LIMIT),
        cost_estimate=FORWARD,
    )(where, *ins, *after)


def per_device(
    plan,
    tokens,
    kept,
    attn_gain,
    attn_shift,
    qkv_weight,
    qv_bias,
    proj_weight,
    proj_bias,
    mlp_gain,
    mlp_shift,
    fc1_weight,
    fc1_bias,
    fc2_weight,
    fc2_bias,
    cotangent,
):
    images, slots, width = tokens.shape
    layers = attn_gain.shape[0]
    rows = images * slots
    n = plan.shards
    deep = qkv_weight.shape[1]
    shard = lax.axis_index("shard")
    c, chip, y = lax.rem(shard, 2), shard // 2, lax.axis_index("rep")
    where = jnp.stack([c, chip, y, y if plan.ny == 2 else 0 * y]).astype(jnp.int32)
    ff = fc2_weight.shape[1] * n
    quarters = fc2_weight.shape[1] // deep
    wide, half_width, half_ff = 3 * width // 2, width // 2, ff // 2
    half_heads = HEADS // 2

    small = jnp.concatenate(
        [attn_gain, attn_shift, qv_bias, proj_bias, mlp_gain, mlp_shift, fc1_bias, fc2_bias], axis=1
    )
    sizes = [v.shape[1] for v in (attn_gain, attn_shift, qv_bias, proj_bias, mlp_gain, mlp_shift, fc1_bias, fc2_bias)]
    lines = small.size // 128
    extra = jnp.pad(small.reshape(lines, 128), ((0, deep - lines), (0, 0)))

    halves = quarters // 2
    lead = 4 * width
    block = n * deep
    each = halves // plan.ny

    gathered, done = [], ()
    for layer in range(layers):
        shards = (qkv_weight, proj_weight, fc1_weight, fc2_weight)
        done = (pack(plan, where, layer, *shards, None if layer else extra, done),)
        gathered.append(lax.all_gather(done[0], "shard", axis=0, tiled=True))
    at_fc1, at_fc2 = lead // block, (lead + ff) // block
    mlp_parts = []
    for layer in range(layers):
        found = {"fc1": [(gathered[layer], ("quarter", block, (at_fc1, halves, k))) for k in range(halves)]}
        found["fc2"] = [(gathered[layer], columns(block, at_fc2 + k, each)) for k in range(each)]
        if plan.ny == 2:
            found["sent"], found["came"] = (), ()
            for k in range(1):
                mine = lax.dynamic_slice(
                    gathered[layer], (0, (at_fc2 + c) * block), (block, block)
                )
                found["sent"] += (mine,)
                found["came"] += (plan.flip(mine, 0),)
                found["fc2"].append((found["came"][k], None))
        mlp_parts.append(found)

    def weight_of(layer, name):
        if name == "qkv":
            return [(gathered[layer], columns(wide, 0, 1))]
        if name == "proj":
            return [(gathered[layer], ("heads", width, 3))]
        return mlp_parts[layer][name]

    every = gathered[0].reshape(n, deep, -1)[:, :lines, lead + ff + 2 * each * block :]
    every = every.reshape(n, layers, small.shape[1]).astype(F32)
    vecs = []
    for layer in range(layers):
        at, d = 0, {}
        for name, size in zip(SMALL, sizes):
            d[name] = every[:, layer, at : at + size].reshape(1, n * size)
            at += size
        q = d["qvb"].reshape(2 * half_heads, 2, HEAD_DIM)
        q = pick(c, q[:, 0], q[:, 1]).reshape(2, half_width)
        d["qvb_c"] = jnp.stack([q[0], jnp.zeros_like(q[0]), q[1]]).reshape(1, wide)
        f = d["f1b"].reshape(n, 2, halves, deep).transpose(1, 2, 0, 3).reshape(2, halves, block)
        f = pick(c, f[0], f[1])
        if plan.ny == 2:
            f = pick(y, f, f[::-1])
        d["f1b_c"] = f.reshape(1, half_ff)
        vecs.append(d)

    kept_oth = plan.core(kept)
    state = tokens.astype(F32).reshape(rows, width)
    live = lax.broadcasted_iota(jnp.int32, (images, slots), 1) < BUFFER + kept[:, None]
    grad = jnp.where(live[:, :, None], cotangent.astype(F32), 0.0).reshape(rows, width)
    low_own = grad.astype(BF)
    low_oth = plan.core(low_own)
    first_own = norm_rows(state, vecs[0]["ag"], vecs[0]["as"]).astype(BF)

    f32_rows, low_rows = ("rows", (rows, width), F32), ("rows", (rows, width), BF)
    wide_rows, ff_rows = ("rows", (rows, wide), BF), ("rows", (rows, half_ff), BF)
    att_outs = [("image", (images, half_heads, slots, slots), BF), ("rows", (rows, half_width), BF)]
    full_sums = ("full", (8, width), F32)

    def call(body, layer, own, names, blocked, whole, outs, after=(), cost=None):
        chosen = [weight_of(layer, name) for name in names]
        k = kept if own else kept_oth
        return row_call(body, where, k, chosen, blocked, whole, outs, images, slots, after, cost or (BACKWARD if after else FORWARD))

    saved = []
    for layer in range(layers):
        v = vecs[layer]
        first_oth = plan.core(first_own)
        sent, came = mlp_parts[layer].get("sent", ()), mlp_parts[layer].get("came", ())
        proj_oth = call(qkv_body, layer, 0, ["qkv"], [first_oth], [v["qvb_c"]], [wide_rows], sent, FORWARD)[0]
        probs_oth, att_oth, part = call(attend_other, layer, 0, ["proj"], [proj_oth], [], att_outs + [f32_rows])
        part = plan.core(part)
        proj_own = call(qkv_body, layer, 1, ["qkv"], [first_own], [v["qvb_c"]], [wide_rows])[0]
        probs_own, att_own, middle, second_own = call(
            attend_own, layer, 1, ["proj"], [proj_own, part, state], [v["pb"], v["mg"], v["ms"]], att_outs + [f32_rows, low_rows])
        second_oth = plan.core(second_own)
        hid_oth, slope_oth = call(up_body, layer, 0, ["fc1"], [second_oth], [v["f1b_c"]], [ff_rows] * 2)
        if layer + 1 < layers:
            part = call(down_other, layer, 0, ["fc2"], [hid_oth], [], [f32_rows])[0]
            part = plan.core(part)
        hid_own, slope_own = call(up_body, layer, 1, ["fc1"], [second_own], [v["f1b_c"]], [ff_rows] * 2)
        saved.append(
            dict(
                state=state,
                first=(first_own, first_oth),
                proj=(proj_own, proj_oth),
                probs=(probs_own, probs_oth),
                att=(att_own, att_oth),
                middle=middle,
                second=(second_own, second_oth),
                hid=(hid_own, hid_oth),
                slope=(slope_own, slope_oth),
            )
        )
        if layer + 1 < layers:
            w = vecs[layer + 1]
            state, first_own = call(
                down_own, layer, 1, ["fc2"], [hid_own, part, middle], [v["f2b"], w["ag"], w["as"]], [f32_rows, low_rows])

    axes = list(range(1 if plan.ny == 1 else 0, plan.bits + 1))
    last_axis, z_axis, x_axis = 1, plan.bits - 1, plan.bits
    y_axis = 0 if plan.ny == 2 else 2
    orders_f1 = [[y_axis, x_axis, z_axis]] * layers
    orders_q = [[[z_axis, y_axis, x_axis], [y_axis, z_axis, x_axis]]] + [[[x_axis, z_axis, y_axis]]] * (layers - 1)
    own_rows = 2 * deep
    tail = width // plan.ny * HEAD_DIM // own_rows
    fused = n == HEADS
    tail = tail if fused else 0
    big = [[None] * 4 for _ in range(layers)]
    sums = [None] * layers
    f2b_sum = jnp.sum(low_own.astype(F32), axis=0, keepdims=True)

    def end_rest(layer, prev):
        group = terms["q", layer] + [terms["f1", layer]]
        ends["rest", layer] = Ending(plan, where, group, last_axis, own_rows, tail, prev)
        return (ends["rest", layer].sent,)

    def place(layer, before, prev):
        return place_grads(
            plan, where, layer, layers, ends["f2", layer], ends["rest", layer], (deep, width, ff, quarters), before, prev
        )

    ends = {}
    prev = (hid_own,) + mlp_parts[layers - 1].get("came", ())
    terms = {}
    for layer in reversed(range(layers)):
        v, s = vecs[layer], saved[layer]
        top = layer == layers - 1

        def grad_fc2(prev):
            term = chip_grad(plan, where, s["hid"], (low_own, low_oth), 2, prev)
            ends["f2", layer] = ChipEnding(plan, where, term)
            return (term,)

        if top:
            prev = grad_fc2(prev)
        pre_oth, part = call(
            mlp_back_other, layer, 0, ["fc2", "fc1"], [low_oth, s["slope"][1]], [], [ff_rows, f32_rows], prev
        )
        part = plan.core(part)
        prev = (pre_oth,)
        if top:
            last_part = call(down_other, layer, 0, ["fc2"], [s["hid"][1]], [], [f32_rows], prev)[0]
            prev = (last_part,)
            last_part = plan.core(last_part)
        else:
            prev = grad_fc2(prev)
            prev += (terms["f1", layer + 1].step(prev[:1]),)
        pre_own, mid_grad, branch_own, sum1 = call(
            mlp_back_own,
            layer,
            1,
            ["fc2", "fc1"],
            [low_own, s["slope"][0], part, s["middle"], grad],
            [v["mg"]],
            [ff_rows, f32_rows, low_rows, full_sums],
            prev,
        )
        branch_oth = plan.core(branch_own)
        prev = (branch_own,)
        if not top:
            prev += (terms["q", layer + 1][0].step(prev),)
        res1 = weight_grad(
            plan, where, s["second"], (pre_own, pre_oth), 1, orders_f1[layer][0], sums=True, extra=tail, relative=True, after=prev
        )
        prev = tuple(res1[:1])
        if not top:
            prev += (terms["q", layer + 1][0].step(prev[:1]),)
            prev += (terms["f1", layer + 1].step(prev[:1]),)
            prev += (ends["f2", layer + 1].core(prev[:1]),)
        dproj_oth, part = call(
            attend_back_other,
            layer,
            0,
            ["proj", "qkv"],
            [branch_oth, s["proj"][1], s["probs"][1]],
            [],
            [wide_rows, f32_rows],
            prev,
        )
        part = plan.core(part)
        prev = (dproj_oth,)
        keep, send = res1[:2]
        if fused:
            keep, send = proj_grad_into(
                plan, where, s["att"], (branch_own, branch_oth), orders_f1[layer][0], keep, send, prev
            )
        else:
            term = t_dot(s["att"][0], branch_own) + t_dot(s["att"][1], branch_oth)
            term = term.astype(BF).reshape(half_heads, HEAD_DIM, width)
            none = jnp.zeros_like(term)
            term = jnp.stack([pick(c, term, none), pick(c, none, term)], axis=1).reshape(width, width)
            term = lax.psum_scatter(term, "shard", scatter_dimension=0, tiled=True)
            big[layer][1] = lax.psum(term, "rep").astype(F32)
        terms["f1", layer] = Term(plan, keep, send, orders_f1[layer])
        prev = (send,)
        if not top:
            prev += (ends["f2", layer + 1].rep(prev[:1]),)
        dproj_own, grad, low_own, sum2 = call(
            attend_back_own,
            layer,
            1,
            ["proj", "qkv"],
            [branch_own, s["proj"][0], s["probs"][0], part, s["state"], mid_grad],
            [v["ag"]],
            [wide_rows, f32_rows, low_rows, full_sums],
            prev,
        )
        prev = (dproj_own,)
        if layer:
            low_oth = plan.core(low_own)
        if not top:
            prev += end_rest(layer + 1, prev[:1])
            prev += (ends["f2", layer].core(prev[:1]),)
        terms["q", layer], q_sums = [], []
        of = len(orders_q[layer])
        for k, order in enumerate(orders_q[layer]):
            resq = weight_grad(
                plan, where, s["first"], (dproj_own, dproj_oth), 1, order[0], sums=True, window=(k, of), after=prev
            )
            terms["q", layer].append(Term(plan, *resq[:2], order))
            q_sums.append(resq[2].reshape(plan.ny, -1))
            prev = (resq[1],)
        q = jnp.concatenate(q_sums, axis=1).reshape(3, half_heads, 1, HEAD_DIM)
        q = jnp.concatenate([q[:1], q[2:]])
        none = jnp.zeros_like(q)
        q = jnp.concatenate([pick(c, q, none), pick(c, none, q)], axis=2)
        f = res1[2].reshape(halves, block)
        if plan.ny == 2:
            f = pick(y, f, f[::-1])
        none = jnp.zeros_like(f)
        f = jnp.concatenate([pick(c, f, none), pick(c, none, f)], axis=0)
        f = f.reshape(quarters, n, deep).swapaxes(0, 1)
        full = {"ag": sum2[0], "as": sum2[1], "qvb": q, "pb": sum1[2], "mg": sum1[0], "ms": sum1[1], "f1b": f, "f2b": f2b_sum}
        f2b_sum = sum2[2]
        vec = jnp.concatenate([full[name].reshape(n, -1) for name in SMALL], axis=1)
        sums[layer] = vec

    vec = jnp.concatenate(sums, axis=0).reshape(layers, n, -1)
    got_vec = plan.core(vec)
    vec_axes = list(axes)

    def step_vec(prev):
        nonlocal vec, got_vec

        def kernel(where, ins, outs):
            outs[0][...] = ins[0][...] + ins[1][...]

        vec = small_call(kernel, where, [vec, got_vec], [(vec.shape, F32)], prev)[0]
        got_vec = plan.flip(vec, vec_axes.pop(0)) if vec_axes else None
        return (vec,)

    prev += (terms["f1", 0].step(prev[:1]),)
    prev += (ends["rest", 1].core(prev[:1]),)
    w = layers - 1
    mixed = call(
        down_last, w, 1, ["fc2"], [saved[w]["hid"][0], last_part, saved[w]["middle"]], [vecs[w]["f2b"]], [low_rows], prev
    )[0]
    qa, qb = terms["q", 0]
    prev = (ends["f2", 0].rep(step_vec((mixed,))),)
    prev = (qa.step(prev),)
    prev = (qb.step(prev),)
    prev = (ends["rest", 1].rep(prev),)
    prev = step_vec(prev)
    prev = (qa.step(prev),)
    prev = (terms["f1", 0].step(prev),)
    prev = (qb.step(prev),)
    prev = step_vec(prev)
    prev = end_rest(0, prev)
    prev = step_vec(prev)
    placed = place(1, None, prev)
    prev = (placed[0],)
    while got_vec is not None:
        prev = step_vec(prev)
    prev = (ends["rest", 0].core(prev + tuple(ends["f2", 0].pair[1:])),)
    prev = (ends["rest", 0].rep(prev),)
    placed = place(0, placed, prev)
    if plan.ny == 1:
        vec = lax.psum(vec, "rep")
    vec = lax.dynamic_slice_in_dim(vec, shard, 1, axis=1)[:, 0]
    out, at = {}, 0
    for name, size in zip(SMALL, sizes):
        out[name] = vec[:, at : at + size]
        at += size
    qkv_g, fc1_g, fc2_g = placed[:3]
    proj_g = placed[3] if fused else jnp.stack([big[layer][1] for layer in range(layers)])
    return (
        mixed.reshape(images, slots, width),
        grad.reshape(images, slots, width),
        out["ag"],
        out["as"],
        qkv_g,
        out["qvb"],
        proj_g,
        out["pb"],
        out["mg"],
        out["ms"],
        fc1_g,
        out["f1b"],
        fc2_g,
        out["f2b"],
    )


def solution(mesh):
    rows = P(("shard", "rep"), None, None)
    vec = P(None, "shard")
    mat = P(None, "shard", None)
    return jax.shard_map(
        partial(per_device, Plan(mesh)),
        mesh=mesh,
        in_specs=(rows, P(("shard", "rep")), vec, vec, mat, vec, mat, vec, vec, vec, mat, vec, mat, vec, rows),
        out_specs=(rows, rows, vec, vec, mat, vec, mat, vec, vec, vec, mat, vec, mat, vec),
        check_vma=False,
    )
```

```python
from functools import partial

import jax
import jax.numpy as jnp
from jax import lax
from jax.experimental import pallas as pl
from jax.experimental.pallas import tpu as pltpu
from jax.sharding import PartitionSpec as P

HEADS = 16
HEAD_DIM = 64
BUFFER = 64
EPS = 1e-06
SCALE = HEAD_DIM ** (-0.5)
AX = ("shard", "rep")
BF = jnp.bfloat16
F32 = jnp.float32
LIMIT = 60 * 2**20
SMALL_LIMIT = 16 * 2**20
ONCE = pl.Buffered(1)
ANY = pl.BlockSpec(memory_space=pl.ANY)
FORWARD = pl.CostEstimate(flops=10**7, bytes_accessed=0, transcendentals=0)
BACKWARD = pl.CostEstimate(flops=10**9 * 30, bytes_accessed=0, transcendentals=0)
SMALL = ("ag", "as", "qvb", "pb", "mg", "ms", "f1b", "f2b")


class Plan:
    def __init__(self, mesh):
        self.shards = mesh.shape["shard"]
        self.rep = mesh.shape["rep"]
        self.chips = self.shards // 2
        self.ny = 2 if self.rep == 2 else 1
        self.bits = self.chips.bit_length() - 1

    def swap(self, v, flip_shard, flip_rep=0):
        pairs = []
        for s in range(self.shards):
            for y in range(self.rep):
                pairs.append((s * self.rep + y, (s ^ flip_shard) * self.rep + (y ^ flip_rep)))
        return lax.ppermute(v, AX, pairs)

    def core(self, v):
        return self.swap(v, 1)

    def flip(self, v, axis):
        if axis == 0:
            return self.swap(v, 0, 1)
        return self.swap(v, 2 << (self.bits - axis))


def dot(x, w):
    return lax.dot_general(x, w, (((1,), (0,)), ((), ())), preferred_element_type=F32)


def dot_t(x, w):
    return lax.dot_general(x, w, (((1,), (1,)), ((), ())), preferred_element_type=F32)


def t_dot(x, w):
    return lax.dot_general(x, w, (((0,), (0,)), ((), ())), preferred_element_type=F32)


def columns(width, first, stride):
    return ("columns", width, (first, stride))


def row_call(body, where, kept, weights, blocked, whole, outs, images, slots, after=(), cost=FORWARD):
    in_specs, args = [], []
    for v, pick_of in (part for w in weights for part in w):
        if pick_of is None:
            in_specs.append(pl.BlockSpec(v.shape, lambda i, w, k: (0, 0), pipeline_mode=ONCE))
            args.append(v)
            continue
        kind, width, first = pick_of
        if kind == "columns":
            spec = pl.BlockSpec((v.shape[0], width), lambda i, w, k, f=first: (0, f[0] + f[1] * w[0]), pipeline_mode=ONCE)
            in_specs.append(spec)
            args.append(v)
        elif kind == "quarter":
            at, stride, part = first
            spec = pl.BlockSpec(
                (v.shape[0], width),
                lambda i, w, k, f=(at, stride, part): (0, f[0] + f[1] * w[0] + jnp.bitwise_xor(f[2], w[3])),
                pipeline_mode=ONCE,
            )
            in_specs.append(spec)
            args.append(v)
        else:
            view = v.reshape(HEADS // 2, 2, HEAD_DIM, v.shape[1])
            spec = pl.BlockSpec((HEADS // 2, None, HEAD_DIM, width), lambda i, w, k, f=first: (0, w[0], 0, f), pipeline_mode=ONCE)
            in_specs.append(spec)
            args.append(view)
    for v in blocked:
        if v.ndim == 2:
            in_specs.append(pl.BlockSpec((slots, v.shape[1]), lambda i, *_: (i, 0)))
        else:
            in_specs.append(pl.BlockSpec((1,) + v.shape[1:], lambda i, *_, n=v.ndim: (i,) + (0,) * (n - 1)))
        args.append(v)
    for v in whole:
        in_specs.append(pl.BlockSpec(v.shape, lambda i, *_, n=v.ndim: (0,) * n))
        args.append(v)
    out_specs, out_shape = [], []
    for kind, shape, dtype in outs:
        out_shape.append(jax.ShapeDtypeStruct(shape, dtype))
        if kind == "rows":
            out_specs.append(pl.BlockSpec((slots, shape[1]), lambda i, *_: (i, 0)))
        elif kind == "image":
            out_specs.append(pl.BlockSpec((1,) + shape[1:], lambda i, *_, n=len(shape): (i,) + (0,) * (n - 1)))
        else:
            out_specs.append(pl.BlockSpec(shape, lambda i, *_, n=len(shape): (0,) * n))
    n_p, n_b, n_in = sum(len(w) for w in weights), len(blocked), len(args)
    in_specs += [ANY] * len(after)
    args += list(after)

    def kernel(where_ref, kept_ref, *refs):
        ins, res = refs[:n_in], refs[n_in + len(after) :]
        held, at = [], 0
        for w in weights:
            held.append(ins[at : at + len(w)])
            at += len(w)
        body(kept_ref, held, ins[n_p : n_p + n_b], ins[n_p + n_b : n_in], res)

    return pl.pallas_call(
        kernel,
        grid_spec=pltpu.PrefetchScalarGridSpec(
            num_scalar_prefetch=2, grid=(images,), in_specs=in_specs, out_specs=out_specs
        ),
        out_shape=out_shape,
        compiler_params=pltpu.CompilerParams(vmem_limit_bytes=LIMIT),
        cost_estimate=cost,
    )(where, kept, *args)


def normed_of(rows):
    width = rows.shape[-1]
    mean = jnp.sum(rows, axis=-1, keepdims=True) * (1.0 / width)
    centered = rows - mean
    spread = jnp.sum(centered * centered, axis=-1, keepdims=True) * (1.0 / width)
    factor = lax.rsqrt(spread + EPS)
    return centered * factor, factor


def norm_rows(rows, gain, shift):
    return normed_of(rows)[0] * gain + shift


def norm_back(dz, rows, gain):
    normed, factor = normed_of(rows)
    width = rows.shape[-1]
    prod = dz * normed
    dn = dz * gain
    m1 = jnp.sum(dn, axis=-1, keepdims=True) * (1.0 / width)
    m2 = jnp.sum(dn * normed, axis=-1, keepdims=True) * (1.0 / width)
    back = factor * (dn - m1 - normed * m2)
    return back, jnp.sum(prod, axis=0, keepdims=True), jnp.sum(dz, axis=0, keepdims=True)


def chunks(total, size):
    size = min(size, total)
    return [(k, size) for k in range(0, total, size)]


def qkv_body(kept, w, blocked, whole, outs):
    x = blocked[0][...]
    for k, n in chunks(outs[0].shape[1], 512):
        cols = pl.ds(k, n)
        outs[0][:, cols] = (dot(x, w[0][0][:, cols]) + whole[0][:, cols]).astype(BF)


def heads_of(ref):
    return ref[...].reshape(-1, ref.shape[-1])


def pairs_dot(x_ref, parts):
    total, at = None, 0
    for w_ref in parts:
        term = dot(x_ref[:, at : at + w_ref.shape[0]], w_ref[...])
        total = term if total is None else total + term
        at += w_ref.shape[0]
    return total


def attend(kept, proj_ref, probs_ref, att_ref):
    slots, third = proj_ref.shape[0], proj_ref.shape[1] // 3
    bound = BUFFER + kept[pl.program_id(0)]
    alive = lax.broadcasted_iota(jnp.int32, (slots, slots), 1) < bound
    outs = []
    for h in range(third // HEAD_DIM):
        lo = h * HEAD_DIM
        q = proj_ref[:, lo : lo + HEAD_DIM]
        k = proj_ref[:, third + lo : third + lo + HEAD_DIM]
        v = proj_ref[:, 2 * third + lo : 2 * third + lo + HEAD_DIM]
        s = jnp.where(alive, dot_t(q, k) * SCALE, -1e30)
        e = jnp.exp(s - jnp.max(s, axis=-1, keepdims=True))
        p = (e * (1.0 / jnp.sum(e, axis=-1, keepdims=True))).astype(BF)
        probs_ref[0, h] = p
        outs.append(dot(p, v).astype(BF))
        if h % 2:
            att_ref[:, lo - HEAD_DIM : lo + HEAD_DIM] = jnp.concatenate(outs, axis=1)
            outs = []


def attend_other(kept, w, blocked, whole, outs):
    attend(kept, blocked[0], outs[0], outs[1])
    outs[2][...] = dot(outs[1][...], heads_of(w[0][0]))


def attend_own(kept, w, blocked, whole, outs):
    attend(kept, blocked[0], outs[0], outs[1])
    middle = blocked[2][...] + (dot(outs[1][...], heads_of(w[0][0])) + blocked[1][...]) + whole[0][...]
    outs[2][...] = middle
    outs[3][...] = norm_rows(middle, whole[1][...], whole[2][...]).astype(BF)


def up_body(kept, w, blocked, whole, outs):
    x = blocked[0][...]
    for k, n in chunks(outs[0].shape[1], 256):
        cols = pl.ds(k, n)
        held = w[0][k // w[0][0].shape[1]]
        pre = dot(x, held[:, pl.ds(k % held.shape[1], n)]) + whole[0][:, cols]
        phi = 0.5 + 0.5 * lax.erf(pre * (2.0**-0.5))
        dens = jnp.exp(-0.5 * (pre * pre)) * 0.3989422804014327
        outs[0][:, cols] = (pre * phi).astype(BF)
        outs[1][:, cols] = (phi + pre * dens).astype(BF)


def down_other(kept, w, blocked, whole, outs):
    outs[0][...] = pairs_dot(blocked[0], w[0])


def down_own(kept, w, blocked, whole, outs):
    state = blocked[2][...] + (pairs_dot(blocked[0], w[0]) + blocked[1][...]) + whole[0][...]
    outs[0][...] = state
    outs[1][...] = norm_rows(state, whole[1][...], whole[2][...]).astype(BF)


def down_last(kept, w, blocked, whole, outs):
    state = blocked[2][...] + (pairs_dot(blocked[0], w[0]) + blocked[1][...]) + whole[0][...]
    alive = lax.broadcasted_iota(jnp.int32, state.shape, 0) < BUFFER + kept[pl.program_id(0)]
    outs[0][...] = jnp.where(alive, state, 0.0).astype(BF)


def mlp_back(w, blocked, outs):
    low = blocked[0][...]
    for k, n in chunks(outs[0].shape[1], 512):
        cols = pl.ds(k, n)
        held, first = w[0][0], 0
        for part in w[0][1:]:
            if k >= first + held.shape[0]:
                first += held.shape[0]
                held = part
        t = dot_t(low, held[pl.ds(k - first, n), :])
        outs[0][:, cols] = (t * blocked[1][:, cols].astype(F32)).astype(BF)
    total, at = None, 0
    for held in w[1]:
        term = dot_t(outs[0][:, at : at + held.shape[1]], held[...])
        total = term if total is None else total + term
        at += held.shape[1]
    return total


def mlp_back_other(kept, w, blocked, whole, outs):
    outs[1][...] = mlp_back(w, blocked, outs)


def add_sums(ref, rows):
    sums = jnp.concatenate(rows + [jnp.zeros((8 - len(rows), rows[0].shape[1]), F32)], axis=0)

    @pl.when(pl.program_id(0) == 0)
    def _():
        ref[...] = sums

    @pl.when(pl.program_id(0) != 0)
    def _():
        ref[...] += sums


def mlp_back_own(kept, w, blocked, whole, outs):
    dz = mlp_back(w, blocked, outs) + blocked[2][...]
    back, gain, shift = norm_back(dz, blocked[3][...], whole[0][...])
    grad = blocked[4][...] + back
    low = grad.astype(BF)
    outs[1][...] = grad
    outs[2][...] = low
    add_sums(outs[3], [gain, shift, jnp.sum(low.astype(F32), axis=0, keepdims=True)])


def attend_back(w, blocked, outs):
    branch, proj_ref, probs_ref = blocked[0], blocked[1], blocked[2]
    third = proj_ref.shape[1] // 3
    datt = dot_t(branch[...], heads_of(w[0][0])).astype(BF)
    pairs = [[], [], []]
    for h in range(third // HEAD_DIM):
        lo = h * HEAD_DIM
        q = proj_ref[:, lo : lo + HEAD_DIM]
        k = proj_ref[:, third + lo : third + lo + HEAD_DIM]
        v = proj_ref[:, 2 * third + lo : 2 * third + lo + HEAD_DIM]
        da = datt[:, lo : lo + HEAD_DIM]
        p = probs_ref[0, h]
        dp = dot_t(da, v)
        pf = p.astype(F32)
        ds = (pf * (dp - jnp.sum(pf * dp, axis=-1, keepdims=True))).astype(BF)
        pairs[0].append((dot(ds, k) * SCALE).astype(BF))
        pairs[1].append((t_dot(ds, q) * SCALE).astype(BF))
        pairs[2].append(t_dot(p, da).astype(BF))
        if h % 2:
            for j in range(3):
                at = j * third + lo - HEAD_DIM
                outs[0][:, at : at + 2 * HEAD_DIM] = jnp.concatenate(pairs[j], axis=1)
            pairs = [[], [], []]
    return dot_t(outs[0][...], w[1][0][...])


def attend_back_other(kept, w, blocked, whole, outs):
    outs[1][...] = attend_back(w, blocked, outs)


def attend_back_own(kept, w, blocked, whole, outs):
    dz = attend_back(w, blocked, outs) + blocked[3][...]
    back, gain, shift = norm_back(dz, blocked[4][...], whole[0][...])
    grad = blocked[5][...] + back
    outs[1][...] = grad
    low = grad.astype(BF)
    outs[2][...] = low
    add_sums(outs[3], [gain, shift, jnp.sum(low.astype(F32), axis=0, keepdims=True)])


def weight_grad(plan, where, xs, ys, groups, first, sums=False, extra=0, relative=False, window=(0, 1), after=()):
    depth, n_x = xs[0].shape
    cols = ys[0].shape[1]
    ny, chips, bits = plan.ny, plan.chips, plan.bits
    half = cols // ny
    size = half // window[1]
    chunk = size if size <= 768 else 512
    steps = size // chunk
    rows = n_x // chips
    part = rows // groups
    dims = [ny] + [2] * bits
    dims[first] = 1
    block = [1] + dims[1:] + [rows, chunk]
    shape = dims + [rows, size + extra]
    n_after = len(after)

    def kernel(where_ref, xo, xt, yo, yt, *rest):
        rest = rest[n_after:]
        keep, send = rest[0], rest[1]
        flip, acc = rest[-2], rest[-1]
        step = pl.program_id(0)

        @pl.when(step == 0)
        def _():
            flip[:, :depth] = xo[...].T
            flip[:, depth:] = xt[...].T

        acc[...] = dot(flip[:, :depth], yo[...]) + dot(flip[:, depth:], yt[...])
        if sums:
            rest[2][...] = jnp.sum(yo[...].astype(F32), axis=0, keepdims=True) + jnp.sum(
                yt[...].astype(F32), axis=0, keepdims=True
            )

        def put(ref, r):
            at = [0]
            for k in range(1, bits + 1):
                at.append((r >> (bits - k)) & 1 if k != first else 0)
            chip = jnp.bitwise_xor(where_ref[1], r)
            for g in range(groups):
                start = pl.multiple_of(g * part * chips + chip * part, 16)
                place = g
                if groups == 2 and ny == 2:
                    place = jnp.bitwise_xor(g, where_ref[2])
                place = pl.multiple_of(place * part, 16)
                ref[tuple(at) + (pl.ds(place, part),)] = acc[pl.ds(start, part)].astype(BF)

        if first:
            for r in range(chips):
                put(send if (r >> (bits - first)) & 1 else keep, r)
        else:

            @pl.when(step < steps)
            def _():
                for r in range(chips):
                    put(keep, r)

            @pl.when(step >= steps)
            def _():
                for r in range(chips):
                    put(send, r)

    per_rep = half // chunk

    def column(i, w):
        own = w[2] if ny == 2 and not relative else 0
        return jnp.bitwise_xor(i // steps, own) * per_rep + window[0] * steps + i % steps

    zeros = (0,) * (bits + 1)
    x_spec = pl.BlockSpec((depth, n_x), lambda i, w: (0, 0), pipeline_mode=ONCE)
    y_spec = pl.BlockSpec((depth, chunk), lambda i, w: (0, column(i, w)))
    if first:
        specs = [pl.BlockSpec(block, lambda i, w: (i // steps,) + zeros + (i % steps,))] * 2
    else:
        specs = [
            pl.BlockSpec(block, lambda i, w: (0,) + zeros + (jnp.minimum(i, steps - 1),)),
            pl.BlockSpec(block, lambda i, w: (0,) + zeros + (jnp.maximum(i - steps, 0),)),
        ]
    out_shape = [jax.ShapeDtypeStruct(shape, BF)] * 2
    if sums:
        own = (lambda w: w[2]) if ny == 2 and not relative else (lambda w: 0)
        specs = specs + [
            pl.BlockSpec((1, chunk), lambda i, w: (0, jnp.bitwise_xor(i // steps, own(w)) * steps + i % steps))
        ]
        out_shape = out_shape + [jax.ShapeDtypeStruct((1, size * ny), F32)]
    return pl.pallas_call(
        kernel,
        grid_spec=pltpu.PrefetchScalarGridSpec(
            num_scalar_prefetch=1,
            grid=(ny * steps,),
            in_specs=[x_spec, x_spec, y_spec, y_spec] + [ANY] * n_after,
            out_specs=specs,
            scratch_shapes=[pltpu.VMEM((n_x, 2 * depth), BF), pltpu.VMEM((n_x, chunk), F32)],
        ),
        out_shape=out_shape,
        compiler_params=pltpu.CompilerParams(vmem_limit_bytes=LIMIT),
        cost_estimate=BACKWARD,
    )(where, *xs, *ys, *after)


def chip_grad(plan, where, xs, ys, groups, after=()):
    depth, n_x = xs[0].shape
    cols = ys[0].shape[1]
    chips = plan.chips
    chunk = min(cols, 512)
    rows = n_x // chips
    part = rows // groups
    n_after = len(after)

    def kernel(where_ref, xo, xt, yo, yt, *rest):
        out, flip, acc = rest[n_after:]

        @pl.when(pl.program_id(0) == 0)
        def _():
            flip[:, :depth] = xo[...].T
            flip[:, depth:] = xt[...].T

        acc[...] = dot(flip[:, :depth], yo[...]) + dot(flip[:, depth:], yt[...])
        for g in range(groups):
            place = jnp.bitwise_xor(g, where_ref[3]) * part
            for chip in range(chips):
                at = pl.ds(pl.multiple_of(place + chip * rows, 16), part)
                first = (g * chips + chip) * part
                out[at, :] = acc[first : first + part].astype(BF)

    x_spec = pl.BlockSpec((depth, n_x), lambda i, w: (0, 0), pipeline_mode=ONCE)
    y_spec = pl.BlockSpec((depth, chunk), lambda i, w: (0, i))
    return pl.pallas_call(
        kernel,
        grid_spec=pltpu.PrefetchScalarGridSpec(
            num_scalar_prefetch=1,
            grid=(cols // chunk,),
            in_specs=[x_spec, x_spec, y_spec, y_spec] + [ANY] * n_after,
            out_specs=pl.BlockSpec((n_x, chunk), lambda i, w: (0, i)),
            scratch_shapes=[pltpu.VMEM((n_x, 2 * depth), BF), pltpu.VMEM((n_x, chunk), F32)],
        ),
        out_shape=jax.ShapeDtypeStruct((n_x, cols), BF),
        compiler_params=pltpu.CompilerParams(vmem_limit_bytes=LIMIT),
        cost_estimate=BACKWARD,
    )(where, *xs, *ys, *after)


def proj_grad_into(plan, where, xs, ys, first, keep, send, after=()):
    depth, n_x = xs[0].shape
    cols = ys[0].shape[1]
    ny, chips, bits = plan.ny, plan.chips, plan.bits
    half = cols // ny
    part = n_x // chips
    width = half * part // keep.shape[-2]
    stacked = half // width
    at_col = keep.shape[-1] // width - 1
    block = [1] + list(keep.shape[1:-1]) + [width]

    n_after = len(after)

    def kernel(where_ref, xo, xt, yo, yt, k_in, s_in, *rest):
        keep_ref, send_ref, acc = rest[n_after:]
        acc[...] = t_dot(xo[...], yo[...]) + t_dot(xt[...], yt[...])

        def put(ref, r):
            at = [0]
            for k in range(1, bits + 1):
                at.append((r >> (bits - k)) & 1 if k != first else 0)
            start = pl.multiple_of(jnp.bitwise_xor(where_ref[1], r) * part, 16)
            for g in range(stacked):
                piece = acc[pl.ds(start, part), g * width : (g + 1) * width]
                ref[tuple(at) + (pl.ds(g * part, part),)] = piece.astype(BF)

        if first:
            for r in range(chips):
                put(send_ref if (r >> (bits - first)) & 1 else keep_ref, r)
        else:

            @pl.when(pl.program_id(0) == 0)
            def _():
                for r in range(chips):
                    put(keep_ref, r)

            @pl.when(pl.program_id(0) != 0)
            def _():
                for r in range(chips):
                    put(send_ref, r)

    zeros = (0,) * (bits + 1)
    own = (lambda w: w[2]) if ny == 2 else (lambda w: 0)
    x_spec = pl.BlockSpec((depth, n_x), lambda i, w: (0, 0), pipeline_mode=ONCE)
    y_spec = pl.BlockSpec((depth, half), lambda i, w: (0, jnp.bitwise_xor(i, own(w))))
    spec = pl.BlockSpec(block, lambda i, w: (i if first else 0,) + zeros + (at_col,))
    return pl.pallas_call(
        kernel,
        grid_spec=pltpu.PrefetchScalarGridSpec(
            num_scalar_prefetch=1,
            grid=(ny,),
            in_specs=[x_spec, x_spec, y_spec, y_spec, ANY, ANY] + [ANY] * n_after,
            out_specs=[spec, spec],
            scratch_shapes=[pltpu.VMEM((n_x, half), F32)],
        ),
        out_shape=[jax.ShapeDtypeStruct(keep.shape, BF)] * 2,
        input_output_aliases={5: 0, 6: 1},
        compiler_params=pltpu.CompilerParams(vmem_limit_bytes=LIMIT),
        cost_estimate=BACKWARD,
    )(where, *xs, *ys, keep, send, *after)


class Term:
    def __init__(self, plan, keep, send, order):
        self.plan, self.keep, self.order = plan, keep, list(order)
        self.got = plan.flip(send, self.order.pop(0))

    def step(self, after):
        axis = self.order.pop(0)
        self.keep, send = combine(self.keep, self.got, axis, after)
        self.got = self.plan.flip(send, axis)
        return send


def combine(keep, got, axis, after):
    shape = keep.shape
    rows, cols = shape[-2:]
    cuts = 2
    block = shape[:-2] + (rows // cuts, cols)
    out = shape[:axis] + (1,) + shape[axis + 1 :]
    out_block = out[:-2] + (rows // cuts, cols)
    lead = len(shape) - 2

    def kernel(k, g, *rest):
        stay, go = rest[-2:]
        for side, ref in ((0, stay), (1, go)):
            at = tuple(pl.ds(side, 1) if d == axis else slice(None) for d in range(lead))
            ref[...] = (k[at].astype(F32) + g[at].astype(F32)).astype(BF)

    index = lambda i: (0,) * lead + (i, 0)
    return pl.pallas_call(
        kernel,
        grid=(cuts,),
        in_specs=[pl.BlockSpec(block, index)] * 2 + [ANY] * len(after),
        out_specs=[pl.BlockSpec(out_block, index)] * 2,
        out_shape=[jax.ShapeDtypeStruct(out, BF)] * 2,
        compiler_params=pltpu.CompilerParams(vmem_limit_bytes=SMALL_LIMIT),
        cost_estimate=BACKWARD,
    )(keep, got, *after)


def last_combine(terms, axis, rows, after):
    ins, specs, widths = [], [], []
    for t in terms:
        ins += [t.keep, t.got]
        widths.append(t.keep.shape[-1] * (t.keep.shape[-2] // rows))
    total = sum(widths)
    n_in = len(ins)

    def kernel(*refs):
        stay, go = refs[-2:]
        at = 0
        for j, t in enumerate(terms):
            k, g = refs[2 * j], refs[2 * j + 1]
            lead = k.ndim - 2
            cols = k.shape[-1]
            for block in range(k.shape[-2] // rows):
                for side, ref in ((0, stay), (1, go)):
                    idx = tuple(side if d == axis else 0 for d in range(lead)) + (pl.ds(block * rows, rows),)
                    ref[:, at : at + cols] = (k[idx].astype(F32) + g[idx].astype(F32)).astype(BF)
                at += cols

    whole = [pl.BlockSpec(v.shape, lambda n=v.ndim: (0,) * n) for v in ins]
    return pl.pallas_call(
        kernel,
        in_specs=whole + [ANY] * len(after),
        out_specs=[pl.BlockSpec((rows, total), lambda: (0, 0))] * 2,
        out_shape=[jax.ShapeDtypeStruct((rows, total), BF)] * 2,
        compiler_params=pltpu.CompilerParams(vmem_limit_bytes=SMALL_LIMIT),
        cost_estimate=BACKWARD,
    )(*ins, *after)


def pick(flag, a, b):
    return jnp.where(flag == 0, a, b)


def small_call(kernel, where, ins, shapes, after, grid=None):
    n = len(ins)

    def body(where_ref, *refs):
        kernel(where_ref, refs[:n], refs[n + len(after) :])

    return pl.pallas_call(
        body,
        grid_spec=pltpu.PrefetchScalarGridSpec(
            num_scalar_prefetch=1,
            grid=(1,),
            in_specs=[pl.BlockSpec(v.shape, lambda i, w, n=v.ndim: (0,) * n) for v in ins] + [ANY] * len(after),
            out_specs=[pl.BlockSpec(s, lambda i, w, n=len(s): (0,) * n) for s, _ in shapes],
        ),
        out_shape=[jax.ShapeDtypeStruct(s, t) for s, t in shapes],
        compiler_params=pltpu.CompilerParams(vmem_limit_bytes=SMALL_LIMIT),
        cost_estimate=BACKWARD,
    )(where, *ins, *after)


class Ending:
    def __init__(self, plan, where, terms, axis, rows, tail, after):
        self.plan, self.where, self.rows, self.tail = plan, where, rows, tail
        self.keep, self.sent = last_combine(terms, axis, rows, after)
        self.got = plan.flip(self.sent, axis)

    def core(self, after):
        rows, tail = self.rows // 2, self.tail
        cols = self.cols = self.keep.shape[1] - tail

        def kernel(where, ins, outs):
            c = where[0]
            for ref, row in ((outs[0], c), (outs[1], 1 - c)):
                at = pl.ds(pl.multiple_of(row * rows, 16), rows)
                ref[:, :cols] = (ins[0][at, :cols].astype(F32) + ins[1][at, :cols].astype(F32)).astype(BF)
            if tail:
                for g in range(2):
                    at = pl.ds(g * rows, rows)
                    piece = ins[0][at, cols:].astype(F32) + ins[1][at, cols:].astype(F32)
                    outs[0][:, cols + g * tail : cols + (g + 1) * tail] = piece.astype(BF)

        shapes = [((rows, cols + 2 * tail), BF), ((rows, cols), BF)]
        self.mine, sent = small_call(kernel, self.where, [self.keep, self.got], shapes, after)
        self.came = self.plan.core(sent)
        return sent

    def rep(self, after):
        rows, cols, tail = self.rows // 2, self.cols, self.tail

        def kernel(where, ins, outs):
            outs[0][:, :cols] = ins[0][:, :cols]
            outs[0][:, cols : 2 * cols] = ins[1][...]
            if tail:
                outs[0][:, 2 * cols :] = ins[0][:, cols:]

        shapes = [((rows, 2 * cols + 2 * tail), BF)]
        v = small_call(kernel, self.where, [self.mine, self.came], shapes, after)[0]
        self.pair = [v, self.plan.flip(v, 0)] if self.plan.ny == 2 else [lax.psum(v, "rep")]
        return v


class ChipEnding:
    def __init__(self, plan, where, term):
        self.plan, self.where = plan, where
        groups = [[2 * chip + c for chip in range(plan.chips)] for c in range(2)]
        self.term = lax.psum_scatter(term, "shard", scatter_dimension=0, axis_index_groups=groups, tiled=True)

    def core(self, after):
        rows, cols = self.term.shape
        part = rows // 4

        def kernel(where, ins, outs):
            c = where[0]
            for ref, row in ((outs[0], c), (outs[1], 1 - c)):
                for k in range(2):
                    at = pl.ds(pl.multiple_of((2 * k + row) * part, 16), part)
                    ref[k * part : (k + 1) * part] = ins[0][at]

        shapes = [((rows // 2, cols), BF)] * 2
        self.mine, sent = small_call(kernel, self.where, [self.term], shapes, after)
        self.came = self.plan.core(sent)
        return sent

    def rep(self, after):
        rows, cols = self.mine.shape

        def kernel(where, ins, outs):
            outs[0][:rows] = ins[0][...]
            outs[0][rows:] = ins[1][...]

        v = small_call(kernel, self.where, [self.mine, self.came], [((2 * rows, cols), BF)], after)[0]
        self.pair = [v, self.plan.flip(v, 0)] if self.plan.ny == 2 else [lax.psum(v, "rep")]
        return v


def place_grads(plan, where, layer, layers, end2, rest, sizes, before, after):
    deep, width, ff, quarters = sizes
    n, ny, halves = plan.shards, plan.ny, quarters // 2
    wide, half_ff = 3 * width // 2, ff // 2
    cols = rest.cols
    fused = bool(rest.tail)
    ins = end2.pair + rest.pair

    def kernel(where_ref, *refs):
        refs_in = refs[: 2 * ny]
        outs = refs[-(4 if fused else 3) :]
        c, y = where_ref[0], where_ref[2]

        def source(p, q, at, size):
            step = (at // 128) * 128
            span = (at + size - step + 127) // 128 * 128
            first = pl.multiple_of(jnp.where(p == c, 0, cols) + step, 128)
            v = refs_in[ny][:, pl.ds(first, span)]
            if ny == 2:
                v = jnp.where(y == q, v, refs_in[ny + 1][:, pl.ds(first, span)])
            return v[:, at - step : at - step + size].astype(F32)

        def core_columns(p, at, size, total, first):
            part = total // ny
            return source(p, at // part, first + at % part, size)

        for k in range(3 * HEADS // 2):
            pieces = [core_columns(p, k * HEAD_DIM, HEAD_DIM, wide, 0) for p in range(2)]
            outs[0][0, :, k * 2 * HEAD_DIM : (k + 1) * 2 * HEAD_DIM] = jnp.concatenate(pieces, axis=1)
        for k in range(n):
            pieces = []
            for p in range(2):
                for h in range(halves):
                    pieces.append(core_columns(p, (h * n + k) * deep, deep, half_ff, wide // ny))
            outs[1][0, :, k * quarters * deep : (k + 1) * quarters * deep] = jnp.concatenate(pieces, axis=1)
        part = width // ny
        for p in range(2):
            at = pl.ds(pl.multiple_of(jnp.where(p == c, 0, halves * deep), 16), halves * deep)
            v = refs_in[0][at].astype(F32)
            if ny == 2:
                v = v + refs_in[1][at].astype(F32)
            outs[2][0, p * halves * deep : (p + 1) * halves * deep] = v
        if fused:
            for q in range(ny):
                v = refs_in[ny][:, 2 * cols :]
                if ny == 2:
                    v = jnp.where(y == q, v, refs_in[ny + 1][:, 2 * cols :])
                outs[3][0, :, q * part : (q + 1) * part] = v.astype(F32)

    shapes = [(deep, 3 * width), (deep, ff), (quarters * deep, width)] + ([(deep, width)] if fused else [])
    in_specs = [pl.BlockSpec(v.shape, lambda i, w: (0, 0)) for v in ins]
    args = list(ins) + list(before or []) + list(after)
    n_before = len(before or [])
    return pl.pallas_call(
        kernel,
        grid_spec=pltpu.PrefetchScalarGridSpec(
            num_scalar_prefetch=1,
            grid=(1,),
            in_specs=in_specs + [ANY] * (n_before + len(after)),
            out_specs=[pl.BlockSpec((1,) + s, lambda i, w: (layer, 0, 0)) for s in shapes],
        ),
        out_shape=[jax.ShapeDtypeStruct((layers,) + s, F32) for s in shapes],
        input_output_aliases={1 + len(ins) + k: k for k in range(n_before)},
        compiler_params=pltpu.CompilerParams(vmem_limit_bytes=LIMIT),
        cost_estimate=BACKWARD,
    )(where, *args)


def pack(plan, where, layer, qkv, proj, fc1, fc2, extra, after):
    deep, width = proj.shape[1:]
    ff, n = fc1.shape[2], plan.shards
    quarters = fc2.shape[1] // deep
    halves = quarters // 2
    each = halves // plan.ny
    ins = [qkv, proj, fc1, fc2] + ([extra] if extra is not None else [])
    total = 4 * width + ff + 2 * each * width + (extra.shape[1] if extra is not None else 0)

    def kernel(where_ref, *refs):
        out = refs[-1]

        def lay(at, pieces):
            held, wide = [], 0
            for p in pieces:
                held.append(p)
                wide += p.shape[1]
                if wide % 128 == 0:
                    out[:, at : at + wide] = held[0] if len(held) == 1 else jnp.concatenate(held, axis=1)
                    at, held, wide = at + wide, [], 0

        for p in range(2):
            cols = [k * 2 * HEAD_DIM + p * HEAD_DIM for k in range(3 * HEADS // 2)]
            lay(p * (3 * width // 2), [refs[0][0, :, k : k + HEAD_DIM] for k in cols])
        out[:, 3 * width : 4 * width] = refs[1][0]
        cols = [s * quarters * deep + k * deep for k in range(quarters) for s in range(n)]
        lay(4 * width, [refs[2][0, :, k : k + deep] for k in cols])
        at = 4 * width + ff
        for p in range(2):
            for k in range(each):
                row = (p * halves + k) * deep + where_ref[3] * deep
                out[:, at : at + width] = refs[3][0, pl.ds(pl.multiple_of(row, 16), deep)]
                at += width
        if extra is not None:
            out[:, at:] = refs[4][...]

    specs = [pl.BlockSpec((1,) + v.shape[1:], lambda i, w: (layer, 0, 0)) for v in ins[:4]]
    specs += [pl.BlockSpec(v.shape, lambda i, w: (0, 0)) for v in ins[4:]]
    return pl.pallas_call(
        kernel,
        grid_spec=pltpu.PrefetchScalarGridSpec(
            num_scalar_prefetch=1,
            grid=(1,),
            in_specs=specs + [ANY] * len(after),
            out_specs=pl.BlockSpec((deep, total), lambda i, w: (0, 0)),
        ),
        out_shape=jax.ShapeDtypeStruct((deep, total), BF),
        compiler_params=pltpu.CompilerParams(vmem_limit_bytes=LIMIT),
        cost_estimate=FORWARD,
    )(where, *ins, *after)


def per_device(
    plan,
    tokens,
    kept,
    attn_gain,
    attn_shift,
    qkv_weight,
    qv_bias,
    proj_weight,
    proj_bias,
    mlp_gain,
    mlp_shift,
    fc1_weight,
    fc1_bias,
    fc2_weight,
    fc2_bias,
    cotangent,
):
    images, slots, width = tokens.shape
    layers = attn_gain.shape[0]
    rows = images * slots
    n = plan.shards
    deep = qkv_weight.shape[1]
    shard = lax.axis_index("shard")
    c, chip, y = lax.rem(shard, 2), shard // 2, lax.axis_index("rep")
    where = jnp.stack([c, chip, y, y if plan.ny == 2 else 0 * y]).astype(jnp.int32)
    ff = fc2_weight.shape[1] * n
    quarters = fc2_weight.shape[1] // deep
    wide, half_width, half_ff = 3 * width // 2, width // 2, ff // 2
    half_heads = HEADS // 2

    small = jnp.concatenate(
        [attn_gain, attn_shift, qv_bias, proj_bias, mlp_gain, mlp_shift, fc1_bias, fc2_bias], axis=1
    )
    sizes = [v.shape[1] for v in (attn_gain, attn_shift, qv_bias, proj_bias, mlp_gain, mlp_shift, fc1_bias, fc2_bias)]
    lines = small.size // 128
    extra = jnp.pad(small.reshape(lines, 128), ((0, deep - lines), (0, 0)))

    halves = quarters // 2
    lead = 4 * width
    block = n * deep
    each = halves // plan.ny

    gathered, done = [], ()
    for layer in range(layers):
        shards = (qkv_weight, proj_weight, fc1_weight, fc2_weight)
        done = (pack(plan, where, layer, *shards, None if layer else extra, done),)
        gathered.append(lax.all_gather(done[0], "shard", axis=0, tiled=True))
    at_fc1, at_fc2 = lead // block, (lead + ff) // block
    mlp_parts = []
    for layer in range(layers):
        found = {"fc1": [(gathered[layer], ("quarter", block, (at_fc1, halves, k))) for k in range(halves)]}
        found["fc2"] = [(gathered[layer], columns(block, at_fc2 + k, each)) for k in range(each)]
        if plan.ny == 2:
            found["sent"], found["came"] = (), ()
            for k in range(1):
                mine = lax.dynamic_slice(
                    gathered[layer], (0, (at_fc2 + c) * block), (block, block)
                )
                found["sent"] += (mine,)
                found["came"] += (plan.flip(mine, 0),)
                found["fc2"].append((found["came"][k], None))
        mlp_parts.append(found)

    def weight_of(layer, name):
        if name == "qkv":
            return [(gathered[layer], columns(wide, 0, 1))]
        if name == "proj":
            return [(gathered[layer], ("heads", width, 3))]
        return mlp_parts[layer][name]

    every = gathered[0].reshape(n, deep, -1)[:, :lines, lead + ff + 2 * each * block :]
    every = every.reshape(n, layers, small.shape[1]).astype(F32)
    vecs = []
    for layer in range(layers):
        at, d = 0, {}
        for name, size in zip(SMALL, sizes):
            d[name] = every[:, layer, at : at + size].reshape(1, n * size)
            at += size
        q = d["qvb"].reshape(2 * half_heads, 2, HEAD_DIM)
        q = pick(c, q[:, 0], q[:, 1]).reshape(2, half_width)
        d["qvb_c"] = jnp.stack([q[0], jnp.zeros_like(q[0]), q[1]]).reshape(1, wide)
        f = d["f1b"].reshape(n, 2, halves, deep).transpose(1, 2, 0, 3).reshape(2, halves, block)
        f = pick(c, f[0], f[1])
        if plan.ny == 2:
            f = pick(y, f, f[::-1])
        d["f1b_c"] = f.reshape(1, half_ff)
        vecs.append(d)

    kept_oth = plan.core(kept)
    state = tokens.astype(F32).reshape(rows, width)
    live = lax.broadcasted_iota(jnp.int32, (images, slots), 1) < BUFFER + kept[:, None]
    grad = jnp.where(live[:, :, None], cotangent.astype(F32), 0.0).reshape(rows, width)
    low_own = grad.astype(BF)
    low_oth = plan.core(low_own)
    first_own = norm_rows(state, vecs[0]["ag"], vecs[0]["as"]).astype(BF)

    f32_rows, low_rows = ("rows", (rows, width), F32), ("rows", (rows, width), BF)
    wide_rows, ff_rows = ("rows", (rows, wide), BF), ("rows", (rows, half_ff), BF)
    att_outs = [("image", (images, half_heads, slots, slots), BF), ("rows", (rows, half_width), BF)]
    full_sums = ("full", (8, width), F32)

    def call(body, layer, own, names, blocked, whole, outs, after=(), cost=None):
        chosen = [weight_of(layer, name) for name in names]
        k = kept if own else kept_oth
        return row_call(body, where, k, chosen, blocked, whole, outs, images, slots, after, cost or (BACKWARD if after else FORWARD))

    saved = []
    for layer in range(layers):
        v = vecs[layer]
        first_oth = plan.core(first_own)
        sent, came = mlp_parts[layer].get("sent", ()), mlp_parts[layer].get("came", ())
        proj_oth = call(qkv_body, layer, 0, ["qkv"], [first_oth], [v["qvb_c"]], [wide_rows], sent, FORWARD)[0]
        probs_oth, att_oth, part = call(attend_other, layer, 0, ["proj"], [proj_oth], [], att_outs + [f32_rows])
        part = plan.core(part)
        proj_own = call(qkv_body, layer, 1, ["qkv"], [first_own], [v["qvb_c"]], [wide_rows])[0]
        probs_own, att_own, middle, second_own = call(
            attend_own, layer, 1, ["proj"], [proj_own, part, state], [v["pb"], v["mg"], v["ms"]], att_outs + [f32_rows, low_rows])
        second_oth = plan.core(second_own)
        hid_oth, slope_oth = call(up_body, layer, 0, ["fc1"], [second_oth], [v["f1b_c"]], [ff_rows] * 2)
        if layer + 1 < layers:
            part = call(down_other, layer, 0, ["fc2"], [hid_oth], [], [f32_rows])[0]
            part = plan.core(part)
        hid_own, slope_own = call(up_body, layer, 1, ["fc1"], [second_own], [v["f1b_c"]], [ff_rows] * 2)
        saved.append(
            dict(
                state=state,
                first=(first_own, first_oth),
                proj=(proj_own, proj_oth),
                probs=(probs_own, probs_oth),
                att=(att_own, att_oth),
                middle=middle,
                second=(second_own, second_oth),
                hid=(hid_own, hid_oth),
                slope=(slope_own, slope_oth),
            )
        )
        if layer + 1 < layers:
            w = vecs[layer + 1]
            state, first_own = call(
                down_own, layer, 1, ["fc2"], [hid_own, part, middle], [v["f2b"], w["ag"], w["as"]], [f32_rows, low_rows])

    axes = list(range(1 if plan.ny == 1 else 0, plan.bits + 1))
    last_axis, z_axis, x_axis = 1, plan.bits - 1, plan.bits
    y_axis = 0 if plan.ny == 2 else 2
    orders_f1 = [[y_axis, x_axis, z_axis]] * layers
    orders_q = [[[z_axis, y_axis, x_axis], [y_axis, z_axis, x_axis]]] + [[[x_axis, z_axis, y_axis]]] * (layers - 1)
    own_rows = 2 * deep
    tail = width // plan.ny * HEAD_DIM // own_rows
    fused = n == HEADS
    tail = tail if fused else 0
    big = [[None] * 4 for _ in range(layers)]
    sums = [None] * layers
    f2b_sum = jnp.sum(low_own.astype(F32), axis=0, keepdims=True)

    def end_rest(layer, prev):
        group = terms["q", layer] + [terms["f1", layer]]
        ends["rest", layer] = Ending(plan, where, group, last_axis, own_rows, tail, prev)
        return (ends["rest", layer].sent,)

    def place(layer, before, prev):
        return place_grads(
            plan, where, layer, layers, ends["f2", layer], ends["rest", layer], (deep, width, ff, quarters), before, prev
        )

    ends = {}
    prev = (hid_own,) + mlp_parts[layers - 1].get("came", ())
    terms = {}
    for layer in reversed(range(layers)):
        v, s = vecs[layer], saved[layer]
        top = layer == layers - 1

        def grad_fc2(prev):
            term = chip_grad(plan, where, s["hid"], (low_own, low_oth), 2, prev)
            ends["f2", layer] = ChipEnding(plan, where, term)
            return (term,)

        if top:
            prev = grad_fc2(prev)
        pre_oth, part = call(
            mlp_back_other, layer, 0, ["fc2", "fc1"], [low_oth, s["slope"][1]], [], [ff_rows, f32_rows], prev
        )
        part = plan.core(part)
        prev = (pre_oth,)
        if top:
            last_part = call(down_other, layer, 0, ["fc2"], [s["hid"][1]], [], [f32_rows], prev)[0]
            prev = (last_part,)
            last_part = plan.core(last_part)
        else:
            prev = grad_fc2(prev)
            prev += (terms["f1", layer + 1].step(prev[:1]),)
        pre_own, mid_grad, branch_own, sum1 = call(
            mlp_back_own,
            layer,
            1,
            ["fc2", "fc1"],
            [low_own, s["slope"][0], part, s["middle"], grad],
            [v["mg"]],
            [ff_rows, f32_rows, low_rows, full_sums],
            prev,
        )
        branch_oth = plan.core(branch_own)
        prev = (branch_own,)
        if not top:
            prev += (terms["q", layer + 1][0].step(prev),)
        res1 = weight_grad(
            plan, where, s["second"], (pre_own, pre_oth), 1, orders_f1[layer][0], sums=True, extra=tail, relative=True, after=prev
        )
        prev = tuple(res1[:1]) + ((last_part,) if top else ())
        if not top:
            prev += (terms["q", layer + 1][0].step(prev[:1]),)
            prev += (terms["f1", layer + 1].step(prev[:1]),)
            prev += (ends["f2", layer + 1].core(prev[:1]),)
        dproj_oth, part = call(
            attend_back_other,
            layer,
            0,
            ["proj", "qkv"],
            [branch_oth, s["proj"][1], s["probs"][1]],
            [],
            [wide_rows, f32_rows],
            prev,
        )
        part = plan.core(part)
        prev = (dproj_oth,)
        keep, send = res1[:2]
        if fused:
            keep, send = proj_grad_into(
                plan, where, s["att"], (branch_own, branch_oth), orders_f1[layer][0], keep, send, prev
            )
        else:
            term = t_dot(s["att"][0], branch_own) + t_dot(s["att"][1], branch_oth)
            term = term.astype(BF).reshape(half_heads, HEAD_DIM, width)
            none = jnp.zeros_like(term)
            term = jnp.stack([pick(c, term, none), pick(c, none, term)], axis=1).reshape(width, width)
            term = lax.psum_scatter(term, "shard", scatter_dimension=0, tiled=True)
            big[layer][1] = lax.psum(term, "rep").astype(F32)
        terms["f1", layer] = Term(plan, keep, send, orders_f1[layer])
        prev = (send,)
        if not top:
            prev += (ends["f2", layer + 1].rep(prev[:1]),)
        dproj_own, grad, low_own, sum2 = call(
            attend_back_own,
            layer,
            1,
            ["proj", "qkv"],
            [branch_own, s["proj"][0], s["probs"][0], part, s["state"], mid_grad],
            [v["ag"]],
            [wide_rows, f32_rows, low_rows, full_sums],
            prev,
        )
        prev = (dproj_own,)
        if layer:
            low_oth = plan.core(low_own)
        if not top:
            prev += end_rest(layer + 1, prev[:1])
            prev += (ends["f2", layer].core(prev[:1]),)
        terms["q", layer], q_sums = [], []
        of = len(orders_q[layer])
        for k, order in enumerate(orders_q[layer]):
            resq = weight_grad(
                plan, where, s["first"], (dproj_own, dproj_oth), 1, order[0], sums=True, window=(k, of), after=prev
            )
            terms["q", layer].append(Term(plan, *resq[:2], order))
            q_sums.append(resq[2].reshape(plan.ny, -1))
            prev = (resq[1],) + (() if top else (ends["f2", layer].came,))
        q = jnp.concatenate(q_sums, axis=1).reshape(3, half_heads, 1, HEAD_DIM)
        q = jnp.concatenate([q[:1], q[2:]])
        none = jnp.zeros_like(q)
        q = jnp.concatenate([pick(c, q, none), pick(c, none, q)], axis=2)
        f = res1[2].reshape(halves, block)
        if plan.ny == 2:
            f = pick(y, f, f[::-1])
        none = jnp.zeros_like(f)
        f = jnp.concatenate([pick(c, f, none), pick(c, none, f)], axis=0)
        f = f.reshape(quarters, n, deep).swapaxes(0, 1)
        full = {"ag": sum2[0], "as": sum2[1], "qvb": q, "pb": sum1[2], "mg": sum1[0], "ms": sum1[1], "f1b": f, "f2b": f2b_sum}
        f2b_sum = sum2[2]
        vec = jnp.concatenate([full[name].reshape(n, -1) for name in SMALL], axis=1)
        sums[layer] = vec

    vec = jnp.concatenate(sums, axis=0).reshape(layers, n, -1)
    got_vec = plan.core(vec)
    vec_axes = list(axes)

    def step_vec(prev):
        nonlocal vec, got_vec

        def kernel(where, ins, outs):
            outs[0][...] = ins[0][...] + ins[1][...]

        vec = small_call(kernel, where, [vec, got_vec], [(vec.shape, F32)], prev)[0]
        got_vec = plan.flip(vec, vec_axes.pop(0)) if vec_axes else None
        return (vec,)

    prev += (terms["f1", 0].step(prev[:1]),)
    prev += (ends["rest", 1].core(prev[:1]),)
    w = layers - 1
    mixed = call(
        down_last, w, 1, ["fc2"], [saved[w]["hid"][0], last_part, saved[w]["middle"]], [vecs[w]["f2b"]], [low_rows], prev
    )[0]
    qa, qb = terms["q", 0]
    prev = (qa.step((mixed, ends["rest", 1].came)),)
    prev = (qb.step(prev),)
    prev = step_vec(prev)
    prev = (qa.step(prev),)
    prev = (terms["f1", 0].step(prev),)
    prev = (qb.step(prev),)
    prev = step_vec(prev)
    prev = end_rest(0, prev)
    prev = (ends["rest", 1].rep(prev),)
    prev = (ends["f2", 0].rep(prev),)
    prev = step_vec(prev)
    placed = place(1, None, prev)
    prev = (placed[0],)
    prev = (ends["rest", 0].core(prev + tuple(ends["f2", 0].pair[1:])),)
    prev = step_vec(prev)
    prev = (ends["rest", 0].rep(prev),)
    while got_vec is not None:
        prev = step_vec(prev)
    placed = place(0, placed, prev)
    if plan.ny == 1:
        vec = lax.psum(vec, "rep")
    vec = lax.dynamic_slice_in_dim(vec, shard, 1, axis=1)[:, 0]
    out, at = {}, 0
    for name, size in zip(SMALL, sizes):
        out[name] = vec[:, at : at + size]
        at += size
    qkv_g, fc1_g, fc2_g = placed[:3]
    proj_g = placed[3] if fused else jnp.stack([big[layer][1] for layer in range(layers)])
    return (
        mixed.reshape(images, slots, width),
        grad.reshape(images, slots, width),
        out["ag"],
        out["as"],
        qkv_g,
        out["qvb"],
        proj_g,
        out["pb"],
        out["mg"],
        out["ms"],
        fc1_g,
        out["f1b"],
        fc2_g,
        out["f2b"],
    )


def solution(mesh):
    rows = P(("shard", "rep"), None, None)
    vec = P(None, "shard")
    mat = P(None, "shard", None)
    return jax.shard_map(
        partial(per_device, Plan(mesh)),
        mesh=mesh,
        in_specs=(rows, P(("shard", "rep")), vec, vec, mat, vec, mat, vec, vec, vec, mat, vec, mat, vec, rows),
        out_specs=(rows, rows, vec, vec, mat, vec, mat, vec, vec, vec, mat, vec, mat, vec),
        check_vma=False,
    )
```

```python
from functools import partial

import jax
import jax.numpy as jnp
from jax import lax
from jax.experimental import pallas as pl
from jax.experimental.pallas import tpu as pltpu
from jax.sharding import PartitionSpec as P

HEADS = 16
HEAD_DIM = 64
BUFFER = 64
EPS = 1e-06
SCALE = HEAD_DIM ** (-0.5)
AX = ("shard", "rep")
BF = jnp.bfloat16
F32 = jnp.float32
LIMIT = 60 * 2**20
SMALL_LIMIT = 16 * 2**20
ONCE = pl.Buffered(1)
ANY = pl.BlockSpec(memory_space=pl.ANY)
FORWARD = pl.CostEstimate(flops=10**7, bytes_accessed=0, transcendentals=0)
BACKWARD = pl.CostEstimate(flops=10**9 * 30, bytes_accessed=0, transcendentals=0)
SMALL = ("ag", "as", "qvb", "pb", "mg", "ms", "f1b", "f2b")


class Plan:
    def __init__(self, mesh):
        self.shards = mesh.shape["shard"]
        self.rep = mesh.shape["rep"]
        self.chips = self.shards // 2
        self.ny = 2 if self.rep == 2 else 1
        self.bits = self.chips.bit_length() - 1

    def swap(self, v, flip_shard, flip_rep=0):
        pairs = []
        for s in range(self.shards):
            for y in range(self.rep):
                pairs.append((s * self.rep + y, (s ^ flip_shard) * self.rep + (y ^ flip_rep)))
        return lax.ppermute(v, AX, pairs)

    def core(self, v):
        return self.swap(v, 1)

    def flip(self, v, axis):
        if axis == 0:
            return self.swap(v, 0, 1)
        return self.swap(v, 2 << (self.bits - axis))


def dot(x, w):
    return lax.dot_general(x, w, (((1,), (0,)), ((), ())), preferred_element_type=F32)


def dot_t(x, w):
    return lax.dot_general(x, w, (((1,), (1,)), ((), ())), preferred_element_type=F32)


def t_dot(x, w):
    return lax.dot_general(x, w, (((0,), (0,)), ((), ())), preferred_element_type=F32)


def columns(width, first, stride):
    return ("columns", width, (first, stride))


class Held:
    def __init__(self, ref, copy):
        self.ref, self.copy, self.shape, self.waited = ref, copy, ref.shape, False

    def ready(self):
        if not self.waited:
            self.waited = True

            @pl.when(pl.program_id(0) == 0)
            def _():
                self.copy.wait()

        return self.ref


def row_call(body, where, kept, weights, blocked, whole, outs, images, slots, after=(), cost=FORWARD):
    in_specs, args, held_shapes, sources = [], [], [], []
    for v, pick_of in (part for w in weights for part in w):
        in_specs.append(ANY)
        if pick_of is None:
            args.append(v)
            held_shapes.append(v.shape)
            sources.append(lambda ref, w: ref)
            continue
        kind, width, first = pick_of
        if kind == "heads":
            args.append(v.reshape(HEADS // 2, 2, HEAD_DIM, v.shape[1]))
            held_shapes.append((HEADS // 2, HEAD_DIM, width))
            sources.append(lambda ref, w, f=first * width, n=width: ref.at[:, w[0], :, pl.ds(f, n)])
            continue
        args.append(v)
        held_shapes.append((v.shape[0], width))
        at, stride, part = first if kind == "quarter" else first + (None,)

        def source(ref, w, at=at, stride=stride, part=part, width=width):
            column = at + stride * w[0]
            if part is not None:
                column = column + jnp.bitwise_xor(part, w[3])
            return ref.at[:, pl.ds(pl.multiple_of(column * width, 128), width)]

        sources.append(source)
    for v in blocked:
        if v.ndim == 2:
            in_specs.append(pl.BlockSpec((slots, v.shape[1]), lambda i, *_: (i, 0)))
        else:
            in_specs.append(pl.BlockSpec((1,) + v.shape[1:], lambda i, *_, n=v.ndim: (i,) + (0,) * (n - 1)))
        args.append(v)
    for v in whole:
        in_specs.append(pl.BlockSpec(v.shape, lambda i, *_, n=v.ndim: (0,) * n))
        args.append(v)
    out_specs, out_shape = [], []
    for kind, shape, dtype in outs:
        out_shape.append(jax.ShapeDtypeStruct(shape, dtype))
        if kind == "rows":
            out_specs.append(pl.BlockSpec((slots, shape[1]), lambda i, *_: (i, 0)))
        elif kind == "image":
            out_specs.append(pl.BlockSpec((1,) + shape[1:], lambda i, *_, n=len(shape): (i,) + (0,) * (n - 1)))
        else:
            out_specs.append(pl.BlockSpec(shape, lambda i, *_, n=len(shape): (0,) * n))
    n_p, n_b, n_in = sum(len(w) for w in weights), len(blocked), len(args)
    in_specs += [ANY] * len(after)
    args += list(after)
    n_out = len(outs)

    def kernel(where_ref, kept_ref, *refs):
        ins, rest = refs[:n_in], refs[n_in + len(after) :]
        res, parts, sems = rest[:n_out], rest[n_out:-1], rest[-1]
        copies = [
            pltpu.make_async_copy(sources[k](ins[k], where_ref), parts[k], sems.at[k]) for k in range(n_p)
        ]

        @pl.when(pl.program_id(0) == 0)
        def _():
            for c in copies:
                c.start()

        held, at = [], 0
        for w in weights:
            held.append([Held(parts[k], copies[k]) for k in range(at, at + len(w))])
            at += len(w)
        body(kept_ref, held, ins[n_p : n_p + n_b], ins[n_p + n_b : n_in], res)
        for h in (h for w in held for h in w):
            h.ready()

    return pl.pallas_call(
        kernel,
        grid_spec=pltpu.PrefetchScalarGridSpec(
            num_scalar_prefetch=2,
            grid=(images,),
            in_specs=in_specs,
            out_specs=out_specs,
            scratch_shapes=[pltpu.VMEM(shape, BF) for shape in held_shapes] + [pltpu.SemaphoreType.DMA((n_p,))],
        ),
        out_shape=out_shape,
        compiler_params=pltpu.CompilerParams(vmem_limit_bytes=LIMIT),
        cost_estimate=cost,
    )(where, kept, *args)


def normed_of(rows):
    width = rows.shape[-1]
    mean = jnp.sum(rows, axis=-1, keepdims=True) * (1.0 / width)
    centered = rows - mean
    spread = jnp.sum(centered * centered, axis=-1, keepdims=True) * (1.0 / width)
    factor = lax.rsqrt(spread + EPS)
    return centered * factor, factor


def norm_rows(rows, gain, shift):
    return normed_of(rows)[0] * gain + shift


def norm_back(dz, rows, gain):
    normed, factor = normed_of(rows)
    width = rows.shape[-1]
    prod = dz * normed
    dn = dz * gain
    m1 = jnp.sum(dn, axis=-1, keepdims=True) * (1.0 / width)
    m2 = jnp.sum(dn * normed, axis=-1, keepdims=True) * (1.0 / width)
    back = factor * (dn - m1 - normed * m2)
    return back, jnp.sum(prod, axis=0, keepdims=True), jnp.sum(dz, axis=0, keepdims=True)


def chunks(total, size):
    size = min(size, total)
    return [(k, size) for k in range(0, total, size)]


def qkv_body(kept, w, blocked, whole, outs):
    x = blocked[0][...]
    for k, n in chunks(outs[0].shape[1], 512):
        cols = pl.ds(k, n)
        outs[0][:, cols] = (dot(x, w[0][0].ready()[:, cols]) + whole[0][:, cols]).astype(BF)


def heads_of(ref):
    return ref.ready()[...].reshape(-1, ref.shape[-1])


def pairs_dot(x_ref, parts):
    total, at = None, 0
    for w_ref in parts:
        term = dot(x_ref[:, at : at + w_ref.shape[0]], w_ref.ready()[...])
        total = term if total is None else total + term
        at += w_ref.shape[0]
    return total


def attend(kept, proj_ref, probs_ref, att_ref):
    slots, third = proj_ref.shape[0], proj_ref.shape[1] // 3
    bound = BUFFER + kept[pl.program_id(0)]
    alive = lax.broadcasted_iota(jnp.int32, (slots, slots), 1) < bound
    outs = []
    for h in range(third // HEAD_DIM):
        lo = h * HEAD_DIM
        q = proj_ref[:, lo : lo + HEAD_DIM]
        k = proj_ref[:, third + lo : third + lo + HEAD_DIM]
        v = proj_ref[:, 2 * third + lo : 2 * third + lo + HEAD_DIM]
        s = jnp.where(alive, dot_t(q, k) * SCALE, -1e30)
        e = jnp.exp(s - jnp.max(s, axis=-1, keepdims=True))
        p = (e * (1.0 / jnp.sum(e, axis=-1, keepdims=True))).astype(BF)
        probs_ref[0, h] = p
        outs.append(dot(p, v).astype(BF))
        if h % 2:
            att_ref[:, lo - HEAD_DIM : lo + HEAD_DIM] = jnp.concatenate(outs, axis=1)
            outs = []


def attend_other(kept, w, blocked, whole, outs):
    attend(kept, blocked[0], outs[0], outs[1])
    outs[2][...] = dot(outs[1][...], heads_of(w[0][0]))


def attend_own(kept, w, blocked, whole, outs):
    attend(kept, blocked[0], outs[0], outs[1])
    middle = blocked[2][...] + (dot(outs[1][...], heads_of(w[0][0])) + blocked[1][...]) + whole[0][...]
    outs[2][...] = middle
    outs[3][...] = norm_rows(middle, whole[1][...], whole[2][...]).astype(BF)


def up_body(kept, w, blocked, whole, outs):
    x = blocked[0][...]
    for k, n in chunks(outs[0].shape[1], 256):
        cols = pl.ds(k, n)
        held = w[0][k // w[0][0].shape[1]]
        pre = dot(x, held.ready()[:, pl.ds(k % held.shape[1], n)]) + whole[0][:, cols]
        phi = 0.5 + 0.5 * lax.erf(pre * (2.0**-0.5))
        dens = jnp.exp(-0.5 * (pre * pre)) * 0.3989422804014327
        outs[0][:, cols] = (pre * phi).astype(BF)
        outs[1][:, cols] = (phi + pre * dens).astype(BF)


def down_other(kept, w, blocked, whole, outs):
    outs[0][...] = pairs_dot(blocked[0], w[0])


def down_own(kept, w, blocked, whole, outs):
    state = blocked[2][...] + (pairs_dot(blocked[0], w[0]) + blocked[1][...]) + whole[0][...]
    outs[0][...] = state
    outs[1][...] = norm_rows(state, whole[1][...], whole[2][...]).astype(BF)


def down_last(kept, w, blocked, whole, outs):
    state = blocked[2][...] + (pairs_dot(blocked[0], w[0]) + blocked[1][...]) + whole[0][...]
    alive = lax.broadcasted_iota(jnp.int32, state.shape, 0) < BUFFER + kept[pl.program_id(0)]
    outs[0][...] = jnp.where(alive, state, 0.0).astype(BF)


def mlp_back(w, blocked, outs):
    low = blocked[0][...]
    for k, n in chunks(outs[0].shape[1], 512):
        cols = pl.ds(k, n)
        held, first = w[0][0], 0
        for part in w[0][1:]:
            if k >= first + held.shape[0]:
                first += held.shape[0]
                held = part
        t = dot_t(low, held.ready()[pl.ds(k - first, n), :])
        outs[0][:, cols] = (t * blocked[1][:, cols].astype(F32)).astype(BF)
    total, at = None, 0
    for held in w[1]:
        term = dot_t(outs[0][:, at : at + held.shape[1]], held.ready()[...])
        total = term if total is None else total + term
        at += held.shape[1]
    return total


def mlp_back_other(kept, w, blocked, whole, outs):
    outs[1][...] = mlp_back(w, blocked, outs)


def add_sums(ref, rows):
    sums = jnp.concatenate(rows + [jnp.zeros((8 - len(rows), rows[0].shape[1]), F32)], axis=0)

    @pl.when(pl.program_id(0) == 0)
    def _():
        ref[...] = sums

    @pl.when(pl.program_id(0) != 0)
    def _():
        ref[...] += sums


def mlp_back_own(kept, w, blocked, whole, outs):
    dz = mlp_back(w, blocked, outs) + blocked[2][...]
    back, gain, shift = norm_back(dz, blocked[3][...], whole[0][...])
    grad = blocked[4][...] + back
    low = grad.astype(BF)
    outs[1][...] = grad
    outs[2][...] = low
    add_sums(outs[3], [gain, shift, jnp.sum(low.astype(F32), axis=0, keepdims=True)])


def attend_back(w, blocked, outs):
    branch, proj_ref, probs_ref = blocked[0], blocked[1], blocked[2]
    third = proj_ref.shape[1] // 3
    datt = dot_t(branch[...], heads_of(w[0][0])).astype(BF)
    pairs = [[], [], []]
    for h in range(third // HEAD_DIM):
        lo = h * HEAD_DIM
        q = proj_ref[:, lo : lo + HEAD_DIM]
        k = proj_ref[:, third + lo : third + lo + HEAD_DIM]
        v = proj_ref[:, 2 * third + lo : 2 * third + lo + HEAD_DIM]
        da = datt[:, lo : lo + HEAD_DIM]
        p = probs_ref[0, h]
        dp = dot_t(da, v)
        pf = p.astype(F32)
        ds = (pf * (dp - jnp.sum(pf * dp, axis=-1, keepdims=True))).astype(BF)
        pairs[0].append((dot(ds, k) * SCALE).astype(BF))
        pairs[1].append((t_dot(ds, q) * SCALE).astype(BF))
        pairs[2].append(t_dot(p, da).astype(BF))
        if h % 2:
            for j in range(3):
                at = j * third + lo - HEAD_DIM
                outs[0][:, at : at + 2 * HEAD_DIM] = jnp.concatenate(pairs[j], axis=1)
            pairs = [[], [], []]
    return dot_t(outs[0][...], w[1][0].ready()[...])


def attend_back_other(kept, w, blocked, whole, outs):
    outs[1][...] = attend_back(w, blocked, outs)


def attend_back_own(kept, w, blocked, whole, outs):
    dz = attend_back(w, blocked, outs) + blocked[3][...]
    back, gain, shift = norm_back(dz, blocked[4][...], whole[0][...])
    grad = blocked[5][...] + back
    outs[1][...] = grad
    low = grad.astype(BF)
    outs[2][...] = low
    add_sums(outs[3], [gain, shift, jnp.sum(low.astype(F32), axis=0, keepdims=True)])


def weight_grad(plan, where, xs, ys, groups, first, sums=False, extra=0, relative=False, window=(0, 1), after=()):
    depth, n_x = xs[0].shape
    cols = ys[0].shape[1]
    ny, chips, bits = plan.ny, plan.chips, plan.bits
    half = cols // ny
    size = half // window[1]
    chunk = size if size <= 768 else 512
    steps = size // chunk
    rows = n_x // chips
    part = rows // groups
    dims = [ny] + [2] * bits
    dims[first] = 1
    block = [1] + dims[1:] + [rows, chunk]
    shape = dims + [rows, size + extra]
    n_after = len(after)

    def kernel(where_ref, xo, xt, yo, yt, *rest):
        rest = rest[n_after:]
        keep, send = rest[0], rest[1]
        flip, acc = rest[-2], rest[-1]
        step = pl.program_id(0)

        @pl.when(step == 0)
        def _():
            flip[:, :depth] = xo[...].T
            flip[:, depth:] = xt[...].T

        acc[...] = dot(flip[:, :depth], yo[...]) + dot(flip[:, depth:], yt[...])
        if sums:
            rest[2][...] = jnp.sum(yo[...].astype(F32), axis=0, keepdims=True) + jnp.sum(
                yt[...].astype(F32), axis=0, keepdims=True
            )

        def put(ref, r):
            at = [0]
            for k in range(1, bits + 1):
                at.append((r >> (bits - k)) & 1 if k != first else 0)
            chip = jnp.bitwise_xor(where_ref[1], r)
            for g in range(groups):
                start = pl.multiple_of(g * part * chips + chip * part, 16)
                place = g
                if groups == 2 and ny == 2:
                    place = jnp.bitwise_xor(g, where_ref[2])
                place = pl.multiple_of(place * part, 16)
                ref[tuple(at) + (pl.ds(place, part),)] = acc[pl.ds(start, part)].astype(BF)

        if first:
            for r in range(chips):
                put(send if (r >> (bits - first)) & 1 else keep, r)
        else:

            @pl.when(step < steps)
            def _():
                for r in range(chips):
                    put(keep, r)

            @pl.when(step >= steps)
            def _():
                for r in range(chips):
                    put(send, r)

    per_rep = half // chunk

    def column(i, w):
        own = w[2] if ny == 2 and not relative else 0
        return jnp.bitwise_xor(i // steps, own) * per_rep + window[0] * steps + i % steps

    zeros = (0,) * (bits + 1)
    x_spec = pl.BlockSpec((depth, n_x), lambda i, w: (0, 0), pipeline_mode=ONCE)
    y_spec = pl.BlockSpec((depth, chunk), lambda i, w: (0, column(i, w)))
    if first:
        specs = [pl.BlockSpec(block, lambda i, w: (i // steps,) + zeros + (i % steps,))] * 2
    else:
        specs = [
            pl.BlockSpec(block, lambda i, w: (0,) + zeros + (jnp.minimum(i, steps - 1),)),
            pl.BlockSpec(block, lambda i, w: (0,) + zeros + (jnp.maximum(i - steps, 0),)),
        ]
    out_shape = [jax.ShapeDtypeStruct(shape, BF)] * 2
    if sums:
        own = (lambda w: w[2]) if ny == 2 and not relative else (lambda w: 0)
        specs = specs + [
            pl.BlockSpec((1, chunk), lambda i, w: (0, jnp.bitwise_xor(i // steps, own(w)) * steps + i % steps))
        ]
        out_shape = out_shape + [jax.ShapeDtypeStruct((1, size * ny), F32)]
    return pl.pallas_call(
        kernel,
        grid_spec=pltpu.PrefetchScalarGridSpec(
            num_scalar_prefetch=1,
            grid=(ny * steps,),
            in_specs=[x_spec, x_spec, y_spec, y_spec] + [ANY] * n_after,
            out_specs=specs,
            scratch_shapes=[pltpu.VMEM((n_x, 2 * depth), BF), pltpu.VMEM((n_x, chunk), F32)],
        ),
        out_shape=out_shape,
        compiler_params=pltpu.CompilerParams(vmem_limit_bytes=LIMIT),
        cost_estimate=BACKWARD,
    )(where, *xs, *ys, *after)


def chip_grad(plan, where, xs, ys, groups, after=()):
    depth, n_x = xs[0].shape
    cols = ys[0].shape[1]
    chips = plan.chips
    chunk = min(cols, 512)
    rows = n_x // chips
    part = rows // groups
    n_after = len(after)

    def kernel(where_ref, xo, xt, yo, yt, *rest):
        out, flip, acc = rest[n_after:]

        @pl.when(pl.program_id(0) == 0)
        def _():
            flip[:, :depth] = xo[...].T
            flip[:, depth:] = xt[...].T

        acc[...] = dot(flip[:, :depth], yo[...]) + dot(flip[:, depth:], yt[...])
        for g in range(groups):
            place = jnp.bitwise_xor(g, where_ref[3]) * part
            for chip in range(chips):
                at = pl.ds(pl.multiple_of(place + chip * rows, 16), part)
                first = (g * chips + chip) * part
                out[at, :] = acc[first : first + part].astype(BF)

    x_spec = pl.BlockSpec((depth, n_x), lambda i, w: (0, 0), pipeline_mode=ONCE)
    y_spec = pl.BlockSpec((depth, chunk), lambda i, w: (0, i))
    return pl.pallas_call(
        kernel,
        grid_spec=pltpu.PrefetchScalarGridSpec(
            num_scalar_prefetch=1,
            grid=(cols // chunk,),
            in_specs=[x_spec, x_spec, y_spec, y_spec] + [ANY] * n_after,
            out_specs=pl.BlockSpec((n_x, chunk), lambda i, w: (0, i)),
            scratch_shapes=[pltpu.VMEM((n_x, 2 * depth), BF), pltpu.VMEM((n_x, chunk), F32)],
        ),
        out_shape=jax.ShapeDtypeStruct((n_x, cols), BF),
        compiler_params=pltpu.CompilerParams(vmem_limit_bytes=LIMIT),
        cost_estimate=BACKWARD,
    )(where, *xs, *ys, *after)


def proj_grad_into(plan, where, xs, ys, first, keep, send, after=()):
    depth, n_x = xs[0].shape
    cols = ys[0].shape[1]
    ny, chips, bits = plan.ny, plan.chips, plan.bits
    half = cols // ny
    part = n_x // chips
    width = half * part // keep.shape[-2]
    stacked = half // width
    at_col = keep.shape[-1] // width - 1
    block = [1] + list(keep.shape[1:-1]) + [width]

    n_after = len(after)

    def kernel(where_ref, xo, xt, yo, yt, k_in, s_in, *rest):
        keep_ref, send_ref, acc = rest[n_after:]
        acc[...] = t_dot(xo[...], yo[...]) + t_dot(xt[...], yt[...])

        def put(ref, r):
            at = [0]
            for k in range(1, bits + 1):
                at.append((r >> (bits - k)) & 1 if k != first else 0)
            start = pl.multiple_of(jnp.bitwise_xor(where_ref[1], r) * part, 16)
            for g in range(stacked):
                piece = acc[pl.ds(start, part), g * width : (g + 1) * width]
                ref[tuple(at) + (pl.ds(g * part, part),)] = piece.astype(BF)

        if first:
            for r in range(chips):
                put(send_ref if (r >> (bits - first)) & 1 else keep_ref, r)
        else:

            @pl.when(pl.program_id(0) == 0)
            def _():
                for r in range(chips):
                    put(keep_ref, r)

            @pl.when(pl.program_id(0) != 0)
            def _():
                for r in range(chips):
                    put(send_ref, r)

    zeros = (0,) * (bits + 1)
    own = (lambda w: w[2]) if ny == 2 else (lambda w: 0)
    x_spec = pl.BlockSpec((depth, n_x), lambda i, w: (0, 0), pipeline_mode=ONCE)
    y_spec = pl.BlockSpec((depth, half), lambda i, w: (0, jnp.bitwise_xor(i, own(w))))
    spec = pl.BlockSpec(block, lambda i, w: (i if first else 0,) + zeros + (at_col,))
    return pl.pallas_call(
        kernel,
        grid_spec=pltpu.PrefetchScalarGridSpec(
            num_scalar_prefetch=1,
            grid=(ny,),
            in_specs=[x_spec, x_spec, y_spec, y_spec, ANY, ANY] + [ANY] * n_after,
            out_specs=[spec, spec],
            scratch_shapes=[pltpu.VMEM((n_x, half), F32)],
        ),
        out_shape=[jax.ShapeDtypeStruct(keep.shape, BF)] * 2,
        input_output_aliases={5: 0, 6: 1},
        compiler_params=pltpu.CompilerParams(vmem_limit_bytes=LIMIT),
        cost_estimate=BACKWARD,
    )(where, *xs, *ys, keep, send, *after)


class Term:
    def __init__(self, plan, keep, send, order):
        self.plan, self.keep, self.order = plan, keep, list(order)
        self.got = plan.flip(send, self.order.pop(0))

    def step(self, after):
        axis = self.order.pop(0)
        self.keep, send = combine(self.keep, self.got, axis, after)
        self.got = self.plan.flip(send, axis)
        return send


def combine(keep, got, axis, after):
    shape = keep.shape
    rows, cols = shape[-2:]
    cuts = 2
    block = shape[:-2] + (rows // cuts, cols)
    out = shape[:axis] + (1,) + shape[axis + 1 :]
    out_block = out[:-2] + (rows // cuts, cols)
    lead = len(shape) - 2

    def kernel(k, g, *rest):
        stay, go = rest[-2:]
        for side, ref in ((0, stay), (1, go)):
            at = tuple(pl.ds(side, 1) if d == axis else slice(None) for d in range(lead))
            ref[...] = (k[at].astype(F32) + g[at].astype(F32)).astype(BF)

    index = lambda i: (0,) * lead + (i, 0)
    return pl.pallas_call(
        kernel,
        grid=(cuts,),
        in_specs=[pl.BlockSpec(block, index)] * 2 + [ANY] * len(after),
        out_specs=[pl.BlockSpec(out_block, index)] * 2,
        out_shape=[jax.ShapeDtypeStruct(out, BF)] * 2,
        compiler_params=pltpu.CompilerParams(vmem_limit_bytes=LIMIT),
        cost_estimate=BACKWARD,
    )(keep, got, *after)


def last_combine(terms, axis, rows, after):
    ins, specs, widths = [], [], []
    for t in terms:
        ins += [t.keep, t.got]
        widths.append(t.keep.shape[-1] * (t.keep.shape[-2] // rows))
    total = sum(widths)
    n_in = len(ins)

    def kernel(*refs):
        stay, go = refs[-2:]
        at = 0
        for j, t in enumerate(terms):
            k, g = refs[2 * j], refs[2 * j + 1]
            lead = k.ndim - 2
            cols = k.shape[-1]
            for block in range(k.shape[-2] // rows):
                for side, ref in ((0, stay), (1, go)):
                    idx = tuple(side if d == axis else 0 for d in range(lead)) + (pl.ds(block * rows, rows),)
                    ref[:, at : at + cols] = (k[idx].astype(F32) + g[idx].astype(F32)).astype(BF)
                at += cols

    whole = [pl.BlockSpec(v.shape, lambda n=v.ndim: (0,) * n) for v in ins]
    return pl.pallas_call(
        kernel,
        in_specs=whole + [ANY] * len(after),
        out_specs=[pl.BlockSpec((rows, total), lambda: (0, 0))] * 2,
        out_shape=[jax.ShapeDtypeStruct((rows, total), BF)] * 2,
        compiler_params=pltpu.CompilerParams(vmem_limit_bytes=SMALL_LIMIT),
        cost_estimate=BACKWARD,
    )(*ins, *after)


def pick(flag, a, b):
    return jnp.where(flag == 0, a, b)


def small_call(kernel, where, ins, shapes, after, grid=None):
    n = len(ins)

    def body(where_ref, *refs):
        kernel(where_ref, refs[:n], refs[n + len(after) :])

    return pl.pallas_call(
        body,
        grid_spec=pltpu.PrefetchScalarGridSpec(
            num_scalar_prefetch=1,
            grid=(1,),
            in_specs=[pl.BlockSpec(v.shape, lambda i, w, n=v.ndim: (0,) * n) for v in ins] + [ANY] * len(after),
            out_specs=[pl.BlockSpec(s, lambda i, w, n=len(s): (0,) * n) for s, _ in shapes],
        ),
        out_shape=[jax.ShapeDtypeStruct(s, t) for s, t in shapes],
        compiler_params=pltpu.CompilerParams(vmem_limit_bytes=SMALL_LIMIT),
        cost_estimate=BACKWARD,
    )(where, *ins, *after)


class Ending:
    def __init__(self, plan, where, terms, axis, rows, tail, after):
        self.plan, self.where, self.rows, self.tail = plan, where, rows, tail
        self.keep, self.sent = last_combine(terms, axis, rows, after)
        self.got = plan.flip(self.sent, axis)

    def core(self, after):
        rows, tail = self.rows // 2, self.tail
        cols = self.cols = self.keep.shape[1] - tail

        def kernel(where, ins, outs):
            c = where[0]
            for ref, row in ((outs[0], c), (outs[1], 1 - c)):
                at = pl.ds(pl.multiple_of(row * rows, 16), rows)
                ref[:, :cols] = (ins[0][at, :cols].astype(F32) + ins[1][at, :cols].astype(F32)).astype(BF)
            if tail:
                for g in range(2):
                    at = pl.ds(g * rows, rows)
                    piece = ins[0][at, cols:].astype(F32) + ins[1][at, cols:].astype(F32)
                    outs[0][:, cols + g * tail : cols + (g + 1) * tail] = piece.astype(BF)

        shapes = [((rows, cols + 2 * tail), BF), ((rows, cols), BF)]
        self.mine, sent = small_call(kernel, self.where, [self.keep, self.got], shapes, after)
        self.came = self.plan.core(sent)
        return sent

    def rep(self, after):
        rows, cols, tail = self.rows // 2, self.cols, self.tail

        def kernel(where, ins, outs):
            outs[0][:, :cols] = ins[0][:, :cols]
            outs[0][:, cols : 2 * cols] = ins[1][...]
            if tail:
                outs[0][:, 2 * cols :] = ins[0][:, cols:]

        shapes = [((rows, 2 * cols + 2 * tail), BF)]
        v = small_call(kernel, self.where, [self.mine, self.came], shapes, after)[0]
        self.pair = [v, self.plan.flip(v, 0)] if self.plan.ny == 2 else [lax.psum(v, "rep")]
        return v


class ChipEnding:
    def __init__(self, plan, where, term):
        self.plan, self.where = plan, where
        groups = [[2 * chip + c for chip in range(plan.chips)] for c in range(2)]
        self.term = lax.psum_scatter(term, "shard", scatter_dimension=0, axis_index_groups=groups, tiled=True)

    def core(self, after):
        rows, cols = self.term.shape
        part = rows // 4

        def kernel(where, ins, outs):
            c = where[0]
            for ref, row in ((outs[0], c), (outs[1], 1 - c)):
                for k in range(2):
                    at = pl.ds(pl.multiple_of((2 * k + row) * part, 16), part)
                    ref[k * part : (k + 1) * part] = ins[0][at]

        shapes = [((rows // 2, cols), BF)] * 2
        self.mine, sent = small_call(kernel, self.where, [self.term], shapes, after)
        self.came = self.plan.core(sent)
        return sent

    def rep(self, after):
        rows, cols = self.mine.shape

        def kernel(where, ins, outs):
            outs[0][:rows] = ins[0][...]
            outs[0][rows:] = ins[1][...]

        v = small_call(kernel, self.where, [self.mine, self.came], [((2 * rows, cols), BF)], after)[0]
        self.pair = [v, self.plan.flip(v, 0)] if self.plan.ny == 2 else [lax.psum(v, "rep")]
        return v


def place_grads(plan, where, layer, layers, end2, rest, sizes, before, after):
    deep, width, ff, quarters = sizes
    n, ny, halves = plan.shards, plan.ny, quarters // 2
    wide, half_ff = 3 * width // 2, ff // 2
    cols = rest.cols
    fused = bool(rest.tail)
    ins = end2.pair + rest.pair

    def kernel(where_ref, *refs):
        refs_in = refs[: 2 * ny]
        outs = refs[-(4 if fused else 3) :]
        c, y = where_ref[0], where_ref[2]

        def source(p, q, at, size):
            step = (at // 128) * 128
            span = (at + size - step + 127) // 128 * 128
            first = pl.multiple_of(jnp.where(p == c, 0, cols) + step, 128)
            v = refs_in[ny][:, pl.ds(first, span)]
            if ny == 2:
                v = jnp.where(y == q, v, refs_in[ny + 1][:, pl.ds(first, span)])
            return v[:, at - step : at - step + size].astype(F32)

        def core_columns(p, at, size, total, first):
            part = total // ny
            return source(p, at // part, first + at % part, size)

        for k in range(3 * HEADS // 2):
            pieces = [core_columns(p, k * HEAD_DIM, HEAD_DIM, wide, 0) for p in range(2)]
            outs[0][0, :, k * 2 * HEAD_DIM : (k + 1) * 2 * HEAD_DIM] = jnp.concatenate(pieces, axis=1)
        for k in range(n):
            pieces = []
            for p in range(2):
                for h in range(halves):
                    pieces.append(core_columns(p, (h * n + k) * deep, deep, half_ff, wide // ny))
            outs[1][0, :, k * quarters * deep : (k + 1) * quarters * deep] = jnp.concatenate(pieces, axis=1)
        part = width // ny
        for p in range(2):
            at = pl.ds(pl.multiple_of(jnp.where(p == c, 0, halves * deep), 16), halves * deep)
            v = refs_in[0][at].astype(F32)
            if ny == 2:
                v = v + refs_in[1][at].astype(F32)
            outs[2][0, p * halves * deep : (p + 1) * halves * deep] = v
        if fused:
            for q in range(ny):
                v = refs_in[ny][:, 2 * cols :]
                if ny == 2:
                    v = jnp.where(y == q, v, refs_in[ny + 1][:, 2 * cols :])
                outs[3][0, :, q * part : (q + 1) * part] = v.astype(F32)

    shapes = [(deep, 3 * width), (deep, ff), (quarters * deep, width)] + ([(deep, width)] if fused else [])
    in_specs = [pl.BlockSpec(v.shape, lambda i, w: (0, 0)) for v in ins]
    args = list(ins) + list(before or []) + list(after)
    n_before = len(before or [])
    return pl.pallas_call(
        kernel,
        grid_spec=pltpu.PrefetchScalarGridSpec(
            num_scalar_prefetch=1,
            grid=(1,),
            in_specs=in_specs + [ANY] * (n_before + len(after)),
            out_specs=[pl.BlockSpec((1,) + s, lambda i, w: (layer, 0, 0)) for s in shapes],
        ),
        out_shape=[jax.ShapeDtypeStruct((layers,) + s, F32) for s in shapes],
        input_output_aliases={1 + len(ins) + k: k for k in range(n_before)},
        compiler_params=pltpu.CompilerParams(vmem_limit_bytes=LIMIT),
        cost_estimate=BACKWARD,
    )(where, *args)


def pack(plan, where, layer, qkv, proj, fc1, fc2, extra, after):
    deep, width = proj.shape[1:]
    ff, n = fc1.shape[2], plan.shards
    quarters = fc2.shape[1] // deep
    halves = quarters // 2
    each = halves // plan.ny
    ins = [qkv, proj, fc1, fc2] + ([extra] if extra is not None else [])
    total = 4 * width + ff + 2 * each * width + (extra.shape[1] if extra is not None else 0)

    def kernel(where_ref, *refs):
        out = refs[-1]

        def lay(at, pieces):
            held, wide = [], 0
            for p in pieces:
                held.append(p)
                wide += p.shape[1]
                if wide % 128 == 0:
                    out[:, at : at + wide] = held[0] if len(held) == 1 else jnp.concatenate(held, axis=1)
                    at, held, wide = at + wide, [], 0

        for p in range(2):
            cols = [k * 2 * HEAD_DIM + p * HEAD_DIM for k in range(3 * HEADS // 2)]
            lay(p * (3 * width // 2), [refs[0][0, :, k : k + HEAD_DIM] for k in cols])
        out[:, 3 * width : 4 * width] = refs[1][0]
        cols = [s * quarters * deep + k * deep for k in range(quarters) for s in range(n)]
        lay(4 * width, [refs[2][0, :, k : k + deep] for k in cols])
        at = 4 * width + ff
        for p in range(2):
            for k in range(each):
                row = (p * halves + k) * deep + where_ref[3] * deep
                out[:, at : at + width] = refs[3][0, pl.ds(pl.multiple_of(row, 16), deep)]
                at += width
        if extra is not None:
            out[:, at:] = refs[4][...]

    specs = [pl.BlockSpec((1,) + v.shape[1:], lambda i, w: (layer, 0, 0)) for v in ins[:4]]
    specs += [pl.BlockSpec(v.shape, lambda i, w: (0, 0)) for v in ins[4:]]
    return pl.pallas_call(
        kernel,
        grid_spec=pltpu.PrefetchScalarGridSpec(
            num_scalar_prefetch=1,
            grid=(1,),
            in_specs=specs + [ANY] * len(after),
            out_specs=pl.BlockSpec((deep, total), lambda i, w: (0, 0)),
        ),
        out_shape=jax.ShapeDtypeStruct((deep, total), BF),
        compiler_params=pltpu.CompilerParams(vmem_limit_bytes=LIMIT),
        cost_estimate=FORWARD,
    )(where, *ins, *after)


def per_device(
    plan,
    tokens,
    kept,
    attn_gain,
    attn_shift,
    qkv_weight,
    qv_bias,
    proj_weight,
    proj_bias,
    mlp_gain,
    mlp_shift,
    fc1_weight,
    fc1_bias,
    fc2_weight,
    fc2_bias,
    cotangent,
):
    images, slots, width = tokens.shape
    layers = attn_gain.shape[0]
    rows = images * slots
    n = plan.shards
    deep = qkv_weight.shape[1]
    shard = lax.axis_index("shard")
    c, chip, y = lax.rem(shard, 2), shard // 2, lax.axis_index("rep")
    where = jnp.stack([c, chip, y, y if plan.ny == 2 else 0 * y]).astype(jnp.int32)
    ff = fc2_weight.shape[1] * n
    quarters = fc2_weight.shape[1] // deep
    wide, half_width, half_ff = 3 * width // 2, width // 2, ff // 2
    half_heads = HEADS // 2

    small = jnp.concatenate(
        [attn_gain, attn_shift, qv_bias, proj_bias, mlp_gain, mlp_shift, fc1_bias, fc2_bias], axis=1
    )
    sizes = [v.shape[1] for v in (attn_gain, attn_shift, qv_bias, proj_bias, mlp_gain, mlp_shift, fc1_bias, fc2_bias)]
    lines = small.size // 128
    extra = jnp.pad(small.reshape(lines, 128), ((0, deep - lines), (0, 0)))

    halves = quarters // 2
    lead = 4 * width
    block = n * deep
    each = halves // plan.ny

    gathered, done = [], ()
    for layer in range(layers):
        shards = (qkv_weight, proj_weight, fc1_weight, fc2_weight)
        done = (pack(plan, where, layer, *shards, None if layer else extra, done),)
        gathered.append(lax.all_gather(done[0], "shard", axis=0, tiled=True))
    at_fc1, at_fc2 = lead // block, (lead + ff) // block
    mlp_parts = []
    for layer in range(layers):
        found = {"fc1": [(gathered[layer], ("quarter", block, (at_fc1, halves, k))) for k in range(halves)]}
        found["fc2"] = [(gathered[layer], columns(block, at_fc2 + k, each)) for k in range(each)]
        if plan.ny == 2:
            found["sent"], found["came"] = (), ()
            for k in range(1):
                mine = lax.dynamic_slice(
                    gathered[layer], (0, (at_fc2 + c) * block), (block, block)
                )
                found["sent"] += (mine,)
                found["came"] += (plan.flip(mine, 0),)
                found["fc2"].append((found["came"][k], None))
        mlp_parts.append(found)

    def weight_of(layer, name):
        if name == "qkv":
            return [(gathered[layer], columns(wide, 0, 1))]
        if name == "proj":
            return [(gathered[layer], ("heads", width, 3))]
        return mlp_parts[layer][name]

    every = gathered[0].reshape(n, deep, -1)[:, :lines, lead + ff + 2 * each * block :]
    every = every.reshape(n, layers, small.shape[1]).astype(F32)
    vecs = []
    for layer in range(layers):
        at, d = 0, {}
        for name, size in zip(SMALL, sizes):
            d[name] = every[:, layer, at : at + size].reshape(1, n * size)
            at += size
        q = d["qvb"].reshape(2 * half_heads, 2, HEAD_DIM)
        q = pick(c, q[:, 0], q[:, 1]).reshape(2, half_width)
        d["qvb_c"] = jnp.stack([q[0], jnp.zeros_like(q[0]), q[1]]).reshape(1, wide)
        f = d["f1b"].reshape(n, 2, halves, deep).transpose(1, 2, 0, 3).reshape(2, halves, block)
        f = pick(c, f[0], f[1])
        if plan.ny == 2:
            f = pick(y, f, f[::-1])
        d["f1b_c"] = f.reshape(1, half_ff)
        vecs.append(d)

    kept_oth = plan.core(kept)
    state = tokens.astype(F32).reshape(rows, width)
    live = lax.broadcasted_iota(jnp.int32, (images, slots), 1) < BUFFER + kept[:, None]
    grad = jnp.where(live[:, :, None], cotangent.astype(F32), 0.0).reshape(rows, width)
    low_own = grad.astype(BF)
    low_oth = plan.core(low_own)
    first_own = norm_rows(state, vecs[0]["ag"], vecs[0]["as"]).astype(BF)

    f32_rows, low_rows = ("rows", (rows, width), F32), ("rows", (rows, width), BF)
    wide_rows, ff_rows = ("rows", (rows, wide), BF), ("rows", (rows, half_ff), BF)
    att_outs = [("image", (images, half_heads, slots, slots), BF), ("rows", (rows, half_width), BF)]
    full_sums = ("full", (8, width), F32)

    def call(body, layer, own, names, blocked, whole, outs, after=(), cost=None):
        chosen = [weight_of(layer, name) for name in names]
        k = kept if own else kept_oth
        return row_call(body, where, k, chosen, blocked, whole, outs, images, slots, after, cost or (BACKWARD if after else FORWARD))

    saved = []
    for layer in range(layers):
        v = vecs[layer]
        first_oth = plan.core(first_own)
        sent, came = mlp_parts[layer].get("sent", ()), mlp_parts[layer].get("came", ())
        proj_oth = call(qkv_body, layer, 0, ["qkv"], [first_oth], [v["qvb_c"]], [wide_rows], sent, FORWARD)[0]
        probs_oth, att_oth, part = call(attend_other, layer, 0, ["proj"], [proj_oth], [], att_outs + [f32_rows])
        part = plan.core(part)
        proj_own = call(qkv_body, layer, 1, ["qkv"], [first_own], [v["qvb_c"]], [wide_rows])[0]
        probs_own, att_own, middle, second_own = call(
            attend_own, layer, 1, ["proj"], [proj_own, part, state], [v["pb"], v["mg"], v["ms"]], att_outs + [f32_rows, low_rows])
        second_oth = plan.core(second_own)
        hid_oth, slope_oth = call(up_body, layer, 0, ["fc1"], [second_oth], [v["f1b_c"]], [ff_rows] * 2)
        if layer + 1 < layers:
            part = call(down_other, layer, 0, ["fc2"], [hid_oth], [], [f32_rows])[0]
            part = plan.core(part)
        hid_own, slope_own = call(up_body, layer, 1, ["fc1"], [second_own], [v["f1b_c"]], [ff_rows] * 2)
        saved.append(
            dict(
                state=state,
                first=(first_own, first_oth),
                proj=(proj_own, proj_oth),
                probs=(probs_own, probs_oth),
                att=(att_own, att_oth),
                middle=middle,
                second=(second_own, second_oth),
                hid=(hid_own, hid_oth),
                slope=(slope_own, slope_oth),
            )
        )
        if layer + 1 < layers:
            w = vecs[layer + 1]
            state, first_own = call(
                down_own, layer, 1, ["fc2"], [hid_own, part, middle], [v["f2b"], w["ag"], w["as"]], [f32_rows, low_rows])

    axes = list(range(1 if plan.ny == 1 else 0, plan.bits + 1))
    last_axis, z_axis, x_axis = 1, plan.bits - 1, plan.bits
    y_axis = 0 if plan.ny == 2 else 2
    orders_f1 = [[y_axis, x_axis, z_axis]] * layers
    orders_q = [[[z_axis, y_axis, x_axis], [y_axis, z_axis, x_axis]]] + [[[x_axis, z_axis, y_axis]]] * (layers - 1)
    own_rows = 2 * deep
    tail = width // plan.ny * HEAD_DIM // own_rows
    fused = n == HEADS
    tail = tail if fused else 0
    big = [[None] * 4 for _ in range(layers)]
    sums = [None] * layers
    f2b_sum = jnp.sum(low_own.astype(F32), axis=0, keepdims=True)

    def end_rest(layer, prev):
        group = terms["q", layer] + [terms["f1", layer]]
        ends["rest", layer] = Ending(plan, where, group, last_axis, own_rows, tail, prev)
        return (ends["rest", layer].sent,)

    def place(layer, before, prev):
        return place_grads(
            plan, where, layer, layers, ends["f2", layer], ends["rest", layer], (deep, width, ff, quarters), before, prev
        )

    ends = {}
    prev = (hid_own,) + mlp_parts[layers - 1].get("came", ())
    terms = {}
    for layer in reversed(range(layers)):
        v, s = vecs[layer], saved[layer]
        top = layer == layers - 1

        def grad_fc2(prev):
            term = chip_grad(plan, where, s["hid"], (low_own, low_oth), 2, prev)
            ends["f2", layer] = ChipEnding(plan, where, term)
            return (term,)

        if top:
            prev = grad_fc2(prev)
        pre_oth, part = call(
            mlp_back_other, layer, 0, ["fc2", "fc1"], [low_oth, s["slope"][1]], [], [ff_rows, f32_rows], prev
        )
        part = plan.core(part)
        prev = (pre_oth,)
        if top:
            last_part = call(down_other, layer, 0, ["fc2"], [s["hid"][1]], [], [f32_rows], prev)[0]
            prev = (last_part,)
            last_part = plan.core(last_part)
        else:
            prev = grad_fc2(prev)
            prev += (terms["f1", layer + 1].step(prev[:1]),)
        pre_own, mid_grad, branch_own, sum1 = call(
            mlp_back_own,
            layer,
            1,
            ["fc2", "fc1"],
            [low_own, s["slope"][0], part, s["middle"], grad],
            [v["mg"]],
            [ff_rows, f32_rows, low_rows, full_sums],
            prev,
        )
        branch_oth = plan.core(branch_own)
        prev = (branch_own,)
        if not top:
            prev += (terms["q", layer + 1][0].step(prev),)
        res1 = weight_grad(
            plan, where, s["second"], (pre_own, pre_oth), 1, orders_f1[layer][0], sums=True, extra=tail, relative=True, after=prev
        )
        prev = tuple(res1[:1]) + ((last_part,) if top else ())
        if not top:
            prev += (terms["q", layer + 1][0].step(prev[:1]),)
            prev += (terms["f1", layer + 1].step(prev[:1]),)
            prev += (ends["f2", layer + 1].core(prev[:1]),)
        dproj_oth, part = call(
            attend_back_other,
            layer,
            0,
            ["proj", "qkv"],
            [branch_oth, s["proj"][1], s["probs"][1]],
            [],
            [wide_rows, f32_rows],
            prev,
        )
        part = plan.core(part)
        prev = (dproj_oth,)
        keep, send = res1[:2]
        if fused:
            keep, send = proj_grad_into(
                plan, where, s["att"], (branch_own, branch_oth), orders_f1[layer][0], keep, send, prev
            )
        else:
            term = t_dot(s["att"][0], branch_own) + t_dot(s["att"][1], branch_oth)
            term = term.astype(BF).reshape(half_heads, HEAD_DIM, width)
            none = jnp.zeros_like(term)
            term = jnp.stack([pick(c, term, none), pick(c, none, term)], axis=1).reshape(width, width)
            term = lax.psum_scatter(term, "shard", scatter_dimension=0, tiled=True)
            big[layer][1] = lax.psum(term, "rep").astype(F32)
        terms["f1", layer] = Term(plan, keep, send, orders_f1[layer])
        prev = (send,)
        if not top:
            prev += (ends["f2", layer + 1].rep(prev[:1]),)
        dproj_own, grad, low_own, sum2 = call(
            attend_back_own,
            layer,
            1,
            ["proj", "qkv"],
            [branch_own, s["proj"][0], s["probs"][0], part, s["state"], mid_grad],
            [v["ag"]],
            [wide_rows, f32_rows, low_rows, full_sums],
            prev,
        )
        prev = (dproj_own,)
        if layer:
            low_oth = plan.core(low_own)
        if not top:
            prev += end_rest(layer + 1, prev[:1])
            prev += (ends["f2", layer].core(prev[:1]),)
        terms["q", layer], q_sums = [], []
        of = len(orders_q[layer])
        for k, order in enumerate(orders_q[layer]):
            resq = weight_grad(
                plan, where, s["first"], (dproj_own, dproj_oth), 1, order[0], sums=True, window=(k, of), after=prev
            )
            terms["q", layer].append(Term(plan, *resq[:2], order))
            q_sums.append(resq[2].reshape(plan.ny, -1))
            prev = (resq[1],) + (() if top else (ends["f2", layer].came,))
        q = jnp.concatenate(q_sums, axis=1).reshape(3, half_heads, 1, HEAD_DIM)
        q = jnp.concatenate([q[:1], q[2:]])
        none = jnp.zeros_like(q)
        q = jnp.concatenate([pick(c, q, none), pick(c, none, q)], axis=2)
        f = res1[2].reshape(halves, block)
        if plan.ny == 2:
            f = pick(y, f, f[::-1])
        none = jnp.zeros_like(f)
        f = jnp.concatenate([pick(c, f, none), pick(c, none, f)], axis=0)
        f = f.reshape(quarters, n, deep).swapaxes(0, 1)
        full = {"ag": sum2[0], "as": sum2[1], "qvb": q, "pb": sum1[2], "mg": sum1[0], "ms": sum1[1], "f1b": f, "f2b": f2b_sum}
        f2b_sum = sum2[2]
        vec = jnp.concatenate([full[name].reshape(n, -1) for name in SMALL], axis=1)
        sums[layer] = vec

    vec = jnp.concatenate(sums, axis=0).reshape(layers, n, -1)
    got_vec = plan.core(vec)
    vec_axes = list(axes)

    def step_vec(prev):
        nonlocal vec, got_vec

        def kernel(where, ins, outs):
            outs[0][...] = ins[0][...] + ins[1][...]

        vec = small_call(kernel, where, [vec, got_vec], [(vec.shape, F32)], prev)[0]
        got_vec = plan.flip(vec, vec_axes.pop(0)) if vec_axes else None
        return (vec,)

    prev += (terms["f1", 0].step(prev[:1]),)
    prev += (ends["rest", 1].core(prev[:1]),)
    w = layers - 1
    mixed = call(
        down_last, w, 1, ["fc2"], [saved[w]["hid"][0], last_part, saved[w]["middle"]], [vecs[w]["f2b"]], [low_rows], prev
    )[0]
    qa, qb = terms["q", 0]
    prev = (qa.step((mixed, ends["rest", 1].came)),)
    prev = (qb.step(prev),)
    prev = step_vec(prev)
    prev = (qa.step(prev),)
    prev = (terms["f1", 0].step(prev),)
    prev = (qb.step(prev),)
    prev = step_vec(prev)
    prev = end_rest(0, prev)
    prev = (ends["rest", 1].rep(prev),)
    prev = (ends["f2", 0].rep(prev),)
    prev = step_vec(prev)
    placed = place(1, None, prev)
    prev = (placed[0],)
    prev = (ends["rest", 0].core(prev + tuple(ends["f2", 0].pair[1:])),)
    prev = step_vec(prev)
    prev = (ends["rest", 0].rep(prev),)
    while got_vec is not None:
        prev = step_vec(prev)
    placed = place(0, placed, prev)
    if plan.ny == 1:
        vec = lax.psum(vec, "rep")
    vec = lax.dynamic_slice_in_dim(vec, shard, 1, axis=1)[:, 0]
    out, at = {}, 0
    for name, size in zip(SMALL, sizes):
        out[name] = vec[:, at : at + size]
        at += size
    qkv_g, fc1_g, fc2_g = placed[:3]
    proj_g = placed[3] if fused else jnp.stack([big[layer][1] for layer in range(layers)])
    return (
        mixed.reshape(images, slots, width),
        grad.reshape(images, slots, width),
        out["ag"],
        out["as"],
        qkv_g,
        out["qvb"],
        proj_g,
        out["pb"],
        out["mg"],
        out["ms"],
        fc1_g,
        out["f1b"],
        fc2_g,
        out["f2b"],
    )


def solution(mesh):
    rows = P(("shard", "rep"), None, None)
    vec = P(None, "shard")
    mat = P(None, "shard", None)
    return jax.shard_map(
        partial(per_device, Plan(mesh)),
        mesh=mesh,
        in_specs=(rows, P(("shard", "rep")), vec, vec, mat, vec, mat, vec, vec, vec, mat, vec, mat, vec, rows),
        out_specs=(rows, rows, vec, vec, mat, vec, mat, vec, vec, vec, mat, vec, mat, vec),
        check_vma=False,
    )
```

```python
from functools import partial

import jax
import jax.numpy as jnp
from jax import lax
from jax.experimental import pallas as pl
from jax.experimental.pallas import tpu as pltpu
from jax.sharding import PartitionSpec as P

HEADS = 16
HEAD_DIM = 64
BUFFER = 64
EPS = 1e-06
SCALE = HEAD_DIM ** (-0.5)
AX = ("shard", "rep")
BF = jnp.bfloat16
F32 = jnp.float32
LIMIT = 60 * 2**20
SMALL_LIMIT = 16 * 2**20
ONCE = pl.Buffered(1)
ANY = pl.BlockSpec(memory_space=pl.ANY)
FORWARD = pl.CostEstimate(flops=10**7, bytes_accessed=0, transcendentals=0)
BACKWARD = pl.CostEstimate(flops=10**9 * 30, bytes_accessed=0, transcendentals=0)
SMALL = ("ag", "as", "qvb", "pb", "mg", "ms", "f1b", "f2b")


class Plan:
    def __init__(self, mesh):
        self.shards = mesh.shape["shard"]
        self.rep = mesh.shape["rep"]
        self.chips = self.shards // 2
        self.ny = 2 if self.rep == 2 else 1
        self.bits = self.chips.bit_length() - 1

    def swap(self, v, flip_shard, flip_rep=0):
        pairs = []
        for s in range(self.shards):
            for y in range(self.rep):
                pairs.append((s * self.rep + y, (s ^ flip_shard) * self.rep + (y ^ flip_rep)))
        return lax.ppermute(v, AX, pairs)

    def core(self, v):
        return self.swap(v, 1)

    def flip(self, v, axis):
        if axis == 0:
            return self.swap(v, 0, 1)
        return self.swap(v, 2 << (self.bits - axis))


def dot(x, w):
    return lax.dot_general(x, w, (((1,), (0,)), ((), ())), preferred_element_type=F32)


def dot_t(x, w):
    return lax.dot_general(x, w, (((1,), (1,)), ((), ())), preferred_element_type=F32)


def t_dot(x, w):
    return lax.dot_general(x, w, (((0,), (0,)), ((), ())), preferred_element_type=F32)


def columns(width, first, stride):
    return ("columns", width, (first, stride))


def row_call(body, where, kept, weights, blocked, whole, outs, images, slots, after=(), cost=FORWARD):
    in_specs, args = [], []
    for v, pick_of in (part for w in weights for part in w):
        if pick_of is None:
            in_specs.append(pl.BlockSpec(v.shape, lambda i, w, k: (0, 0), pipeline_mode=ONCE))
            args.append(v)
            continue
        kind, width, first = pick_of
        if kind == "columns":
            spec = pl.BlockSpec((v.shape[0], width), lambda i, w, k, f=first: (0, f[0] + f[1] * w[0]), pipeline_mode=ONCE)
            in_specs.append(spec)
            args.append(v)
        elif kind == "quarter":
            at, stride, part = first
            spec = pl.BlockSpec(
                (v.shape[0], width),
                lambda i, w, k, f=(at, stride, part): (0, f[0] + f[1] * w[0] + jnp.bitwise_xor(f[2], w[3])),
                pipeline_mode=ONCE,
            )
            in_specs.append(spec)
            args.append(v)
        else:
            view = v.reshape(HEADS // 2, 2, HEAD_DIM, v.shape[1])
            spec = pl.BlockSpec((HEADS // 2, None, HEAD_DIM, width), lambda i, w, k, f=first: (0, w[0], 0, f), pipeline_mode=ONCE)
            in_specs.append(spec)
            args.append(view)
    for v in blocked:
        if v.ndim == 2:
            in_specs.append(pl.BlockSpec((slots, v.shape[1]), lambda i, *_: (i, 0)))
        else:
            in_specs.append(pl.BlockSpec((1,) + v.shape[1:], lambda i, *_, n=v.ndim: (i,) + (0,) * (n - 1)))
        args.append(v)
    for v in whole:
        in_specs.append(pl.BlockSpec(v.shape, lambda i, *_, n=v.ndim: (0,) * n))
        args.append(v)
    out_specs, out_shape = [], []
    for kind, shape, dtype in outs:
        out_shape.append(jax.ShapeDtypeStruct(shape, dtype))
        if kind == "rows":
            out_specs.append(pl.BlockSpec((slots, shape[1]), lambda i, *_: (i, 0)))
        elif kind == "image":
            out_specs.append(pl.BlockSpec((1,) + shape[1:], lambda i, *_, n=len(shape): (i,) + (0,) * (n - 1)))
        else:
            out_specs.append(pl.BlockSpec(shape, lambda i, *_, n=len(shape): (0,) * n))
    n_p, n_b, n_in = sum(len(w) for w in weights), len(blocked), len(args)
    in_specs += [ANY] * len(after)
    args += list(after)

    def kernel(where_ref, kept_ref, *refs):
        ins, res = refs[:n_in], refs[n_in + len(after) :]
        held, at = [], 0
        for w in weights:
            held.append(ins[at : at + len(w)])
            at += len(w)
        body(kept_ref, held, ins[n_p : n_p + n_b], ins[n_p + n_b : n_in], res)

    return pl.pallas_call(
        kernel,
        grid_spec=pltpu.PrefetchScalarGridSpec(
            num_scalar_prefetch=2, grid=(images,), in_specs=in_specs, out_specs=out_specs
        ),
        out_shape=out_shape,
        compiler_params=pltpu.CompilerParams(vmem_limit_bytes=LIMIT),
        cost_estimate=cost,
    )(where, kept, *args)


def normed_of(rows):
    width = rows.shape[-1]
    mean = jnp.sum(rows, axis=-1, keepdims=True) * (1.0 / width)
    centered = rows - mean
    spread = jnp.sum(centered * centered, axis=-1, keepdims=True) * (1.0 / width)
    factor = lax.rsqrt(spread + EPS)
    return centered * factor, factor


def norm_rows(rows, gain, shift):
    return normed_of(rows)[0] * gain + shift


def norm_back(dz, rows, gain):
    normed, factor = normed_of(rows)
    width = rows.shape[-1]
    prod = dz * normed
    dn = dz * gain
    m1 = jnp.sum(dn, axis=-1, keepdims=True) * (1.0 / width)
    m2 = jnp.sum(dn * normed, axis=-1, keepdims=True) * (1.0 / width)
    back = factor * (dn - m1 - normed * m2)
    return back, jnp.sum(prod, axis=0, keepdims=True), jnp.sum(dz, axis=0, keepdims=True)


def chunks(total, size):
    size = min(size, total)
    return [(k, size) for k in range(0, total, size)]


def qkv_body(kept, w, blocked, whole, outs):
    x = blocked[0][...]
    for k, n in chunks(outs[0].shape[1], 512):
        cols = pl.ds(k, n)
        outs[0][:, cols] = (dot(x, w[0][0][:, cols]) + whole[0][:, cols]).astype(BF)


def heads_of(ref):
    return ref[...].reshape(-1, ref.shape[-1])


def pairs_dot(x_ref, parts):
    total, at = None, 0
    for w_ref in parts:
        term = dot(x_ref[:, at : at + w_ref.shape[0]], w_ref[...])
        total = term if total is None else total + term
        at += w_ref.shape[0]
    return total


def attend(kept, proj_ref, probs_ref, att_ref):
    slots, third = proj_ref.shape[0], proj_ref.shape[1] // 3
    bound = BUFFER + kept[pl.program_id(0)]
    alive = lax.broadcasted_iota(jnp.int32, (slots, slots), 1) < bound
    outs = []
    for h in range(third // HEAD_DIM):
        lo = h * HEAD_DIM
        q = proj_ref[:, lo : lo + HEAD_DIM]
        k = proj_ref[:, third + lo : third + lo + HEAD_DIM]
        v = proj_ref[:, 2 * third + lo : 2 * third + lo + HEAD_DIM]
        s = jnp.where(alive, dot_t(q, k) * SCALE, -1e30)
        e = jnp.exp(s - jnp.max(s, axis=-1, keepdims=True))
        p = (e * (1.0 / jnp.sum(e, axis=-1, keepdims=True))).astype(BF)
        probs_ref[0, h] = p
        outs.append(dot(p, v).astype(BF))
        if h % 2:
            att_ref[:, lo - HEAD_DIM : lo + HEAD_DIM] = jnp.concatenate(outs, axis=1)
            outs = []


def attend_other(kept, w, blocked, whole, outs):
    attend(kept, blocked[0], outs[0], outs[1])
    outs[2][...] = dot(outs[1][...], heads_of(w[0][0]))


def attend_own(kept, w, blocked, whole, outs):
    attend(kept, blocked[0], outs[0], outs[1])
    middle = blocked[2][...] + (dot(outs[1][...], heads_of(w[0][0])) + blocked[1][...]) + whole[0][...]
    outs[2][...] = middle
    outs[3][...] = norm_rows(middle, whole[1][...], whole[2][...]).astype(BF)


def up_body(kept, w, blocked, whole, outs):
    x = blocked[0][...]
    for k, n in chunks(outs[0].shape[1], 256):
        cols = pl.ds(k, n)
        held = w[0][k // w[0][0].shape[1]]
        pre = dot(x, held[:, pl.ds(k % held.shape[1], n)]) + whole[0][:, cols]
        phi = 0.5 + 0.5 * lax.erf(pre * (2.0**-0.5))
        dens = jnp.exp(-0.5 * (pre * pre)) * 0.3989422804014327
        outs[0][:, cols] = (pre * phi).astype(BF)
        outs[1][:, cols] = (phi + pre * dens).astype(BF)


def down_other(kept, w, blocked, whole, outs):
    outs[0][...] = pairs_dot(blocked[0], w[0])


def down_own(kept, w, blocked, whole, outs):
    state = blocked[2][...] + (pairs_dot(blocked[0], w[0]) + blocked[1][...]) + whole[0][...]
    outs[0][...] = state
    outs[1][...] = norm_rows(state, whole[1][...], whole[2][...]).astype(BF)


def down_last(kept, w, blocked, whole, outs):
    state = blocked[2][...] + (pairs_dot(blocked[0], w[0]) + blocked[1][...]) + whole[0][...]
    alive = lax.broadcasted_iota(jnp.int32, state.shape, 0) < BUFFER + kept[pl.program_id(0)]
    outs[0][...] = jnp.where(alive, state, 0.0).astype(BF)


def mlp_back(w, blocked, outs):
    low = blocked[0][...]
    for k, n in chunks(outs[0].shape[1], 512):
        cols = pl.ds(k, n)
        held, first = w[0][0], 0
        for part in w[0][1:]:
            if k >= first + held.shape[0]:
                first += held.shape[0]
                held = part
        t = dot_t(low, held[pl.ds(k - first, n), :])
        outs[0][:, cols] = (t * blocked[1][:, cols].astype(F32)).astype(BF)
    total, at = None, 0
    for held in w[1]:
        term = dot_t(outs[0][:, at : at + held.shape[1]], held[...])
        total = term if total is None else total + term
        at += held.shape[1]
    return total


def mlp_back_other(kept, w, blocked, whole, outs):
    outs[1][...] = mlp_back(w, blocked, outs)


def add_sums(ref, rows):
    sums = jnp.concatenate(rows + [jnp.zeros((8 - len(rows), rows[0].shape[1]), F32)], axis=0)

    @pl.when(pl.program_id(0) == 0)
    def _():
        ref[...] = sums

    @pl.when(pl.program_id(0) != 0)
    def _():
        ref[...] += sums


def mlp_back_own(kept, w, blocked, whole, outs):
    dz = mlp_back(w, blocked, outs) + blocked[2][...]
    back, gain, shift = norm_back(dz, blocked[3][...], whole[0][...])
    grad = blocked[4][...] + back
    low = grad.astype(BF)
    outs[1][...] = grad
    outs[2][...] = low
    add_sums(outs[3], [gain, shift, jnp.sum(low.astype(F32), axis=0, keepdims=True)])


def attend_back(w, blocked, outs):
    branch, proj_ref, probs_ref = blocked[0], blocked[1], blocked[2]
    third = proj_ref.shape[1] // 3
    datt = dot_t(branch[...], heads_of(w[0][0])).astype(BF)
    pairs = [[], [], []]
    for h in range(third // HEAD_DIM):
        lo = h * HEAD_DIM
        q = proj_ref[:, lo : lo + HEAD_DIM]
        k = proj_ref[:, third + lo : third + lo + HEAD_DIM]
        v = proj_ref[:, 2 * third + lo : 2 * third + lo + HEAD_DIM]
        da = datt[:, lo : lo + HEAD_DIM]
        p = probs_ref[0, h]
        dp = dot_t(da, v)
        pf = p.astype(F32)
        ds = (pf * (dp - jnp.sum(pf * dp, axis=-1, keepdims=True))).astype(BF)
        pairs[0].append((dot(ds, k) * SCALE).astype(BF))
        pairs[1].append((t_dot(ds, q) * SCALE).astype(BF))
        pairs[2].append(t_dot(p, da).astype(BF))
        if h % 2:
            for j in range(3):
                at = j * third + lo - HEAD_DIM
                outs[0][:, at : at + 2 * HEAD_DIM] = jnp.concatenate(pairs[j], axis=1)
            pairs = [[], [], []]
    return dot_t(outs[0][...], w[1][0][...])


def attend_back_other(kept, w, blocked, whole, outs):
    outs[1][...] = attend_back(w, blocked, outs)


def attend_back_own(kept, w, blocked, whole, outs):
    dz = attend_back(w, blocked, outs) + blocked[3][...]
    back, gain, shift = norm_back(dz, blocked[4][...], whole[0][...])
    grad = blocked[5][...] + back
    outs[1][...] = grad
    low = grad.astype(BF)
    outs[2][...] = low
    add_sums(outs[3], [gain, shift, jnp.sum(low.astype(F32), axis=0, keepdims=True)])


def weight_grad(plan, where, xs, ys, groups, first, sums=False, extra=0, relative=False, after=()):
    depth, n_x = xs[0].shape
    cols = ys[0].shape[1]
    ny, chips, bits = plan.ny, plan.chips, plan.bits
    half = cols // ny
    size = half
    chunk = size if size <= 768 else 512
    steps = size // chunk
    rows = n_x // chips
    part = rows // groups
    dims = [ny] + [2] * bits
    dims[first] = 1
    block = [1] + dims[1:] + [rows, chunk]
    shape = dims + [rows, size + extra]
    n_after = len(after)

    def kernel(where_ref, xo, xt, yo, yt, *rest):
        rest = rest[n_after:]
        keep, send = rest[0], rest[1]
        flip, acc = rest[-2], rest[-1]
        step = pl.program_id(0)

        @pl.when(step == 0)
        def _():
            flip[:, :depth] = xo[...].T
            flip[:, depth:] = xt[...].T

        acc[...] = dot(flip[:, :depth], yo[...]) + dot(flip[:, depth:], yt[...])
        if sums:
            rest[2][...] = jnp.sum(yo[...].astype(F32), axis=0, keepdims=True) + jnp.sum(
                yt[...].astype(F32), axis=0, keepdims=True
            )

        def put(ref, r):
            at = [0]
            for k in range(1, bits + 1):
                at.append((r >> (bits - k)) & 1 if k != first else 0)
            chip = jnp.bitwise_xor(where_ref[1], r)
            for g in range(groups):
                start = pl.multiple_of(g * part * chips + chip * part, 16)
                place = g
                if groups == 2 and ny == 2:
                    place = jnp.bitwise_xor(g, where_ref[2])
                place = pl.multiple_of(place * part, 16)
                ref[tuple(at) + (pl.ds(place, part),)] = acc[pl.ds(start, part)].astype(BF)

        if first:
            for r in range(chips):
                put(send if (r >> (bits - first)) & 1 else keep, r)
        else:

            @pl.when(step < steps)
            def _():
                for r in range(chips):
                    put(keep, r)

            @pl.when(step >= steps)
            def _():
                for r in range(chips):
                    put(send, r)

    per_rep = half // chunk

    def column(i, w):
        own = w[2] if ny == 2 and not relative else 0
        return jnp.bitwise_xor(i // steps, own) * per_rep + i % steps

    zeros = (0,) * (bits + 1)
    x_spec = pl.BlockSpec((depth, n_x), lambda i, w: (0, 0), pipeline_mode=ONCE)
    y_spec = pl.BlockSpec((depth, chunk), lambda i, w: (0, column(i, w)))
    if first:
        specs = [pl.BlockSpec(block, lambda i, w: (i // steps,) + zeros + (i % steps,))] * 2
    else:
        specs = [
            pl.BlockSpec(block, lambda i, w: (0,) + zeros + (jnp.minimum(i, steps - 1),)),
            pl.BlockSpec(block, lambda i, w: (0,) + zeros + (jnp.maximum(i - steps, 0),)),
        ]
    out_shape = [jax.ShapeDtypeStruct(shape, BF)] * 2
    if sums:
        own = (lambda w: w[2]) if ny == 2 and not relative else (lambda w: 0)
        specs = specs + [
            pl.BlockSpec((1, chunk), lambda i, w: (0, jnp.bitwise_xor(i // steps, own(w)) * steps + i % steps))
        ]
        out_shape = out_shape + [jax.ShapeDtypeStruct((1, size * ny), F32)]
    return pl.pallas_call(
        kernel,
        grid_spec=pltpu.PrefetchScalarGridSpec(
            num_scalar_prefetch=1,
            grid=(ny * steps,),
            in_specs=[x_spec, x_spec, y_spec, y_spec] + [ANY] * n_after,
            out_specs=specs,
            scratch_shapes=[pltpu.VMEM((n_x, 2 * depth), BF), pltpu.VMEM((n_x, chunk), F32)],
        ),
        out_shape=out_shape,
        compiler_params=pltpu.CompilerParams(vmem_limit_bytes=LIMIT),
        cost_estimate=BACKWARD,
    )(where, *xs, *ys, *after)


def parted_grad(plan, where, xs, ys, firsts, after=()):
    depth, n_x = xs[0].shape
    cols = ys[0].shape[1]
    ny, chips, bits = plan.ny, plan.chips, plan.bits
    parts = len(firsts)
    chunk = cols // ny // parts
    rows = n_x // chips
    n_after = len(after)

    def kernel(where_ref, xo, xt, yo, yt, *rest):
        outs, sums, flip, acc = rest[n_after:-3], rest[-3], rest[-2], rest[-1]
        step = pl.program_id(0)

        @pl.when(step == 0)
        def _():
            flip[:, :depth] = xo[...].T
            flip[:, depth:] = xt[...].T

        acc[...] = dot(flip[:, :depth], yo[...]) + dot(flip[:, depth:], yt[...])
        total = jnp.sum(yo[...].astype(F32), axis=0, keepdims=True)
        sums[...] = total + jnp.sum(yt[...].astype(F32), axis=0, keepdims=True)

        def put(ref, r, first):
            at = [0]
            for k in range(1, bits + 1):
                at.append((r >> (bits - k)) & 1 if k != first else 0)
            start = pl.multiple_of(jnp.bitwise_xor(where_ref[1], r) * rows, 16)
            ref[tuple(at)] = acc[pl.ds(start, rows)].astype(BF)

        for p, first in enumerate(firsts):
            keep, send = outs[2 * p], outs[2 * p + 1]
            if first:

                @pl.when(step % parts == p)
                def _(keep=keep, send=send, first=first):
                    for r in range(chips):
                        put(send if (r >> (bits - first)) & 1 else keep, r, first)
            else:

                @pl.when(step == p)
                def _(keep=keep, first=first):
                    for r in range(chips):
                        put(keep, r, first)

                @pl.when(step == parts + p)
                def _(send=send, first=first):
                    for r in range(chips):
                        put(send, r, first)

    def column(i, w):
        own = w[2] if ny == 2 else 0
        return jnp.bitwise_xor(i // parts, own) * parts + i % parts

    zeros = (0,) * (bits + 2)
    x_spec = pl.BlockSpec((depth, n_x), lambda i, w: (0, 0), pipeline_mode=ONCE)
    y_spec = pl.BlockSpec((depth, chunk), lambda i, w: (0, column(i, w)))
    specs, shapes = [], []
    for first in firsts:
        dims = [ny] + [2] * bits
        dims[first] = 1
        block = [1] + dims[1:] + [rows, chunk]
        index = (lambda i, w: (i // parts,) + zeros) if first else (lambda i, w: (0,) + zeros)
        specs += [pl.BlockSpec(block, index)] * 2
        shapes += [jax.ShapeDtypeStruct(dims + [rows, chunk], BF)] * 2
    res = pl.pallas_call(
        kernel,
        grid_spec=pltpu.PrefetchScalarGridSpec(
            num_scalar_prefetch=1,
            grid=(ny * parts,),
            in_specs=[x_spec, x_spec, y_spec, y_spec] + [ANY] * n_after,
            out_specs=specs + [pl.BlockSpec((1, chunk), lambda i, w: (0, column(i, w)))],
            scratch_shapes=[pltpu.VMEM((n_x, 2 * depth), BF), pltpu.VMEM((n_x, chunk), F32)],
        ),
        out_shape=shapes + [jax.ShapeDtypeStruct((1, cols), F32)],
        compiler_params=pltpu.CompilerParams(vmem_limit_bytes=LIMIT),
        cost_estimate=BACKWARD,
    )(where, *xs, *ys, *after)
    return [res[2 * p : 2 * p + 2] for p in range(parts)], res[-1]


def chip_grad(plan, where, xs, ys, groups, after=()):
    depth, n_x = xs[0].shape
    cols = ys[0].shape[1]
    chips = plan.chips
    chunk = min(cols, 512)
    rows = n_x // chips
    part = rows // groups
    n_after = len(after)

    def kernel(where_ref, xo, xt, yo, yt, *rest):
        out, flip, acc = rest[n_after:]

        @pl.when(pl.program_id(0) == 0)
        def _():
            flip[:, :depth] = xo[...].T
            flip[:, depth:] = xt[...].T

        acc[...] = dot(flip[:, :depth], yo[...]) + dot(flip[:, depth:], yt[...])
        for g in range(groups):
            place = jnp.bitwise_xor(g, where_ref[3]) * part
            for chip in range(chips):
                at = pl.ds(pl.multiple_of(place + chip * rows, 16), part)
                first = (g * chips + chip) * part
                out[at, :] = acc[first : first + part].astype(BF)

    x_spec = pl.BlockSpec((depth, n_x), lambda i, w: (0, 0), pipeline_mode=ONCE)
    y_spec = pl.BlockSpec((depth, chunk), lambda i, w: (0, i))
    return pl.pallas_call(
        kernel,
        grid_spec=pltpu.PrefetchScalarGridSpec(
            num_scalar_prefetch=1,
            grid=(cols // chunk,),
            in_specs=[x_spec, x_spec, y_spec, y_spec] + [ANY] * n_after,
            out_specs=pl.BlockSpec((n_x, chunk), lambda i, w: (0, i)),
            scratch_shapes=[pltpu.VMEM((n_x, 2 * depth), BF), pltpu.VMEM((n_x, chunk), F32)],
        ),
        out_shape=jax.ShapeDtypeStruct((n_x, cols), BF),
        compiler_params=pltpu.CompilerParams(vmem_limit_bytes=LIMIT),
        cost_estimate=BACKWARD,
    )(where, *xs, *ys, *after)


def proj_grad_into(plan, where, xs, ys, first, keep, send, after=()):
    depth, n_x = xs[0].shape
    cols = ys[0].shape[1]
    ny, chips, bits = plan.ny, plan.chips, plan.bits
    half = cols // ny
    part = n_x // chips
    width = half * part // keep.shape[-2]
    stacked = half // width
    at_col = keep.shape[-1] // width - 1
    block = [1] + list(keep.shape[1:-1]) + [width]

    n_after = len(after)

    def kernel(where_ref, xo, xt, yo, yt, k_in, s_in, *rest):
        keep_ref, send_ref, acc = rest[n_after:]
        acc[...] = t_dot(xo[...], yo[...]) + t_dot(xt[...], yt[...])

        def put(ref, r):
            at = [0]
            for k in range(1, bits + 1):
                at.append((r >> (bits - k)) & 1 if k != first else 0)
            start = pl.multiple_of(jnp.bitwise_xor(where_ref[1], r) * part, 16)
            for g in range(stacked):
                piece = acc[pl.ds(start, part), g * width : (g + 1) * width]
                ref[tuple(at) + (pl.ds(g * part, part),)] = piece.astype(BF)

        if first:
            for r in range(chips):
                put(send_ref if (r >> (bits - first)) & 1 else keep_ref, r)
        else:

            @pl.when(pl.program_id(0) == 0)
            def _():
                for r in range(chips):
                    put(keep_ref, r)

            @pl.when(pl.program_id(0) != 0)
            def _():
                for r in range(chips):
                    put(send_ref, r)

    zeros = (0,) * (bits + 1)
    own = (lambda w: w[2]) if ny == 2 else (lambda w: 0)
    x_spec = pl.BlockSpec((depth, n_x), lambda i, w: (0, 0), pipeline_mode=ONCE)
    y_spec = pl.BlockSpec((depth, half), lambda i, w: (0, jnp.bitwise_xor(i, own(w))))
    spec = pl.BlockSpec(block, lambda i, w: (i if first else 0,) + zeros + (at_col,))
    return pl.pallas_call(
        kernel,
        grid_spec=pltpu.PrefetchScalarGridSpec(
            num_scalar_prefetch=1,
            grid=(ny,),
            in_specs=[x_spec, x_spec, y_spec, y_spec, ANY, ANY] + [ANY] * n_after,
            out_specs=[spec, spec],
            scratch_shapes=[pltpu.VMEM((n_x, half), F32)],
        ),
        out_shape=[jax.ShapeDtypeStruct(keep.shape, BF)] * 2,
        input_output_aliases={5: 0, 6: 1},
        compiler_params=pltpu.CompilerParams(vmem_limit_bytes=LIMIT),
        cost_estimate=BACKWARD,
    )(where, *xs, *ys, keep, send, *after)


class Term:
    def __init__(self, plan, keep, send, order):
        self.plan, self.keep, self.order = plan, keep, list(order)
        self.got = plan.flip(send, self.order.pop(0))

    def step(self, after):
        axis = self.order.pop(0)
        self.keep, send = combine(self.keep, self.got, axis, after)
        self.got = self.plan.flip(send, axis)
        return send


def combine(keep, got, axis, after):
    shape = keep.shape
    rows, cols = shape[-2:]
    cuts = 2
    block = shape[:-2] + (rows // cuts, cols)
    out = shape[:axis] + (1,) + shape[axis + 1 :]
    out_block = out[:-2] + (rows // cuts, cols)
    lead = len(shape) - 2

    def kernel(k, g, *rest):
        stay, go = rest[-2:]
        for side, ref in ((0, stay), (1, go)):
            at = tuple(pl.ds(side, 1) if d == axis else slice(None) for d in range(lead))
            ref[...] = (k[at].astype(F32) + g[at].astype(F32)).astype(BF)

    index = lambda i: (0,) * lead + (i, 0)
    return pl.pallas_call(
        kernel,
        grid=(cuts,),
        in_specs=[pl.BlockSpec(block, index)] * 2 + [ANY] * len(after),
        out_specs=[pl.BlockSpec(out_block, index)] * 2,
        out_shape=[jax.ShapeDtypeStruct(out, BF)] * 2,
        compiler_params=pltpu.CompilerParams(vmem_limit_bytes=LIMIT),
        cost_estimate=BACKWARD,
    )(keep, got, *after)


def last_combine(terms, axis, rows, after):
    ins, specs, widths = [], [], []
    for t in terms:
        ins += [t.keep, t.got]
        widths.append(t.keep.shape[-1] * (t.keep.shape[-2] // rows))
    total = sum(widths)
    n_in = len(ins)

    def kernel(*refs):
        stay, go = refs[-2:]
        at = 0
        for j, t in enumerate(terms):
            k, g = refs[2 * j], refs[2 * j + 1]
            lead = k.ndim - 2
            cols = k.shape[-1]
            for block in range(k.shape[-2] // rows):
                for side, ref in ((0, stay), (1, go)):
                    idx = tuple(side if d == axis else 0 for d in range(lead)) + (pl.ds(block * rows, rows),)
                    ref[:, at : at + cols] = (k[idx].astype(F32) + g[idx].astype(F32)).astype(BF)
                at += cols

    whole = [pl.BlockSpec(v.shape, lambda n=v.ndim: (0,) * n) for v in ins]
    return pl.pallas_call(
        kernel,
        in_specs=whole + [ANY] * len(after),
        out_specs=[pl.BlockSpec((rows, total), lambda: (0, 0))] * 2,
        out_shape=[jax.ShapeDtypeStruct((rows, total), BF)] * 2,
        compiler_params=pltpu.CompilerParams(vmem_limit_bytes=SMALL_LIMIT),
        cost_estimate=BACKWARD,
    )(*ins, *after)


def pick(flag, a, b):
    return jnp.where(flag == 0, a, b)


def small_call(kernel, where, ins, shapes, after, grid=None):
    n = len(ins)

    def body(where_ref, *refs):
        kernel(where_ref, refs[:n], refs[n + len(after) :])

    return pl.pallas_call(
        body,
        grid_spec=pltpu.PrefetchScalarGridSpec(
            num_scalar_prefetch=1,
            grid=(1,),
            in_specs=[pl.BlockSpec(v.shape, lambda i, w, n=v.ndim: (0,) * n) for v in ins] + [ANY] * len(after),
            out_specs=[pl.BlockSpec(s, lambda i, w, n=len(s): (0,) * n) for s, _ in shapes],
        ),
        out_shape=[jax.ShapeDtypeStruct(s, t) for s, t in shapes],
        compiler_params=pltpu.CompilerParams(vmem_limit_bytes=SMALL_LIMIT),
        cost_estimate=BACKWARD,
    )(where, *ins, *after)


class Ending:
    def __init__(self, plan, where, terms, axis, rows, tail, after):
        self.plan, self.where, self.rows, self.tail = plan, where, rows, tail
        self.keep, self.sent = last_combine(terms, axis, rows, after)
        self.got = plan.flip(self.sent, axis)

    def core(self, after):
        rows, tail = self.rows // 2, self.tail
        cols = self.cols = self.keep.shape[1] - tail

        def kernel(where, ins, outs):
            c = where[0]
            for ref, row in ((outs[0], c), (outs[1], 1 - c)):
                at = pl.ds(pl.multiple_of(row * rows, 16), rows)
                ref[:, :cols] = (ins[0][at, :cols].astype(F32) + ins[1][at, :cols].astype(F32)).astype(BF)
            if tail:
                for g in range(2):
                    at = pl.ds(g * rows, rows)
                    piece = ins[0][at, cols:].astype(F32) + ins[1][at, cols:].astype(F32)
                    outs[0][:, cols + g * tail : cols + (g + 1) * tail] = piece.astype(BF)

        shapes = [((rows, cols + 2 * tail), BF), ((rows, cols), BF)]
        self.mine, sent = small_call(kernel, self.where, [self.keep, self.got], shapes, after)
        self.came = self.plan.core(sent)
        return sent

    def rep(self, after):
        rows, cols, tail = self.rows // 2, self.cols, self.tail

        def kernel(where, ins, outs):
            outs[0][:, :cols] = ins[0][:, :cols]
            outs[0][:, cols : 2 * cols] = ins[1][...]
            if tail:
                outs[0][:, 2 * cols :] = ins[0][:, cols:]

        shapes = [((rows, 2 * cols + 2 * tail), BF)]
        v = small_call(kernel, self.where, [self.mine, self.came], shapes, after)[0]
        self.pair = [v, self.plan.flip(v, 0)] if self.plan.ny == 2 else [lax.psum(v, "rep")]
        return v


class ChipEnding:
    def __init__(self, plan, where, term):
        self.plan, self.where = plan, where
        groups = [[2 * chip + c for chip in range(plan.chips)] for c in range(2)]
        self.term = lax.psum_scatter(term, "shard", scatter_dimension=0, axis_index_groups=groups, tiled=True)

    def core(self, after):
        rows, cols = self.term.shape
        part = rows // 4

        def kernel(where, ins, outs):
            c = where[0]
            for ref, row in ((outs[0], c), (outs[1], 1 - c)):
                for k in range(2):
                    at = pl.ds(pl.multiple_of((2 * k + row) * part, 16), part)
                    ref[k * part : (k + 1) * part] = ins[0][at]

        shapes = [((rows // 2, cols), BF)] * 2
        self.mine, sent = small_call(kernel, self.where, [self.term], shapes, after)
        self.came = self.plan.core(sent)
        return sent

    def rep(self, after):
        rows, cols = self.mine.shape

        def kernel(where, ins, outs):
            outs[0][:rows] = ins[0][...]
            outs[0][rows:] = ins[1][...]

        v = small_call(kernel, self.where, [self.mine, self.came], [((2 * rows, cols), BF)], after)[0]
        self.pair = [v, self.plan.flip(v, 0)] if self.plan.ny == 2 else [lax.psum(v, "rep")]
        return v


def place_grads(plan, where, layer, layers, end2, rest, sizes, before, after):
    deep, width, ff, quarters = sizes
    n, ny, halves = plan.shards, plan.ny, quarters // 2
    wide, half_ff = 3 * width // 2, ff // 2
    cols = rest.cols
    fused = bool(rest.tail)
    ins = end2.pair + rest.pair

    def kernel(where_ref, *refs):
        refs_in = refs[: 2 * ny]
        outs = refs[-(4 if fused else 3) :]
        c, y = where_ref[0], where_ref[2]

        def source(p, q, at, size):
            step = (at // 128) * 128
            span = (at + size - step + 127) // 128 * 128
            first = pl.multiple_of(jnp.where(p == c, 0, cols) + step, 128)
            v = refs_in[ny][:, pl.ds(first, span)]
            if ny == 2:
                v = jnp.where(y == q, v, refs_in[ny + 1][:, pl.ds(first, span)])
            return v[:, at - step : at - step + size].astype(F32)

        def core_columns(p, at, size, total, first):
            part = total // ny
            return source(p, at // part, first + at % part, size)

        for k in range(3 * HEADS // 2):
            pieces = [core_columns(p, k * HEAD_DIM, HEAD_DIM, wide, 0) for p in range(2)]
            outs[0][0, :, k * 2 * HEAD_DIM : (k + 1) * 2 * HEAD_DIM] = jnp.concatenate(pieces, axis=1)
        for k in range(n):
            pieces = []
            for p in range(2):
                for h in range(halves):
                    pieces.append(core_columns(p, (h * n + k) * deep, deep, half_ff, wide // ny))
            outs[1][0, :, k * quarters * deep : (k + 1) * quarters * deep] = jnp.concatenate(pieces, axis=1)
        part = width // ny
        for p in range(2):
            at = pl.ds(pl.multiple_of(jnp.where(p == c, 0, halves * deep), 16), halves * deep)
            v = refs_in[0][at].astype(F32)
            if ny == 2:
                v = v + refs_in[1][at].astype(F32)
            outs[2][0, p * halves * deep : (p + 1) * halves * deep] = v
        if fused:
            for q in range(ny):
                v = refs_in[ny][:, 2 * cols :]
                if ny == 2:
                    v = jnp.where(y == q, v, refs_in[ny + 1][:, 2 * cols :])
                outs[3][0, :, q * part : (q + 1) * part] = v.astype(F32)

    shapes = [(deep, 3 * width), (deep, ff), (quarters * deep, width)] + ([(deep, width)] if fused else [])
    in_specs = [pl.BlockSpec(v.shape, lambda i, w: (0, 0)) for v in ins]
    args = list(ins) + list(before or []) + list(after)
    n_before = len(before or [])
    return pl.pallas_call(
        kernel,
        grid_spec=pltpu.PrefetchScalarGridSpec(
            num_scalar_prefetch=1,
            grid=(1,),
            in_specs=in_specs + [ANY] * (n_before + len(after)),
            out_specs=[pl.BlockSpec((1,) + s, lambda i, w: (layer, 0, 0)) for s in shapes],
        ),
        out_shape=[jax.ShapeDtypeStruct((layers,) + s, F32) for s in shapes],
        input_output_aliases={1 + len(ins) + k: k for k in range(n_before)},
        compiler_params=pltpu.CompilerParams(vmem_limit_bytes=LIMIT),
        cost_estimate=BACKWARD,
    )(where, *args)


def pack(plan, where, layer, qkv, proj, fc1, fc2, extra, after):
    deep, width = proj.shape[1:]
    ff, n = fc1.shape[2], plan.shards
    quarters = fc2.shape[1] // deep
    halves = quarters // 2
    each = halves // plan.ny
    ins = [qkv, proj, fc1, fc2] + ([extra] if extra is not None else [])
    total = 4 * width + ff + 2 * each * width + (extra.shape[1] if extra is not None else 0)

    def kernel(where_ref, *refs):
        out = refs[-1]

        def lay(at, pieces):
            held, wide = [], 0
            for p in pieces:
                held.append(p)
                wide += p.shape[1]
                if wide % 128 == 0:
                    out[:, at : at + wide] = held[0] if len(held) == 1 else jnp.concatenate(held, axis=1)
                    at, held, wide = at + wide, [], 0

        for p in range(2):
            cols = [k * 2 * HEAD_DIM + p * HEAD_DIM for k in range(3 * HEADS // 2)]
            lay(p * (3 * width // 2), [refs[0][0, :, k : k + HEAD_DIM] for k in cols])
        out[:, 3 * width : 4 * width] = refs[1][0]
        cols = [s * quarters * deep + k * deep for k in range(quarters) for s in range(n)]
        lay(4 * width, [refs[2][0, :, k : k + deep] for k in cols])
        at = 4 * width + ff
        for p in range(2):
            for k in range(each):
                row = (p * halves + k) * deep + where_ref[3] * deep
                out[:, at : at + width] = refs[3][0, pl.ds(pl.multiple_of(row, 16), deep)]
                at += width
        if extra is not None:
            out[:, at:] = refs[4][...]

    specs = [pl.BlockSpec((1,) + v.shape[1:], lambda i, w: (layer, 0, 0)) for v in ins[:4]]
    specs += [pl.BlockSpec(v.shape, lambda i, w: (0, 0)) for v in ins[4:]]
    return pl.pallas_call(
        kernel,
        grid_spec=pltpu.PrefetchScalarGridSpec(
            num_scalar_prefetch=1,
            grid=(1,),
            in_specs=specs + [ANY] * len(after),
            out_specs=pl.BlockSpec((deep, total), lambda i, w: (0, 0)),
        ),
        out_shape=jax.ShapeDtypeStruct((deep, total), BF),
        compiler_params=pltpu.CompilerParams(vmem_limit_bytes=LIMIT),
        cost_estimate=FORWARD,
    )(where, *ins, *after)


def per_device(
    plan,
    tokens,
    kept,
    attn_gain,
    attn_shift,
    qkv_weight,
    qv_bias,
    proj_weight,
    proj_bias,
    mlp_gain,
    mlp_shift,
    fc1_weight,
    fc1_bias,
    fc2_weight,
    fc2_bias,
    cotangent,
):
    images, slots, width = tokens.shape
    layers = attn_gain.shape[0]
    rows = images * slots
    n = plan.shards
    deep = qkv_weight.shape[1]
    shard = lax.axis_index("shard")
    c, chip, y = lax.rem(shard, 2), shard // 2, lax.axis_index("rep")
    where = jnp.stack([c, chip, y, y if plan.ny == 2 else 0 * y]).astype(jnp.int32)
    ff = fc2_weight.shape[1] * n
    quarters = fc2_weight.shape[1] // deep
    wide, half_width, half_ff = 3 * width // 2, width // 2, ff // 2
    half_heads = HEADS // 2

    small = jnp.concatenate(
        [attn_gain, attn_shift, qv_bias, proj_bias, mlp_gain, mlp_shift, fc1_bias, fc2_bias], axis=1
    )
    sizes = [v.shape[1] for v in (attn_gain, attn_shift, qv_bias, proj_bias, mlp_gain, mlp_shift, fc1_bias, fc2_bias)]
    lines = small.size // 128
    extra = jnp.pad(small.reshape(lines, 128), ((0, deep - lines), (0, 0)))

    halves = quarters // 2
    lead = 4 * width
    block = n * deep
    each = halves // plan.ny

    gathered, done = [], ()
    for layer in range(layers):
        shards = (qkv_weight, proj_weight, fc1_weight, fc2_weight)
        done = (pack(plan, where, layer, *shards, None if layer else extra, done),)
        gathered.append(lax.all_gather(done[0], "shard", axis=0, tiled=True))
    at_fc1, at_fc2 = lead // block, (lead + ff) // block
    mlp_parts = []
    for layer in range(layers):
        found = {"fc1": [(gathered[layer], ("quarter", block, (at_fc1, halves, k))) for k in range(halves)]}
        found["fc2"] = [(gathered[layer], columns(block, at_fc2 + k, each)) for k in range(each)]
        if plan.ny == 2:
            found["sent"], found["came"] = (), ()
            for k in range(1):
                mine = lax.dynamic_slice(
                    gathered[layer], (0, (at_fc2 + c) * block), (block, block)
                )
                found["sent"] += (mine,)
                found["came"] += (plan.flip(mine, 0),)
                found["fc2"].append((found["came"][k], None))
        mlp_parts.append(found)

    def weight_of(layer, name):
        if name == "qkv":
            return [(gathered[layer], columns(wide, 0, 1))]
        if name == "proj":
            return [(gathered[layer], ("heads", width, 3))]
        return mlp_parts[layer][name]

    every = gathered[0].reshape(n, deep, -1)[:, :lines, lead + ff + 2 * each * block :]
    every = every.reshape(n, layers, small.shape[1]).astype(F32)
    vecs = []
    for layer in range(layers):
        at, d = 0, {}
        for name, size in zip(SMALL, sizes):
            d[name] = every[:, layer, at : at + size].reshape(1, n * size)
            at += size
        q = d["qvb"].reshape(2 * half_heads, 2, HEAD_DIM)
        q = pick(c, q[:, 0], q[:, 1]).reshape(2, half_width)
        d["qvb_c"] = jnp.stack([q[0], jnp.zeros_like(q[0]), q[1]]).reshape(1, wide)
        f = d["f1b"].reshape(n, 2, halves, deep).transpose(1, 2, 0, 3).reshape(2, halves, block)
        f = pick(c, f[0], f[1])
        if plan.ny == 2:
            f = pick(y, f, f[::-1])
        d["f1b_c"] = f.reshape(1, half_ff)
        vecs.append(d)

    kept_oth = plan.core(kept)
    state = tokens.astype(F32).reshape(rows, width)
    live = lax.broadcasted_iota(jnp.int32, (images, slots), 1) < BUFFER + kept[:, None]
    grad = jnp.where(live[:, :, None], cotangent.astype(F32), 0.0).reshape(rows, width)
    low_own = grad.astype(BF)
    low_oth = plan.core(low_own)
    first_own = norm_rows(state, vecs[0]["ag"], vecs[0]["as"]).astype(BF)

    f32_rows, low_rows = ("rows", (rows, width), F32), ("rows", (rows, width), BF)
    wide_rows, ff_rows = ("rows", (rows, wide), BF), ("rows", (rows, half_ff), BF)
    att_outs = [("image", (images, half_heads, slots, slots), BF), ("rows", (rows, half_width), BF)]
    full_sums = ("full", (8, width), F32)

    def call(body, layer, own, names, blocked, whole, outs, after=(), cost=None):
        chosen = [weight_of(layer, name) for name in names]
        k = kept if own else kept_oth
        return row_call(body, where, k, chosen, blocked, whole, outs, images, slots, after, cost or (BACKWARD if after else FORWARD))

    saved = []
    for layer in range(layers):
        v = vecs[layer]
        first_oth = plan.core(first_own)
        sent, came = mlp_parts[layer].get("sent", ()), mlp_parts[layer].get("came", ())
        proj_oth = call(qkv_body, layer, 0, ["qkv"], [first_oth], [v["qvb_c"]], [wide_rows], sent, FORWARD)[0]
        probs_oth, att_oth, part = call(attend_other, layer, 0, ["proj"], [proj_oth], [], att_outs + [f32_rows])
        part = plan.core(part)
        proj_own = call(qkv_body, layer, 1, ["qkv"], [first_own], [v["qvb_c"]], [wide_rows])[0]
        probs_own, att_own, middle, second_own = call(
            attend_own, layer, 1, ["proj"], [proj_own, part, state], [v["pb"], v["mg"], v["ms"]], att_outs + [f32_rows, low_rows])
        second_oth = plan.core(second_own)
        hid_oth, slope_oth = call(up_body, layer, 0, ["fc1"], [second_oth], [v["f1b_c"]], [ff_rows] * 2)
        if layer + 1 < layers:
            part = call(down_other, layer, 0, ["fc2"], [hid_oth], [], [f32_rows])[0]
            part = plan.core(part)
        hid_own, slope_own = call(up_body, layer, 1, ["fc1"], [second_own], [v["f1b_c"]], [ff_rows] * 2)
        saved.append(
            dict(
                state=state,
                first=(first_own, first_oth),
                proj=(proj_own, proj_oth),
                probs=(probs_own, probs_oth),
                att=(att_own, att_oth),
                middle=middle,
                second=(second_own, second_oth),
                hid=(hid_own, hid_oth),
                slope=(slope_own, slope_oth),
            )
        )
        if layer + 1 < layers:
            w = vecs[layer + 1]
            state, first_own = call(
                down_own, layer, 1, ["fc2"], [hid_own, part, middle], [v["f2b"], w["ag"], w["as"]], [f32_rows, low_rows])

    axes = list(range(1 if plan.ny == 1 else 0, plan.bits + 1))
    last_axis, z_axis, x_axis = 1, plan.bits - 1, plan.bits
    y_axis = 0 if plan.ny == 2 else 2
    orders_f1 = [[y_axis, x_axis, z_axis]] * layers
    orders_q = [[[z_axis, y_axis, x_axis], [y_axis, z_axis, x_axis]]] + [[[x_axis, z_axis, y_axis]]] * (layers - 1)
    own_rows = 2 * deep
    tail = width // plan.ny * HEAD_DIM // own_rows
    fused = n == HEADS
    tail = tail if fused else 0
    big = [[None] * 4 for _ in range(layers)]
    sums = [None] * layers
    f2b_sum = jnp.sum(low_own.astype(F32), axis=0, keepdims=True)

    def end_rest(layer, prev):
        group = terms["q", layer] + [terms["f1", layer]]
        ends["rest", layer] = Ending(plan, where, group, last_axis, own_rows, tail, prev)
        return (ends["rest", layer].sent,)

    def place(layer, before, prev):
        return place_grads(
            plan, where, layer, layers, ends["f2", layer], ends["rest", layer], (deep, width, ff, quarters), before, prev
        )

    ends = {}
    prev = (hid_own,) + mlp_parts[layers - 1].get("came", ())
    terms = {}
    for layer in reversed(range(layers)):
        v, s = vecs[layer], saved[layer]
        top = layer == layers - 1

        def grad_fc2(prev):
            term = chip_grad(plan, where, s["hid"], (low_own, low_oth), 2, prev)
            ends["f2", layer] = ChipEnding(plan, where, term)
            return (term,)

        if top:
            prev = grad_fc2(prev)
        pre_oth, part = call(
            mlp_back_other, layer, 0, ["fc2", "fc1"], [low_oth, s["slope"][1]], [], [ff_rows, f32_rows], prev
        )
        part = plan.core(part)
        prev = (pre_oth,)
        if top:
            last_part = call(down_other, layer, 0, ["fc2"], [s["hid"][1]], [], [f32_rows], prev)[0]
            prev = (last_part,)
            last_part = plan.core(last_part)
        else:
            prev = grad_fc2(prev)
            prev += (terms["f1", layer + 1].step(prev[:1]),)
        pre_own, mid_grad, branch_own, sum1 = call(
            mlp_back_own,
            layer,
            1,
            ["fc2", "fc1"],
            [low_own, s["slope"][0], part, s["middle"], grad],
            [v["mg"]],
            [ff_rows, f32_rows, low_rows, full_sums],
            prev,
        )
        branch_oth = plan.core(branch_own)
        prev = (branch_own,)
        if not top:
            prev += (terms["q", layer + 1][0].step(prev),)
        res1 = weight_grad(
            plan, where, s["second"], (pre_own, pre_oth), 1, orders_f1[layer][0], sums=True, extra=tail, relative=True, after=prev
        )
        prev = tuple(res1[:1]) + ((last_part,) if top else ())
        if not top:
            prev += (terms["q", layer + 1][0].step(prev[:1]),)
            prev += (terms["f1", layer + 1].step(prev[:1]),)
            prev += (ends["f2", layer + 1].core(prev[:1]),)
        dproj_oth, part = call(
            attend_back_other,
            layer,
            0,
            ["proj", "qkv"],
            [branch_oth, s["proj"][1], s["probs"][1]],
            [],
            [wide_rows, f32_rows],
            prev,
        )
        part = plan.core(part)
        prev = (dproj_oth,)
        keep, send = res1[:2]
        if fused:
            keep, send = proj_grad_into(
                plan, where, s["att"], (branch_own, branch_oth), orders_f1[layer][0], keep, send, prev
            )
        else:
            term = t_dot(s["att"][0], branch_own) + t_dot(s["att"][1], branch_oth)
            term = term.astype(BF).reshape(half_heads, HEAD_DIM, width)
            none = jnp.zeros_like(term)
            term = jnp.stack([pick(c, term, none), pick(c, none, term)], axis=1).reshape(width, width)
            term = lax.psum_scatter(term, "shard", scatter_dimension=0, tiled=True)
            big[layer][1] = lax.psum(term, "rep").astype(F32)
        terms["f1", layer] = Term(plan, keep, send, orders_f1[layer])
        prev = (send,)
        if not top:
            prev += (ends["f2", layer + 1].rep(prev[:1]),)
        dproj_own, grad, low_own, sum2 = call(
            attend_back_own,
            layer,
            1,
            ["proj", "qkv"],
            [branch_own, s["proj"][0], s["probs"][0], part, s["state"], mid_grad],
            [v["ag"]],
            [wide_rows, f32_rows, low_rows, full_sums],
            prev,
        )
        prev = (dproj_own,)
        if layer:
            low_oth = plan.core(low_own)
        if not top:
            prev += end_rest(layer + 1, prev[:1])
        pairs, q_sums = parted_grad(
            plan, where, s["first"], (dproj_own, dproj_oth), [order[0] for order in orders_q[layer]], prev
        )
        terms["q", layer] = [Term(plan, *pair, order) for pair, order in zip(pairs, orders_q[layer])]
        prev = (pairs[0][1],)
        q = q_sums.reshape(3, half_heads, 1, HEAD_DIM)
        q = jnp.concatenate([q[:1], q[2:]])
        none = jnp.zeros_like(q)
        q = jnp.concatenate([pick(c, q, none), pick(c, none, q)], axis=2)
        f = res1[2].reshape(halves, block)
        if plan.ny == 2:
            f = pick(y, f, f[::-1])
        none = jnp.zeros_like(f)
        f = jnp.concatenate([pick(c, f, none), pick(c, none, f)], axis=0)
        f = f.reshape(quarters, n, deep).swapaxes(0, 1)
        full = {"ag": sum2[0], "as": sum2[1], "qvb": q, "pb": sum1[2], "mg": sum1[0], "ms": sum1[1], "f1b": f, "f2b": f2b_sum}
        f2b_sum = sum2[2]
        vec = jnp.concatenate([full[name].reshape(n, -1) for name in SMALL], axis=1)
        sums[layer] = vec

    vec = jnp.concatenate(sums, axis=0).reshape(layers, n, -1)
    got_vec = plan.core(vec)
    vec_axes = list(axes)

    def step_vec(prev):
        nonlocal vec, got_vec

        def kernel(where, ins, outs):
            outs[0][...] = ins[0][...] + ins[1][...]

        vec = small_call(kernel, where, [vec, got_vec], [(vec.shape, F32)], prev)[0]
        got_vec = plan.flip(vec, vec_axes.pop(0)) if vec_axes else None
        return (vec,)

    prev += (terms["f1", 0].step(prev),)
    w = layers - 1
    mixed = call(
        down_last, w, 1, ["fc2"], [saved[w]["hid"][0], last_part, saved[w]["middle"]], [vecs[w]["f2b"]], [low_rows], prev
    )[0]
    qa, qb = terms["q", 0]
    prev = (ends["rest", 1].core((mixed,)),)
    prev = (qa.step(prev),)
    prev = (qb.step(prev + (ends["rest", 1].came,)),)
    prev = step_vec(prev)
    prev = (qa.step(prev),)
    prev = (terms["f1", 0].step(prev),)
    prev = (ends["f2", 0].core(prev),)
    prev = (qb.step(prev),)
    prev = step_vec(prev)
    prev = end_rest(0, prev)
    prev = (ends["rest", 1].rep(prev),)
    prev = (ends["f2", 0].rep(prev),)
    prev = step_vec(prev)
    placed = place(1, None, prev)
    prev = (placed[0],)
    prev = (ends["rest", 0].core(prev + tuple(ends["f2", 0].pair[1:])),)
    prev = step_vec(prev)
    prev = (ends["rest", 0].rep(prev),)
    while got_vec is not None:
        prev = step_vec(prev)
    placed = place(0, placed, prev)
    if plan.ny == 1:
        vec = lax.psum(vec, "rep")
    vec = lax.dynamic_slice_in_dim(vec, shard, 1, axis=1)[:, 0]
    out, at = {}, 0
    for name, size in zip(SMALL, sizes):
        out[name] = vec[:, at : at + size]
        at += size
    qkv_g, fc1_g, fc2_g = placed[:3]
    proj_g = placed[3] if fused else jnp.stack([big[layer][1] for layer in range(layers)])
    return (
        mixed.reshape(images, slots, width),
        grad.reshape(images, slots, width),
        out["ag"],
        out["as"],
        qkv_g,
        out["qvb"],
        proj_g,
        out["pb"],
        out["mg"],
        out["ms"],
        fc1_g,
        out["f1b"],
        fc2_g,
        out["f2b"],
    )


def solution(mesh):
    rows = P(("shard", "rep"), None, None)
    vec = P(None, "shard")
    mat = P(None, "shard", None)
    return jax.shard_map(
        partial(per_device, Plan(mesh)),
        mesh=mesh,
        in_specs=(rows, P(("shard", "rep")), vec, vec, mat, vec, mat, vec, vec, vec, mat, vec, mat, vec, rows),
        out_specs=(rows, rows, vec, vec, mat, vec, mat, vec, vec, vec, mat, vec, mat, vec),
        check_vma=False,
    )
```

```python
from functools import partial

import jax
import jax.numpy as jnp
from jax import lax
from jax.experimental import pallas as pl
from jax.experimental.pallas import tpu as pltpu
from jax.sharding import PartitionSpec as P

HEADS = 16
HEAD_DIM = 64
BUFFER = 64
EPS = 1e-06
SCALE = HEAD_DIM ** (-0.5)
AX = ("shard", "rep")
BF = jnp.bfloat16
F32 = jnp.float32
LIMIT = 60 * 2**20
SMALL_LIMIT = 16 * 2**20
ONCE = pl.Buffered(1)
ANY = pl.BlockSpec(memory_space=pl.ANY)
FORWARD = pl.CostEstimate(flops=10**7, bytes_accessed=0, transcendentals=0)
BACKWARD = pl.CostEstimate(flops=10**9 * 30, bytes_accessed=0, transcendentals=0)
SMALL = ("ag", "as", "qvb", "pb", "mg", "ms", "f1b", "f2b")


class Plan:
    def __init__(self, mesh):
        self.shards = mesh.shape["shard"]
        self.rep = mesh.shape["rep"]
        self.chips = self.shards // 2
        self.ny = 2 if self.rep == 2 else 1
        self.bits = self.chips.bit_length() - 1

    def swap(self, v, flip_shard, flip_rep=0):
        pairs = []
        for s in range(self.shards):
            for y in range(self.rep):
                pairs.append((s * self.rep + y, (s ^ flip_shard) * self.rep + (y ^ flip_rep)))
        return lax.ppermute(v, AX, pairs)

    def core(self, v):
        return self.swap(v, 1)

    def flip(self, v, axis):
        if axis == 0:
            return self.swap(v, 0, 1)
        return self.swap(v, 2 << (self.bits - axis))


def dot(x, w):
    return lax.dot_general(x, w, (((1,), (0,)), ((), ())), preferred_element_type=F32)


def dot_t(x, w):
    return lax.dot_general(x, w, (((1,), (1,)), ((), ())), preferred_element_type=F32)


def t_dot(x, w):
    return lax.dot_general(x, w, (((0,), (0,)), ((), ())), preferred_element_type=F32)


def columns(width, first, stride):
    return ("columns", width, (first, stride))


def row_call(body, where, kept, weights, blocked, whole, outs, images, slots, after=(), cost=FORWARD):
    in_specs, args = [], []
    for v, pick_of in (part for w in weights for part in w):
        if pick_of is None:
            in_specs.append(pl.BlockSpec(v.shape, lambda i, w, k: (0, 0), pipeline_mode=ONCE))
            args.append(v)
            continue
        kind, width, first = pick_of
        if kind == "columns":
            spec = pl.BlockSpec((v.shape[0], width), lambda i, w, k, f=first: (0, f[0] + f[1] * w[0]), pipeline_mode=ONCE)
            in_specs.append(spec)
            args.append(v)
        elif kind == "quarter":
            at, stride, part = first
            spec = pl.BlockSpec(
                (v.shape[0], width),
                lambda i, w, k, f=(at, stride, part): (0, f[0] + f[1] * w[0] + jnp.bitwise_xor(f[2], w[3])),
                pipeline_mode=ONCE,
            )
            in_specs.append(spec)
            args.append(v)
        else:
            view = v.reshape(HEADS // 2, 2, HEAD_DIM, v.shape[1])
            spec = pl.BlockSpec((HEADS // 2, None, HEAD_DIM, width), lambda i, w, k, f=first: (0, w[0], 0, f), pipeline_mode=ONCE)
            in_specs.append(spec)
            args.append(view)
    for v in blocked:
        if v.ndim == 2:
            in_specs.append(pl.BlockSpec((slots, v.shape[1]), lambda i, *_: (i, 0)))
        else:
            in_specs.append(pl.BlockSpec((1,) + v.shape[1:], lambda i, *_, n=v.ndim: (i,) + (0,) * (n - 1)))
        args.append(v)
    for v in whole:
        in_specs.append(pl.BlockSpec(v.shape, lambda i, *_, n=v.ndim: (0,) * n))
        args.append(v)
    out_specs, out_shape = [], []
    for kind, shape, dtype in outs:
        out_shape.append(jax.ShapeDtypeStruct(shape, dtype))
        if kind == "rows":
            out_specs.append(pl.BlockSpec((slots, shape[1]), lambda i, *_: (i, 0)))
        elif kind == "image":
            out_specs.append(pl.BlockSpec((1,) + shape[1:], lambda i, *_, n=len(shape): (i,) + (0,) * (n - 1)))
        else:
            out_specs.append(pl.BlockSpec(shape, lambda i, *_, n=len(shape): (0,) * n))
    n_p, n_b, n_in = sum(len(w) for w in weights), len(blocked), len(args)
    in_specs += [ANY] * len(after)
    args += list(after)

    def kernel(where_ref, kept_ref, *refs):
        ins, res = refs[:n_in], refs[n_in + len(after) :]
        held, at = [], 0
        for w in weights:
            held.append(ins[at : at + len(w)])
            at += len(w)
        body(kept_ref, held, ins[n_p : n_p + n_b], ins[n_p + n_b : n_in], res)

    return pl.pallas_call(
        kernel,
        grid_spec=pltpu.PrefetchScalarGridSpec(
            num_scalar_prefetch=2, grid=(images,), in_specs=in_specs, out_specs=out_specs
        ),
        out_shape=out_shape,
        compiler_params=pltpu.CompilerParams(vmem_limit_bytes=LIMIT),
        cost_estimate=cost,
    )(where, kept, *args)


def normed_of(rows):
    width = rows.shape[-1]
    mean = jnp.sum(rows, axis=-1, keepdims=True) * (1.0 / width)
    centered = rows - mean
    spread = jnp.sum(centered * centered, axis=-1, keepdims=True) * (1.0 / width)
    factor = lax.rsqrt(spread + EPS)
    return centered * factor, factor


def norm_rows(rows, gain, shift):
    return normed_of(rows)[0] * gain + shift


def norm_back(dz, rows, gain):
    normed, factor = normed_of(rows)
    width = rows.shape[-1]
    prod = dz * normed
    dn = dz * gain
    m1 = jnp.sum(dn, axis=-1, keepdims=True) * (1.0 / width)
    m2 = jnp.sum(dn * normed, axis=-1, keepdims=True) * (1.0 / width)
    back = factor * (dn - m1 - normed * m2)
    return back, jnp.sum(prod, axis=0, keepdims=True), jnp.sum(dz, axis=0, keepdims=True)


def chunks(total, size):
    size = min(size, total)
    return [(k, size) for k in range(0, total, size)]


def qkv_body(kept, w, blocked, whole, outs):
    x = blocked[0][...]
    for k, n in chunks(outs[0].shape[1], 512):
        cols = pl.ds(k, n)
        outs[0][:, cols] = (dot(x, w[0][0][:, cols]) + whole[0][:, cols]).astype(BF)


def heads_of(ref):
    return ref[...].reshape(-1, ref.shape[-1])


def pairs_dot(x_ref, parts):
    total, at = None, 0
    for w_ref in parts:
        term = dot(x_ref[:, at : at + w_ref.shape[0]], w_ref[...])
        total = term if total is None else total + term
        at += w_ref.shape[0]
    return total


def attend(kept, proj_ref, probs_ref, att_ref):
    slots, third = proj_ref.shape[0], proj_ref.shape[1] // 3
    bound = BUFFER + kept[pl.program_id(0)]
    alive = lax.broadcasted_iota(jnp.int32, (slots, slots), 1) < bound
    outs = []
    for h in range(third // HEAD_DIM):
        lo = h * HEAD_DIM
        q = proj_ref[:, lo : lo + HEAD_DIM]
        k = proj_ref[:, third + lo : third + lo + HEAD_DIM]
        v = proj_ref[:, 2 * third + lo : 2 * third + lo + HEAD_DIM]
        s = jnp.where(alive, dot_t(q, k) * SCALE, -1e30)
        e = jnp.exp(s - jnp.max(s, axis=-1, keepdims=True))
        p = (e * (1.0 / jnp.sum(e, axis=-1, keepdims=True))).astype(BF)
        probs_ref[0, h] = p
        outs.append(dot(p, v).astype(BF))
        if h % 2:
            att_ref[:, lo - HEAD_DIM : lo + HEAD_DIM] = jnp.concatenate(outs, axis=1)
            outs = []


def attend_other(kept, w, blocked, whole, outs):
    attend(kept, blocked[0], outs[0], outs[1])
    outs[2][...] = dot(outs[1][...], heads_of(w[0][0]))


def attend_own(kept, w, blocked, whole, outs):
    attend(kept, blocked[0], outs[0], outs[1])
    middle = blocked[2][...] + (dot(outs[1][...], heads_of(w[0][0])) + blocked[1][...]) + whole[0][...]
    outs[2][...] = middle
    outs[3][...] = norm_rows(middle, whole[1][...], whole[2][...]).astype(BF)


def up_body(kept, w, blocked, whole, outs):
    x = blocked[0][...]
    for k, n in chunks(outs[0].shape[1], 256):
        cols = pl.ds(k, n)
        held = w[0][k // w[0][0].shape[1]]
        pre = dot(x, held[:, pl.ds(k % held.shape[1], n)]) + whole[0][:, cols]
        phi = 0.5 + 0.5 * lax.erf(pre * (2.0**-0.5))
        dens = jnp.exp(-0.5 * (pre * pre)) * 0.3989422804014327
        outs[0][:, cols] = (pre * phi).astype(BF)
        outs[1][:, cols] = (phi + pre * dens).astype(BF)


def down_other(kept, w, blocked, whole, outs):
    outs[0][...] = pairs_dot(blocked[0], w[0])


def down_own(kept, w, blocked, whole, outs):
    state = blocked[2][...] + (pairs_dot(blocked[0], w[0]) + blocked[1][...]) + whole[0][...]
    outs[0][...] = state
    outs[1][...] = norm_rows(state, whole[1][...], whole[2][...]).astype(BF)


def down_last(kept, w, blocked, whole, outs):
    state = blocked[2][...] + (pairs_dot(blocked[0], w[0]) + blocked[1][...]) + whole[0][...]
    alive = lax.broadcasted_iota(jnp.int32, state.shape, 0) < BUFFER + kept[pl.program_id(0)]
    outs[0][...] = jnp.where(alive, state, 0.0).astype(BF)


def mlp_back(w, blocked, outs):
    low = blocked[0][...]
    for k, n in chunks(outs[0].shape[1], 512):
        cols = pl.ds(k, n)
        held, first = w[0][0], 0
        for part in w[0][1:]:
            if k >= first + held.shape[0]:
                first += held.shape[0]
                held = part
        t = dot_t(low, held[pl.ds(k - first, n), :])
        outs[0][:, cols] = (t * blocked[1][:, cols].astype(F32)).astype(BF)
    total, at = None, 0
    for held in w[1]:
        term = dot_t(outs[0][:, at : at + held.shape[1]], held[...])
        total = term if total is None else total + term
        at += held.shape[1]
    return total


def mlp_back_other(kept, w, blocked, whole, outs):
    outs[1][...] = mlp_back(w, blocked, outs)


def add_sums(ref, rows):
    sums = jnp.concatenate(rows + [jnp.zeros((8 - len(rows), rows[0].shape[1]), F32)], axis=0)

    @pl.when(pl.program_id(0) == 0)
    def _():
        ref[...] = sums

    @pl.when(pl.program_id(0) != 0)
    def _():
        ref[...] += sums


def mlp_back_own(kept, w, blocked, whole, outs):
    dz = mlp_back(w, blocked, outs) + blocked[2][...]
    back, gain, shift = norm_back(dz, blocked[3][...], whole[0][...])
    grad = blocked[4][...] + back
    low = grad.astype(BF)
    outs[1][...] = grad
    outs[2][...] = low
    add_sums(outs[3], [gain, shift, jnp.sum(low.astype(F32), axis=0, keepdims=True)])


def attend_back(w, blocked, outs):
    branch, proj_ref, probs_ref = blocked[0], blocked[1], blocked[2]
    third = proj_ref.shape[1] // 3
    datt = dot_t(branch[...], heads_of(w[0][0])).astype(BF)
    pairs = [[], [], []]
    for h in range(third // HEAD_DIM):
        lo = h * HEAD_DIM
        q = proj_ref[:, lo : lo + HEAD_DIM]
        k = proj_ref[:, third + lo : third + lo + HEAD_DIM]
        v = proj_ref[:, 2 * third + lo : 2 * third + lo + HEAD_DIM]
        da = datt[:, lo : lo + HEAD_DIM]
        p = probs_ref[0, h]
        dp = dot_t(da, v)
        pf = p.astype(F32)
        ds = (pf * (dp - jnp.sum(pf * dp, axis=-1, keepdims=True))).astype(BF)
        pairs[0].append((dot(ds, k) * SCALE).astype(BF))
        pairs[1].append((t_dot(ds, q) * SCALE).astype(BF))
        pairs[2].append(t_dot(p, da).astype(BF))
        if h % 2:
            for j in range(3):
                at = j * third + lo - HEAD_DIM
                outs[0][:, at : at + 2 * HEAD_DIM] = jnp.concatenate(pairs[j], axis=1)
            pairs = [[], [], []]
    return dot_t(outs[0][...], w[1][0][...])


def attend_back_other(kept, w, blocked, whole, outs):
    outs[1][...] = attend_back(w, blocked, outs)


def attend_back_own(kept, w, blocked, whole, outs):
    dz = attend_back(w, blocked, outs) + blocked[3][...]
    back, gain, shift = norm_back(dz, blocked[4][...], whole[0][...])
    grad = blocked[5][...] + back
    outs[1][...] = grad
    low = grad.astype(BF)
    outs[2][...] = low
    add_sums(outs[3], [gain, shift, jnp.sum(low.astype(F32), axis=0, keepdims=True)])


def weight_grad(plan, where, xs, ys, groups, first, sums=False, extra=0, relative=False, after=()):
    depth, n_x = xs[0].shape
    cols = ys[0].shape[1]
    ny, chips, bits = plan.ny, plan.chips, plan.bits
    half = cols // ny
    size = half
    chunk = size if size <= 768 else 512
    steps = size // chunk
    rows = n_x // chips
    part = rows // groups
    dims = [ny] + [2] * bits
    dims[first] = 1
    block = [1] + dims[1:] + [rows, chunk]
    shape = dims + [rows, size + extra]
    n_after = len(after)

    def kernel(where_ref, xo, xt, yo, yt, *rest):
        rest = rest[n_after:]
        keep, send = rest[0], rest[1]
        flip, acc = rest[-2], rest[-1]
        step = pl.program_id(0)

        @pl.when(step == 0)
        def _():
            flip[:, :depth] = xo[...].T
            flip[:, depth:] = xt[...].T

        acc[...] = dot(flip[:, :depth], yo[...]) + dot(flip[:, depth:], yt[...])
        if sums:
            rest[2][...] = jnp.sum(yo[...].astype(F32), axis=0, keepdims=True) + jnp.sum(
                yt[...].astype(F32), axis=0, keepdims=True
            )

        def put(ref, r):
            at = [0]
            for k in range(1, bits + 1):
                at.append((r >> (bits - k)) & 1 if k != first else 0)
            chip = jnp.bitwise_xor(where_ref[1], r)
            for g in range(groups):
                start = pl.multiple_of(g * part * chips + chip * part, 16)
                place = g
                if groups == 2 and ny == 2:
                    place = jnp.bitwise_xor(g, where_ref[2])
                place = pl.multiple_of(place * part, 16)
                ref[tuple(at) + (pl.ds(place, part),)] = acc[pl.ds(start, part)].astype(BF)

        if first:
            for r in range(chips):
                put(send if (r >> (bits - first)) & 1 else keep, r)
        else:

            @pl.when(step < steps)
            def _():
                for r in range(chips):
                    put(keep, r)

            @pl.when(step >= steps)
            def _():
                for r in range(chips):
                    put(send, r)

    per_rep = half // chunk

    def column(i, w):
        own = w[2] if ny == 2 and not relative else 0
        return jnp.bitwise_xor(i // steps, own) * per_rep + i % steps

    zeros = (0,) * (bits + 1)
    x_spec = pl.BlockSpec((depth, n_x), lambda i, w: (0, 0), pipeline_mode=ONCE)
    y_spec = pl.BlockSpec((depth, chunk), lambda i, w: (0, column(i, w)))
    if first:
        specs = [pl.BlockSpec(block, lambda i, w: (i // steps,) + zeros + (i % steps,))] * 2
    else:
        specs = [
            pl.BlockSpec(block, lambda i, w: (0,) + zeros + (jnp.minimum(i, steps - 1),)),
            pl.BlockSpec(block, lambda i, w: (0,) + zeros + (jnp.maximum(i - steps, 0),)),
        ]
    out_shape = [jax.ShapeDtypeStruct(shape, BF)] * 2
    if sums:
        own = (lambda w: w[2]) if ny == 2 and not relative else (lambda w: 0)
        specs = specs + [
            pl.BlockSpec((1, chunk), lambda i, w: (0, jnp.bitwise_xor(i // steps, own(w)) * steps + i % steps))
        ]
        out_shape = out_shape + [jax.ShapeDtypeStruct((1, size * ny), F32)]
    return pl.pallas_call(
        kernel,
        grid_spec=pltpu.PrefetchScalarGridSpec(
            num_scalar_prefetch=1,
            grid=(ny * steps,),
            in_specs=[x_spec, x_spec, y_spec, y_spec] + [ANY] * n_after,
            out_specs=specs,
            scratch_shapes=[pltpu.VMEM((n_x, 2 * depth), BF), pltpu.VMEM((n_x, chunk), F32)],
        ),
        out_shape=out_shape,
        compiler_params=pltpu.CompilerParams(vmem_limit_bytes=LIMIT),
        cost_estimate=BACKWARD,
    )(where, *xs, *ys, *after)


def parted_grad(plan, where, xs, ys, firsts, after=()):
    depth, n_x = xs[0].shape
    cols = ys[0].shape[1]
    ny, chips, bits = plan.ny, plan.chips, plan.bits
    parts = len(firsts)
    chunk = cols // ny // parts
    rows = n_x // chips
    n_after = len(after)

    def kernel(where_ref, xo, xt, yo, yt, *rest):
        outs, sums, flip, acc = rest[n_after:-3], rest[-3], rest[-2], rest[-1]
        step = pl.program_id(0)

        @pl.when(step == 0)
        def _():
            flip[:, :depth] = xo[...].T
            flip[:, depth:] = xt[...].T

        acc[...] = dot(flip[:, :depth], yo[...]) + dot(flip[:, depth:], yt[...])
        total = jnp.sum(yo[...].astype(F32), axis=0, keepdims=True)
        sums[...] = total + jnp.sum(yt[...].astype(F32), axis=0, keepdims=True)

        def put(ref, r, first):
            at = [0]
            for k in range(1, bits + 1):
                at.append((r >> (bits - k)) & 1 if k != first else 0)
            start = pl.multiple_of(jnp.bitwise_xor(where_ref[1], r) * rows, 16)
            ref[tuple(at)] = acc[pl.ds(start, rows)].astype(BF)

        for p, first in enumerate(firsts):
            keep, send = outs[2 * p], outs[2 * p + 1]
            if first:

                @pl.when(step % parts == p)
                def _(keep=keep, send=send, first=first):
                    for r in range(chips):
                        put(send if (r >> (bits - first)) & 1 else keep, r, first)
            else:

                @pl.when(step == p)
                def _(keep=keep, first=first):
                    for r in range(chips):
                        put(keep, r, first)

                @pl.when(step == parts + p)
                def _(send=send, first=first):
                    for r in range(chips):
                        put(send, r, first)

    def column(i, w):
        own = w[2] if ny == 2 else 0
        return jnp.bitwise_xor(i // parts, own) * parts + i % parts

    zeros = (0,) * (bits + 2)
    x_spec = pl.BlockSpec((depth, n_x), lambda i, w: (0, 0), pipeline_mode=ONCE)
    y_spec = pl.BlockSpec((depth, chunk), lambda i, w: (0, column(i, w)))
    specs, shapes = [], []
    for first in firsts:
        dims = [ny] + [2] * bits
        dims[first] = 1
        block = [1] + dims[1:] + [rows, chunk]
        index = (lambda i, w: (i // parts,) + zeros) if first else (lambda i, w: (0,) + zeros)
        specs += [pl.BlockSpec(block, index)] * 2
        shapes += [jax.ShapeDtypeStruct(dims + [rows, chunk], BF)] * 2
    res = pl.pallas_call(
        kernel,
        grid_spec=pltpu.PrefetchScalarGridSpec(
            num_scalar_prefetch=1,
            grid=(ny * parts,),
            in_specs=[x_spec, x_spec, y_spec, y_spec] + [ANY] * n_after,
            out_specs=specs + [pl.BlockSpec((1, chunk), lambda i, w: (0, column(i, w)))],
            scratch_shapes=[pltpu.VMEM((n_x, 2 * depth), BF), pltpu.VMEM((n_x, chunk), F32)],
        ),
        out_shape=shapes + [jax.ShapeDtypeStruct((1, cols), F32)],
        compiler_params=pltpu.CompilerParams(vmem_limit_bytes=LIMIT),
        cost_estimate=BACKWARD,
    )(where, *xs, *ys, *after)
    return [res[2 * p : 2 * p + 2] for p in range(parts)], res[-1]


def chip_grad(plan, where, xs, ys, groups, after=()):
    depth, n_x = xs[0].shape
    cols = ys[0].shape[1]
    chips = plan.chips
    chunk = min(cols, 512)
    rows = n_x // chips
    part = rows // groups
    n_after = len(after)

    def kernel(where_ref, xo, xt, yo, yt, *rest):
        out, flip, acc = rest[n_after:]

        @pl.when(pl.program_id(0) == 0)
        def _():
            flip[:, :depth] = xo[...].T
            flip[:, depth:] = xt[...].T

        acc[...] = dot(flip[:, :depth], yo[...]) + dot(flip[:, depth:], yt[...])
        for g in range(groups):
            place = jnp.bitwise_xor(g, where_ref[3]) * part
            for chip in range(chips):
                at = pl.ds(pl.multiple_of(place + chip * rows, 16), part)
                first = (g * chips + chip) * part
                out[at, :] = acc[first : first + part].astype(BF)

    x_spec = pl.BlockSpec((depth, n_x), lambda i, w: (0, 0), pipeline_mode=ONCE)
    y_spec = pl.BlockSpec((depth, chunk), lambda i, w: (0, i))
    return pl.pallas_call(
        kernel,
        grid_spec=pltpu.PrefetchScalarGridSpec(
            num_scalar_prefetch=1,
            grid=(cols // chunk,),
            in_specs=[x_spec, x_spec, y_spec, y_spec] + [ANY] * n_after,
            out_specs=pl.BlockSpec((n_x, chunk), lambda i, w: (0, i)),
            scratch_shapes=[pltpu.VMEM((n_x, 2 * depth), BF), pltpu.VMEM((n_x, chunk), F32)],
        ),
        out_shape=jax.ShapeDtypeStruct((n_x, cols), BF),
        compiler_params=pltpu.CompilerParams(vmem_limit_bytes=LIMIT),
        cost_estimate=BACKWARD,
    )(where, *xs, *ys, *after)


def proj_grad_into(plan, where, xs, ys, first, keep, send, after=()):
    depth, n_x = xs[0].shape
    cols = ys[0].shape[1]
    ny, chips, bits = plan.ny, plan.chips, plan.bits
    half = cols // ny
    part = n_x // chips
    width = half * part // keep.shape[-2]
    stacked = half // width
    at_col = keep.shape[-1] // width - 1
    block = [1] + list(keep.shape[1:-1]) + [width]

    n_after = len(after)

    def kernel(where_ref, xo, xt, yo, yt, k_in, s_in, *rest):
        keep_ref, send_ref, acc = rest[n_after:]
        acc[...] = t_dot(xo[...], yo[...]) + t_dot(xt[...], yt[...])

        def put(ref, r):
            at = [0]
            for k in range(1, bits + 1):
                at.append((r >> (bits - k)) & 1 if k != first else 0)
            start = pl.multiple_of(jnp.bitwise_xor(where_ref[1], r) * part, 16)
            for g in range(stacked):
                piece = acc[pl.ds(start, part), g * width : (g + 1) * width]
                ref[tuple(at) + (pl.ds(g * part, part),)] = piece.astype(BF)

        if first:
            for r in range(chips):
                put(send_ref if (r >> (bits - first)) & 1 else keep_ref, r)
        else:

            @pl.when(pl.program_id(0) == 0)
            def _():
                for r in range(chips):
                    put(keep_ref, r)

            @pl.when(pl.program_id(0) != 0)
            def _():
                for r in range(chips):
                    put(send_ref, r)

    zeros = (0,) * (bits + 1)
    own = (lambda w: w[2]) if ny == 2 else (lambda w: 0)
    x_spec = pl.BlockSpec((depth, n_x), lambda i, w: (0, 0), pipeline_mode=ONCE)
    y_spec = pl.BlockSpec((depth, half), lambda i, w: (0, jnp.bitwise_xor(i, own(w))))
    spec = pl.BlockSpec(block, lambda i, w: (i if first else 0,) + zeros + (at_col,))
    return pl.pallas_call(
        kernel,
        grid_spec=pltpu.PrefetchScalarGridSpec(
            num_scalar_prefetch=1,
            grid=(ny,),
            in_specs=[x_spec, x_spec, y_spec, y_spec, ANY, ANY] + [ANY] * n_after,
            out_specs=[spec, spec],
            scratch_shapes=[pltpu.VMEM((n_x, half), F32)],
        ),
        out_shape=[jax.ShapeDtypeStruct(keep.shape, BF)] * 2,
        input_output_aliases={5: 0, 6: 1},
        compiler_params=pltpu.CompilerParams(vmem_limit_bytes=LIMIT),
        cost_estimate=BACKWARD,
    )(where, *xs, *ys, keep, send, *after)


class Term:
    def __init__(self, plan, keep, send, order):
        self.plan, self.keep, self.order = plan, keep, list(order)
        self.got = plan.flip(send, self.order.pop(0))

    def step(self, after):
        axis = self.order.pop(0)
        self.keep, send = combine(self.keep, self.got, axis, after)
        self.got = self.plan.flip(send, axis)
        return send


def combine(keep, got, axis, after):
    shape = keep.shape
    rows, cols = shape[-2:]
    cuts = 2
    block = shape[:-2] + (rows // cuts, cols)
    out = shape[:axis] + (1,) + shape[axis + 1 :]
    out_block = out[:-2] + (rows // cuts, cols)
    lead = len(shape) - 2

    def kernel(k, g, *rest):
        stay, go = rest[-2:]
        for side, ref in ((0, stay), (1, go)):
            at = tuple(pl.ds(side, 1) if d == axis else slice(None) for d in range(lead))
            ref[...] = (k[at].astype(F32) + g[at].astype(F32)).astype(BF)

    index = lambda i: (0,) * lead + (i, 0)
    return pl.pallas_call(
        kernel,
        grid=(cuts,),
        in_specs=[pl.BlockSpec(block, index)] * 2 + [ANY] * len(after),
        out_specs=[pl.BlockSpec(out_block, index)] * 2,
        out_shape=[jax.ShapeDtypeStruct(out, BF)] * 2,
        compiler_params=pltpu.CompilerParams(vmem_limit_bytes=LIMIT),
        cost_estimate=BACKWARD,
    )(keep, got, *after)


def last_combine(terms, axis, rows, after):
    ins, specs, widths = [], [], []
    for t in terms:
        ins += [t.keep, t.got]
        widths.append(t.keep.shape[-1] * (t.keep.shape[-2] // rows))
    total = sum(widths)
    n_in = len(ins)

    def kernel(*refs):
        stay, go = refs[-2:]
        at = 0
        for j, t in enumerate(terms):
            k, g = refs[2 * j], refs[2 * j + 1]
            lead = k.ndim - 2
            cols = k.shape[-1]
            for block in range(k.shape[-2] // rows):
                for side, ref in ((0, stay), (1, go)):
                    idx = tuple(side if d == axis else 0 for d in range(lead)) + (pl.ds(block * rows, rows),)
                    ref[:, at : at + cols] = (k[idx].astype(F32) + g[idx].astype(F32)).astype(BF)
                at += cols

    whole = [pl.BlockSpec(v.shape, lambda n=v.ndim: (0,) * n) for v in ins]
    return pl.pallas_call(
        kernel,
        in_specs=whole + [ANY] * len(after),
        out_specs=[pl.BlockSpec((rows, total), lambda: (0, 0))] * 2,
        out_shape=[jax.ShapeDtypeStruct((rows, total), BF)] * 2,
        compiler_params=pltpu.CompilerParams(vmem_limit_bytes=SMALL_LIMIT),
        cost_estimate=BACKWARD,
    )(*ins, *after)


def pick(flag, a, b):
    return jnp.where(flag == 0, a, b)


def small_call(kernel, where, ins, shapes, after, grid=None):
    n = len(ins)

    def body(where_ref, *refs):
        kernel(where_ref, refs[:n], refs[n + len(after) :])

    return pl.pallas_call(
        body,
        grid_spec=pltpu.PrefetchScalarGridSpec(
            num_scalar_prefetch=1,
            grid=(1,),
            in_specs=[pl.BlockSpec(v.shape, lambda i, w, n=v.ndim: (0,) * n) for v in ins] + [ANY] * len(after),
            out_specs=[pl.BlockSpec(s, lambda i, w, n=len(s): (0,) * n) for s, _ in shapes],
        ),
        out_shape=[jax.ShapeDtypeStruct(s, t) for s, t in shapes],
        compiler_params=pltpu.CompilerParams(vmem_limit_bytes=SMALL_LIMIT),
        cost_estimate=BACKWARD,
    )(where, *ins, *after)


class Ending:
    def __init__(self, plan, where, terms, axis, rows, tail, after):
        self.plan, self.where, self.rows, self.tail = plan, where, rows, tail
        self.keep, self.sent = last_combine(terms, axis, rows, after)
        self.got = plan.flip(self.sent, axis)

    def core(self, after):
        rows, tail = self.rows // 2, self.tail
        cols = self.cols = self.keep.shape[1] - tail

        def kernel(where, ins, outs):
            c = where[0]
            for ref, row in ((outs[0], c), (outs[1], 1 - c)):
                at = pl.ds(pl.multiple_of(row * rows, 16), rows)
                ref[:, :cols] = (ins[0][at, :cols].astype(F32) + ins[1][at, :cols].astype(F32)).astype(BF)
            if tail:
                for g in range(2):
                    at = pl.ds(g * rows, rows)
                    piece = ins[0][at, cols:].astype(F32) + ins[1][at, cols:].astype(F32)
                    outs[0][:, cols + g * tail : cols + (g + 1) * tail] = piece.astype(BF)

        shapes = [((rows, cols + 2 * tail), BF), ((rows, cols), BF)]
        self.mine, sent = small_call(kernel, self.where, [self.keep, self.got], shapes, after)
        self.came = self.plan.core(sent)
        return sent

    def rep(self, after):
        rows, cols, tail = self.rows // 2, self.cols, self.tail

        def kernel(where, ins, outs):
            outs[0][:, :cols] = ins[0][:, :cols]
            outs[0][:, cols : 2 * cols] = ins[1][...]
            if tail:
                outs[0][:, 2 * cols :] = ins[0][:, cols:]

        shapes = [((rows, 2 * cols + 2 * tail), BF)]
        v = small_call(kernel, self.where, [self.mine, self.came], shapes, after)[0]
        self.pair = [v, self.plan.flip(v, 0)] if self.plan.ny == 2 else [lax.psum(v, "rep")]
        return v


class ChipEnding:
    def __init__(self, plan, where, term):
        self.plan, self.where = plan, where
        groups = [[2 * chip + c for chip in range(plan.chips)] for c in range(2)]
        self.term = lax.psum_scatter(term, "shard", scatter_dimension=0, axis_index_groups=groups, tiled=True)

    def core(self, after):
        rows, cols = self.term.shape
        part = rows // 4

        def kernel(where, ins, outs):
            c = where[0]
            for ref, row in ((outs[0], c), (outs[1], 1 - c)):
                for k in range(2):
                    at = pl.ds(pl.multiple_of((2 * k + row) * part, 16), part)
                    ref[k * part : (k + 1) * part] = ins[0][at]

        shapes = [((rows // 2, cols), BF)] * 2
        self.mine, sent = small_call(kernel, self.where, [self.term], shapes, after)
        self.came = self.plan.core(sent)
        return sent

    def rep(self, after):
        rows, cols = self.mine.shape

        def kernel(where, ins, outs):
            outs[0][:rows] = ins[0][...]
            outs[0][rows:] = ins[1][...]

        v = small_call(kernel, self.where, [self.mine, self.came], [((2 * rows, cols), BF)], after)[0]
        self.pair = [v, self.plan.flip(v, 0)] if self.plan.ny == 2 else [lax.psum(v, "rep")]
        return v


def place_grads(plan, where, layer, layers, end2, rest, sizes, before, after):
    deep, width, ff, quarters = sizes
    n, ny, halves = plan.shards, plan.ny, quarters // 2
    wide, half_ff = 3 * width // 2, ff // 2
    cols = rest.cols
    fused = bool(rest.tail)
    ins = end2.pair + rest.pair

    def kernel(where_ref, *refs):
        refs_in = refs[: 2 * ny]
        outs = refs[-(4 if fused else 3) :]
        c, y = where_ref[0], where_ref[2]

        def source(p, q, at, size):
            step = (at // 128) * 128
            span = (at + size - step + 127) // 128 * 128
            first = pl.multiple_of(jnp.where(p == c, 0, cols) + step, 128)
            v = refs_in[ny][:, pl.ds(first, span)]
            if ny == 2:
                v = jnp.where(y == q, v, refs_in[ny + 1][:, pl.ds(first, span)])
            return v[:, at - step : at - step + size].astype(F32)

        def core_columns(p, at, size, total, first):
            part = total // ny
            return source(p, at // part, first + at % part, size)

        for k in range(3 * HEADS // 2):
            pieces = [core_columns(p, k * HEAD_DIM, HEAD_DIM, wide, 0) for p in range(2)]
            outs[0][0, :, k * 2 * HEAD_DIM : (k + 1) * 2 * HEAD_DIM] = jnp.concatenate(pieces, axis=1)
        for k in range(n):
            pieces = []
            for p in range(2):
                for h in range(halves):
                    pieces.append(core_columns(p, (h * n + k) * deep, deep, half_ff, wide // ny))
            outs[1][0, :, k * quarters * deep : (k + 1) * quarters * deep] = jnp.concatenate(pieces, axis=1)
        part = width // ny
        for p in range(2):
            at = pl.ds(pl.multiple_of(jnp.where(p == c, 0, halves * deep), 16), halves * deep)
            v = refs_in[0][at].astype(F32)
            if ny == 2:
                v = v + refs_in[1][at].astype(F32)
            outs[2][0, p * halves * deep : (p + 1) * halves * deep] = v
        if fused:
            for q in range(ny):
                v = refs_in[ny][:, 2 * cols :]
                if ny == 2:
                    v = jnp.where(y == q, v, refs_in[ny + 1][:, 2 * cols :])
                outs[3][0, :, q * part : (q + 1) * part] = v.astype(F32)

    shapes = [(deep, 3 * width), (deep, ff), (quarters * deep, width)] + ([(deep, width)] if fused else [])
    in_specs = [pl.BlockSpec(v.shape, lambda i, w: (0, 0)) for v in ins]
    args = list(ins) + list(before or []) + list(after)
    n_before = len(before or [])
    return pl.pallas_call(
        kernel,
        grid_spec=pltpu.PrefetchScalarGridSpec(
            num_scalar_prefetch=1,
            grid=(1,),
            in_specs=in_specs + [ANY] * (n_before + len(after)),
            out_specs=[pl.BlockSpec((1,) + s, lambda i, w: (layer, 0, 0)) for s in shapes],
        ),
        out_shape=[jax.ShapeDtypeStruct((layers,) + s, F32) for s in shapes],
        input_output_aliases={1 + len(ins) + k: k for k in range(n_before)},
        compiler_params=pltpu.CompilerParams(vmem_limit_bytes=LIMIT),
        cost_estimate=BACKWARD,
    )(where, *args)


def pack(plan, where, layer, qkv, proj, fc1, fc2, extra, after):
    deep, width = proj.shape[1:]
    ff, n = fc1.shape[2], plan.shards
    quarters = fc2.shape[1] // deep
    halves = quarters // 2
    each = halves // plan.ny
    ins = [qkv, proj, fc1, fc2] + ([extra] if extra is not None else [])
    total = 4 * width + ff + 2 * each * width + (extra.shape[1] if extra is not None else 0)

    def kernel(where_ref, *refs):
        out = refs[-1]

        def lay(at, pieces):
            held, wide = [], 0
            for p in pieces:
                held.append(p)
                wide += p.shape[1]
                if wide % 128 == 0:
                    out[:, at : at + wide] = held[0] if len(held) == 1 else jnp.concatenate(held, axis=1)
                    at, held, wide = at + wide, [], 0

        for p in range(2):
            cols = [k * 2 * HEAD_DIM + p * HEAD_DIM for k in range(3 * HEADS // 2)]
            lay(p * (3 * width // 2), [refs[0][0, :, k : k + HEAD_DIM] for k in cols])
        out[:, 3 * width : 4 * width] = refs[1][0]
        cols = [s * quarters * deep + k * deep for k in range(quarters) for s in range(n)]
        lay(4 * width, [refs[2][0, :, k : k + deep] for k in cols])
        at = 4 * width + ff
        for p in range(2):
            for k in range(each):
                row = (p * halves + k) * deep + where_ref[3] * deep
                out[:, at : at + width] = refs[3][0, pl.ds(pl.multiple_of(row, 16), deep)]
                at += width
        if extra is not None:
            out[:, at:] = refs[4][...]

    specs = [pl.BlockSpec((1,) + v.shape[1:], lambda i, w: (layer, 0, 0)) for v in ins[:4]]
    specs += [pl.BlockSpec(v.shape, lambda i, w: (0, 0)) for v in ins[4:]]
    return pl.pallas_call(
        kernel,
        grid_spec=pltpu.PrefetchScalarGridSpec(
            num_scalar_prefetch=1,
            grid=(1,),
            in_specs=specs + [ANY] * len(after),
            out_specs=pl.BlockSpec((deep, total), lambda i, w: (0, 0)),
        ),
        out_shape=jax.ShapeDtypeStruct((deep, total), BF),
        compiler_params=pltpu.CompilerParams(vmem_limit_bytes=LIMIT),
        cost_estimate=FORWARD,
    )(where, *ins, *after)


def per_device(
    plan,
    tokens,
    kept,
    attn_gain,
    attn_shift,
    qkv_weight,
    qv_bias,
    proj_weight,
    proj_bias,
    mlp_gain,
    mlp_shift,
    fc1_weight,
    fc1_bias,
    fc2_weight,
    fc2_bias,
    cotangent,
):
    images, slots, width = tokens.shape
    layers = attn_gain.shape[0]
    rows = images * slots
    n = plan.shards
    deep = qkv_weight.shape[1]
    shard = lax.axis_index("shard")
    c, chip, y = lax.rem(shard, 2), shard // 2, lax.axis_index("rep")
    where = jnp.stack([c, chip, y, y if plan.ny == 2 else 0 * y]).astype(jnp.int32)
    ff = fc2_weight.shape[1] * n
    quarters = fc2_weight.shape[1] // deep
    wide, half_width, half_ff = 3 * width // 2, width // 2, ff // 2
    half_heads = HEADS // 2

    small = jnp.concatenate(
        [attn_gain, attn_shift, qv_bias, proj_bias, mlp_gain, mlp_shift, fc1_bias, fc2_bias], axis=1
    )
    sizes = [v.shape[1] for v in (attn_gain, attn_shift, qv_bias, proj_bias, mlp_gain, mlp_shift, fc1_bias, fc2_bias)]
    lines = small.size // 128
    extra = jnp.pad(small.reshape(lines, 128), ((0, deep - lines), (0, 0)))

    halves = quarters // 2
    lead = 4 * width
    block = n * deep
    each = halves // plan.ny

    gathered, done = [], ()
    for layer in range(layers):
        shards = (qkv_weight, proj_weight, fc1_weight, fc2_weight)
        done = (pack(plan, where, layer, *shards, None if layer else extra, done),)
        gathered.append(lax.all_gather(done[0], "shard", axis=0, tiled=True))
    at_fc1, at_fc2 = lead // block, (lead + ff) // block
    mlp_parts = []
    for layer in range(layers):
        found = {"fc1": [(gathered[layer], ("quarter", block, (at_fc1, halves, k))) for k in range(halves)]}
        found["fc2"] = [(gathered[layer], columns(block, at_fc2 + k, each)) for k in range(each)]
        if plan.ny == 2:
            found["sent"], found["came"] = (), ()
            for k in range(1):
                mine = lax.dynamic_slice(
                    gathered[layer], (0, (at_fc2 + c) * block), (block, block)
                )
                found["sent"] += (mine,)
                found["came"] += (plan.flip(mine, 0),)
                found["fc2"].append((found["came"][k], None))
        mlp_parts.append(found)

    def weight_of(layer, name):
        if name == "qkv":
            return [(gathered[layer], columns(wide, 0, 1))]
        if name == "proj":
            return [(gathered[layer], ("heads", width, 3))]
        return mlp_parts[layer][name]

    every = gathered[0].reshape(n, deep, -1)[:, :lines, lead + ff + 2 * each * block :]
    every = every.reshape(n, layers, small.shape[1]).astype(F32)
    vecs = []
    for layer in range(layers):
        at, d = 0, {}
        for name, size in zip(SMALL, sizes):
            d[name] = every[:, layer, at : at + size].reshape(1, n * size)
            at += size
        q = d["qvb"].reshape(2 * half_heads, 2, HEAD_DIM)
        q = pick(c, q[:, 0], q[:, 1]).reshape(2, half_width)
        d["qvb_c"] = jnp.stack([q[0], jnp.zeros_like(q[0]), q[1]]).reshape(1, wide)
        f = d["f1b"].reshape(n, 2, halves, deep).transpose(1, 2, 0, 3).reshape(2, halves, block)
        f = pick(c, f[0], f[1])
        if plan.ny == 2:
            f = pick(y, f, f[::-1])
        d["f1b_c"] = f.reshape(1, half_ff)
        vecs.append(d)

    kept_oth = plan.core(kept)
    state = tokens.astype(F32).reshape(rows, width)
    live = lax.broadcasted_iota(jnp.int32, (images, slots), 1) < BUFFER + kept[:, None]
    grad = jnp.where(live[:, :, None], cotangent.astype(F32), 0.0).reshape(rows, width)
    low_own = grad.astype(BF)
    low_oth = plan.core(low_own)
    first_own = norm_rows(state, vecs[0]["ag"], vecs[0]["as"]).astype(BF)

    f32_rows, low_rows = ("rows", (rows, width), F32), ("rows", (rows, width), BF)
    wide_rows, ff_rows = ("rows", (rows, wide), BF), ("rows", (rows, half_ff), BF)
    att_outs = [("image", (images, half_heads, slots, slots), BF), ("rows", (rows, half_width), BF)]
    full_sums = ("full", (8, width), F32)

    def call(body, layer, own, names, blocked, whole, outs, after=(), cost=None):
        chosen = [weight_of(layer, name) for name in names]
        k = kept if own else kept_oth
        return row_call(body, where, k, chosen, blocked, whole, outs, images, slots, after, cost or (BACKWARD if after else FORWARD))

    saved = []
    for layer in range(layers):
        v = vecs[layer]
        first_oth = plan.core(first_own)
        sent, came = mlp_parts[layer].get("sent", ()), mlp_parts[layer].get("came", ())
        proj_oth = call(qkv_body, layer, 0, ["qkv"], [first_oth], [v["qvb_c"]], [wide_rows], sent, FORWARD)[0]
        probs_oth, att_oth, part = call(attend_other, layer, 0, ["proj"], [proj_oth], [], att_outs + [f32_rows])
        part = plan.core(part)
        proj_own = call(qkv_body, layer, 1, ["qkv"], [first_own], [v["qvb_c"]], [wide_rows])[0]
        probs_own, att_own, middle, second_own = call(
            attend_own, layer, 1, ["proj"], [proj_own, part, state], [v["pb"], v["mg"], v["ms"]], att_outs + [f32_rows, low_rows])
        second_oth = plan.core(second_own)
        hid_oth, slope_oth = call(up_body, layer, 0, ["fc1"], [second_oth], [v["f1b_c"]], [ff_rows] * 2)
        if layer + 1 < layers:
            part = call(down_other, layer, 0, ["fc2"], [hid_oth], [], [f32_rows])[0]
            part = plan.core(part)
        hid_own, slope_own = call(up_body, layer, 1, ["fc1"], [second_own], [v["f1b_c"]], [ff_rows] * 2)
        saved.append(
            dict(
                state=state,
                first=(first_own, first_oth),
                proj=(proj_own, proj_oth),
                probs=(probs_own, probs_oth),
                att=(att_own, att_oth),
                middle=middle,
                second=(second_own, second_oth),
                hid=(hid_own, hid_oth),
                slope=(slope_own, slope_oth),
            )
        )
        if layer + 1 < layers:
            w = vecs[layer + 1]
            state, first_own = call(
                down_own, layer, 1, ["fc2"], [hid_own, part, middle], [v["f2b"], w["ag"], w["as"]], [f32_rows, low_rows])

    axes = list(range(1 if plan.ny == 1 else 0, plan.bits + 1))
    last_axis, z_axis, x_axis = 1, plan.bits - 1, plan.bits
    y_axis = 0 if plan.ny == 2 else 2
    orders_f1 = [[y_axis, x_axis, z_axis]] * layers
    orders_q = [[[z_axis, y_axis, x_axis], [x_axis, z_axis, y_axis]]] + [[[x_axis, z_axis, y_axis]]] * (layers - 1)
    own_rows = 2 * deep
    tail = width // plan.ny * HEAD_DIM // own_rows
    fused = n == HEADS
    tail = tail if fused else 0
    big = [[None] * 4 for _ in range(layers)]
    sums = [None] * layers
    f2b_sum = jnp.sum(low_own.astype(F32), axis=0, keepdims=True)

    def end_rest(layer, prev):
        group = terms["q", layer] + [terms["f1", layer]]
        ends["rest", layer] = Ending(plan, where, group, last_axis, own_rows, tail, prev)
        return (ends["rest", layer].sent,)

    def place(layer, before, prev):
        return place_grads(
            plan, where, layer, layers, ends["f2", layer], ends["rest", layer], (deep, width, ff, quarters), before, prev
        )

    ends = {}
    prev = (hid_own,) + mlp_parts[layers - 1].get("came", ())
    terms = {}
    for layer in reversed(range(layers)):
        v, s = vecs[layer], saved[layer]
        top = layer == layers - 1

        def grad_fc2(prev):
            term = chip_grad(plan, where, s["hid"], (low_own, low_oth), 2, prev)
            ends["f2", layer] = ChipEnding(plan, where, term)
            return (term,)

        if top:
            prev = grad_fc2(prev)
        pre_oth, part = call(
            mlp_back_other, layer, 0, ["fc2", "fc1"], [low_oth, s["slope"][1]], [], [ff_rows, f32_rows], prev
        )
        part = plan.core(part)
        prev = (pre_oth,)
        if top:
            last_part = call(down_other, layer, 0, ["fc2"], [s["hid"][1]], [], [f32_rows], prev)[0]
            prev = (last_part,)
            last_part = plan.core(last_part)
        else:
            prev = grad_fc2(prev)
            prev += (terms["f1", layer + 1].step(prev[:1]),)
        pre_own, mid_grad, branch_own, sum1 = call(
            mlp_back_own,
            layer,
            1,
            ["fc2", "fc1"],
            [low_own, s["slope"][0], part, s["middle"], grad],
            [v["mg"]],
            [ff_rows, f32_rows, low_rows, full_sums],
            prev,
        )
        branch_oth = plan.core(branch_own)
        prev = (branch_own,)
        if not top:
            prev += (terms["q", layer + 1][0].step(prev),)
        res1 = weight_grad(
            plan, where, s["second"], (pre_own, pre_oth), 1, orders_f1[layer][0], sums=True, extra=tail, relative=True, after=prev
        )
        prev = tuple(res1[:1]) + ((last_part,) if top else ())
        if not top:
            prev += (terms["q", layer + 1][0].step(prev[:1]),)
            prev += (ends["f2", layer + 1].core(prev[:1]),)
        dproj_oth, part = call(
            attend_back_other,
            layer,
            0,
            ["proj", "qkv"],
            [branch_oth, s["proj"][1], s["probs"][1]],
            [],
            [wide_rows, f32_rows],
            prev,
        )
        part = plan.core(part)
        prev = (dproj_oth,)
        keep, send = res1[:2]
        if fused:
            keep, send = proj_grad_into(
                plan, where, s["att"], (branch_own, branch_oth), orders_f1[layer][0], keep, send, prev
            )
        else:
            term = t_dot(s["att"][0], branch_own) + t_dot(s["att"][1], branch_oth)
            term = term.astype(BF).reshape(half_heads, HEAD_DIM, width)
            none = jnp.zeros_like(term)
            term = jnp.stack([pick(c, term, none), pick(c, none, term)], axis=1).reshape(width, width)
            term = lax.psum_scatter(term, "shard", scatter_dimension=0, tiled=True)
            big[layer][1] = lax.psum(term, "rep").astype(F32)
        terms["f1", layer] = Term(plan, keep, send, orders_f1[layer])
        prev = (send,)
        if not top:
            prev += (terms["f1", layer + 1].step(prev[:1]),)
            prev += (ends["f2", layer + 1].rep(prev[:1]),)
        dproj_own, grad, low_own, sum2 = call(
            attend_back_own,
            layer,
            1,
            ["proj", "qkv"],
            [branch_own, s["proj"][0], s["probs"][0], part, s["state"], mid_grad],
            [v["ag"]],
            [wide_rows, f32_rows, low_rows, full_sums],
            prev,
        )
        prev = (dproj_own,)
        if layer:
            low_oth = plan.core(low_own)
        if not top:
            prev += end_rest(layer + 1, prev[:1])
        pairs, q_sums = parted_grad(
            plan, where, s["first"], (dproj_own, dproj_oth), [order[0] for order in orders_q[layer]], prev
        )
        terms["q", layer] = [Term(plan, *pair, order) for pair, order in zip(pairs, orders_q[layer])]
        prev = (pairs[0][1],)
        q = q_sums.reshape(3, half_heads, 1, HEAD_DIM)
        q = jnp.concatenate([q[:1], q[2:]])
        none = jnp.zeros_like(q)
        q = jnp.concatenate([pick(c, q, none), pick(c, none, q)], axis=2)
        f = res1[2].reshape(halves, block)
        if plan.ny == 2:
            f = pick(y, f, f[::-1])
        none = jnp.zeros_like(f)
        f = jnp.concatenate([pick(c, f, none), pick(c, none, f)], axis=0)
        f = f.reshape(quarters, n, deep).swapaxes(0, 1)
        full = {"ag": sum2[0], "as": sum2[1], "qvb": q, "pb": sum1[2], "mg": sum1[0], "ms": sum1[1], "f1b": f, "f2b": f2b_sum}
        f2b_sum = sum2[2]
        vec = jnp.concatenate([full[name].reshape(n, -1) for name in SMALL], axis=1)
        sums[layer] = vec

    vec = jnp.concatenate(sums, axis=0).reshape(layers, n, -1)
    got_vec = plan.core(vec)
    vec_axes = list(axes)

    def step_vec(prev):
        nonlocal vec, got_vec

        def kernel(where, ins, outs):
            outs[0][...] = ins[0][...] + ins[1][...]

        vec = small_call(kernel, where, [vec, got_vec], [(vec.shape, F32)], prev)[0]
        got_vec = plan.flip(vec, vec_axes.pop(0)) if vec_axes else None
        return (vec,)

    w = layers - 1
    mixed = call(
        down_last, w, 1, ["fc2"], [saved[w]["hid"][0], last_part, saved[w]["middle"]], [vecs[w]["f2b"]], [low_rows], prev
    )[0]
    qa, qb = terms["q", 0]
    prev = (terms["f1", 0].step((mixed,)),)
    prev = (ends["rest", 1].core(prev),)
    prev = (qa.step(prev),)
    prev = (qb.step(prev + (ends["rest", 1].came,)),)
    prev = step_vec(prev)
    prev = (qa.step(prev),)
    prev = (terms["f1", 0].step(prev),)
    prev = (ends["f2", 0].core(prev),)
    prev = (qb.step(prev),)
    prev = step_vec(prev)
    prev = end_rest(0, prev)
    prev = (ends["rest", 1].rep(prev),)
    prev = (ends["f2", 0].rep(prev),)
    prev = step_vec(prev)
    placed = place(1, None, prev)
    prev = (placed[0],)
    prev = (ends["rest", 0].core(prev + tuple(ends["f2", 0].pair[1:])),)
    prev = step_vec(prev)
    prev = (ends["rest", 0].rep(prev),)
    while got_vec is not None:
        prev = step_vec(prev)
    placed = place(0, placed, prev)
    if plan.ny == 1:
        vec = lax.psum(vec, "rep")
    vec = lax.dynamic_slice_in_dim(vec, shard, 1, axis=1)[:, 0]
    out, at = {}, 0
    for name, size in zip(SMALL, sizes):
        out[name] = vec[:, at : at + size]
        at += size
    qkv_g, fc1_g, fc2_g = placed[:3]
    proj_g = placed[3] if fused else jnp.stack([big[layer][1] for layer in range(layers)])
    return (
        mixed.reshape(images, slots, width),
        grad.reshape(images, slots, width),
        out["ag"],
        out["as"],
        qkv_g,
        out["qvb"],
        proj_g,
        out["pb"],
        out["mg"],
        out["ms"],
        fc1_g,
        out["f1b"],
        fc2_g,
        out["f2b"],
    )


def solution(mesh):
    rows = P(("shard", "rep"), None, None)
    vec = P(None, "shard")
    mat = P(None, "shard", None)
    return jax.shard_map(
        partial(per_device, Plan(mesh)),
        mesh=mesh,
        in_specs=(rows, P(("shard", "rep")), vec, vec, mat, vec, mat, vec, vec, vec, mat, vec, mat, vec, rows),
        out_specs=(rows, rows, vec, vec, mat, vec, mat, vec, vec, vec, mat, vec, mat, vec),
        check_vma=False,
    )
```

```python
from functools import partial

import jax
import jax.numpy as jnp
from jax import lax
from jax.experimental import pallas as pl
from jax.experimental.pallas import tpu as pltpu
from jax.sharding import PartitionSpec as P

HEADS = 16
HEAD_DIM = 64
BUFFER = 64
EPS = 1e-06
SCALE = HEAD_DIM ** (-0.5)
AX = ("shard", "rep")
BF = jnp.bfloat16
F32 = jnp.float32
LIMIT = 60 * 2**20
SMALL_LIMIT = 16 * 2**20
ONCE = pl.Buffered(1)
ANY = pl.BlockSpec(memory_space=pl.ANY)
FORWARD = pl.CostEstimate(flops=10**7, bytes_accessed=0, transcendentals=0)
BACKWARD = pl.CostEstimate(flops=10**9 * 30, bytes_accessed=0, transcendentals=0)
SMALL = ("ag", "as", "qvb", "pb", "mg", "ms", "f1b", "f2b")


class Plan:
    def __init__(self, mesh):
        self.shards = mesh.shape["shard"]
        self.rep = mesh.shape["rep"]
        self.chips = self.shards // 2
        self.ny = 2 if self.rep == 2 else 1
        self.bits = self.chips.bit_length() - 1

    def swap(self, v, flip_shard, flip_rep=0):
        pairs = []
        for s in range(self.shards):
            for y in range(self.rep):
                pairs.append((s * self.rep + y, (s ^ flip_shard) * self.rep + (y ^ flip_rep)))
        return lax.ppermute(v, AX, pairs)

    def core(self, v):
        return self.swap(v, 1)

    def flip(self, v, axis):
        if axis == 0:
            return self.swap(v, 0, 1)
        return self.swap(v, 2 << (self.bits - axis))


def dot(x, w):
    return lax.dot_general(x, w, (((1,), (0,)), ((), ())), preferred_element_type=F32)


def dot_t(x, w):
    return lax.dot_general(x, w, (((1,), (1,)), ((), ())), preferred_element_type=F32)


def t_dot(x, w):
    return lax.dot_general(x, w, (((0,), (0,)), ((), ())), preferred_element_type=F32)


def columns(width, first, stride):
    return ("columns", width, (first, stride))


def row_call(body, where, kept, weights, blocked, whole, outs, images, slots, after=(), cost=FORWARD):
    in_specs, args = [], []
    for v, pick_of in (part for w in weights for part in w):
        if pick_of is None:
            in_specs.append(pl.BlockSpec(v.shape, lambda i, w, k: (0, 0), pipeline_mode=ONCE))
            args.append(v)
            continue
        kind, width, first = pick_of
        if kind == "columns":
            spec = pl.BlockSpec((v.shape[0], width), lambda i, w, k, f=first: (0, f[0] + f[1] * w[0]), pipeline_mode=ONCE)
            in_specs.append(spec)
            args.append(v)
        elif kind == "quarter":
            at, stride, part = first
            spec = pl.BlockSpec(
                (v.shape[0], width),
                lambda i, w, k, f=(at, stride, part): (0, f[0] + f[1] * w[0] + jnp.bitwise_xor(f[2], w[3])),
                pipeline_mode=ONCE,
            )
            in_specs.append(spec)
            args.append(v)
        else:
            view = v.reshape(HEADS // 2, 2, HEAD_DIM, v.shape[1])
            spec = pl.BlockSpec((HEADS // 2, None, HEAD_DIM, width), lambda i, w, k, f=first: (0, w[0], 0, f), pipeline_mode=ONCE)
            in_specs.append(spec)
            args.append(view)
    for v in blocked:
        if v.ndim == 2:
            in_specs.append(pl.BlockSpec((slots, v.shape[1]), lambda i, *_: (i, 0)))
        else:
            in_specs.append(pl.BlockSpec((1,) + v.shape[1:], lambda i, *_, n=v.ndim: (i,) + (0,) * (n - 1)))
        args.append(v)
    for v in whole:
        in_specs.append(pl.BlockSpec(v.shape, lambda i, *_, n=v.ndim: (0,) * n))
        args.append(v)
    out_specs, out_shape = [], []
    for kind, shape, dtype in outs:
        out_shape.append(jax.ShapeDtypeStruct(shape, dtype))
        if kind == "rows":
            out_specs.append(pl.BlockSpec((slots, shape[1]), lambda i, *_: (i, 0)))
        elif kind == "image":
            out_specs.append(pl.BlockSpec((1,) + shape[1:], lambda i, *_, n=len(shape): (i,) + (0,) * (n - 1)))
        else:
            out_specs.append(pl.BlockSpec(shape, lambda i, *_, n=len(shape): (0,) * n))
    n_p, n_b, n_in = sum(len(w) for w in weights), len(blocked), len(args)
    in_specs += [ANY] * len(after)
    args += list(after)

    def kernel(where_ref, kept_ref, *refs):
        ins, res = refs[:n_in], refs[n_in + len(after) :]
        held, at = [], 0
        for w in weights:
            held.append(ins[at : at + len(w)])
            at += len(w)
        body(kept_ref, held, ins[n_p : n_p + n_b], ins[n_p + n_b : n_in], res)

    return pl.pallas_call(
        kernel,
        grid_spec=pltpu.PrefetchScalarGridSpec(
            num_scalar_prefetch=2, grid=(images,), in_specs=in_specs, out_specs=out_specs
        ),
        out_shape=out_shape,
        compiler_params=pltpu.CompilerParams(vmem_limit_bytes=LIMIT),
        cost_estimate=cost,
    )(where, kept, *args)


def normed_of(rows):
    width = rows.shape[-1]
    mean = jnp.sum(rows, axis=-1, keepdims=True) * (1.0 / width)
    centered = rows - mean
    spread = jnp.sum(centered * centered, axis=-1, keepdims=True) * (1.0 / width)
    factor = lax.rsqrt(spread + EPS)
    return centered * factor, factor


def norm_rows(rows, gain, shift):
    return normed_of(rows)[0] * gain + shift


def norm_back(dz, rows, gain):
    normed, factor = normed_of(rows)
    width = rows.shape[-1]
    prod = dz * normed
    dn = dz * gain
    m1 = jnp.sum(dn, axis=-1, keepdims=True) * (1.0 / width)
    m2 = jnp.sum(dn * normed, axis=-1, keepdims=True) * (1.0 / width)
    back = factor * (dn - m1 - normed * m2)
    return back, jnp.sum(prod, axis=0, keepdims=True), jnp.sum(dz, axis=0, keepdims=True)


def chunks(total, size):
    size = min(size, total)
    return [(k, size) for k in range(0, total, size)]


def qkv_body(kept, w, blocked, whole, outs):
    x = blocked[0][...]
    for k, n in chunks(outs[0].shape[1], 512):
        cols = pl.ds(k, n)
        outs[0][:, cols] = (dot(x, w[0][0][:, cols]) + whole[0][:, cols]).astype(BF)


def heads_of(ref):
    return ref[...].reshape(-1, ref.shape[-1])


def pairs_dot(x_ref, parts):
    total, at = None, 0
    for w_ref in parts:
        term = dot(x_ref[:, at : at + w_ref.shape[0]], w_ref[...])
        total = term if total is None else total + term
        at += w_ref.shape[0]
    return total


def attend(kept, proj_ref, probs_ref, att_ref):
    slots, third = proj_ref.shape[0], proj_ref.shape[1] // 3
    bound = BUFFER + kept[pl.program_id(0)]
    alive = lax.broadcasted_iota(jnp.int32, (slots, slots), 1) < bound
    outs = []
    for h in range(third // HEAD_DIM):
        lo = h * HEAD_DIM
        q = proj_ref[:, lo : lo + HEAD_DIM]
        k = proj_ref[:, third + lo : third + lo + HEAD_DIM]
        v = proj_ref[:, 2 * third + lo : 2 * third + lo + HEAD_DIM]
        s = jnp.where(alive, dot_t(q, k) * SCALE, -1e30)
        e = jnp.exp(s - jnp.max(s, axis=-1, keepdims=True))
        p = (e * (1.0 / jnp.sum(e, axis=-1, keepdims=True))).astype(BF)
        probs_ref[0, h] = p
        outs.append(dot(p, v).astype(BF))
        if h % 2:
            att_ref[:, lo - HEAD_DIM : lo + HEAD_DIM] = jnp.concatenate(outs, axis=1)
            outs = []


def attend_other(kept, w, blocked, whole, outs):
    attend(kept, blocked[0], outs[0], outs[1])
    outs[2][...] = dot(outs[1][...], heads_of(w[0][0]))


def attend_own(kept, w, blocked, whole, outs):
    attend(kept, blocked[0], outs[0], outs[1])
    middle = blocked[2][...] + (dot(outs[1][...], heads_of(w[0][0])) + blocked[1][...]) + whole[0][...]
    outs[2][...] = middle
    outs[3][...] = norm_rows(middle, whole[1][...], whole[2][...]).astype(BF)


def up_body(kept, w, blocked, whole, outs):
    x = blocked[0][...]
    for k, n in chunks(outs[0].shape[1], 256):
        cols = pl.ds(k, n)
        held = w[0][k // w[0][0].shape[1]]
        pre = dot(x, held[:, pl.ds(k % held.shape[1], n)]) + whole[0][:, cols]
        phi = 0.5 + 0.5 * lax.erf(pre * (2.0**-0.5))
        dens = jnp.exp(-0.5 * (pre * pre)) * 0.3989422804014327
        outs[0][:, cols] = (pre * phi).astype(BF)
        outs[1][:, cols] = (phi + pre * dens).astype(BF)


def down_other(kept, w, blocked, whole, outs):
    outs[0][...] = pairs_dot(blocked[0], w[0])


def down_own(kept, w, blocked, whole, outs):
    state = blocked[2][...] + (pairs_dot(blocked[0], w[0]) + blocked[1][...]) + whole[0][...]
    outs[0][...] = state
    outs[1][...] = norm_rows(state, whole[1][...], whole[2][...]).astype(BF)


def down_last(kept, w, blocked, whole, outs):
    state = blocked[2][...] + (pairs_dot(blocked[0], w[0]) + blocked[1][...]) + whole[0][...]
    alive = lax.broadcasted_iota(jnp.int32, state.shape, 0) < BUFFER + kept[pl.program_id(0)]
    outs[0][...] = jnp.where(alive, state, 0.0).astype(BF)


def mlp_back(w, blocked, outs):
    low = blocked[0][...]
    for k, n in chunks(outs[0].shape[1], 512):
        cols = pl.ds(k, n)
        held, first = w[0][0], 0
        for part in w[0][1:]:
            if k >= first + held.shape[0]:
                first += held.shape[0]
                held = part
        t = dot_t(low, held[pl.ds(k - first, n), :])
        outs[0][:, cols] = (t * blocked[1][:, cols].astype(F32)).astype(BF)
    total, at = None, 0
    for held in w[1]:
        term = dot_t(outs[0][:, at : at + held.shape[1]], held[...])
        total = term if total is None else total + term
        at += held.shape[1]
    return total


def mlp_back_other(kept, w, blocked, whole, outs):
    outs[1][...] = mlp_back(w, blocked, outs)


def add_sums(ref, rows):
    sums = jnp.concatenate(rows + [jnp.zeros((8 - len(rows), rows[0].shape[1]), F32)], axis=0)

    @pl.when(pl.program_id(0) == 0)
    def _():
        ref[...] = sums

    @pl.when(pl.program_id(0) != 0)
    def _():
        ref[...] += sums


def mlp_back_own(kept, w, blocked, whole, outs):
    dz = mlp_back(w, blocked, outs) + blocked[2][...]
    back, gain, shift = norm_back(dz, blocked[3][...], whole[0][...])
    grad = blocked[4][...] + back
    low = grad.astype(BF)
    outs[1][...] = grad
    outs[2][...] = low
    add_sums(outs[3], [gain, shift, jnp.sum(low.astype(F32), axis=0, keepdims=True)])


def attend_back(w, blocked, outs):
    branch, proj_ref, probs_ref = blocked[0], blocked[1], blocked[2]
    third = proj_ref.shape[1] // 3
    datt = dot_t(branch[...], heads_of(w[0][0])).astype(BF)
    pairs = [[], [], []]
    for h in range(third // HEAD_DIM):
        lo = h * HEAD_DIM
        q = proj_ref[:, lo : lo + HEAD_DIM]
        k = proj_ref[:, third + lo : third + lo + HEAD_DIM]
        v = proj_ref[:, 2 * third + lo : 2 * third + lo + HEAD_DIM]
        da = datt[:, lo : lo + HEAD_DIM]
        p = probs_ref[0, h]
        dp = dot_t(da, v)
        pf = p.astype(F32)
        ds = (pf * (dp - jnp.sum(pf * dp, axis=-1, keepdims=True))).astype(BF)
        pairs[0].append((dot(ds, k) * SCALE).astype(BF))
        pairs[1].append((t_dot(ds, q) * SCALE).astype(BF))
        pairs[2].append(t_dot(p, da).astype(BF))
        if h % 2:
            for j in range(3):
                at = j * third + lo - HEAD_DIM
                outs[0][:, at : at + 2 * HEAD_DIM] = jnp.concatenate(pairs[j], axis=1)
            pairs = [[], [], []]
    return dot_t(outs[0][...], w[1][0][...])


def attend_back_other(kept, w, blocked, whole, outs):
    outs[1][...] = attend_back(w, blocked, outs)


def attend_back_own(kept, w, blocked, whole, outs):
    dz = attend_back(w, blocked, outs) + blocked[3][...]
    back, gain, shift = norm_back(dz, blocked[4][...], whole[0][...])
    grad = blocked[5][...] + back
    outs[1][...] = grad
    low = grad.astype(BF)
    outs[2][...] = low
    add_sums(outs[3], [gain, shift, jnp.sum(low.astype(F32), axis=0, keepdims=True)])


def weight_grad(plan, where, xs, ys, groups, first, sums=False, extra=0, relative=False, window=(0, 1), after=()):
    depth, n_x = xs[0].shape
    cols = ys[0].shape[1]
    ny, chips, bits = plan.ny, plan.chips, plan.bits
    half = cols // ny
    size = half // window[1]
    chunk = size if size <= 768 else 512
    steps = size // chunk
    rows = n_x // chips
    part = rows // groups
    dims = [ny] + [2] * bits
    dims[first] = 1
    block = [1] + dims[1:] + [rows, chunk]
    shape = dims + [rows, size + extra]
    n_after = len(after)

    def kernel(where_ref, xo, xt, yo, yt, *rest):
        rest = rest[n_after:]
        keep, send = rest[0], rest[1]
        flip, acc = rest[-2], rest[-1]
        step = pl.program_id(0)

        @pl.when(step == 0)
        def _():
            flip[:, :depth] = xo[...].T
            flip[:, depth:] = xt[...].T

        acc[...] = dot(flip[:, :depth], yo[...]) + dot(flip[:, depth:], yt[...])
        if sums:
            rest[2][...] = jnp.sum(yo[...].astype(F32), axis=0, keepdims=True) + jnp.sum(
                yt[...].astype(F32), axis=0, keepdims=True
            )

        def put(ref, r):
            at = [0]
            for k in range(1, bits + 1):
                at.append((r >> (bits - k)) & 1 if k != first else 0)
            chip = jnp.bitwise_xor(where_ref[1], r)
            for g in range(groups):
                start = pl.multiple_of(g * part * chips + chip * part, 16)
                place = g
                if groups == 2 and ny == 2:
                    place = jnp.bitwise_xor(g, where_ref[2])
                place = pl.multiple_of(place * part, 16)
                ref[tuple(at) + (pl.ds(place, part),)] = acc[pl.ds(start, part)].astype(BF)

        if first:
            for r in range(chips):
                put(send if (r >> (bits - first)) & 1 else keep, r)
        else:

            @pl.when(step < steps)
            def _():
                for r in range(chips):
                    put(keep, r)

            @pl.when(step >= steps)
            def _():
                for r in range(chips):
                    put(send, r)

    per_rep = half // chunk

    def column(i, w):
        own = w[2] if ny == 2 and not relative else 0
        return jnp.bitwise_xor(i // steps, own) * per_rep + window[0] * steps + i % steps

    zeros = (0,) * (bits + 1)
    x_spec = pl.BlockSpec((depth, n_x), lambda i, w: (0, 0), pipeline_mode=ONCE)
    y_spec = pl.BlockSpec((depth, chunk), lambda i, w: (0, column(i, w)))
    if first:
        specs = [pl.BlockSpec(block, lambda i, w: (i // steps,) + zeros + (i % steps,))] * 2
    else:
        specs = [
            pl.BlockSpec(block, lambda i, w: (0,) + zeros + (jnp.minimum(i, steps - 1),)),
            pl.BlockSpec(block, lambda i, w: (0,) + zeros + (jnp.maximum(i - steps, 0),)),
        ]
    out_shape = [jax.ShapeDtypeStruct(shape, BF)] * 2
    if sums:
        own = (lambda w: w[2]) if ny == 2 and not relative else (lambda w: 0)
        specs = specs + [
            pl.BlockSpec((1, chunk), lambda i, w: (0, jnp.bitwise_xor(i // steps, own(w)) * steps + i % steps))
        ]
        out_shape = out_shape + [jax.ShapeDtypeStruct((1, size * ny), F32)]
    return pl.pallas_call(
        kernel,
        grid_spec=pltpu.PrefetchScalarGridSpec(
            num_scalar_prefetch=1,
            grid=(ny * steps,),
            in_specs=[x_spec, x_spec, y_spec, y_spec] + [ANY] * n_after,
            out_specs=specs,
            scratch_shapes=[pltpu.VMEM((n_x, 2 * depth), BF), pltpu.VMEM((n_x, chunk), F32)],
        ),
        out_shape=out_shape,
        compiler_params=pltpu.CompilerParams(vmem_limit_bytes=LIMIT),
        cost_estimate=BACKWARD,
    )(where, *xs, *ys, *after)


def chip_grad(plan, where, xs, ys, groups, after=()):
    depth, n_x = xs[0].shape
    cols = ys[0].shape[1]
    chips = plan.chips
    chunk = min(cols, 512)
    rows = n_x // chips
    part = rows // groups
    n_after = len(after)

    def kernel(where_ref, xo, xt, yo, yt, *rest):
        out, flip, acc = rest[n_after:]

        @pl.when(pl.program_id(0) == 0)
        def _():
            flip[:, :depth] = xo[...].T
            flip[:, depth:] = xt[...].T

        acc[...] = dot(flip[:, :depth], yo[...]) + dot(flip[:, depth:], yt[...])
        for g in range(groups):
            place = jnp.bitwise_xor(g, where_ref[3]) * part
            for chip in range(chips):
                at = pl.ds(pl.multiple_of(place + chip * rows, 16), part)
                first = (g * chips + chip) * part
                out[at, :] = acc[first : first + part].astype(BF)

    x_spec = pl.BlockSpec((depth, n_x), lambda i, w: (0, 0), pipeline_mode=ONCE)
    y_spec = pl.BlockSpec((depth, chunk), lambda i, w: (0, i))
    return pl.pallas_call(
        kernel,
        grid_spec=pltpu.PrefetchScalarGridSpec(
            num_scalar_prefetch=1,
            grid=(cols // chunk,),
            in_specs=[x_spec, x_spec, y_spec, y_spec] + [ANY] * n_after,
            out_specs=pl.BlockSpec((n_x, chunk), lambda i, w: (0, i)),
            scratch_shapes=[pltpu.VMEM((n_x, 2 * depth), BF), pltpu.VMEM((n_x, chunk), F32)],
        ),
        out_shape=jax.ShapeDtypeStruct((n_x, cols), BF),
        compiler_params=pltpu.CompilerParams(vmem_limit_bytes=LIMIT),
        cost_estimate=BACKWARD,
    )(where, *xs, *ys, *after)


def proj_grad_into(plan, where, xs, ys, first, keep, send, after=()):
    depth, n_x = xs[0].shape
    cols = ys[0].shape[1]
    ny, chips, bits = plan.ny, plan.chips, plan.bits
    half = cols // ny
    part = n_x // chips
    width = half * part // keep.shape[-2]
    stacked = half // width
    at_col = keep.shape[-1] // width - 1
    block = [1] + list(keep.shape[1:-1]) + [width]

    n_after = len(after)

    def kernel(where_ref, xo, xt, yo, yt, k_in, s_in, *rest):
        keep_ref, send_ref, acc = rest[n_after:]
        acc[...] = t_dot(xo[...], yo[...]) + t_dot(xt[...], yt[...])

        def put(ref, r):
            at = [0]
            for k in range(1, bits + 1):
                at.append((r >> (bits - k)) & 1 if k != first else 0)
            start = pl.multiple_of(jnp.bitwise_xor(where_ref[1], r) * part, 16)
            for g in range(stacked):
                piece = acc[pl.ds(start, part), g * width : (g + 1) * width]
                ref[tuple(at) + (pl.ds(g * part, part),)] = piece.astype(BF)

        if first:
            for r in range(chips):
                put(send_ref if (r >> (bits - first)) & 1 else keep_ref, r)
        else:

            @pl.when(pl.program_id(0) == 0)
            def _():
                for r in range(chips):
                    put(keep_ref, r)

            @pl.when(pl.program_id(0) != 0)
            def _():
                for r in range(chips):
                    put(send_ref, r)

    zeros = (0,) * (bits + 1)
    own = (lambda w: w[2]) if ny == 2 else (lambda w: 0)
    x_spec = pl.BlockSpec((depth, n_x), lambda i, w: (0, 0), pipeline_mode=ONCE)
    y_spec = pl.BlockSpec((depth, half), lambda i, w: (0, jnp.bitwise_xor(i, own(w))))
    spec = pl.BlockSpec(block, lambda i, w: (i if first else 0,) + zeros + (at_col,))
    return pl.pallas_call(
        kernel,
        grid_spec=pltpu.PrefetchScalarGridSpec(
            num_scalar_prefetch=1,
            grid=(ny,),
            in_specs=[x_spec, x_spec, y_spec, y_spec, ANY, ANY] + [ANY] * n_after,
            out_specs=[spec, spec],
            scratch_shapes=[pltpu.VMEM((n_x, half), F32)],
        ),
        out_shape=[jax.ShapeDtypeStruct(keep.shape, BF)] * 2,
        input_output_aliases={5: 0, 6: 1},
        compiler_params=pltpu.CompilerParams(vmem_limit_bytes=LIMIT),
        cost_estimate=BACKWARD,
    )(where, *xs, *ys, keep, send, *after)


class Term:
    def __init__(self, plan, keep, send, order):
        self.plan, self.keep, self.order = plan, keep, list(order)
        self.got = plan.flip(send, self.order.pop(0))

    def step(self, after):
        axis = self.order.pop(0)
        self.keep, send = combine(self.keep, self.got, axis, after)
        self.got = self.plan.flip(send, axis)
        return send


def combine(keep, got, axis, after):
    shape = keep.shape
    rows, cols = shape[-2:]
    cuts = 2
    block = shape[:-2] + (rows // cuts, cols)
    out = shape[:axis] + (1,) + shape[axis + 1 :]
    out_block = out[:-2] + (rows // cuts, cols)
    lead = len(shape) - 2

    def kernel(k, g, *rest):
        stay, go = rest[-2:]
        for side, ref in ((0, stay), (1, go)):
            at = tuple(pl.ds(side, 1) if d == axis else slice(None) for d in range(lead))
            ref[...] = (k[at].astype(F32) + g[at].astype(F32)).astype(BF)

    index = lambda i: (0,) * lead + (i, 0)
    return pl.pallas_call(
        kernel,
        grid=(cuts,),
        in_specs=[pl.BlockSpec(block, index)] * 2 + [ANY] * len(after),
        out_specs=[pl.BlockSpec(out_block, index)] * 2,
        out_shape=[jax.ShapeDtypeStruct(out, BF)] * 2,
        compiler_params=pltpu.CompilerParams(vmem_limit_bytes=SMALL_LIMIT),
        cost_estimate=BACKWARD,
    )(keep, got, *after)


def last_combine(terms, axis, rows, after):
    ins, specs, widths = [], [], []
    for t in terms:
        ins += [t.keep, t.got]
        widths.append(t.keep.shape[-1] * (t.keep.shape[-2] // rows))
    total = sum(widths)
    n_in = len(ins)

    def kernel(*refs):
        stay, go = refs[-2:]
        at = 0
        for j, t in enumerate(terms):
            k, g = refs[2 * j], refs[2 * j + 1]
            lead = k.ndim - 2
            cols = k.shape[-1]
            for block in range(k.shape[-2] // rows):
                for side, ref in ((0, stay), (1, go)):
                    idx = tuple(side if d == axis else 0 for d in range(lead)) + (pl.ds(block * rows, rows),)
                    ref[:, at : at + cols] = (k[idx].astype(F32) + g[idx].astype(F32)).astype(BF)
                at += cols

    whole = [pl.BlockSpec(v.shape, lambda n=v.ndim: (0,) * n) for v in ins]
    return pl.pallas_call(
        kernel,
        in_specs=whole + [ANY] * len(after),
        out_specs=[pl.BlockSpec((rows, total), lambda: (0, 0))] * 2,
        out_shape=[jax.ShapeDtypeStruct((rows, total), BF)] * 2,
        compiler_params=pltpu.CompilerParams(vmem_limit_bytes=SMALL_LIMIT),
        cost_estimate=BACKWARD,
    )(*ins, *after)


def pick(flag, a, b):
    return jnp.where(flag == 0, a, b)


def small_call(kernel, where, ins, shapes, after, grid=None):
    n = len(ins)

    def body(where_ref, *refs):
        kernel(where_ref, refs[:n], refs[n + len(after) :])

    return pl.pallas_call(
        body,
        grid_spec=pltpu.PrefetchScalarGridSpec(
            num_scalar_prefetch=1,
            grid=(1,),
            in_specs=[pl.BlockSpec(v.shape, lambda i, w, n=v.ndim: (0,) * n) for v in ins] + [ANY] * len(after),
            out_specs=[pl.BlockSpec(s, lambda i, w, n=len(s): (0,) * n) for s, _ in shapes],
        ),
        out_shape=[jax.ShapeDtypeStruct(s, t) for s, t in shapes],
        compiler_params=pltpu.CompilerParams(vmem_limit_bytes=SMALL_LIMIT),
        cost_estimate=BACKWARD,
    )(where, *ins, *after)


class Ending:
    def __init__(self, plan, where, terms, axis, rows, tail, after):
        self.plan, self.where, self.rows, self.tail = plan, where, rows, tail
        self.keep, self.sent = last_combine(terms, axis, rows, after)
        self.got = plan.flip(self.sent, axis)

    def core(self, after):
        rows, tail = self.rows // 2, self.tail
        cols = self.cols = self.keep.shape[1] - tail

        def kernel(where, ins, outs):
            c = where[0]
            for ref, row in ((outs[0], c), (outs[1], 1 - c)):
                at = pl.ds(pl.multiple_of(row * rows, 16), rows)
                ref[:, :cols] = (ins[0][at, :cols].astype(F32) + ins[1][at, :cols].astype(F32)).astype(BF)
            if tail:
                for g in range(2):
                    at = pl.ds(g * rows, rows)
                    piece = ins[0][at, cols:].astype(F32) + ins[1][at, cols:].astype(F32)
                    outs[0][:, cols + g * tail : cols + (g + 1) * tail] = piece.astype(BF)

        shapes = [((rows, cols + 2 * tail), BF), ((rows, cols), BF)]
        self.mine, sent = small_call(kernel, self.where, [self.keep, self.got], shapes, after)
        self.came = self.plan.core(sent)
        return sent

    def rep(self, after):
        rows, cols, tail = self.rows // 2, self.cols, self.tail

        def kernel(where, ins, outs):
            outs[0][:, :cols] = ins[0][:, :cols]
            outs[0][:, cols : 2 * cols] = ins[1][...]
            if tail:
                outs[0][:, 2 * cols :] = ins[0][:, cols:]

        shapes = [((rows, 2 * cols + 2 * tail), BF)]
        v = small_call(kernel, self.where, [self.mine, self.came], shapes, after)[0]
        self.pair = [v, self.plan.flip(v, 0)] if self.plan.ny == 2 else [lax.psum(v, "rep")]
        return v


class ChipEnding:
    def __init__(self, plan, where, term):
        self.plan, self.where = plan, where
        groups = [[2 * chip + c for chip in range(plan.chips)] for c in range(2)]
        self.term = lax.psum_scatter(term, "shard", scatter_dimension=0, axis_index_groups=groups, tiled=True)

    def core(self, after):
        rows, cols = self.term.shape
        part = rows // 4

        def kernel(where, ins, outs):
            c = where[0]
            for ref, row in ((outs[0], c), (outs[1], 1 - c)):
                for k in range(2):
                    at = pl.ds(pl.multiple_of((2 * k + row) * part, 16), part)
                    ref[k * part : (k + 1) * part] = ins[0][at]

        shapes = [((rows // 2, cols), BF)] * 2
        self.mine, sent = small_call(kernel, self.where, [self.term], shapes, after)
        self.came = self.plan.core(sent)
        return sent

    def rep(self, after):
        rows, cols = self.mine.shape

        def kernel(where, ins, outs):
            outs[0][:rows] = ins[0][...]
            outs[0][rows:] = ins[1][...]

        v = small_call(kernel, self.where, [self.mine, self.came], [((2 * rows, cols), BF)], after)[0]
        self.pair = [v, self.plan.flip(v, 0)] if self.plan.ny == 2 else [lax.psum(v, "rep")]
        return v


def place_grads(plan, where, layer, layers, end2, rest, sizes, before, after):
    deep, width, ff, quarters = sizes
    n, ny, halves = plan.shards, plan.ny, quarters // 2
    wide, half_ff = 3 * width // 2, ff // 2
    cols = rest.cols
    fused = bool(rest.tail)
    ins = end2.pair + rest.pair

    def kernel(where_ref, *refs):
        refs_in = refs[: 2 * ny]
        outs = refs[-(4 if fused else 3) :]
        c, y = where_ref[0], where_ref[2]

        def source(p, q, at, size):
            step = (at // 128) * 128
            span = (at + size - step + 127) // 128 * 128
            first = pl.multiple_of(jnp.where(p == c, 0, cols) + step, 128)
            v = refs_in[ny][:, pl.ds(first, span)]
            if ny == 2:
                v = jnp.where(y == q, v, refs_in[ny + 1][:, pl.ds(first, span)])
            return v[:, at - step : at - step + size].astype(F32)

        def core_columns(p, at, size, total, first):
            part = total // ny
            return source(p, at // part, first + at % part, size)

        for k in range(3 * HEADS // 2):
            pieces = [core_columns(p, k * HEAD_DIM, HEAD_DIM, wide, 0) for p in range(2)]
            outs[0][0, :, k * 2 * HEAD_DIM : (k + 1) * 2 * HEAD_DIM] = jnp.concatenate(pieces, axis=1)
        for k in range(n):
            pieces = []
            for p in range(2):
                for h in range(halves):
                    pieces.append(core_columns(p, (h * n + k) * deep, deep, half_ff, wide // ny))
            outs[1][0, :, k * quarters * deep : (k + 1) * quarters * deep] = jnp.concatenate(pieces, axis=1)
        part = width // ny
        for p in range(2):
            at = pl.ds(pl.multiple_of(jnp.where(p == c, 0, halves * deep), 16), halves * deep)
            v = refs_in[0][at].astype(F32)
            if ny == 2:
                v = v + refs_in[1][at].astype(F32)
            outs[2][0, p * halves * deep : (p + 1) * halves * deep] = v
        if fused:
            for q in range(ny):
                v = refs_in[ny][:, 2 * cols :]
                if ny == 2:
                    v = jnp.where(y == q, v, refs_in[ny + 1][:, 2 * cols :])
                outs[3][0, :, q * part : (q + 1) * part] = v.astype(F32)

    shapes = [(deep, 3 * width), (deep, ff), (quarters * deep, width)] + ([(deep, width)] if fused else [])
    in_specs = [pl.BlockSpec(v.shape, lambda i, w: (0, 0)) for v in ins]
    args = list(ins) + list(before or []) + list(after)
    n_before = len(before or [])
    return pl.pallas_call(
        kernel,
        grid_spec=pltpu.PrefetchScalarGridSpec(
            num_scalar_prefetch=1,
            grid=(1,),
            in_specs=in_specs + [ANY] * (n_before + len(after)),
            out_specs=[pl.BlockSpec((1,) + s, lambda i, w: (layer, 0, 0)) for s in shapes],
        ),
        out_shape=[jax.ShapeDtypeStruct((layers,) + s, F32) for s in shapes],
        input_output_aliases={1 + len(ins) + k: k for k in range(n_before)},
        compiler_params=pltpu.CompilerParams(vmem_limit_bytes=LIMIT),
        cost_estimate=BACKWARD,
    )(where, *args)


def pack(plan, where, layer, qkv, proj, fc1, fc2, extra, after):
    deep, width = proj.shape[1:]
    ff, n = fc1.shape[2], plan.shards
    quarters = fc2.shape[1] // deep
    halves = quarters // 2
    each = halves // plan.ny
    ins = [qkv, proj, fc1, fc2] + ([extra] if extra is not None else [])
    total = 4 * width + ff + 2 * each * width + (extra.shape[1] if extra is not None else 0)

    def kernel(where_ref, *refs):
        out = refs[-1]

        def lay(at, pieces):
            held, wide = [], 0
            for p in pieces:
                held.append(p)
                wide += p.shape[1]
                if wide % 128 == 0:
                    out[:, at : at + wide] = held[0] if len(held) == 1 else jnp.concatenate(held, axis=1)
                    at, held, wide = at + wide, [], 0

        for p in range(2):
            cols = [k * 2 * HEAD_DIM + p * HEAD_DIM for k in range(3 * HEADS // 2)]
            lay(p * (3 * width // 2), [refs[0][0, :, k : k + HEAD_DIM] for k in cols])
        out[:, 3 * width : 4 * width] = refs[1][0]
        cols = [s * quarters * deep + k * deep for k in range(quarters) for s in range(n)]
        lay(4 * width, [refs[2][0, :, k : k + deep] for k in cols])
        at = 4 * width + ff
        for p in range(2):
            for k in range(each):
                row = (p * halves + k) * deep + where_ref[3] * deep
                out[:, at : at + width] = refs[3][0, pl.ds(pl.multiple_of(row, 16), deep)]
                at += width
        if extra is not None:
            out[:, at:] = refs[4][...]

    specs = [pl.BlockSpec((1,) + v.shape[1:], lambda i, w: (layer, 0, 0)) for v in ins[:4]]
    specs += [pl.BlockSpec(v.shape, lambda i, w: (0, 0)) for v in ins[4:]]
    return pl.pallas_call(
        kernel,
        grid_spec=pltpu.PrefetchScalarGridSpec(
            num_scalar_prefetch=1,
            grid=(1,),
            in_specs=specs + [ANY] * len(after),
            out_specs=pl.BlockSpec((deep, total), lambda i, w: (0, 0)),
        ),
        out_shape=jax.ShapeDtypeStruct((deep, total), BF),
        compiler_params=pltpu.CompilerParams(vmem_limit_bytes=LIMIT),
        cost_estimate=FORWARD,
    )(where, *ins, *after)


def per_device(
    plan,
    tokens,
    kept,
    attn_gain,
    attn_shift,
    qkv_weight,
    qv_bias,
    proj_weight,
    proj_bias,
    mlp_gain,
    mlp_shift,
    fc1_weight,
    fc1_bias,
    fc2_weight,
    fc2_bias,
    cotangent,
):
    images, slots, width = tokens.shape
    layers = attn_gain.shape[0]
    rows = images * slots
    n = plan.shards
    deep = qkv_weight.shape[1]
    shard = lax.axis_index("shard")
    c, chip, y = lax.rem(shard, 2), shard // 2, lax.axis_index("rep")
    where = jnp.stack([c, chip, y, y if plan.ny == 2 else 0 * y]).astype(jnp.int32)
    ff = fc2_weight.shape[1] * n
    quarters = fc2_weight.shape[1] // deep
    wide, half_width, half_ff = 3 * width // 2, width // 2, ff // 2
    half_heads = HEADS // 2

    small = jnp.concatenate(
        [attn_gain, attn_shift, qv_bias, proj_bias, mlp_gain, mlp_shift, fc1_bias, fc2_bias], axis=1
    )
    sizes = [v.shape[1] for v in (attn_gain, attn_shift, qv_bias, proj_bias, mlp_gain, mlp_shift, fc1_bias, fc2_bias)]
    lines = small.size // 128
    extra = jnp.pad(small.reshape(lines, 128), ((0, deep - lines), (0, 0)))

    halves = quarters // 2
    lead = 4 * width
    block = n * deep
    each = halves // plan.ny

    gathered, done = [], ()
    for layer in range(layers):
        shards = (qkv_weight, proj_weight, fc1_weight, fc2_weight)
        done = (pack(plan, where, layer, *shards, None if layer else extra, done),)
        gathered.append(lax.all_gather(done[0], "shard", axis=0, tiled=True))
    at_fc1, at_fc2 = lead // block, (lead + ff) // block
    mlp_parts = []
    for layer in range(layers):
        found = {"fc1": [(gathered[layer], ("quarter", block, (at_fc1, halves, k))) for k in range(halves)]}
        found["fc2"] = [(gathered[layer], columns(block, at_fc2 + k, each)) for k in range(each)]
        if plan.ny == 2:
            found["sent"], found["came"] = (), ()
            for k in range(1):
                mine = lax.dynamic_slice(
                    gathered[layer], (0, (at_fc2 + c) * block), (block, block)
                )
                found["sent"] += (mine,)
                found["came"] += (plan.flip(mine, 0),)
                found["fc2"].append((found["came"][k], None))
        mlp_parts.append(found)

    def weight_of(layer, name):
        if name == "qkv":
            return [(gathered[layer], columns(wide, 0, 1))]
        if name == "proj":
            return [(gathered[layer], ("heads", width, 3))]
        return mlp_parts[layer][name]

    every = gathered[0].reshape(n, deep, -1)[:, :lines, lead + ff + 2 * each * block :]
    every = every.reshape(n, layers, small.shape[1]).astype(F32)
    vecs = []
    for layer in range(layers):
        at, d = 0, {}
        for name, size in zip(SMALL, sizes):
            d[name] = every[:, layer, at : at + size].reshape(1, n * size)
            at += size
        q = d["qvb"].reshape(2 * half_heads, 2, HEAD_DIM)
        q = pick(c, q[:, 0], q[:, 1]).reshape(2, half_width)
        d["qvb_c"] = jnp.stack([q[0], jnp.zeros_like(q[0]), q[1]]).reshape(1, wide)
        f = d["f1b"].reshape(n, 2, halves, deep).transpose(1, 2, 0, 3).reshape(2, halves, block)
        f = pick(c, f[0], f[1])
        if plan.ny == 2:
            f = pick(y, f, f[::-1])
        d["f1b_c"] = f.reshape(1, half_ff)
        vecs.append(d)

    kept_oth = plan.core(kept)
    state = tokens.astype(F32).reshape(rows, width)
    live = lax.broadcasted_iota(jnp.int32, (images, slots), 1) < BUFFER + kept[:, None]
    grad = jnp.where(live[:, :, None], cotangent.astype(F32), 0.0).reshape(rows, width)
    low_own = grad.astype(BF)
    low_oth = plan.core(low_own)
    first_own = norm_rows(state, vecs[0]["ag"], vecs[0]["as"]).astype(BF)

    f32_rows, low_rows = ("rows", (rows, width), F32), ("rows", (rows, width), BF)
    wide_rows, ff_rows = ("rows", (rows, wide), BF), ("rows", (rows, half_ff), BF)
    att_outs = [("image", (images, half_heads, slots, slots), BF), ("rows", (rows, half_width), BF)]
    full_sums = ("full", (8, width), F32)

    def call(body, layer, own, names, blocked, whole, outs, after=(), cost=None):
        chosen = [weight_of(layer, name) for name in names]
        k = kept if own else kept_oth
        return row_call(body, where, k, chosen, blocked, whole, outs, images, slots, after, cost or (BACKWARD if after else FORWARD))

    saved = []
    for layer in range(layers):
        v = vecs[layer]
        first_oth = plan.core(first_own)
        sent, came = mlp_parts[layer].get("sent", ()), mlp_parts[layer].get("came", ())
        proj_oth = call(qkv_body, layer, 0, ["qkv"], [first_oth], [v["qvb_c"]], [wide_rows], sent, FORWARD)[0]
        probs_oth, att_oth, part = call(attend_other, layer, 0, ["proj"], [proj_oth], [], att_outs + [f32_rows])
        part = plan.core(part)
        proj_own = call(qkv_body, layer, 1, ["qkv"], [first_own], [v["qvb_c"]], [wide_rows])[0]
        probs_own, att_own, middle, second_own = call(
            attend_own, layer, 1, ["proj"], [proj_own, part, state], [v["pb"], v["mg"], v["ms"]], att_outs + [f32_rows, low_rows])
        second_oth = plan.core(second_own)
        hid_oth, slope_oth = call(up_body, layer, 0, ["fc1"], [second_oth], [v["f1b_c"]], [ff_rows] * 2)
        if layer + 1 < layers:
            part = call(down_other, layer, 0, ["fc2"], [hid_oth], [], [f32_rows])[0]
            part = plan.core(part)
        hid_own, slope_own = call(up_body, layer, 1, ["fc1"], [second_own], [v["f1b_c"]], [ff_rows] * 2)
        saved.append(
            dict(
                state=state,
                first=(first_own, first_oth),
                proj=(proj_own, proj_oth),
                probs=(probs_own, probs_oth),
                att=(att_own, att_oth),
                middle=middle,
                second=(second_own, second_oth),
                hid=(hid_own, hid_oth),
                slope=(slope_own, slope_oth),
            )
        )
        if layer + 1 < layers:
            w = vecs[layer + 1]
            state, first_own = call(
                down_own, layer, 1, ["fc2"], [hid_own, part, middle], [v["f2b"], w["ag"], w["as"]], [f32_rows, low_rows])

    axes = list(range(1 if plan.ny == 1 else 0, plan.bits + 1))
    last_axis, z_axis, x_axis = 1, plan.bits - 1, plan.bits
    y_axis = 0 if plan.ny == 2 else 2
    orders_f1 = [[y_axis, x_axis, z_axis]] * layers
    orders_q = [[[z_axis, y_axis, x_axis], [x_axis, z_axis, y_axis]]] + [[[x_axis, z_axis, y_axis]]] * (layers - 1)
    own_rows = 2 * deep
    tail = width // plan.ny * HEAD_DIM // own_rows
    fused = n == HEADS
    tail = tail if fused else 0
    big = [[None] * 4 for _ in range(layers)]
    sums = [None] * layers
    f2b_sum = jnp.sum(low_own.astype(F32), axis=0, keepdims=True)

    def end_rest(layer, prev):
        group = terms["q", layer] + [terms["f1", layer]]
        ends["rest", layer] = Ending(plan, where, group, last_axis, own_rows, tail, prev)
        return (ends["rest", layer].sent,)

    def place(layer, before, prev):
        return place_grads(
            plan, where, layer, layers, ends["f2", layer], ends["rest", layer], (deep, width, ff, quarters), before, prev
        )

    ends = {}
    prev = (hid_own,) + mlp_parts[layers - 1].get("came", ())
    terms = {}
    for layer in reversed(range(layers)):
        v, s = vecs[layer], saved[layer]
        top = layer == layers - 1

        def grad_fc2(prev):
            term = chip_grad(plan, where, s["hid"], (low_own, low_oth), 2, prev)
            ends["f2", layer] = ChipEnding(plan, where, term)
            return (term,)

        if top:
            prev = grad_fc2(prev)
        pre_oth, part = call(
            mlp_back_other, layer, 0, ["fc2", "fc1"], [low_oth, s["slope"][1]], [], [ff_rows, f32_rows], prev
        )
        part = plan.core(part)
        prev = (pre_oth,)
        if top:
            last_part = call(down_other, layer, 0, ["fc2"], [s["hid"][1]], [], [f32_rows], prev)[0]
            prev = (last_part,)
            last_part = plan.core(last_part)
        else:
            prev = grad_fc2(prev)
            prev += (terms["f1", layer + 1].step(prev[:1]),)
        pre_own, mid_grad, branch_own, sum1 = call(
            mlp_back_own,
            layer,
            1,
            ["fc2", "fc1"],
            [low_own, s["slope"][0], part, s["middle"], grad],
            [v["mg"]],
            [ff_rows, f32_rows, low_rows, full_sums],
            prev,
        )
        branch_oth = plan.core(branch_own)
        prev = (branch_own,)
        if not top:
            prev += (terms["q", layer + 1][0].step(prev),)
        res1 = weight_grad(
            plan, where, s["second"], (pre_own, pre_oth), 1, orders_f1[layer][0], sums=True, extra=tail, relative=True, after=prev
        )
        prev = tuple(res1[:1]) + ((last_part,) if top else ())
        if not top:
            prev += (terms["q", layer + 1][0].step(prev[:1]),)
            prev += (terms["f1", layer + 1].step(prev[:1]),)
            prev += (ends["f2", layer + 1].core(prev[:1]),)
        dproj_oth, part = call(
            attend_back_other,
            layer,
            0,
            ["proj", "qkv"],
            [branch_oth, s["proj"][1], s["probs"][1]],
            [],
            [wide_rows, f32_rows],
            prev,
        )
        part = plan.core(part)
        prev = (dproj_oth,)
        keep, send = res1[:2]
        if fused:
            keep, send = proj_grad_into(
                plan, where, s["att"], (branch_own, branch_oth), orders_f1[layer][0], keep, send, prev
            )
        else:
            term = t_dot(s["att"][0], branch_own) + t_dot(s["att"][1], branch_oth)
            term = term.astype(BF).reshape(half_heads, HEAD_DIM, width)
            none = jnp.zeros_like(term)
            term = jnp.stack([pick(c, term, none), pick(c, none, term)], axis=1).reshape(width, width)
            term = lax.psum_scatter(term, "shard", scatter_dimension=0, tiled=True)
            big[layer][1] = lax.psum(term, "rep").astype(F32)
        terms["f1", layer] = Term(plan, keep, send, orders_f1[layer])
        prev = (send,)
        if not top:
            prev += (ends["f2", layer + 1].rep(prev[:1]),)
        dproj_own, grad, low_own, sum2 = call(
            attend_back_own,
            layer,
            1,
            ["proj", "qkv"],
            [branch_own, s["proj"][0], s["probs"][0], part, s["state"], mid_grad],
            [v["ag"]],
            [wide_rows, f32_rows, low_rows, full_sums],
            prev,
        )
        prev = (dproj_own,)
        if layer:
            low_oth = plan.core(low_own)
        if not top:
            prev += end_rest(layer + 1, prev[:1])
            prev += (ends["f2", layer].core(prev[:1]),)
        terms["q", layer], q_sums = [], []
        of = len(orders_q[layer])
        for k, order in enumerate(orders_q[layer]):
            resq = weight_grad(
                plan, where, s["first"], (dproj_own, dproj_oth), 1, order[0], sums=True, window=(k, of), after=prev
            )
            terms["q", layer].append(Term(plan, *resq[:2], order))
            q_sums.append(resq[2].reshape(plan.ny, -1))
            prev = (resq[1],) + (() if top else (ends["f2", layer].came,))
        q = jnp.concatenate(q_sums, axis=1).reshape(3, half_heads, 1, HEAD_DIM)
        q = jnp.concatenate([q[:1], q[2:]])
        none = jnp.zeros_like(q)
        q = jnp.concatenate([pick(c, q, none), pick(c, none, q)], axis=2)
        f = res1[2].reshape(halves, block)
        if plan.ny == 2:
            f = pick(y, f, f[::-1])
        none = jnp.zeros_like(f)
        f = jnp.concatenate([pick(c, f, none), pick(c, none, f)], axis=0)
        f = f.reshape(quarters, n, deep).swapaxes(0, 1)
        full = {"ag": sum2[0], "as": sum2[1], "qvb": q, "pb": sum1[2], "mg": sum1[0], "ms": sum1[1], "f1b": f, "f2b": f2b_sum}
        f2b_sum = sum2[2]
        vec = jnp.concatenate([full[name].reshape(n, -1) for name in SMALL], axis=1)
        sums[layer] = vec

    vec = jnp.concatenate(sums, axis=0).reshape(layers, n, -1)
    got_vec = plan.core(vec)
    vec_axes = list(axes)

    def step_vec(prev):
        nonlocal vec, got_vec

        def kernel(where, ins, outs):
            outs[0][...] = ins[0][...] + ins[1][...]

        vec = small_call(kernel, where, [vec, got_vec], [(vec.shape, F32)], prev)[0]
        got_vec = plan.flip(vec, vec_axes.pop(0)) if vec_axes else None
        return (vec,)

    prev += (terms["f1", 0].step(prev[:1]),)
    prev += (ends["rest", 1].core(prev[:1]),)
    w = layers - 1
    mixed = call(
        down_last, w, 1, ["fc2"], [saved[w]["hid"][0], last_part, saved[w]["middle"]], [vecs[w]["f2b"]], [low_rows], prev
    )[0]
    qa, qb = terms["q", 0]
    prev = (qa.step((mixed, ends["rest", 1].came)),)
    prev = (qb.step(prev),)
    prev = step_vec(prev)
    prev = (qa.step(prev),)
    prev = (terms["f1", 0].step(prev),)
    prev = (qb.step(prev),)
    prev = step_vec(prev)
    prev = end_rest(0, prev)
    prev = (ends["rest", 1].rep(prev),)
    prev = (ends["f2", 0].rep(prev),)
    prev = step_vec(prev)
    placed = place(1, None, prev)
    prev = (placed[0],)
    prev = (ends["rest", 0].core(prev + tuple(ends["f2", 0].pair[1:])),)
    prev = step_vec(prev)
    prev = (ends["rest", 0].rep(prev),)
    while got_vec is not None:
        prev = step_vec(prev)
    placed = place(0, placed, prev)
    if plan.ny == 1:
        vec = lax.psum(vec, "rep")
    vec = lax.dynamic_slice_in_dim(vec, shard, 1, axis=1)[:, 0]
    out, at = {}, 0
    for name, size in zip(SMALL, sizes):
        out[name] = vec[:, at : at + size]
        at += size
    qkv_g, fc1_g, fc2_g = placed[:3]
    proj_g = placed[3] if fused else jnp.stack([big[layer][1] for layer in range(layers)])
    return (
        mixed.reshape(images, slots, width),
        grad.reshape(images, slots, width),
        out["ag"],
        out["as"],
        qkv_g,
        out["qvb"],
        proj_g,
        out["pb"],
        out["mg"],
        out["ms"],
        fc1_g,
        out["f1b"],
        fc2_g,
        out["f2b"],
    )


def solution(mesh):
    rows = P(("shard", "rep"), None, None)
    vec = P(None, "shard")
    mat = P(None, "shard", None)
    return jax.shard_map(
        partial(per_device, Plan(mesh)),
        mesh=mesh,
        in_specs=(rows, P(("shard", "rep")), vec, vec, mat, vec, mat, vec, vec, vec, mat, vec, mat, vec, rows),
        out_specs=(rows, rows, vec, vec, mat, vec, mat, vec, vec, vec, mat, vec, mat, vec),
        check_vma=False,
    )
```
